32 devices in a mesh: seg: 16 (over z, x, core), rad: 2 (over y).
Axes of the slice: x: 2, y: 2, z: 4, core: 2. Of those that a mesh axis runs over, the one named last changes fastest.
Arguments:
- start_vector: float32 [16, 3, 2, 384, 768], P('seg', None, 'rad'), may hold values from -12 to 12
- coupling: bfloat16 [16, 3, 3, 2, 384, 768], P('seg', None, None, 'rad'), may hold values from -1.796875 to 1.796875
- advect: float32 [2], P('rad'), may hold values from 0.001 to 0.004
Outputs:
- next_basis: float32 [16, 3, 2, 384, 768], P('seg', None, 'rad')
- hessenberg: float32 [6], replicated
The draws below stay inside these ranges and needn't reach their ends.
All inputs are finite; a program needn't handle non-finite values.
Results may differ from the reference program's by a relative error of at most 0.008.
Values may be sent and summed in bfloat16 or wider, within the bound.
No kernel may reach another device: no remote copies, remote signals or barrier semaphores. Data moves between devices by JAX's collectives and lax.ppermute only.
A program may use at most 128 MiB of HBM per device.

```python
import math
import jax
import jax.numpy as jnp
from jax import lax

M = 384
K = 768
RADIAL_ALL = 256
WINDOW_START = 124
STEPS = 1
NR = 2
SEGS = 16


def draw_start_vector(key, part):
    k_noise, k_scale = jax.random.split(key, 2)
    seg_pos = jnp.arange(SEGS, dtype=jnp.float32) / max(SEGS - 1, 1)
    rad_pos = jnp.arange(NR, dtype=jnp.float32) / max(NR - 1, 1)
    jitter = jax.random.uniform(k_scale, (SEGS, 3, NR), jnp.float32)
    log_scale = math.log(3.0) * (seg_pos[:, None, None] + rad_pos[None, None, :] + jitter) - math.log(9.0)
    scaling = jnp.exp(log_scale)[..., None, None]
    noise_draw = jnp.clip(jax.random.normal(k_noise, (SEGS, 3, NR, M, K), jnp.float32), -4.0, 4.0)
    return (noise_draw * scaling).astype(jnp.float32)


def level_of(stream_key, shape, shards, smallest, largest):
    def one(axis_at, parts):
        steps = jax.random.uniform(jax.random.fold_in(jax.random.fold_in(stream_key, 6), axis_at), (parts,), jnp.float32, smallest / len(shards), largest / len(shards))
        return jnp.repeat(jnp.exp(steps), shape[axis_at] // parts).reshape((-1,) + (1,) * (len(shape) - axis_at - 1))

    level = one(*shards[0])
    for cut in shards[1:]:
        level = level * one(*cut)
    return level


def centred(own_key, dims, deviation, bound, cuts=(), kind=jnp.bfloat16):
    drawn = jax.random.normal(own_key, dims, jnp.float32) * deviation
    if len(cuts) > 0:
        drawn = level_of(own_key, dims, cuts, -0.22, 0.18) * drawn
    return jnp.clip(drawn, min=-bound, max=bound).astype(kind)


def setup_inputs(seed: int = 0) -> dict:
    keys = jax.random.split(jax.random.key(seed), 4)
    return {
        "start_vector": draw_start_vector(jax.random.fold_in(keys[3], 71), 0),
        "coupling": centred(keys[1], (SEGS, 3, 3, NR, M, K), 0.3, 1.796875, ((0, 16), (3, 2))),
        "advect": jnp.clip(jnp.exp(math.log(0.004) - 1.3862944 * jax.random.uniform(keys[2], (NR,), jnp.float32) ** level_of(keys[2], (NR,), ((0, 2),), -0.2, 0.2)), 0.001, 0.004),
    }


RADIAL_GAIN = 0.25
VISC_AXIAL = 4.0
VISC_TURN = 0.05

def make_tables(count):
    index = jnp.arange(count, dtype=jnp.int32)
    half_len = count // 2
    freq = jnp.where(index <= half_len, index, index - half_len)
    phase = freq[:, None] * index[None, :] % count
    angle = 2.0 * math.pi / count * phase.astype(jnp.float32)
    synth = jnp.where((index <= half_len)[:, None], jnp.cos(angle), jnp.sin(angle))
    weight = jnp.where((index == 0) | (index == half_len), 1.0 / count, 2.0 / count).astype(jnp.float32)
    analysis = weight[:, None] * synth
    return (synth.astype(jnp.bfloat16), analysis.astype(jnp.bfloat16), freq)

def make_divisor(radius_index, all_rows, freq_m, freq_k, modes_m, modes_k):
    radius = (radius_index.astype(jnp.float32) + 0.5) / all_rows
    axial = (freq_k.astype(jnp.float32) / (modes_k // 2)) ** 2
    turning = (freq_m.astype(jnp.float32) / (modes_m // 2)) ** 2
    return 1.0 + VISC_AXIAL * axial[None, None, :] + VISC_TURN * turning[None, :, None] / (radius * radius)[:, None, None]

def axial_derivative(field):
    half_len = field.shape[-1] // 2
    wavenum = jnp.arange(1, half_len, dtype=jnp.int32).astype(jnp.float32)
    zeros_col = jnp.zeros(field.shape[:-1] + (1,), jnp.float32)
    return jnp.concatenate([zeros_col, wavenum * field[..., half_len + 1:], zeros_col, -wavenum * field[..., 1:half_len]], axis=-1)

def tangent(field, couple, advect, tables, divisor):
    synth_m, anal_m, synth_k, anal_k = tables
    rounded = field.astype(jnp.bfloat16)
    section_one = jnp.einsum('crmk,kz->crmz', rounded.astype(jnp.float32), synth_k.astype(jnp.float32)).astype(jnp.bfloat16)
    physical = jnp.einsum('mt,crmz->crtz', synth_m.astype(jnp.float32), section_one.astype(jnp.float32))
    mixed = lax.optimization_barrier(jnp.sum(couple.astype(jnp.float32) * physical[None], axis=1)).astype(jnp.bfloat16)
    section_two = jnp.einsum('crtz,kz->crtk', mixed.astype(jnp.float32), anal_k.astype(jnp.float32)).astype(jnp.bfloat16)
    spectral = jnp.einsum('mt,crtk->crmk', anal_m.astype(jnp.float32), section_two.astype(jnp.float32))
    deriv = axial_derivative(field)
    padded = jnp.pad(rounded.astype(jnp.float32), ((0, 0), (1, 1), (0, 0), (0, 0)))
    radial = RADIAL_GAIN * (padded[:, 2:] - 2.0 * padded[:, 1:-1] + padded[:, :-2])
    return (field + spectral - advect[None, :, None, None] * deriv + radial) / divisor

def reference(start_vector, coupling, advect):
    synth_m, anal_m, freq_m = make_tables(M)
    synth_k, anal_k, freq_k = make_tables(K)
    tables = (synth_m, anal_m, synth_k, anal_k)
    radius_index = jnp.arange(NR, dtype=jnp.int32) + WINDOW_START
    divisor = make_divisor(radius_index, RADIAL_ALL, freq_m, freq_k, M, K)
    cells = float(SEGS * 3 * NR * M * K)

    def inner(left, right):
        return jnp.sum(left * right) / cells

    def apply(vector):

        def one(pair):
            field, couple = pair
            for step in range(STEPS):
                field = tangent(field, couple, advect, tables, divisor)
            return field
        stepped = lax.map(one, (vector, coupling))
        return stepped - jnp.roll(vector, -1, axis=0)
    start_norm = jnp.sqrt(inner(start_vector, start_vector))
    basis_one = start_vector / start_norm
    image_one = apply(basis_one)
    upper_one = inner(image_one, basis_one)
    residual_one = image_one - upper_one * basis_one
    lower_one = jnp.sqrt(inner(residual_one, residual_one))
    basis_two = residual_one / lower_one
    image_two = apply(basis_two)
    upper_two = inner(image_two, basis_one)
    middle_two = inner(image_two, basis_two)
    residual_two = image_two - upper_two * basis_one - middle_two * basis_two
    lower_two = jnp.sqrt(inner(residual_two, residual_two))
    next_basis = residual_two / lower_two
    hessenberg = jnp.stack([start_norm, upper_one, lower_one, upper_two, middle_two, lower_two]).astype(jnp.float32)
    return (next_basis, hessenberg)
```

```python
import functools
import math

import jax
import jax.numpy as jnp
from jax import lax
from jax.experimental import pallas as pl
from jax.experimental.pallas import tpu as pltpu
from jax.sharding import PartitionSpec as P

RADIAL_ALL = 256
WINDOW_START = 124
RADIAL_GAIN = 0.25
VISC_AXIAL = 4.0
VISC_TURN = 0.05

F32 = jnp.float32
BF16 = jnp.bfloat16
VMEM_LIMIT = 56 * 1024 * 1024
ROWS = 128
COLS = 256


def kernel_params():
    return pltpu.CompilerParams(vmem_limit_bytes=VMEM_LIMIT)


def cost(flops, moved):
    return pl.CostEstimate(flops=int(flops), bytes_accessed=int(moved), transcendentals=0)


def sine_turns(y):
    x = y * F32(2.0 * math.pi)
    x2 = x * x
    acc = F32(1.0 / 6227020800.0)
    for c in (-1.0 / 39916800.0, 1.0 / 362880.0, -1.0 / 5040.0, 1.0 / 120.0, -1.0 / 6.0, 1.0):
        acc = acc * x2 + F32(c)
    return acc * x


def trig_block(row0, rows, cols, mode_axis, count, weighted):
    half = count // 2
    r = lax.broadcasted_iota(jnp.int32, (rows, cols), 0) + row0
    c = lax.broadcasted_iota(jnp.int32, (rows, cols), 1)
    mode, point = (r, c) if mode_axis == 0 else (c, r)
    is_cos = mode <= half
    freq = jnp.where(is_cos, mode, mode - half).astype(F32)
    phase = freq * point.astype(F32) - jnp.where(is_cos, F32(0.0), F32(count // 4))
    phase = phase - F32(count) * jnp.floor(phase * F32(1.0 / count))
    value = -sine_turns(F32(0.25) - jnp.abs(phase * F32(1.0 / count) - F32(0.5)))
    if weighted:
        edge = (mode == 0) | (mode == half)
        value = value * jnp.where(edge, F32(1.0 / count), F32(2.0 / count))
    return value.astype(BF16)


def tables_kernel(count_m, count_k, synth_k, anal_kt, synth_mt, anal_m):
    def fill(ref, mode_axis, count, weighted):
        @pl.loop(0, count // ROWS)
        def _(i):
            at = pl.multiple_of(i * ROWS, ROWS)
            ref[pl.ds(at, ROWS), :] = trig_block(at, ROWS, count, mode_axis, count, weighted)

    fill(synth_k, 0, count_k, False)
    fill(synth_mt, 1, count_m, False)
    fill(anal_kt, 1, count_k, True)
    fill(anal_m, 0, count_m, True)


def make_tables(count_m, count_k):
    shapes = [(count_k, count_k)] * 2 + [(count_m, count_m)] * 2
    return pl.pallas_call(
        functools.partial(tables_kernel, count_m, count_k),
        out_shape=[jax.ShapeDtypeStruct(s, BF16) for s in shapes],
        compiler_params=kernel_params(),
        cost_estimate=cost(40 * 2 * (count_m**2 + count_k**2), 4 * (count_m**2 + count_k**2)),
        name="tables",
    )()


def transform_kernel(x, couple, synth_k, synth_mt, anal_kt, out, one, phys, mixed):
    chans, modes_m, modes_k = x.shape

    for c in range(chans):

        @pl.loop(0, modes_m // ROWS)
        def _(i):
            at = pl.ds(pl.multiple_of(i * ROWS, ROWS), ROWS)
            one[c, at, :] = jnp.dot(x[c, at, :], synth_k[...], preferred_element_type=F32).astype(BF16)

    @pl.loop(0, modes_k // COLS)
    def _(z):
        zs = pl.ds(pl.multiple_of(z * COLS, COLS), COLS)
        for j in range(chans):
            phys[j] = jnp.dot(synth_mt[...], one[j, :, zs], preferred_element_type=F32)

        @pl.loop(0, modes_m // 16)
        def _(i):
            ts = pl.ds(pl.multiple_of(i * 16, 16), 16)
            parts = [phys[j, ts, :] for j in range(chans)]
            for c in range(chans):
                total = couple[c, 0, ts, zs].astype(F32) * parts[0]
                for j in range(1, chans):
                    total += couple[c, j, ts, zs].astype(F32) * parts[j]
                mixed[c, ts, zs] = total.astype(BF16)

    for c in range(chans):

        @pl.loop(0, modes_m // ROWS)
        def _(i):
            at = pl.ds(pl.multiple_of(i * ROWS, ROWS), ROWS)
            out[c, at, :] = jnp.dot(mixed[c, at, :], anal_kt[...], preferred_element_type=F32).astype(BF16)


def transform(x, couple, tables):
    chans, modes_m, modes_k = x.shape
    synth_k, anal_kt, synth_mt, _ = tables
    size = chans * modes_m * modes_k
    return pl.pallas_call(
        transform_kernel,
        out_shape=jax.ShapeDtypeStruct(x.shape, BF16),
        scratch_shapes=[
            pltpu.VMEM(x.shape, BF16),
            pltpu.VMEM((chans, modes_m, COLS), F32),
            pltpu.VMEM(x.shape, BF16),
        ],
        compiler_params=kernel_params(),
        cost_estimate=cost(2 * size * (2 * modes_k + modes_m), 2 * size * (2 + chans)),
        name="transform",
    )(x, couple, synth_k, synth_mt, anal_kt)


def inverse_divisor(row0, rows, modes_m, modes_k, radius_row):
    m = lax.broadcasted_iota(jnp.int32, (rows, 1), 0) + row0
    k = lax.broadcasted_iota(jnp.int32, (1, modes_k), 1)
    fm = jnp.where(m <= modes_m // 2, m, m - modes_m // 2).astype(F32) / F32(modes_m // 2)
    fk = jnp.where(k <= modes_k // 2, k, k - modes_k // 2).astype(F32) / F32(modes_k // 2)
    radius = (radius_row + F32(0.5)) / F32(RADIAL_ALL)
    turning = F32(VISC_TURN) * fm * fm / (radius * radius)
    return F32(1.0) / (F32(1.0) + F32(VISC_AXIAL) * fk * fk + turning)


BAND = 16


def local_kernel(scal, v, vb, two, anal_m, recv, out, out_b, spec):
    chans, modes_m, modes_k = v.shape
    half = modes_k // 2
    for c in range(chans):
        spec[c] = jnp.dot(anal_m[...], two[c], preferred_element_type=F32)
    wave = lax.broadcasted_iota(jnp.int32, (1, half), 1).astype(F32) * scal[0]

    @pl.loop(0, modes_m // BAND)
    def _(i):
        row0 = pl.multiple_of(i * BAND, BAND)
        at = pl.ds(row0, BAND)
        inv = inverse_divisor(row0, BAND, modes_m, modes_k, scal[1])
        for c in range(chans):
            low, high = v[c, at, :half], v[c, at, half:]
            for lo, own, drift in ((0, low, -wave * high), (half, high, wave * low)):
                ks = slice(lo, lo + half)
                mid = F32(-2.0 * RADIAL_GAIN) * vb[c, at, ks].astype(F32)
                value = (own + spec[c, at, ks] + drift + mid) * inv[:, ks]
                value = value - recv[c, at, ks].astype(F32)
                out[c, at, ks] = value
                out_b[c, at, ks] = value.astype(BF16)


def local_part(scal, v, vb, two, tables, recv):
    size = math.prod(v.shape)
    vm = pl.BlockSpec(memory_space=pltpu.VMEM)
    return pl.pallas_call(
        local_kernel,
        out_shape=[jax.ShapeDtypeStruct(v.shape, F32), jax.ShapeDtypeStruct(v.shape, BF16)],
        in_specs=[pl.BlockSpec(memory_space=pltpu.SMEM)] + [vm] * 5,
        scratch_shapes=[pltpu.VMEM(v.shape, F32)],
        compiler_params=kernel_params(),
        cost_estimate=cost(2 * size * v.shape[1], size * 16),
        name="local_part",
    )(scal, v, vb, two, tables[3], recv)


def first_kernel(count, scal, *refs):
    part, planes, (out, out_b) = refs[0], refs[1 : 1 + count], refs[1 + count :]
    chans, modes_m, modes_k = part.shape

    @pl.loop(0, modes_m // BAND)
    def _(i):
        row0 = pl.multiple_of(i * BAND, BAND)
        at = pl.ds(row0, BAND)
        inv = inverse_divisor(row0, BAND, modes_m, modes_k, scal[1]) * F32(RADIAL_GAIN)
        for c in range(chans):
            near = planes[0][c, at, :].astype(F32)
            for plane in planes[1:]:
                near += plane[c, at, :].astype(F32)
            value = part[c, at, :] + near * inv
            out[c, at, :] = value
            out_b[c, at, :] = value.astype(BF16)


def first_image(scal, part, planes):
    size = math.prod(part.shape)
    vm = pl.BlockSpec(memory_space=pltpu.VMEM)
    return pl.pallas_call(
        functools.partial(first_kernel, len(planes)),
        out_shape=[jax.ShapeDtypeStruct(part.shape, F32), jax.ShapeDtypeStruct(part.shape, BF16)],
        in_specs=[pl.BlockSpec(memory_space=pltpu.SMEM)] + [vm] * (1 + len(planes)),
        compiler_params=kernel_params(),
        cost_estimate=cost(6 * size, size * (10 + 2 * len(planes))),
        name="first_image",
    )(scal, part, *planes)


def second_kernel(count, paired, scal, *refs):
    v, u1, part = refs[:3]
    planes, (out, gram, acc) = refs[3 : 3 + count], refs[3 + count :]
    chans, modes_m, modes_k = part.shape
    acc[...] = jnp.zeros_like(acc)

    @pl.loop(0, modes_m // BAND)
    def _(i):
        row0 = pl.multiple_of(i * BAND, BAND)
        at = pl.ds(row0, BAND)
        inv = inverse_divisor(row0, BAND, modes_m, modes_k, scal[1]) * F32(RADIAL_GAIN)
        if paired:
            other = inverse_divisor(row0, BAND, modes_m, modes_k, scal[2]) * F32(RADIAL_GAIN)
        sums = [jnp.zeros((BAND, modes_k), F32) for _ in range(6)]
        for c in range(chans):
            x0, x1 = v[c, at, :], u1[c, at, :]
            near = planes[0][c, at, :].astype(F32)
            for plane in planes[1:]:
                near += plane[c, at, :].astype(F32)
            if paired:
                near += other * x0
            x2 = part[c, at, :] + near * inv
            out[c, at, :] = x2
            for n, (a, b) in enumerate(((x0, x0), (x0, x1), (x1, x1), (x0, x2), (x1, x2), (x2, x2))):
                sums[n] += a * b
        for n in range(6):
            total = sums[n][:8] + sums[n][8:]
            acc[n] += functools.reduce(
                lambda a, b: a + b, [total[:, k : k + 128] for k in range(0, modes_k, 128)]
            )

    gram[...] = jnp.zeros_like(gram)
    for n in range(6):
        gram[n : n + 1, :] = jnp.broadcast_to(jnp.sum(acc[n], keepdims=True), (1, 128))


def second_image(scal, v, u1, part, planes, paired):
    size = math.prod(part.shape)
    vm = pl.BlockSpec(memory_space=pltpu.VMEM)
    return pl.pallas_call(
        functools.partial(second_kernel, len(planes), paired),
        out_shape=[jax.ShapeDtypeStruct(part.shape, F32), jax.ShapeDtypeStruct((8, 128), F32)],
        in_specs=[pl.BlockSpec(memory_space=pltpu.SMEM)] + [vm] * (3 + len(planes)),
        scratch_shapes=[pltpu.VMEM((6, 8, 128), F32)],
        compiler_params=kernel_params(),
        cost_estimate=cost(18 * size, size * (16 + 2 * len(planes))),
        name="second_image",
    )(scal, v, u1, part, *planes)


def combine_kernel(cells, gram, u0, u1, u2, out, hess):
    chans, modes_m, modes_k = u0.shape
    g = gram[...] * F32(1.0 / cells)
    g00, g01, g11, g02, g12, g22 = (g[n : n + 1, :] for n in range(6))
    n0 = jnp.sqrt(g00)
    h11 = g01 / g00
    s = jnp.sqrt(g11 - h11 * g01)
    h21 = s / n0
    w0 = g02 - h11 * g01
    w1 = g12 - h11 * g11
    ww = g22 - F32(2.0) * h11 * g12 + h11 * h11 * g11
    h12 = w0 / (s * n0)
    h22 = (w1 - h11 * w0) / (s * s)
    h32 = jnp.sqrt(ww / (s * s) - h12 * h12 - h22 * h22)
    scale = F32(1.0) / (s * h32)
    c2 = scale
    c1 = -(h11 + h22) * scale
    c0 = h22 * h11 * scale - h12 / (n0 * h32)
    for n, value in enumerate((n0, h11, h21, h12, h22, h32)):
        hess[n] = value[0, 0]

    @pl.loop(0, modes_m // 8)
    def _(i):
        at = pl.ds(pl.multiple_of(i * 8, 8), 8)
        for c in range(chans):
            for k in range(0, modes_k, 128):
                ks = slice(k, k + 128)
                out[c, at, ks] = c0 * u0[c, at, ks] + c1 * u1[c, at, ks] + c2 * u2[c, at, ks]


def combine(cells, gram, u0, u1, u2):
    size = math.prod(u0.shape)
    vm = pl.BlockSpec(memory_space=pltpu.VMEM)
    return pl.pallas_call(
        functools.partial(combine_kernel, cells),
        out_shape=[jax.ShapeDtypeStruct(u0.shape, F32), jax.ShapeDtypeStruct((6,), F32)],
        in_specs=[vm] * 4,
        out_specs=[vm, pl.BlockSpec(memory_space=pltpu.SMEM)],
        compiler_params=kernel_params(),
        cost_estimate=cost(5 * size, size * 16),
        name="combine",
    )(gram, u0, u1, u2)


def shifted(value, axis, steps):
    count = lax.axis_size(axis)
    return lax.ppermute(value, axis, [(i, (i + steps) % count) for i in range(count)])


def neighbour_planes(value, axis):
    count = lax.axis_size(axis)
    if count == 2:
        return [lax.ppermute(value, axis, [(0, 1), (1, 0)])]
    up = [(i, i + 1) for i in range(count - 1)]
    return [lax.ppermute(value, axis, up), lax.ppermute(value, axis, [(b, a) for a, b in up])]


def sum_everywhere(value, axes):
    count = math.prod(lax.axis_size(a) for a in axes)
    if count & (count - 1):
        return lax.psum(value, axes)
    step = 1
    while step < count:
        width = min(4, count // step)
        terms = [value]
        for n in range(1, width):
            terms.append(lax.ppermute(value, axes, [(i, i ^ (n * step)) for i in range(count)]))
        while len(terms) > 1:
            terms = [terms[i] + terms[i + 1] for i in range(0, len(terms), 2)]
        value = terms[0]
        step *= width
    return value


def on_device(start_vector, coupling, advect):
    rows_here = start_vector.shape[2]
    assert rows_here == 1
    chans, modes_m, modes_k = start_vector.shape[1], start_vector.shape[3], start_vector.shape[4]
    v = start_vector.reshape(chans, modes_m, modes_k)
    couple = coupling.reshape(chans, chans, modes_m, modes_k)
    devices = lax.axis_size("seg") * lax.axis_size("rad")
    cells = float(devices * v.size)
    paired = lax.axis_size("rad") == 2

    plane = (WINDOW_START + lax.axis_index("rad")).astype(F32)
    mate = (WINDOW_START + 1 - lax.axis_index("rad")).astype(F32)
    scal = jnp.stack([advect[0], plane, mate])

    vb = v.astype(BF16)
    near_one = neighbour_planes(vb, "rad")
    next_one = shifted(vb, "seg", -1)
    tables = make_tables(modes_m, modes_k)
    two = transform(vb, couple, tables)
    part, part_b = local_part(scal, v, vb, two, tables, next_one)
    if paired:
        near_two = neighbour_planes(part_b, "rad")
    u1, u1b = first_image(scal, part, near_one)
    if not paired:
        near_two = neighbour_planes(u1b, "rad")
    next_two = shifted(u1b, "seg", -1)
    two = transform(u1b, couple, tables)
    part, _ = local_part(scal, u1, u1b, two, tables, next_two)
    u2, gram = second_image(scal, v, u1, part, near_two, paired)
    gram = sum_everywhere(gram, ("seg", "rad"))
    basis, hess = combine(cells, gram, v, u1, u2)
    return basis.reshape(start_vector.shape), hess


def solution(mesh):
    return jax.shard_map(
        on_device,
        mesh=mesh,
        in_specs=(
            P("seg", None, "rad", None, None),
            P("seg", None, None, "rad", None, None),
            P("rad"),
        ),
        out_specs=(P("seg", None, "rad", None, None), P()),
        check_vma=False,
    )
```

```python
import functools
import math

import jax
import jax.numpy as jnp
from jax import lax
from jax.experimental import pallas as pl
from jax.experimental.pallas import tpu as pltpu
from jax.sharding import PartitionSpec as P

RADIAL_ALL = 256
WINDOW_START = 124
RADIAL_GAIN = 0.25
VISC_AXIAL = 4.0
VISC_TURN = 0.05

F32 = jnp.float32
BF16 = jnp.bfloat16
VMEM_LIMIT = 14 * 1024 * 1024
ROWS = 128
COLS = 256
BAND = 16

IN_SMEM = pl.BlockSpec(memory_space=pltpu.SMEM)
IN_VMEM = pl.BlockSpec(memory_space=pltpu.VMEM)
IN_HBM = pl.BlockSpec(memory_space=pltpu.HBM)


def kernel_call(body, name, args, in_specs, outs, out_specs=None, scratch=()):
    held = [
        a if s is IN_SMEM else pltpu.with_memory_space_constraint(a, s.memory_space)
        for a, s in zip(args, in_specs)
    ]
    more = {} if out_specs is None else {"out_specs": out_specs}
    return pl.pallas_call(
        body,
        out_shape=outs,
        in_specs=in_specs,
        scratch_shapes=list(scratch),
        compiler_params=pltpu.CompilerParams(vmem_limit_bytes=VMEM_LIMIT),
        cost_estimate=pl.CostEstimate(flops=1000, bytes_accessed=1000, transcendentals=0),
        name=name,
        **more,
    )(*held)


def sine_turns(y):
    x = y * F32(2.0 * math.pi)
    x2 = x * x
    acc = F32(1.0 / 6227020800.0)
    for c in (-1.0 / 39916800.0, 1.0 / 362880.0, -1.0 / 5040.0, 1.0 / 120.0, -1.0 / 6.0, 1.0):
        acc = acc * x2 + F32(c)
    return acc * x


def trig_block(row0, rows, cols, mode_axis, count, weighted):
    half = count // 2
    r = lax.broadcasted_iota(jnp.int32, (rows, cols), 0) + row0
    c = lax.broadcasted_iota(jnp.int32, (rows, cols), 1)
    mode, point = (r, c) if mode_axis == 0 else (c, r)
    is_cos = mode <= half
    freq = jnp.where(is_cos, mode, mode - half).astype(F32)
    phase = freq * point.astype(F32) - jnp.where(is_cos, F32(0.0), F32(count // 4))
    phase = phase - F32(count) * jnp.floor(phase * F32(1.0 / count))
    value = -sine_turns(F32(0.25) - jnp.abs(phase * F32(1.0 / count) - F32(0.5)))
    if weighted:
        edge = (mode == 0) | (mode == half)
        value = value * jnp.where(edge, F32(1.0 / count), F32(2.0 / count))
    return value.astype(BF16)


def tables_kernel(count_m, count_k, synth_k, anal_kt, synth_mt, anal_m):
    def fill(ref, mode_axis, count, weighted):
        @pl.loop(0, count // ROWS)
        def _(i):
            at = pl.multiple_of(i * ROWS, ROWS)
            ref[pl.ds(at, ROWS), :] = trig_block(at, ROWS, count, mode_axis, count, weighted)

    fill(synth_k, 0, count_k, False)
    fill(synth_mt, 1, count_m, False)
    fill(anal_kt, 1, count_k, True)
    fill(anal_m, 0, count_m, True)


def make_tables(count_m, count_k):
    shapes = [(count_k, count_k)] * 2 + [(count_m, count_m)] * 2
    return kernel_call(
        functools.partial(tables_kernel, count_m, count_k),
        "tables",
        [],
        [],
        [pltpu.VMEM(s, BF16) for s in shapes],
    )


def channels(refs):
    return [ref.at[i] for ref in refs for i in range(ref.shape[0])]


def taker(refs):
    refs = list(refs)

    def take():
        return refs.pop(0)

    def take_list(count):
        out, refs[:count] = refs[:count], []
        return out

    return take, take_list


def round_kernel(first, v, field, rounded, sem):
    copy = pltpu.make_async_copy(v.at[pl.ds(first, field.shape[0])], field, sem)
    copy.start()
    copy.wait()
    rounded[...] = field[...].astype(BF16)


def take_group(v, first, count):
    shape = (count,) + v.shape[1:]
    return kernel_call(
        functools.partial(round_kernel, first),
        "take_group",
        [v],
        [IN_HBM],
        [pltpu.VMEM(shape, F32), pltpu.VMEM(shape, BF16)],
        scratch=[pltpu.SemaphoreType.DMA],
    )


def transform_kernel(groups, *refs):
    take, take_list = taker(refs)
    x = channels(take_list(groups))
    couple, synth_k, synth_mt, anal_kt, out, one, phys, mixed = take_list(8)
    chans = len(x)
    modes_m, modes_k = x[0].shape

    for c in range(chans):

        @pl.loop(0, modes_m // ROWS)
        def _(i):
            at = pl.ds(pl.multiple_of(i * ROWS, ROWS), ROWS)
            one[c, at, :] = jnp.dot(x[c][at, :], synth_k[...], preferred_element_type=F32).astype(BF16)

    @pl.loop(0, modes_k // COLS)
    def _(z):
        zs = pl.ds(pl.multiple_of(z * COLS, COLS), COLS)
        for j in range(chans):
            phys[j] = jnp.dot(synth_mt[...], one[j, :, zs], preferred_element_type=F32)

        @pl.loop(0, modes_m // BAND)
        def _(i):
            ts = pl.ds(pl.multiple_of(i * BAND, BAND), BAND)
            parts = [phys[j, ts, :] for j in range(chans)]
            for c in range(chans):
                total = couple[c, 0, ts, zs].astype(F32) * parts[0]
                for j in range(1, chans):
                    total += couple[c, j, ts, zs].astype(F32) * parts[j]
                mixed[c, ts, zs] = total.astype(BF16)

    for c in range(chans):

        @pl.loop(0, modes_m // ROWS)
        def _(i):
            at = pl.ds(pl.multiple_of(i * ROWS, ROWS), ROWS)
            out[c, at, :] = jnp.dot(mixed[c, at, :], anal_kt[...], preferred_element_type=F32).astype(BF16)


def transform(x, couple, tables):
    chans, _, modes_m, modes_k = couple.shape
    synth_k, anal_kt, synth_mt, _ = tables
    shape = (chans, modes_m, modes_k)
    return kernel_call(
        functools.partial(transform_kernel, len(x)),
        "transform",
        [*x, couple, synth_k, synth_mt, anal_kt],
        [IN_VMEM] * (len(x) + 4),
        pltpu.VMEM(shape, BF16),
        scratch=[
            pltpu.VMEM(shape, BF16),
            pltpu.VMEM((chans, modes_m, COLS), F32),
            pltpu.VMEM(shape, BF16),
        ],
    )


def inverse_divisor(row0, rows, modes_m, modes_k, radius_row):
    m = lax.broadcasted_iota(jnp.int32, (rows, 1), 0) + row0
    k = lax.broadcasted_iota(jnp.int32, (1, modes_k), 1)
    fm = jnp.where(m <= modes_m // 2, m, m - modes_m // 2).astype(F32) / F32(modes_m // 2)
    fk = jnp.where(k <= modes_k // 2, k, k - modes_k // 2).astype(F32) / F32(modes_k // 2)
    radius = (radius_row + F32(0.5)) / F32(RADIAL_ALL)
    turning = F32(VISC_TURN) * fm * fm / (radius * radius)
    return F32(1.0) / (F32(1.0) + F32(VISC_AXIAL) * fk * fk + turning)


def local_kernel(groups, scal, *refs):
    take, take_list = taker(refs)
    v, vb, recv = (channels(take_list(n)) for n in groups[:3])
    two, anal_m, out = take(), take(), take()
    out_b = channels(take_list(groups[3]))
    spec = take()
    chans, modes_m, modes_k = two.shape
    half = modes_k // 2
    for c in range(chans):
        spec[c] = jnp.dot(anal_m[...], two[c], preferred_element_type=F32)
    wave = lax.broadcasted_iota(jnp.int32, (1, half), 1).astype(F32) * scal[0]

    @pl.loop(0, modes_m // BAND)
    def _(i):
        row0 = pl.multiple_of(i * BAND, BAND)
        at = pl.ds(row0, BAND)
        inv = inverse_divisor(row0, BAND, modes_m, modes_k, scal[1])
        for c in range(chans):
            low, high = v[c][at, :half], v[c][at, half:]
            for lo, own, drift in ((0, low, -wave * high), (half, high, wave * low)):
                ks = slice(lo, lo + half)
                mid = F32(-2.0 * RADIAL_GAIN) * vb[c][at, ks].astype(F32)
                value = (own + spec[c, at, ks] + drift + mid) * inv[:, ks]
                if recv:
                    value = value - recv[c][at, ks].astype(F32)
                out[c, at, ks] = value
                if out_b:
                    out_b[c][at, ks] = value.astype(BF16)


def local_part(scal, v, vb, two, tables, recv=(), sizes=()):
    shape = two.shape
    args = [scal, *v, *vb, *recv, two, tables[3]]
    outs = [pltpu.VMEM(shape, F32)] + [pltpu.VMEM((n,) + shape[1:], BF16) for n in sizes]
    parts = kernel_call(
        functools.partial(local_kernel, (len(v), len(vb), len(recv), len(sizes))),
        "local_part",
        args,
        [IN_SMEM] + [IN_VMEM] * (len(args) - 1),
        outs,
        scratch=[pltpu.VMEM(shape, F32)],
    )
    return parts[0], parts[1:]


def added(planes, c, at):
    near = planes[0][c][at, :].astype(F32)
    for plane in planes[1:]:
        near += plane[c][at, :].astype(F32)
    return near


def first_kernel(groups, sides, scal, part, *refs):
    take, take_list = taker(refs)
    planes = [channels(take_list(groups)) for _ in range(sides)]
    out, out_b = take(), channels(refs[-part.shape[0] :])
    chans, modes_m, modes_k = part.shape

    @pl.loop(0, modes_m // BAND)
    def _(i):
        row0 = pl.multiple_of(i * BAND, BAND)
        at = pl.ds(row0, BAND)
        inv = inverse_divisor(row0, BAND, modes_m, modes_k, scal[1]) * F32(RADIAL_GAIN)
        for c in range(chans):
            value = part[c, at, :] + added(planes, c, at) * inv
            out[c, at, :] = value
            out_b[c][at, :] = value.astype(BF16)


def first_image(scal, part, sides):
    args = [scal, part, *(x for side in sides for x in side)]
    return kernel_call(
        functools.partial(first_kernel, len(sides[0]), len(sides)),
        "first_image",
        args,
        [IN_SMEM] + [IN_VMEM] * (len(args) - 1),
        [pltpu.VMEM(part.shape, F32)]
        + [pltpu.VMEM((1,) + part.shape[1:], BF16)] * part.shape[0],
    )


def second_kernel(first, groups, sides, paired, carried, scal, *refs):
    take, take_list = taker(refs)
    v, recv = (channels(take_list(n)) for n in groups)
    u1, part = take(), take()
    planes = [channels([take()]) for _ in range(sides)]
    before = take() if carried else None
    out, gram, acc = take(), take(), take()
    count, modes_m, modes_k = out.shape
    acc[...] = jnp.zeros_like(acc)

    @pl.loop(0, modes_m // BAND)
    def _(i):
        row0 = pl.multiple_of(i * BAND, BAND)
        at = pl.ds(row0, BAND)
        inv = inverse_divisor(row0, BAND, modes_m, modes_k, scal[1]) * F32(RADIAL_GAIN)
        if paired:
            mate = inverse_divisor(row0, BAND, modes_m, modes_k, scal[2]) * F32(RADIAL_GAIN)
        for g in range(count):
            c = first + g
            x0, x1 = v[c][at, :], u1[c, at, :]
            near = added(planes, g, at)
            if paired:
                near += mate * x0
            x2 = part[c, at, :] - recv[c][at, :].astype(F32) + near * inv
            out[g, at, :] = x2
            for n, (a, b) in enumerate(((x0, x0), (x0, x1), (x1, x1), (x0, x2), (x1, x2), (x2, x2))):
                total = a * b
                total = sum(total[r : r + 8] for r in range(0, BAND, 8))
                acc[n] += sum(total[:, k : k + 128] for k in range(0, modes_k, 128))

    gram[...] = before[...] if carried else jnp.zeros_like(gram)
    for n in range(6):
        gram[n : n + 1, :] += jnp.sum(acc[n], axis=0, keepdims=True)


def second_image(scal, first, v, u1, part, recv, planes, paired, before):
    args = [scal, *v, *recv, u1, part, *planes] + ([] if before is None else [before])
    return kernel_call(
        functools.partial(
            second_kernel, first, (len(v), len(recv)), len(planes), paired, before is not None
        ),
        "second_image",
        args,
        [IN_SMEM] + [IN_VMEM] * (len(args) - 1),
        [pltpu.VMEM(planes[0].shape, F32), pltpu.VMEM((8, 128), F32)],
        scratch=[pltpu.VMEM((6, 8, 128), F32)],
    )


def combine_kernel(cells, terms, counts, *refs):
    take, take_list = taker(refs)
    grams = take_list(terms)
    u0, u1, u2 = (channels(take_list(n)) for n in counts)
    out, hess, held, sems = take_list(4)
    chans, modes_m, modes_k = out.shape
    g = jnp.sum(tree_sum([t[...] for t in grams]), axis=1, keepdims=True) * F32(1.0 / cells)
    g = jnp.broadcast_to(g, (8, 128))
    g00, g01, g11, g02, g12, g22 = (g[n : n + 1, :] for n in range(6))
    n0 = jnp.sqrt(g00)
    h11 = g01 / g00
    s = jnp.sqrt(g11 - h11 * g01)
    h21 = s / n0
    w0 = g02 - h11 * g01
    w1 = g12 - h11 * g11
    ww = g22 - F32(2.0) * h11 * g12 + h11 * h11 * g11
    h12 = w0 / (s * n0)
    h22 = (w1 - h11 * w0) / (s * s)
    h32 = jnp.sqrt(ww / (s * s) - h12 * h12 - h22 * h22)
    c2 = F32(1.0) / (s * h32)
    c1 = -(h11 + h22) * c2
    c0 = h22 * h11 * c2 - h12 / (n0 * h32)
    for n, value in enumerate((n0, h11, h21, h12, h22, h32)):
        hess[n] = value[0, 0]

    copies = []
    for c in range(chans):
        for r in range(0, modes_m, ROWS):

            @pl.loop(r // 8, (r + ROWS) // 8)
            def _(i):
                at = pl.ds(pl.multiple_of(i * 8, 8), 8)
                for k in range(0, modes_k, 128):
                    ks = slice(k, k + 128)
                    held[c, at, ks] = c0 * u0[c][at, ks] + c1 * u1[c][at, ks] + c2 * u2[c][at, ks]

            rows = pl.ds(r, ROWS)
            copy = pltpu.make_async_copy(held.at[c, rows], out.at[c, rows], sems.at[len(copies)])
            copy.start()
            copies.append(copy)
    for copy in copies:
        copy.wait()


def combine(cells, shape, grams, u0, u1, u2):
    chans, modes_m, modes_k = shape
    args = [*grams, *u0, *u1, *u2]
    return kernel_call(
        functools.partial(combine_kernel, cells, len(grams), (len(u0), len(u1), len(u2))),
        "combine",
        args,
        [IN_VMEM] * len(args),
        [jax.ShapeDtypeStruct(shape, F32), jax.ShapeDtypeStruct((6,), F32)],
        out_specs=[IN_HBM, IN_SMEM],
        scratch=[
            pltpu.VMEM(shape, F32),
            pltpu.SemaphoreType.DMA((chans * (modes_m // ROWS),)),
        ],
    )


def shifted(value, axis, steps):
    count = lax.axis_size(axis)
    return lax.ppermute(value, axis, [(i, (i + steps) % count) for i in range(count)])


def neighbour_planes(value, axis):
    count = lax.axis_size(axis)
    if count == 2:
        return [lax.ppermute(value, axis, [(0, 1), (1, 0)])]
    up = [(i, i + 1) for i in range(count - 1)]
    return [lax.ppermute(value, axis, up), lax.ppermute(value, axis, [(b, a) for a, b in up])]


def tree_sum(terms):
    while len(terms) > 1:
        terms = [terms[i] + terms[i + 1] for i in range(0, len(terms), 2)]
    return terms[0]


def exchanged(value, axes):
    count = math.prod(lax.axis_size(a) for a in axes)
    if count & (count - 1):
        return [lax.psum(value, axes)]
    step, terms = 1, [value]
    while step < count:
        value = tree_sum(terms)
        width = min(8, count // step)
        terms = [value] + [
            lax.ppermute(value, axes, [(i, i ^ (n * step)) for i in range(count)])
            for n in range(1, width)
        ]
        step *= width
    return terms


def on_device(start_vector, coupling, advect):
    _, chans, rows_here, modes_m, modes_k = start_vector.shape
    assert rows_here == 1
    start = start_vector.reshape(chans, modes_m, modes_k)
    couple = coupling.reshape(chans, chans, modes_m, modes_k)
    devices = lax.axis_size("seg") * lax.axis_size("rad")
    cells = float(devices * start.size)
    paired = lax.axis_size("rad") == 2

    plane = (WINDOW_START + lax.axis_index("rad")).astype(F32)
    mate = (WINDOW_START + 1 - lax.axis_index("rad")).astype(F32)
    scal = jnp.stack([advect[0], plane, mate])

    sizes_one, sizes_two = (1, chans - 1), (chans - 1, 1)

    u0, u0b, near_one, first = [], [], [], 0
    for size in sizes_one:
        field, rounded = take_group(start, first, size)
        first += size
        u0.append(field)
        u0b.append(rounded)
        near_one.append(neighbour_planes(rounded, "rad"))
    next_one = [shifted(x, "seg", -1) for x in u0b]
    tables = make_tables(modes_m, modes_k)
    two = transform(u0b, couple, tables)
    part, part_b = local_part(scal, u0, u0b, two, tables, next_one, sizes_two)
    if paired:
        near_two = [neighbour_planes(x, "rad") for x in part_b]
    u1, *u1b = first_image(scal, part, list(zip(*near_one)))
    if not paired:
        sizes_two = (1,) * chans
        near_two = [neighbour_planes(x, "rad") for x in u1b]
    next_two = [shifted(x, "seg", -1) for x in u1b]
    two = transform(u1b, couple, tables)
    part, _ = local_part(scal, [u1], u1b, two, tables)
    u2, gram, first = [], None, 0
    for size, planes in zip(sizes_two, near_two):
        field, gram = second_image(scal, first, u0, u1, part, next_two, planes, paired, gram)
        first += size
        u2.append(field)
    basis, hess = combine(cells, start.shape, exchanged(gram, ("seg", "rad")), u0, [u1], u2)
    return basis.reshape(start_vector.shape), hess


def solution(mesh):
    return jax.shard_map(
        on_device,
        mesh=mesh,
        in_specs=(
            P("seg", None, "rad", None, None),
            P("seg", None, None, "rad", None, None),
            P("rad"),
        ),
        out_specs=(P("seg", None, "rad", None, None), P()),
        check_vma=False,
    )
```

```python
import functools
import math

import jax
import jax.numpy as jnp
from jax import lax
from jax.experimental import pallas as pl
from jax.experimental.pallas import tpu as pltpu
from jax.sharding import PartitionSpec as P

RADIAL_ALL = 256
WINDOW_START = 124
RADIAL_GAIN = 0.25
VISC_AXIAL = 4.0
VISC_TURN = 0.05

F32 = jnp.float32
BF16 = jnp.bfloat16
VMEM_LIMIT = 8 * 1024 * 1024
TRANSFORM_LIMIT = 22 * 1024 * 1024
ROWS = 128
COLS = 256
BAND = 16

IN_SMEM = pl.BlockSpec(memory_space=pltpu.SMEM)
IN_VMEM = pl.BlockSpec(memory_space=pltpu.VMEM)
IN_HBM = pl.BlockSpec(memory_space=pltpu.HBM)


def kernel_call(body, name, args, in_specs, outs, out_specs=None, scratch=(), limit=VMEM_LIMIT):
    held = [
        a if s is IN_SMEM else pltpu.with_memory_space_constraint(a, s.memory_space)
        for a, s in zip(args, in_specs)
    ]
    more = {} if out_specs is None else {"out_specs": out_specs}
    return pl.pallas_call(
        body,
        out_shape=outs,
        in_specs=in_specs,
        scratch_shapes=list(scratch),
        compiler_params=pltpu.CompilerParams(vmem_limit_bytes=limit),
        cost_estimate=pl.CostEstimate(flops=1000, bytes_accessed=1000, transcendentals=0),
        name=name,
        **more,
    )(*held)


def sine_turns(y):
    x = y * F32(2.0 * math.pi)
    x2 = x * x
    acc = F32(1.0 / 6227020800.0)
    for c in (-1.0 / 39916800.0, 1.0 / 362880.0, -1.0 / 5040.0, 1.0 / 120.0, -1.0 / 6.0, 1.0):
        acc = acc * x2 + F32(c)
    return acc * x


def trig_block(row0, rows, cols, mode_axis, count, weighted):
    half = count // 2
    r = lax.broadcasted_iota(jnp.int32, (rows, cols), 0) + row0
    c = lax.broadcasted_iota(jnp.int32, (rows, cols), 1)
    mode, point = (r, c) if mode_axis == 0 else (c, r)
    is_cos = mode <= half
    freq = jnp.where(is_cos, mode, mode - half).astype(F32)
    phase = freq * point.astype(F32) - jnp.where(is_cos, F32(0.0), F32(count // 4))
    phase = phase - F32(count) * jnp.floor(phase * F32(1.0 / count))
    value = -sine_turns(F32(0.25) - jnp.abs(phase * F32(1.0 / count) - F32(0.5)))
    if weighted:
        edge = (mode == 0) | (mode == half)
        value = value * jnp.where(edge, F32(1.0 / count), F32(2.0 / count))
    return value.astype(BF16)


def fill_table(ref, mode_axis, weighted):
    count = ref.shape[0]

    @pl.loop(0, count // ROWS)
    def _(i):
        at = pl.multiple_of(i * ROWS, ROWS)
        ref[pl.ds(at, ROWS), :] = trig_block(at, ROWS, count, mode_axis, count, weighted)


def channels(refs):
    return [ref.at[i] for ref in refs for i in range(ref.shape[0])]


def taker(refs):
    refs = list(refs)

    def take():
        return refs.pop(0)

    def take_list(count):
        out, refs[:count] = refs[:count], []
        return out

    return take, take_list


def round_kernel(v, field, whole, *refs):
    pieces, sems = refs[:-1], refs[-1]
    copies = [
        pltpu.make_async_copy(v.at[c], field.at[c], sems.at[c]) for c in range(len(pieces))
    ]
    for copy in copies:
        copy.start()
    for c, copy in enumerate(copies):
        copy.wait()

        @pl.loop(0, v.shape[1] // BAND)
        def _(i):
            at = pl.ds(pl.multiple_of(i * BAND, BAND), BAND)
            value = field[c, at, :].astype(BF16)
            whole[c, at, :] = value
            pieces[c][0, at, :] = value


def take_start(v):
    chans, rest = v.shape[0], v.shape[1:]
    field, whole, *pieces = kernel_call(
        round_kernel,
        "take_start",
        [v],
        [IN_HBM],
        [pltpu.VMEM(v.shape, F32), pltpu.VMEM(v.shape, BF16)]
        + [pltpu.VMEM((1, *rest), BF16)] * chans,
        scratch=[pltpu.SemaphoreType.DMA((chans,))],
    )
    return field, whole, pieces


def transform_kernel(groups, build, *refs):
    take, take_list = taker(refs)
    x = channels(take_list(groups))
    couple_far = take()
    tables_far = None if build else take_list(3)
    out = take()
    if build:
        tables_far, anal_m = take_list(3), take()
    one, phys, mixed, couple, synth_k, synth_mt, anal_kt, sems = take_list(8)
    near = (synth_k, synth_mt, anal_kt)
    chans, modes_m, modes_k = out.shape
    load = pltpu.make_async_copy(couple_far, couple, sems.at[3])
    if build:
        moves = [pltpu.make_async_copy(n, f, sems.at[i]) for i, (n, f) in enumerate(zip(near, tables_far))]
    else:
        moves = [pltpu.make_async_copy(f, n, sems.at[i]) for i, (n, f) in enumerate(zip(near, tables_far))]
        for move in moves[:2]:
            move.start()
    load.start()
    if not build:
        moves[2].start()

    def ready(i, mode_axis, weighted):
        if build:
            fill_table(near[i], mode_axis, weighted)
            moves[i].start()
        else:
            moves[i].wait()

    ready(0, 0, False)
    for c in range(chans):

        @pl.loop(0, modes_m // ROWS)
        def _(i):
            at = pl.ds(pl.multiple_of(i * ROWS, ROWS), ROWS)
            one[c, at, :] = jnp.dot(x[c][at, :], synth_k[...], preferred_element_type=F32).astype(BF16)

    ready(1, 1, False)
    load.wait()

    @pl.loop(0, modes_k // COLS)
    def _(z):
        zs = pl.ds(pl.multiple_of(z * COLS, COLS), COLS)
        for j in range(chans):
            phys[j] = jnp.dot(synth_mt[...], one[j, :, zs], preferred_element_type=F32)

        @pl.loop(0, modes_m // BAND)
        def _(i):
            ts = pl.ds(pl.multiple_of(i * BAND, BAND), BAND)
            parts = [phys[j, ts, :] for j in range(chans)]
            for c in range(chans):
                total = couple[c, 0, ts, zs].astype(F32) * parts[0]
                for j in range(1, chans):
                    total += couple[c, j, ts, zs].astype(F32) * parts[j]
                mixed[c, ts, zs] = total.astype(BF16)

    ready(2, 1, True)
    for c in range(chans):

        @pl.loop(0, modes_m // ROWS)
        def _(i):
            at = pl.ds(pl.multiple_of(i * ROWS, ROWS), ROWS)
            out[c, at, :] = jnp.dot(mixed[c, at, :], anal_kt[...], preferred_element_type=F32).astype(BF16)

    if build:
        fill_table(anal_m, 0, True)
        for move in moves:
            move.wait()


def transform(x, couple, tables=None):
    chans, _, modes_m, modes_k = couple.shape
    shape = (chans, modes_m, modes_k)
    sizes = [(modes_k, modes_k), (modes_m, modes_m), (modes_k, modes_k)]
    build = tables is None
    far = [] if build else list(tables[:3])
    outs, out_specs = [pltpu.VMEM(shape, BF16)], [IN_VMEM]
    if build:
        outs += [pltpu.HBM(n, BF16) for n in sizes] + [pltpu.VMEM((modes_m, modes_m), BF16)]
        out_specs += [IN_HBM] * 3 + [IN_VMEM]
    result = kernel_call(
        functools.partial(transform_kernel, len(x), build),
        "transform",
        [*x, couple, *far],
        [IN_VMEM] * len(x) + [IN_HBM] * (1 + len(far)),
        outs,
        out_specs=out_specs,
        scratch=[
            pltpu.VMEM(shape, BF16),
            pltpu.VMEM((chans, modes_m, COLS), F32),
            pltpu.VMEM(shape, BF16),
            pltpu.VMEM(couple.shape, BF16),
            *[pltpu.VMEM(n, BF16) for n in sizes],
            pltpu.SemaphoreType.DMA((4,)),
        ],
        limit=TRANSFORM_LIMIT,
    )
    return result[0], (result[1:] if build else tables)


def inverse_divisor(row0, rows, modes_m, modes_k, radius_row):
    m = lax.broadcasted_iota(jnp.int32, (rows, 1), 0) + row0
    k = lax.broadcasted_iota(jnp.int32, (1, modes_k), 1)
    fm = jnp.where(m <= modes_m // 2, m, m - modes_m // 2).astype(F32) / F32(modes_m // 2)
    fk = jnp.where(k <= modes_k // 2, k, k - modes_k // 2).astype(F32) / F32(modes_k // 2)
    radius = (radius_row + F32(0.5)) / F32(RADIAL_ALL)
    turning = F32(VISC_TURN) * fm * fm / (radius * radius)
    return F32(1.0) / (F32(1.0) + F32(VISC_AXIAL) * fk * fk + turning)


def local_kernel(groups, last, paired, scal, *refs):
    take, take_list = taker(refs)
    v, vb, recv = (channels(take_list(n)) for n in groups[:3])
    two, anal_m = take(), take()
    if last:
        u0, out, scale, gram, spec, acc = take_list(6)
        acc[...] = jnp.zeros_like(acc)
    else:
        out, out_b, spec = take(), channels(take_list(groups[3])), take()
    chans, modes_m, modes_k = two.shape
    half = modes_k // 2
    for c in range(chans):
        spec[c] = jnp.dot(anal_m[...], two[c], preferred_element_type=F32)
    wave = lax.broadcasted_iota(jnp.int32, (1, half), 1).astype(F32) * scal[0]

    @pl.loop(0, modes_m // BAND)
    def _(i):
        row0 = pl.multiple_of(i * BAND, BAND)
        at = pl.ds(row0, BAND)
        inv = inverse_divisor(row0, BAND, modes_m, modes_k, scal[1])
        if last:
            scale[at, :] = inv * F32(RADIAL_GAIN)
            if paired:
                mate = inverse_divisor(row0, BAND, modes_m, modes_k, scal[2]) * F32(RADIAL_GAIN**2)
        for c in range(chans):
            low, high = v[c][at, :half], v[c][at, half:]
            for lo, own, drift in ((0, low, -wave * high), (half, high, wave * low)):
                ks = slice(lo, lo + half)
                mid = F32(-2.0 * RADIAL_GAIN) * vb[c][at, ks].astype(F32)
                total = own + spec[c, at, ks] + drift + mid
                if last:
                    x0 = u0[c, at, ks]
                    if paired:
                        total += mate[:, ks] * x0
                    for n, (a, b) in enumerate(((x0, x0), (x0, own), (own, own))):
                        add_tile(acc, n, a * b)
                value = total * inv[:, ks] - recv[c][at, ks].astype(F32)
                out[c, at, ks] = value
                if not last:
                    out_b[c][at, ks] = value.astype(BF16)

    if last:
        gram[...] = jnp.zeros_like(gram)
        for n in range(3):
            gram[n : n + 1, :] = jnp.sum(acc[n], axis=0, keepdims=True)


def add_tile(acc, n, value):
    value = sum(value[r : r + 8] for r in range(0, value.shape[0], 8))
    acc[n] += sum(value[:, k : k + 128] for k in range(0, value.shape[1], 128))


def local_first(scal, v, vb, recv, two, tables, sizes):
    shape = two.shape
    args = [scal, *v, *vb, *recv, two, tables[3]]
    part, *part_b = kernel_call(
        functools.partial(local_kernel, (len(v), len(vb), len(recv), len(sizes)), False, False),
        "local_first",
        args,
        [IN_SMEM] + [IN_VMEM] * (len(args) - 1),
        [pltpu.VMEM(shape, F32)] + [pltpu.VMEM((n,) + shape[1:], BF16) for n in sizes],
        scratch=[pltpu.VMEM(shape, F32)],
    )
    return part, part_b


def local_last(scal, v, vb, recv, two, tables, u0, paired):
    shape = two.shape
    args = [scal, *v, *vb, *recv, two, tables[3], u0]
    return kernel_call(
        functools.partial(local_kernel, (len(v), len(vb), len(recv)), True, paired),
        "local_last",
        args,
        [IN_SMEM] + [IN_VMEM] * (len(args) - 1),
        [pltpu.VMEM(shape, F32), pltpu.VMEM(shape[1:], F32), pltpu.VMEM((8, 128), F32)],
        scratch=[pltpu.VMEM(shape, F32), pltpu.VMEM((3, 8, 128), F32)],
    )


def added(planes, c, at):
    near = planes[0][c][at, :].astype(F32)
    for plane in planes[1:]:
        near += plane[c][at, :].astype(F32)
    return near


def first_kernel(groups, sides, scal, part, *refs):
    take, take_list = taker(refs)
    planes = [channels(take_list(groups)) for _ in range(sides)]
    out, out_b = take(), channels(refs[-part.shape[0] :])
    chans, modes_m, modes_k = part.shape

    @pl.loop(0, modes_m // BAND)
    def _(i):
        row0 = pl.multiple_of(i * BAND, BAND)
        at = pl.ds(row0, BAND)
        inv = inverse_divisor(row0, BAND, modes_m, modes_k, scal[1]) * F32(RADIAL_GAIN)
        for c in range(chans):
            value = part[c, at, :] + added(planes, c, at) * inv
            out[c, at, :] = value
            out_b[c][at, :] = value.astype(BF16)


def first_image(scal, part, sides):
    args = [scal, part, *(x for side in sides for x in side)]
    return kernel_call(
        functools.partial(first_kernel, len(sides[0]), len(sides)),
        "first_image",
        args,
        [IN_SMEM] + [IN_VMEM] * (len(args) - 1),
        [pltpu.VMEM(part.shape, F32)]
        + [pltpu.VMEM((1,) + part.shape[1:], BF16)] * part.shape[0],
    )


def second_kernel(first, sides, scale, u0, u1, part, before, *refs):
    take, take_list = taker(refs)
    planes = [channels([take()]) for _ in range(sides)]
    out, gram, acc = take_list(3)
    count, modes_m, _ = out.shape
    acc[...] = jnp.zeros_like(acc)

    @pl.loop(0, modes_m // BAND)
    def _(i):
        at = pl.ds(pl.multiple_of(i * BAND, BAND), BAND)
        for g in range(count):
            x2 = part[first + g, at, :] + added(planes, g, at) * scale[at, :]
            out[g, at, :] = x2
            for n, x in enumerate((u0[first + g, at, :], u1[first + g, at, :], x2)):
                add_tile(acc, n, x * x2)

    rows = [jnp.sum(acc[n], axis=0, keepdims=True) for n in range(3)]
    total = before[...] + jnp.concatenate([jnp.zeros((3, 128), F32), *rows, jnp.zeros((2, 128), F32)], axis=0)
    gram[...] = jnp.broadcast_to(total, gram.shape)


def second_image(first, scale, u0, u1, part, before, planes, slots=None):
    tile = (8, 128) if slots is None else (slots, 8, 128)
    args = [scale, u0, u1, part, before, *planes]
    return kernel_call(
        functools.partial(second_kernel, first, len(planes)),
        "second_image",
        args,
        [IN_VMEM] * len(args),
        [pltpu.VMEM(planes[0].shape, F32), pltpu.VMEM(tile, F32)],
        scratch=[pltpu.VMEM((3, 8, 128), F32)],
    )


def combine_kernel(cells, counts, grams, *refs):
    take, take_list = taker(refs)
    u0, u1, u2 = (channels(take_list(n)) for n in counts)
    out, hess, held, sems = take_list(4)
    chans, modes_m, modes_k = out.shape
    g = jnp.sum(jnp.sum(grams[...], axis=0), axis=1, keepdims=True) * F32(1.0 / cells)
    g = jnp.broadcast_to(g, (8, 128))
    g00, g01, g11, g02, g12, g22 = (g[n : n + 1, :] for n in range(6))
    n0 = jnp.sqrt(g00)
    h11 = g01 / g00
    s = jnp.sqrt(g11 - h11 * g01)
    h21 = s / n0
    w0 = g02 - h11 * g01
    w1 = g12 - h11 * g11
    ww = g22 - F32(2.0) * h11 * g12 + h11 * h11 * g11
    h12 = w0 / (s * n0)
    h22 = (w1 - h11 * w0) / (s * s)
    h32 = jnp.sqrt(ww / (s * s) - h12 * h12 - h22 * h22)
    c2 = F32(1.0) / (s * h32)
    c1 = -(h11 + h22) * c2
    c0 = h22 * h11 * c2 - h12 / (n0 * h32)
    for n, value in enumerate((n0, h11, h21, h12, h22, h32)):
        hess[n] = value[0, 0]

    copies = []
    for c in range(chans):
        for r in range(0, modes_m, ROWS):

            @pl.loop(r // 8, (r + ROWS) // 8)
            def _(i):
                at = pl.ds(pl.multiple_of(i * 8, 8), 8)
                for k in range(0, modes_k, 128):
                    ks = slice(k, k + 128)
                    held[c, at, ks] = c0 * u0[c][at, ks] + c1 * u1[c][at, ks] + c2 * u2[c][at, ks]

            rows = pl.ds(r, ROWS)
            copy = pltpu.make_async_copy(held.at[c, rows], out.at[c, rows], sems.at[len(copies)])
            copy.start()
            copies.append(copy)
    for copy in copies:
        copy.wait()


def combine(cells, shape, grams, u0, u1, u2):
    chans, modes_m, modes_k = shape
    args = [grams, *u0, *u1, *u2]
    return kernel_call(
        functools.partial(combine_kernel, cells, (len(u0), len(u1), len(u2))),
        "combine",
        args,
        [IN_VMEM] * len(args),
        [jax.ShapeDtypeStruct(shape, F32), jax.ShapeDtypeStruct((6,), F32)],
        out_specs=[IN_HBM, IN_SMEM],
        scratch=[
            pltpu.VMEM(shape, F32),
            pltpu.SemaphoreType.DMA((chans * (modes_m // ROWS),)),
        ],
    )


def shifted(value, axis, steps):
    count = lax.axis_size(axis)
    return lax.ppermute(value, axis, [(i, (i + steps) % count) for i in range(count)])


def neighbour_planes(value, axis):
    count = lax.axis_size(axis)
    if count == 2:
        return [lax.ppermute(value, axis, [(0, 1), (1, 0)])]
    up = [(i, i + 1) for i in range(count - 1)]
    return [lax.ppermute(value, axis, up), lax.ppermute(value, axis, [(b, a) for a, b in up])]


def on_device(start_vector, coupling, advect):
    _, chans, rows_here, modes_m, modes_k = start_vector.shape
    assert rows_here == 1
    start = start_vector.reshape(chans, modes_m, modes_k)
    couple = coupling.reshape(chans, chans, modes_m, modes_k)
    devices = lax.axis_size("seg") * lax.axis_size("rad")
    cells = float(devices * start.size)
    paired = lax.axis_size("rad") == 2

    plane = (WINDOW_START + lax.axis_index("rad")).astype(F32)
    mate = (WINDOW_START + 1 - lax.axis_index("rad")).astype(F32)
    scal = jnp.stack([advect[0], plane, mate])

    sizes = (chans - 1, 1) if paired else (1,) * chans

    u0, u0b, pieces = take_start(start)
    near_one = neighbour_planes(u0b, "rad")
    next_one = [shifted(x, "seg", -1) for x in pieces]
    two, tables = transform([u0b], couple)
    part, part_b = local_first(scal, [u0], [u0b], next_one, two, tables, sizes)
    if paired:
        near_two = [neighbour_planes(x, "rad") for x in part_b]
    u1, *u1b = first_image(scal, part, [[x] for x in near_one])
    if not paired:
        near_two = [neighbour_planes(x, "rad") for x in u1b]
    next_two = [shifted(x, "seg", -1) for x in u1b]
    two, _ = transform(u1b, couple, tables)
    part, scale, gram = local_last(scal, [u1], u1b, next_two, two, tables, u0, paired)
    u2, first = [], 0
    for size, planes in zip(sizes, near_two):
        slots = devices if first + size == chans else None
        field, gram = second_image(first, scale, u0, u1, part, gram, planes, slots)
        first += size
        u2.append(field)
    grams = lax.all_to_all(gram, ("seg", "rad"), 0, 0)
    basis, hess = combine(cells, start.shape, grams, [u0], [u1], u2)
    return basis.reshape(start_vector.shape), hess


def solution(mesh):
    return jax.shard_map(
        on_device,
        mesh=mesh,
        in_specs=(
            P("seg", None, "rad", None, None),
            P("seg", None, None, "rad", None, None),
            P("rad"),
        ),
        out_specs=(P("seg", None, "rad", None, None), P()),
        check_vma=False,
    )
```

```python
import functools
import math

import jax
import jax.numpy as jnp
from jax import lax
from jax.experimental import pallas as pl
from jax.experimental.pallas import tpu as pltpu
from jax.sharding import PartitionSpec as P

RADIAL_ALL = 256
WINDOW_START = 124
RADIAL_GAIN = 0.25
VISC_AXIAL = 4.0
VISC_TURN = 0.05

F32 = jnp.float32
BF16 = jnp.bfloat16
VMEM_LIMIT = 8 * 1024 * 1024
TRANSFORM_LIMIT = 22 * 1024 * 1024
ROWS = 128
COLS = 256
BAND = 16

IN_SMEM = pl.BlockSpec(memory_space=pltpu.SMEM)
IN_VMEM = pl.BlockSpec(memory_space=pltpu.VMEM)
IN_HBM = pl.BlockSpec(memory_space=pltpu.HBM)


def kernel_call(body, name, args, in_specs, outs, out_specs=None, scratch=(), limit=VMEM_LIMIT):
    held = [
        a if s is IN_SMEM else pltpu.with_memory_space_constraint(a, s.memory_space)
        for a, s in zip(args, in_specs)
    ]
    more = {} if out_specs is None else {"out_specs": out_specs}
    return pl.pallas_call(
        body,
        out_shape=outs,
        in_specs=in_specs,
        scratch_shapes=list(scratch),
        compiler_params=pltpu.CompilerParams(vmem_limit_bytes=limit),
        cost_estimate=pl.CostEstimate(flops=1000, bytes_accessed=1000, transcendentals=0),
        name=name,
        **more,
    )(*held)


def sine_turns(y):
    x = y * F32(2.0 * math.pi)
    x2 = x * x
    acc = F32(1.0 / 6227020800.0)
    for c in (-1.0 / 39916800.0, 1.0 / 362880.0, -1.0 / 5040.0, 1.0 / 120.0, -1.0 / 6.0, 1.0):
        acc = acc * x2 + F32(c)
    return acc * x


def trig_block(row0, rows, cols, mode_axis, count, weighted):
    half = count // 2
    r = lax.broadcasted_iota(jnp.int32, (rows, cols), 0) + row0
    c = lax.broadcasted_iota(jnp.int32, (rows, cols), 1)
    mode, point = (r, c) if mode_axis == 0 else (c, r)
    is_cos = mode <= half
    freq = jnp.where(is_cos, mode, mode - half).astype(F32)
    phase = freq * point.astype(F32) - jnp.where(is_cos, F32(0.0), F32(count // 4))
    phase = phase - F32(count) * jnp.floor(phase * F32(1.0 / count))
    value = -sine_turns(F32(0.25) - jnp.abs(phase * F32(1.0 / count) - F32(0.5)))
    if weighted:
        edge = (mode == 0) | (mode == half)
        value = value * jnp.where(edge, F32(1.0 / count), F32(2.0 / count))
    return value.astype(BF16)


def fill_table(ref, mode_axis, weighted):
    count = ref.shape[0]

    @pl.loop(0, count // ROWS)
    def _(i):
        at = pl.multiple_of(i * ROWS, ROWS)
        ref[pl.ds(at, ROWS), :] = trig_block(at, ROWS, count, mode_axis, count, weighted)


def channels(refs):
    return [ref.at[i] for ref in refs for i in range(ref.shape[0])]


def taker(refs):
    refs = list(refs)

    def take():
        return refs.pop(0)

    def take_list(count):
        out, refs[:count] = refs[:count], []
        return out

    return take, take_list


def hold_kernel(v, whole, field, *refs):
    pieces, sem = refs[:-1], refs[-1]
    copy = pltpu.make_async_copy(v, field, sem)
    copy.start()
    for c, piece in enumerate(pieces):
        piece[0] = whole[c]
    copy.wait()


def hold_start(v, whole):
    chans, rest = v.shape[0], v.shape[1:]
    field, *pieces = kernel_call(
        hold_kernel,
        "hold_start",
        [v, whole],
        [IN_HBM, IN_VMEM],
        [pltpu.VMEM(v.shape, F32)] + [pltpu.VMEM((1, *rest), BF16)] * chans,
        scratch=[pltpu.SemaphoreType.DMA],
    )
    return field, pieces


def transform_kernel(groups, build, *refs):
    take, take_list = taker(refs)
    x = channels(take_list(groups))
    couple_far = take()
    tables_far = None if build else take_list(3)
    out = take()
    if build:
        tables_far, anal_m = take_list(3), take()
    one, phys, mixed, couple, synth_k, synth_mt, anal_kt, sems = take_list(8)
    near = (synth_k, synth_mt, anal_kt)
    chans, modes_m, modes_k = out.shape
    load = pltpu.make_async_copy(couple_far, couple, sems.at[3])
    if build:
        moves = [pltpu.make_async_copy(n, f, sems.at[i]) for i, (n, f) in enumerate(zip(near, tables_far))]
    else:
        moves = [pltpu.make_async_copy(f, n, sems.at[i]) for i, (n, f) in enumerate(zip(near, tables_far))]
        for move in moves[:2]:
            move.start()
    load.start()
    if not build:
        moves[2].start()

    def ready(i, mode_axis, weighted):
        if build:
            fill_table(near[i], mode_axis, weighted)
            moves[i].start()
        else:
            moves[i].wait()

    ready(0, 0, False)
    for c in range(chans):

        @pl.loop(0, modes_m // ROWS)
        def _(i):
            at = pl.ds(pl.multiple_of(i * ROWS, ROWS), ROWS)
            one[c, at, :] = jnp.dot(x[c][at, :], synth_k[...], preferred_element_type=F32).astype(BF16)

    ready(1, 1, False)
    load.wait()

    @pl.loop(0, modes_k // COLS)
    def _(z):
        zs = pl.ds(pl.multiple_of(z * COLS, COLS), COLS)
        for j in range(chans):
            phys[j] = jnp.dot(synth_mt[...], one[j, :, zs], preferred_element_type=F32)

        @pl.loop(0, modes_m // BAND)
        def _(i):
            ts = pl.ds(pl.multiple_of(i * BAND, BAND), BAND)
            parts = [phys[j, ts, :] for j in range(chans)]
            for c in range(chans):
                total = couple[c, 0, ts, zs].astype(F32) * parts[0]
                for j in range(1, chans):
                    total += couple[c, j, ts, zs].astype(F32) * parts[j]
                mixed[c, ts, zs] = total.astype(BF16)

    ready(2, 1, True)
    for c in range(chans):

        @pl.loop(0, modes_m // ROWS)
        def _(i):
            at = pl.ds(pl.multiple_of(i * ROWS, ROWS), ROWS)
            out[c, at, :] = jnp.dot(mixed[c, at, :], anal_kt[...], preferred_element_type=F32).astype(BF16)

    if build:
        fill_table(anal_m, 0, True)
        for move in moves:
            move.wait()


def transform(x, couple, tables=None):
    chans, _, modes_m, modes_k = couple.shape
    shape = (chans, modes_m, modes_k)
    sizes = [(modes_k, modes_k), (modes_m, modes_m), (modes_k, modes_k)]
    build = tables is None
    far = [] if build else list(tables[:3])
    outs, out_specs = [pltpu.VMEM(shape, BF16)], [IN_VMEM]
    if build:
        outs += [pltpu.HBM(n, BF16) for n in sizes] + [pltpu.VMEM((modes_m, modes_m), BF16)]
        out_specs += [IN_HBM] * 3 + [IN_VMEM]
    result = kernel_call(
        functools.partial(transform_kernel, len(x), build),
        "transform",
        [*x, couple, *far],
        [IN_VMEM] * len(x) + [IN_HBM] * (1 + len(far)),
        outs,
        out_specs=out_specs,
        scratch=[
            pltpu.VMEM(shape, BF16),
            pltpu.VMEM((chans, modes_m, COLS), F32),
            pltpu.VMEM(shape, BF16),
            pltpu.VMEM(couple.shape, BF16),
            *[pltpu.VMEM(n, BF16) for n in sizes],
            pltpu.SemaphoreType.DMA((4,)),
        ],
        limit=TRANSFORM_LIMIT,
    )
    return result[0], (result[1:] if build else tables)


def inverse_divisor(row0, rows, modes_m, modes_k, radius_row):
    m = lax.broadcasted_iota(jnp.int32, (rows, 1), 0) + row0
    k = lax.broadcasted_iota(jnp.int32, (1, modes_k), 1)
    fm = jnp.where(m <= modes_m // 2, m, m - modes_m // 2).astype(F32) / F32(modes_m // 2)
    fk = jnp.where(k <= modes_k // 2, k, k - modes_k // 2).astype(F32) / F32(modes_k // 2)
    radius = (radius_row + F32(0.5)) / F32(RADIAL_ALL)
    turning = F32(VISC_TURN) * fm * fm / (radius * radius)
    return F32(1.0) / (F32(1.0) + F32(VISC_AXIAL) * fk * fk + turning)


def local_kernel(groups, last, paired, scal, *refs):
    take, take_list = taker(refs)
    v, vb, recv = (channels(take_list(n)) for n in groups[:3])
    two, anal_m = take(), take()
    if last:
        u0, out, scale, gram, spec, acc = take_list(6)
        acc[...] = jnp.zeros_like(acc)
    else:
        out, out_b, spec = take(), channels(take_list(groups[3])), take()
    chans, modes_m, modes_k = two.shape
    half = modes_k // 2
    for c in range(chans):
        spec[c] = jnp.dot(anal_m[...], two[c], preferred_element_type=F32)
    wave = lax.broadcasted_iota(jnp.int32, (1, half), 1).astype(F32) * scal[0]

    @pl.loop(0, modes_m // BAND)
    def _(i):
        row0 = pl.multiple_of(i * BAND, BAND)
        at = pl.ds(row0, BAND)
        inv = inverse_divisor(row0, BAND, modes_m, modes_k, scal[1])
        if last:
            scale[at, :] = inv * F32(RADIAL_GAIN)
            if paired:
                mate = inverse_divisor(row0, BAND, modes_m, modes_k, scal[2]) * F32(RADIAL_GAIN**2)
        for c in range(chans):
            low, high = v[c][at, :half], v[c][at, half:]
            for lo, own, drift in ((0, low, -wave * high), (half, high, wave * low)):
                ks = slice(lo, lo + half)
                mid = F32(-2.0 * RADIAL_GAIN) * vb[c][at, ks].astype(F32)
                total = own + spec[c, at, ks] + drift + mid
                if last:
                    x0 = u0[c, at, ks]
                    if paired:
                        total += mate[:, ks] * x0
                    for n, (a, b) in enumerate(((x0, x0), (x0, own), (own, own))):
                        add_tile(acc, n, a * b)
                value = total * inv[:, ks] - recv[c][at, ks].astype(F32)
                out[c, at, ks] = value
                if not last:
                    out_b[c][at, ks] = value.astype(BF16)

    if last:
        gram[...] = jnp.zeros_like(gram)
        for n in range(3):
            gram[n : n + 1, :] = jnp.sum(acc[n], axis=0, keepdims=True)


def add_tile(acc, n, value):
    value = sum(value[r : r + 8] for r in range(0, value.shape[0], 8))
    acc[n] += sum(value[:, k : k + 128] for k in range(0, value.shape[1], 128))


def local_first(scal, v, vb, recv, two, tables, sizes):
    shape = two.shape
    args = [scal, *v, *vb, *recv, two, tables[3]]
    part, *part_b = kernel_call(
        functools.partial(local_kernel, (len(v), len(vb), len(recv), len(sizes)), False, False),
        "local_first",
        args,
        [IN_SMEM] + [IN_VMEM] * (len(args) - 1),
        [pltpu.VMEM(shape, F32)] + [pltpu.VMEM((n,) + shape[1:], BF16) for n in sizes],
        scratch=[pltpu.VMEM(shape, F32)],
    )
    return part, part_b


def local_last(scal, v, vb, recv, two, tables, u0, paired):
    shape = two.shape
    args = [scal, *v, *vb, *recv, two, tables[3], u0]
    return kernel_call(
        functools.partial(local_kernel, (len(v), len(vb), len(recv)), True, paired),
        "local_last",
        args,
        [IN_SMEM] + [IN_VMEM] * (len(args) - 1),
        [pltpu.VMEM(shape, F32), pltpu.VMEM(shape[1:], F32), pltpu.VMEM((8, 128), F32)],
        scratch=[pltpu.VMEM(shape, F32), pltpu.VMEM((3, 8, 128), F32)],
    )


def added(planes, c, at):
    near = planes[0][c][at, :].astype(F32)
    for plane in planes[1:]:
        near += plane[c][at, :].astype(F32)
    return near


def first_kernel(groups, sides, scal, part, *refs):
    take, take_list = taker(refs)
    planes = [channels(take_list(groups)) for _ in range(sides)]
    out, out_b = take(), channels(refs[-part.shape[0] :])
    chans, modes_m, modes_k = part.shape

    @pl.loop(0, modes_m // BAND)
    def _(i):
        row0 = pl.multiple_of(i * BAND, BAND)
        at = pl.ds(row0, BAND)
        inv = inverse_divisor(row0, BAND, modes_m, modes_k, scal[1]) * F32(RADIAL_GAIN)
        for c in range(chans):
            value = part[c, at, :] + added(planes, c, at) * inv
            out[c, at, :] = value
            out_b[c][at, :] = value.astype(BF16)


def first_image(scal, part, sides):
    args = [scal, part, *(x for side in sides for x in side)]
    return kernel_call(
        functools.partial(first_kernel, len(sides[0]), len(sides)),
        "first_image",
        args,
        [IN_SMEM] + [IN_VMEM] * (len(args) - 1),
        [pltpu.VMEM(part.shape, F32)]
        + [pltpu.VMEM((1,) + part.shape[1:], BF16)] * part.shape[0],
    )


def second_kernel(first, sides, done, scale, u0, u1, part, before, *refs):
    take, take_list = taker(refs)
    planes = [channels([take()]) for _ in range(sides)]
    out, gram, acc = take_list(3)
    count, modes_m, _ = out.shape
    acc[...] = jnp.zeros_like(acc)

    @pl.loop(0, modes_m // BAND)
    def _(i):
        at = pl.ds(pl.multiple_of(i * BAND, BAND), BAND)
        for g in range(count):
            x2 = part[first + g, at, :] + added(planes, g, at) * scale[at, :]
            out[g, at, :] = x2
            for n, x in enumerate((u0[first + g, at, :], u1[first + g, at, :], x2)):
                add_tile(acc, n, x * x2)

    rows = [jnp.sum(acc[n], axis=0, keepdims=True) for n in range(3)]
    total = before[...] + jnp.concatenate([jnp.zeros((3, 128), F32), *rows, jnp.zeros((2, 128), F32)], axis=0)
    if done:
        total = jnp.sum(total, axis=1, keepdims=True)
        total = jnp.sum(jnp.where(on_diagonal(), total, F32(0.0)), axis=0, keepdims=True)
    gram[...] = jnp.broadcast_to(total, gram.shape)


def on_diagonal():
    rows, lanes = (lax.broadcasted_iota(jnp.int32, (8, 128), n) for n in (0, 1))
    return rows == lanes


def second_image(first, scale, u0, u1, part, before, planes, slots=None):
    done = slots is not None
    tile = (slots, 128) if done else (8, 128)
    args = [scale, u0, u1, part, before, *planes]
    return kernel_call(
        functools.partial(second_kernel, first, len(planes), done),
        "second_image",
        args,
        [IN_VMEM] * len(args),
        [pltpu.VMEM(planes[0].shape, F32), pltpu.VMEM(tile, F32)],
        scratch=[pltpu.VMEM((3, 8, 128), F32)],
    )


def combine_kernel(cells, counts, grams, *refs):
    take, take_list = taker(refs)
    u0, u1, u2 = (channels(take_list(n)) for n in counts)
    out, hess, held, sems = take_list(4)
    chans, modes_m, modes_k = out.shape
    g = jnp.sum(grams[...], axis=0, keepdims=True) * F32(1.0 / cells)
    g = jnp.sum(jnp.where(on_diagonal(), g, F32(0.0)), axis=1, keepdims=True)
    g = jnp.broadcast_to(g, (8, 128))
    g00, g01, g11, g02, g12, g22 = (g[n : n + 1, :] for n in range(6))
    n0 = jnp.sqrt(g00)
    h11 = g01 / g00
    s = jnp.sqrt(g11 - h11 * g01)
    h21 = s / n0
    w0 = g02 - h11 * g01
    w1 = g12 - h11 * g11
    ww = g22 - F32(2.0) * h11 * g12 + h11 * h11 * g11
    h12 = w0 / (s * n0)
    h22 = (w1 - h11 * w0) / (s * s)
    h32 = jnp.sqrt(ww / (s * s) - h12 * h12 - h22 * h22)
    c2 = F32(1.0) / (s * h32)
    c1 = -(h11 + h22) * c2
    c0 = h22 * h11 * c2 - h12 / (n0 * h32)
    for n, value in enumerate((n0, h11, h21, h12, h22, h32)):
        hess[n] = value[0, 0]

    wide = [jnp.concatenate([x] * (modes_k // 128), axis=1) for x in (c0, c1, c2)]
    copies = []
    for c in range(chans):
        for r in range(0, modes_m, ROWS):

            @pl.loop(r // BAND, (r + ROWS) // BAND)
            def _(i):
                at = pl.ds(pl.multiple_of(i * BAND, BAND), BAND)
                held[c, at, :] = wide[0] * u0[c][at, :] + wide[1] * u1[c][at, :] + wide[2] * u2[c][at, :]

            rows = pl.ds(r, ROWS)
            copy = pltpu.make_async_copy(held.at[c, rows], out.at[c, rows], sems.at[len(copies)])
            copy.start()
            copies.append(copy)
    for copy in copies:
        copy.wait()


def combine(cells, shape, grams, u0, u1, u2):
    chans, modes_m, modes_k = shape
    args = [grams, *u0, *u1, *u2]
    return kernel_call(
        functools.partial(combine_kernel, cells, (len(u0), len(u1), len(u2))),
        "combine",
        args,
        [IN_VMEM] * len(args),
        [jax.ShapeDtypeStruct(shape, F32), jax.ShapeDtypeStruct((6,), F32)],
        out_specs=[IN_HBM, IN_SMEM],
        scratch=[
            pltpu.VMEM(shape, F32),
            pltpu.SemaphoreType.DMA((chans * (modes_m // ROWS),)),
        ],
    )


def shifted(value, axis, steps):
    count = lax.axis_size(axis)
    return lax.ppermute(value, axis, [(i, (i + steps) % count) for i in range(count)])


def neighbour_planes(value, axis):
    count = lax.axis_size(axis)
    if count == 2:
        return [lax.ppermute(value, axis, [(0, 1), (1, 0)])]
    up = [(i, i + 1) for i in range(count - 1)]
    return [lax.ppermute(value, axis, up), lax.ppermute(value, axis, [(b, a) for a, b in up])]


def on_device(start_vector, coupling, advect):
    _, chans, rows_here, modes_m, modes_k = start_vector.shape
    assert rows_here == 1
    start = start_vector.reshape(chans, modes_m, modes_k)
    couple = coupling.reshape(chans, chans, modes_m, modes_k)
    devices = lax.axis_size("seg") * lax.axis_size("rad")
    cells = float(devices * start.size)
    paired = lax.axis_size("rad") == 2

    plane = (WINDOW_START + lax.axis_index("rad")).astype(F32)
    mate = (WINDOW_START + 1 - lax.axis_index("rad")).astype(F32)
    scal = jnp.stack([advect[0], plane, mate])

    sizes = (chans - 1, 1) if paired else (1,) * chans

    u0b = start.astype(BF16)
    near_one = neighbour_planes(u0b, "rad")
    u0, pieces = hold_start(start, u0b)
    next_one = [shifted(x, "seg", -1) for x in pieces]
    two, tables = transform([u0b], couple)
    part, part_b = local_first(scal, [u0], [u0b], next_one, two, tables, sizes)
    if paired:
        near_two = [neighbour_planes(x, "rad") for x in part_b]
    u1, *u1b = first_image(scal, part, [[x] for x in near_one])
    if not paired:
        near_two = [neighbour_planes(x, "rad") for x in u1b]
    next_two = [shifted(x, "seg", -1) for x in u1b]
    two, _ = transform(u1b, couple, tables)
    part, scale, gram = local_last(scal, [u1], u1b, next_two, two, tables, u0, paired)
    u2, first = [], 0
    for size, planes in zip(sizes, near_two):
        slots = devices if first + size == chans else None
        field, gram = second_image(first, scale, u0, u1, part, gram, planes, slots)
        first += size
        u2.append(field)
    grams = lax.all_to_all(gram, ("seg", "rad"), 0, 0)
    basis, hess = combine(cells, start.shape, grams, [u0], [u1], u2)
    return basis.reshape(start_vector.shape), hess


def solution(mesh):
    return jax.shard_map(
        on_device,
        mesh=mesh,
        in_specs=(
            P("seg", None, "rad", None, None),
            P("seg", None, None, "rad", None, None),
            P("rad"),
        ),
        out_specs=(P("seg", None, "rad", None, None), P()),
        check_vma=False,
    )
```

```python
import functools
import math

import jax
import jax.numpy as jnp
from jax import lax
from jax.experimental import pallas as pl
from jax.experimental.pallas import tpu as pltpu
from jax.sharding import PartitionSpec as P

RADIAL_ALL = 256
WINDOW_START = 124
RADIAL_GAIN = 0.25
VISC_AXIAL = 4.0
VISC_TURN = 0.05

F32 = jnp.float32
BF16 = jnp.bfloat16
VMEM_LIMIT = 8 * 1024 * 1024
TRANSFORM_LIMIT = 22 * 1024 * 1024
ROWS = 128
COLS = 256
BAND = 16

IN_SMEM = pl.BlockSpec(memory_space=pltpu.SMEM)
IN_VMEM = pl.BlockSpec(memory_space=pltpu.VMEM)
IN_HBM = pl.BlockSpec(memory_space=pltpu.HBM)


def kernel_call(body, name, args, in_specs, outs, out_specs=None, scratch=(), limit=VMEM_LIMIT):
    held = [
        a if s is IN_SMEM else pltpu.with_memory_space_constraint(a, s.memory_space)
        for a, s in zip(args, in_specs)
    ]
    more = {} if out_specs is None else {"out_specs": out_specs}
    return pl.pallas_call(
        body,
        out_shape=outs,
        in_specs=in_specs,
        scratch_shapes=list(scratch),
        compiler_params=pltpu.CompilerParams(vmem_limit_bytes=limit),
        cost_estimate=pl.CostEstimate(flops=1000, bytes_accessed=1000, transcendentals=0),
        name=name,
        **more,
    )(*held)


def sine_turns(y):
    x = y * F32(2.0 * math.pi)
    x2 = x * x
    acc = F32(1.0 / 6227020800.0)
    for c in (-1.0 / 39916800.0, 1.0 / 362880.0, -1.0 / 5040.0, 1.0 / 120.0, -1.0 / 6.0, 1.0):
        acc = acc * x2 + F32(c)
    return acc * x


def trig_block(row0, rows, cols, mode_axis, count, weighted):
    half = count // 2
    r = lax.broadcasted_iota(jnp.int32, (rows, cols), 0) + row0
    c = lax.broadcasted_iota(jnp.int32, (rows, cols), 1)
    mode, point = (r, c) if mode_axis == 0 else (c, r)
    is_cos = mode <= half
    freq = jnp.where(is_cos, mode, mode - half).astype(F32)
    phase = freq * point.astype(F32) - jnp.where(is_cos, F32(0.0), F32(count // 4))
    phase = phase - F32(count) * jnp.floor(phase * F32(1.0 / count))
    value = -sine_turns(F32(0.25) - jnp.abs(phase * F32(1.0 / count) - F32(0.5)))
    if weighted:
        edge = (mode == 0) | (mode == half)
        value = value * jnp.where(edge, F32(1.0 / count), F32(2.0 / count))
    return value.astype(BF16)


def fill_table(ref, mode_axis, weighted):
    count = ref.shape[0]

    @pl.loop(0, count // ROWS)
    def _(i):
        at = pl.multiple_of(i * ROWS, ROWS)
        ref[pl.ds(at, ROWS), :] = trig_block(at, ROWS, count, mode_axis, count, weighted)


def channels(refs):
    return [ref.at[i] for ref in refs for i in range(ref.shape[0])]


def taker(refs):
    refs = list(refs)

    def take():
        return refs.pop(0)

    def take_list(count):
        out, refs[:count] = refs[:count], []
        return out

    return take, take_list


def take_kernel(v, field, whole, *refs):
    pieces, sems = refs[:-1], refs[-1]
    spans = [(c, pl.ds(r, ROWS)) for c in range(len(pieces)) for r in range(0, v.shape[1], ROWS)]
    copies = [
        pltpu.make_async_copy(v.at[span], field.at[span], sems.at[n]) for n, span in enumerate(spans)
    ]
    for copy in copies:
        copy.start()
    for (c, rows), copy in zip(spans, copies):
        copy.wait()
        value = field[c, rows, :].astype(BF16)
        whole[c, rows, :] = value
        pieces[c][0, rows, :] = value


def take_start(v):
    chans, modes_m, modes_k = v.shape
    field, whole, *pieces = kernel_call(
        take_kernel,
        "take_start",
        [v],
        [IN_HBM],
        [pltpu.VMEM(v.shape, F32), pltpu.VMEM(v.shape, BF16)]
        + [pltpu.VMEM((1, modes_m, modes_k), BF16)] * chans,
        scratch=[pltpu.SemaphoreType.DMA((chans * (modes_m // ROWS),))],
    )
    return field, whole, pieces


def transform_kernel(groups, build, *refs):
    take, take_list = taker(refs)
    x = channels(take_list(groups))
    couple_far = take()
    tables_far = None if build else take_list(3)
    out = take()
    if build:
        tables_far, anal_m = take_list(3), take()
    one, phys, mixed, couple, synth_k, synth_mt, anal_kt, sems = take_list(8)
    near = (synth_k, synth_mt, anal_kt)
    chans, modes_m, modes_k = out.shape
    load = pltpu.make_async_copy(couple_far, couple, sems.at[3])
    if build:
        moves = [pltpu.make_async_copy(n, f, sems.at[i]) for i, (n, f) in enumerate(zip(near, tables_far))]
    else:
        moves = [pltpu.make_async_copy(f, n, sems.at[i]) for i, (n, f) in enumerate(zip(near, tables_far))]
        for move in moves[:2]:
            move.start()
    load.start()
    if not build:
        moves[2].start()

    def ready(i, mode_axis, weighted):
        if build:
            fill_table(near[i], mode_axis, weighted)
            moves[i].start()
        else:
            moves[i].wait()

    ready(0, 0, False)
    for c in range(chans):

        @pl.loop(0, modes_m // ROWS)
        def _(i):
            at = pl.ds(pl.multiple_of(i * ROWS, ROWS), ROWS)
            one[c, at, :] = jnp.dot(x[c][at, :], synth_k[...], preferred_element_type=F32).astype(BF16)

    ready(1, 1, False)
    load.wait()

    @pl.loop(0, modes_k // COLS)
    def _(z):
        zs = pl.ds(pl.multiple_of(z * COLS, COLS), COLS)
        for j in range(chans):
            phys[j] = jnp.dot(synth_mt[...], one[j, :, zs], preferred_element_type=F32)

        @pl.loop(0, modes_m // BAND)
        def _(i):
            ts = pl.ds(pl.multiple_of(i * BAND, BAND), BAND)
            parts = [phys[j, ts, :] for j in range(chans)]
            for c in range(chans):
                total = couple[c, 0, ts, zs].astype(F32) * parts[0]
                for j in range(1, chans):
                    total += couple[c, j, ts, zs].astype(F32) * parts[j]
                mixed[c, ts, zs] = total.astype(BF16)

    ready(2, 1, True)
    for c in range(chans):

        @pl.loop(0, modes_m // ROWS)
        def _(i):
            at = pl.ds(pl.multiple_of(i * ROWS, ROWS), ROWS)
            out[c, at, :] = jnp.dot(mixed[c, at, :], anal_kt[...], preferred_element_type=F32).astype(BF16)

    if build:
        fill_table(anal_m, 0, True)
        for move in moves:
            move.wait()


def transform(x, couple, tables=None):
    chans, _, modes_m, modes_k = couple.shape
    shape = (chans, modes_m, modes_k)
    sizes = [(modes_k, modes_k), (modes_m, modes_m), (modes_k, modes_k)]
    build = tables is None
    far = [] if build else list(tables[:3])
    outs, out_specs = [pltpu.VMEM(shape, BF16)], [IN_VMEM]
    if build:
        outs += [pltpu.HBM(n, BF16) for n in sizes] + [pltpu.VMEM((modes_m, modes_m), BF16)]
        out_specs += [IN_HBM] * 3 + [IN_VMEM]
    result = kernel_call(
        functools.partial(transform_kernel, len(x), build),
        "transform",
        [*x, couple, *far],
        [IN_VMEM] * len(x) + [IN_HBM] * (1 + len(far)),
        outs,
        out_specs=out_specs,
        scratch=[
            pltpu.VMEM(shape, BF16),
            pltpu.VMEM((chans, modes_m, COLS), F32),
            pltpu.VMEM(shape, BF16),
            pltpu.VMEM(couple.shape, BF16),
            *[pltpu.VMEM(n, BF16) for n in sizes],
            pltpu.SemaphoreType.DMA((4,)),
        ],
        limit=TRANSFORM_LIMIT,
    )
    return result[0], (result[1:] if build else tables)


def own_plane():
    return WINDOW_START + lax.axis_index("rad")


def paired_plane():
    return WINDOW_START + 1 - lax.axis_index("rad")


def inverse_divisor(row0, rows, modes_m, modes_k, plane):
    m = lax.broadcasted_iota(jnp.int32, (rows, 1), 0) + row0
    k = lax.broadcasted_iota(jnp.int32, (1, modes_k), 1)
    fm = jnp.where(m <= modes_m // 2, m, m - modes_m // 2).astype(F32) / F32(modes_m // 2)
    fk = jnp.where(k <= modes_k // 2, k, k - modes_k // 2).astype(F32) / F32(modes_k // 2)
    radius = (jnp.full((1, 1), plane, jnp.int32).astype(F32) + F32(0.5)) / F32(RADIAL_ALL)
    turning = F32(VISC_TURN) * fm * fm / (radius * radius)
    return F32(1.0) / (F32(1.0) + F32(VISC_AXIAL) * fk * fk + turning)


def local_kernel(groups, last, paired, advect, *refs):
    take, take_list = taker(refs)
    v, vb, recv = (channels(take_list(n)) for n in groups[:3])
    two, anal_m = take(), take()
    if last:
        u0, out, scale, gram, spec, acc = take_list(6)
        acc[...] = jnp.zeros_like(acc)
    else:
        out, out_b, spec = take(), channels(take_list(groups[3])), take()
    chans, modes_m, modes_k = two.shape
    half = modes_k // 2
    for c in range(chans):
        spec[c] = jnp.dot(anal_m[...], two[c], preferred_element_type=F32)
    wave = lax.broadcasted_iota(jnp.int32, (1, half), 1).astype(F32) * advect[0]

    @pl.loop(0, modes_m // BAND)
    def _(i):
        row0 = pl.multiple_of(i * BAND, BAND)
        at = pl.ds(row0, BAND)
        inv = inverse_divisor(row0, BAND, modes_m, modes_k, own_plane())
        if last:
            scale[at, :] = inv * F32(RADIAL_GAIN)
            if paired:
                mate = inverse_divisor(row0, BAND, modes_m, modes_k, paired_plane()) * F32(RADIAL_GAIN**2)
        for c in range(chans):
            low, high = v[c][at, :half], v[c][at, half:]
            for lo, own, drift in ((0, low, -wave * high), (half, high, wave * low)):
                ks = slice(lo, lo + half)
                mid = F32(-2.0 * RADIAL_GAIN) * vb[c][at, ks].astype(F32)
                total = own + spec[c, at, ks] + drift + mid
                if last:
                    x0 = u0[c, at, ks]
                    if paired:
                        total += mate[:, ks] * x0
                    for n, (a, b) in enumerate(((x0, x0), (x0, own), (own, own))):
                        add_tile(acc, n, a * b)
                value = total * inv[:, ks] - recv[c][at, ks].astype(F32)
                out[c, at, ks] = value
                if not last:
                    out_b[c][at, ks] = value.astype(BF16)

    if last:
        gram[...] = jnp.zeros_like(gram)
        for n in range(3):
            gram[n : n + 1, :] = jnp.sum(acc[n], axis=0, keepdims=True)


def add_tile(acc, n, value):
    value = sum(value[r : r + 8] for r in range(0, value.shape[0], 8))
    acc[n] += sum(value[:, k : k + 128] for k in range(0, value.shape[1], 128))


def local_first(advect, v, vb, recv, two, tables, sizes):
    shape = two.shape
    args = [advect, *v, *vb, *recv, two, tables[3]]
    part, *part_b = kernel_call(
        functools.partial(local_kernel, (len(v), len(vb), len(recv), len(sizes)), False, False),
        "local_first",
        args,
        [IN_SMEM] + [IN_VMEM] * (len(args) - 1),
        [pltpu.VMEM(shape, F32)] + [pltpu.VMEM((n,) + shape[1:], BF16) for n in sizes],
        scratch=[pltpu.VMEM(shape, F32)],
    )
    return part, part_b


def local_last(advect, v, vb, recv, two, tables, u0, paired):
    shape = two.shape
    args = [advect, *v, *vb, *recv, two, tables[3], u0]
    return kernel_call(
        functools.partial(local_kernel, (len(v), len(vb), len(recv)), True, paired),
        "local_last",
        args,
        [IN_SMEM] + [IN_VMEM] * (len(args) - 1),
        [pltpu.VMEM(shape, F32), pltpu.VMEM(shape[1:], F32), pltpu.VMEM((8, 128), F32)],
        scratch=[pltpu.VMEM(shape, F32), pltpu.VMEM((3, 8, 128), F32)],
    )


def added(planes, c, at):
    near = planes[0][c][at, :].astype(F32)
    for plane in planes[1:]:
        near += plane[c][at, :].astype(F32)
    return near


def first_kernel(groups, sides, part, *refs):
    take, take_list = taker(refs)
    planes = [channels(take_list(groups)) for _ in range(sides)]
    out, out_b = take(), channels(refs[-part.shape[0] :])
    chans, modes_m, modes_k = part.shape

    @pl.loop(0, modes_m // BAND)
    def _(i):
        row0 = pl.multiple_of(i * BAND, BAND)
        at = pl.ds(row0, BAND)
        inv = inverse_divisor(row0, BAND, modes_m, modes_k, own_plane()) * F32(RADIAL_GAIN)
        for c in range(chans):
            value = part[c, at, :] + added(planes, c, at) * inv
            out[c, at, :] = value
            out_b[c][at, :] = value.astype(BF16)


def first_image(part, sides):
    args = [part, *(x for side in sides for x in side)]
    return kernel_call(
        functools.partial(first_kernel, len(sides[0]), len(sides)),
        "first_image",
        args,
        [IN_VMEM] * len(args),
        [pltpu.VMEM(part.shape, F32)]
        + [pltpu.VMEM((1,) + part.shape[1:], BF16)] * part.shape[0],
    )


def second_kernel(first, sides, done, scale, u0, u1, part, before, *refs):
    take, take_list = taker(refs)
    planes = [channels([take()]) for _ in range(sides)]
    out, gram, acc = take_list(3)
    count, modes_m, _ = out.shape
    acc[...] = jnp.zeros_like(acc)

    @pl.loop(0, modes_m // BAND)
    def _(i):
        at = pl.ds(pl.multiple_of(i * BAND, BAND), BAND)
        for g in range(count):
            x2 = part[first + g, at, :] + added(planes, g, at) * scale[at, :]
            out[g, at, :] = x2
            for n, x in enumerate((u0[first + g, at, :], u1[first + g, at, :], x2)):
                add_tile(acc, n, x * x2)

    rows = [jnp.sum(acc[n], axis=0, keepdims=True) for n in range(3)]
    total = before[...] + jnp.concatenate([jnp.zeros((3, 128), F32), *rows, jnp.zeros((2, 128), F32)], axis=0)
    if done:
        total = jnp.sum(total, axis=1, keepdims=True)
        total = jnp.sum(jnp.where(on_diagonal(), total, F32(0.0)), axis=0, keepdims=True)
    gram[...] = jnp.broadcast_to(total, gram.shape)


def on_diagonal():
    rows, lanes = (lax.broadcasted_iota(jnp.int32, (8, 128), n) for n in (0, 1))
    return rows == lanes


def second_image(first, scale, u0, u1, part, before, planes, slots=None):
    done = slots is not None
    tile = (slots, 128) if done else (8, 128)
    args = [scale, u0, u1, part, before, *planes]
    return kernel_call(
        functools.partial(second_kernel, first, len(planes), done),
        "second_image",
        args,
        [IN_VMEM] * len(args),
        [pltpu.VMEM(planes[0].shape, F32), pltpu.VMEM(tile, F32)],
        scratch=[pltpu.VMEM((3, 8, 128), F32)],
    )


def combine_kernel(cells, counts, grams, *refs):
    take, take_list = taker(refs)
    u0, u1, u2 = (channels(take_list(n)) for n in counts)
    out, hess, held, sems = take_list(4)
    chans, modes_m, modes_k = out.shape
    g = jnp.sum(grams[...], axis=0, keepdims=True) * F32(1.0 / cells)
    g = jnp.sum(jnp.where(on_diagonal(), g, F32(0.0)), axis=1, keepdims=True)
    g = jnp.broadcast_to(g, (8, 128))
    g00, g01, g11, g02, g12, g22 = (g[n : n + 1, :] for n in range(6))
    n0 = jnp.sqrt(g00)
    h11 = g01 / g00
    s = jnp.sqrt(g11 - h11 * g01)
    h21 = s / n0
    w0 = g02 - h11 * g01
    w1 = g12 - h11 * g11
    ww = g22 - F32(2.0) * h11 * g12 + h11 * h11 * g11
    h12 = w0 / (s * n0)
    h22 = (w1 - h11 * w0) / (s * s)
    h32 = jnp.sqrt(ww / (s * s) - h12 * h12 - h22 * h22)
    c2 = F32(1.0) / (s * h32)
    c1 = -(h11 + h22) * c2
    c0 = h22 * h11 * c2 - h12 / (n0 * h32)
    for n, value in enumerate((n0, h11, h21, h12, h22, h32)):
        hess[n] = value[0, 0]

    wide = [jnp.concatenate([x] * (modes_k // 128), axis=1) for x in (c0, c1, c2)]
    copies = []
    for c in range(chans):
        for r in range(0, modes_m, ROWS):

            @pl.loop(r // BAND, (r + ROWS) // BAND)
            def _(i):
                at = pl.ds(pl.multiple_of(i * BAND, BAND), BAND)
                held[c, at, :] = wide[0] * u0[c][at, :] + wide[1] * u1[c][at, :] + wide[2] * u2[c][at, :]

            rows = pl.ds(r, ROWS)
            copy = pltpu.make_async_copy(held.at[c, rows], out.at[c, rows], sems.at[len(copies)])
            copy.start()
            copies.append(copy)
    for copy in copies:
        copy.wait()


def combine(cells, shape, grams, u0, u1, u2):
    chans, modes_m, modes_k = shape
    args = [grams, *u0, *u1, *u2]
    return kernel_call(
        functools.partial(combine_kernel, cells, (len(u0), len(u1), len(u2))),
        "combine",
        args,
        [IN_VMEM] * len(args),
        [jax.ShapeDtypeStruct(shape, F32), jax.ShapeDtypeStruct((6,), F32)],
        out_specs=[IN_HBM, IN_SMEM],
        scratch=[
            pltpu.VMEM(shape, F32),
            pltpu.SemaphoreType.DMA((chans * (modes_m // ROWS),)),
        ],
    )


def shifted(value, axis, steps):
    count = lax.axis_size(axis)
    return lax.ppermute(value, axis, [(i, (i + steps) % count) for i in range(count)])


def neighbour_planes(value, axis):
    count = lax.axis_size(axis)
    if count == 2:
        return [lax.ppermute(value, axis, [(0, 1), (1, 0)])]
    up = [(i, i + 1) for i in range(count - 1)]
    return [lax.ppermute(value, axis, up), lax.ppermute(value, axis, [(b, a) for a, b in up])]


def on_device(start_vector, coupling, advect):
    _, chans, rows_here, modes_m, modes_k = start_vector.shape
    assert rows_here == 1
    start = start_vector.reshape(chans, modes_m, modes_k)
    couple = coupling.reshape(chans, chans, modes_m, modes_k)
    devices = lax.axis_size("seg") * lax.axis_size("rad")
    cells = float(devices * start.size)
    paired = lax.axis_size("rad") == 2

    sizes = (chans - 1, 1) if paired else (1,) * chans

    u0, u0b, pieces = take_start(start)
    near_one = neighbour_planes(u0b, "rad")
    next_one = [shifted(x, "seg", -1) for x in pieces]
    two, tables = transform([u0b], couple)
    part, part_b = local_first(advect, [u0], [u0b], next_one, two, tables, sizes)
    if paired:
        near_two = [neighbour_planes(x, "rad") for x in part_b]
    u1, *u1b = first_image(part, [[x] for x in near_one])
    if not paired:
        near_two = [neighbour_planes(x, "rad") for x in u1b]
    next_two = [shifted(x, "seg", -1) for x in u1b]
    two, _ = transform(u1b, couple, tables)
    part, scale, gram = local_last(advect, [u1], u1b, next_two, two, tables, u0, paired)
    u2, first = [], 0
    for size, planes in zip(sizes, near_two):
        slots = devices if first + size == chans else None
        field, gram = second_image(first, scale, u0, u1, part, gram, planes, slots)
        first += size
        u2.append(field)
    grams = lax.all_to_all(gram, ("seg", "rad"), 0, 0)
    basis, hess = combine(cells, start.shape, grams, [u0], [u1], u2)
    return basis.reshape(start_vector.shape), hess


def solution(mesh):
    return jax.shard_map(
        on_device,
        mesh=mesh,
        in_specs=(
            P("seg", None, "rad", None, None),
            P("seg", None, None, "rad", None, None),
            P("rad"),
        ),
        out_specs=(P("seg", None, "rad", None, None), P()),
        check_vma=False,
    )
```

```python
import functools
import math

import jax
import jax.numpy as jnp
from jax import lax
from jax.experimental import pallas as pl
from jax.experimental.pallas import tpu as pltpu
from jax.sharding import PartitionSpec as P

RADIAL_ALL = 256
WINDOW_START = 124
RADIAL_GAIN = 0.25
VISC_AXIAL = 4.0
VISC_TURN = 0.05

F32 = jnp.float32
BF16 = jnp.bfloat16
VMEM_LIMIT = 8 * 1024 * 1024
TRANSFORM_LIMIT = 22 * 1024 * 1024
ROWS = 128
COLS = 256
BAND = 16

IN_SMEM = pl.BlockSpec(memory_space=pltpu.SMEM)
IN_VMEM = pl.BlockSpec(memory_space=pltpu.VMEM)
IN_HBM = pl.BlockSpec(memory_space=pltpu.HBM)


def kernel_call(body, name, args, in_specs, outs, out_specs=None, scratch=(), limit=VMEM_LIMIT):
    held = [
        a if s is IN_SMEM else pltpu.with_memory_space_constraint(a, s.memory_space)
        for a, s in zip(args, in_specs)
    ]
    more = {} if out_specs is None else {"out_specs": out_specs}
    return pl.pallas_call(
        body,
        out_shape=outs,
        in_specs=in_specs,
        scratch_shapes=list(scratch),
        compiler_params=pltpu.CompilerParams(vmem_limit_bytes=limit),
        cost_estimate=pl.CostEstimate(flops=1000, bytes_accessed=1000, transcendentals=0),
        name=name,
        **more,
    )(*held)


def sine_turns(y):
    x = y * F32(2.0 * math.pi)
    x2 = x * x
    acc = F32(1.0 / 6227020800.0)
    for c in (-1.0 / 39916800.0, 1.0 / 362880.0, -1.0 / 5040.0, 1.0 / 120.0, -1.0 / 6.0, 1.0):
        acc = acc * x2 + F32(c)
    return acc * x


def trig_block(row0, rows, cols, mode_axis, count, weighted):
    half = count // 2
    r = lax.broadcasted_iota(jnp.int32, (rows, cols), 0) + row0
    c = lax.broadcasted_iota(jnp.int32, (rows, cols), 1)
    mode, point = (r, c) if mode_axis == 0 else (c, r)
    is_cos = mode <= half
    freq = jnp.where(is_cos, mode, mode - half).astype(F32)
    phase = freq * point.astype(F32) - jnp.where(is_cos, F32(0.0), F32(count // 4))
    phase = phase - F32(count) * jnp.floor(phase * F32(1.0 / count))
    value = -sine_turns(F32(0.25) - jnp.abs(phase * F32(1.0 / count) - F32(0.5)))
    if weighted:
        edge = (mode == 0) | (mode == half)
        value = value * jnp.where(edge, F32(1.0 / count), F32(2.0 / count))
    return value.astype(BF16)


def fill_table(ref, mode_axis, weighted):
    count = ref.shape[0]

    @pl.loop(0, count // ROWS)
    def _(i):
        at = pl.multiple_of(i * ROWS, ROWS)
        ref[pl.ds(at, ROWS), :] = trig_block(at, ROWS, count, mode_axis, count, weighted)


def channels(refs):
    return [ref.at[i] for ref in refs for i in range(ref.shape[0])]


def taker(refs):
    refs = list(refs)

    def take():
        return refs.pop(0)

    def take_list(count):
        out, refs[:count] = refs[:count], []
        return out

    return take, take_list


def take_kernel(v, field, whole, *refs):
    pieces, sems = refs[:-1], refs[-1]
    spans = [(c, pl.ds(r, ROWS)) for c in range(len(pieces)) for r in range(0, v.shape[1], ROWS)]
    copies = [
        pltpu.make_async_copy(v.at[span], field.at[span], sems.at[n]) for n, span in enumerate(spans)
    ]
    for copy in copies:
        copy.start()
    for (c, rows), copy in zip(spans, copies):
        copy.wait()
        value = field[c, rows, :].astype(BF16)
        whole[c, rows, :] = value
        pieces[c][0, rows, :] = value


def take_start(v):
    chans, modes_m, modes_k = v.shape
    field, whole, *pieces = kernel_call(
        take_kernel,
        "take_start",
        [v],
        [IN_HBM],
        [pltpu.VMEM(v.shape, F32), pltpu.VMEM(v.shape, BF16)]
        + [pltpu.VMEM((1, modes_m, modes_k), BF16)] * chans,
        scratch=[pltpu.SemaphoreType.DMA((chans * (modes_m // ROWS),))],
    )
    return field, whole, pieces


def transform_kernel(groups, build, *refs):
    take, take_list = taker(refs)
    x = channels(take_list(groups))
    couple_far = take()
    tables_far = None if build else take_list(3)
    out = take()
    if build:
        tables_far, anal_m = take_list(3), take()
    one, phys, mixed, couple, synth_k, synth_mt, anal_kt, sems = take_list(8)
    near = (synth_k, synth_mt, anal_kt)
    chans, modes_m, modes_k = out.shape
    load = pltpu.make_async_copy(couple_far, couple, sems.at[3])
    if build:
        moves = [pltpu.make_async_copy(n, f, sems.at[i]) for i, (n, f) in enumerate(zip(near, tables_far))]
    else:
        moves = [pltpu.make_async_copy(f, n, sems.at[i]) for i, (n, f) in enumerate(zip(near, tables_far))]
        for move in moves[:2]:
            move.start()
    load.start()
    if not build:
        moves[2].start()

    def ready(i, mode_axis, weighted):
        if build:
            fill_table(near[i], mode_axis, weighted)
            moves[i].start()
        else:
            moves[i].wait()

    ready(0, 0, False)
    for c in range(chans):

        @pl.loop(0, modes_m // ROWS)
        def _(i):
            at = pl.ds(pl.multiple_of(i * ROWS, ROWS), ROWS)
            one[c, at, :] = jnp.dot(x[c][at, :], synth_k[...], preferred_element_type=F32).astype(BF16)

    ready(1, 1, False)
    load.wait()

    @pl.loop(0, modes_k // COLS)
    def _(z):
        zs = pl.ds(pl.multiple_of(z * COLS, COLS), COLS)
        for j in range(chans):
            phys[j] = jnp.dot(synth_mt[...], one[j, :, zs], preferred_element_type=F32)

        @pl.loop(0, modes_m // BAND)
        def _(i):
            ts = pl.ds(pl.multiple_of(i * BAND, BAND), BAND)
            parts = [phys[j, ts, :] for j in range(chans)]
            for c in range(chans):
                total = couple[c, 0, ts, zs].astype(F32) * parts[0]
                for j in range(1, chans):
                    total += couple[c, j, ts, zs].astype(F32) * parts[j]
                mixed[c, ts, zs] = total.astype(BF16)

    ready(2, 1, True)
    for c in range(chans):

        @pl.loop(0, modes_m // ROWS)
        def _(i):
            at = pl.ds(pl.multiple_of(i * ROWS, ROWS), ROWS)
            out[c, at, :] = jnp.dot(mixed[c, at, :], anal_kt[...], preferred_element_type=F32).astype(BF16)

    if build:
        fill_table(anal_m, 0, True)
        for move in moves:
            move.wait()


def transform(x, couple, tables=None):
    chans, _, modes_m, modes_k = couple.shape
    shape = (chans, modes_m, modes_k)
    sizes = [(modes_k, modes_k), (modes_m, modes_m), (modes_k, modes_k)]
    build = tables is None
    far = [] if build else list(tables[:3])
    outs, out_specs = [pltpu.VMEM(shape, BF16)], [IN_VMEM]
    if build:
        outs += [pltpu.HBM(n, BF16) for n in sizes] + [pltpu.VMEM((modes_m, modes_m), BF16)]
        out_specs += [IN_HBM] * 3 + [IN_VMEM]
    result = kernel_call(
        functools.partial(transform_kernel, len(x), build),
        "transform",
        [*x, couple, *far],
        [IN_VMEM] * len(x) + [IN_HBM] * (1 + len(far)),
        outs,
        out_specs=out_specs,
        scratch=[
            pltpu.VMEM(shape, BF16),
            pltpu.VMEM((chans, modes_m, COLS), F32),
            pltpu.VMEM(shape, BF16),
            pltpu.VMEM(couple.shape, BF16),
            *[pltpu.VMEM(n, BF16) for n in sizes],
            pltpu.SemaphoreType.DMA((4,)),
        ],
        limit=TRANSFORM_LIMIT,
    )
    return result[0], (result[1:] if build else tables)


def own_plane():
    return WINDOW_START + lax.axis_index("rad")


def paired_plane():
    return WINDOW_START + 1 - lax.axis_index("rad")


def inverse_divisor(row0, rows, modes_m, modes_k, plane):
    m = lax.broadcasted_iota(jnp.int32, (rows, 1), 0) + row0
    k = lax.broadcasted_iota(jnp.int32, (1, modes_k), 1)
    fm = jnp.where(m <= modes_m // 2, m, m - modes_m // 2).astype(F32) / F32(modes_m // 2)
    fk = jnp.where(k <= modes_k // 2, k, k - modes_k // 2).astype(F32) / F32(modes_k // 2)
    radius = (jnp.full((1, 1), plane, jnp.int32).astype(F32) + F32(0.5)) / F32(RADIAL_ALL)
    turning = F32(VISC_TURN) * fm * fm / (radius * radius)
    return F32(1.0) / (F32(1.0) + F32(VISC_AXIAL) * fk * fk + turning)


def local_kernel(groups, last, paired, advect, *refs):
    take, take_list = taker(refs)
    v, vb, recv = (channels(take_list(n)) for n in groups[:3])
    two, anal_m = take(), take()
    if last:
        u0, out, scale, gram, spec, acc = take_list(6)
        acc[...] = jnp.zeros_like(acc)
    else:
        out, out_b, spec = take(), channels(take_list(groups[3])), take()
    chans, modes_m, modes_k = two.shape
    half = modes_k // 2
    for c in range(chans):
        spec[c] = jnp.dot(anal_m[...], two[c], preferred_element_type=F32)
    wave = lax.broadcasted_iota(jnp.int32, (1, half), 1).astype(F32) * advect[0]

    @pl.loop(0, modes_m // BAND)
    def _(i):
        row0 = pl.multiple_of(i * BAND, BAND)
        at = pl.ds(row0, BAND)
        inv = inverse_divisor(row0, BAND, modes_m, modes_k, own_plane())
        if last:
            scale[at, :] = inv * F32(RADIAL_GAIN)
            if paired:
                mate = inverse_divisor(row0, BAND, modes_m, modes_k, paired_plane()) * F32(RADIAL_GAIN**2)
        for c in range(chans):
            low, high = v[c][at, :half], v[c][at, half:]
            for lo, own, drift in ((0, low, -wave * high), (half, high, wave * low)):
                ks = slice(lo, lo + half)
                mid = F32(-2.0 * RADIAL_GAIN) * vb[c][at, ks].astype(F32)
                total = own + spec[c, at, ks] + drift + mid
                if last:
                    x0 = u0[c, at, ks]
                    if paired:
                        total += mate[:, ks] * x0
                    for n, (a, b) in enumerate(((x0, x0), (x0, own), (own, own))):
                        add_tile(acc, n, a * b)
                value = total * inv[:, ks] - recv[c][at, ks].astype(F32)
                out[c, at, ks] = value
                if not last:
                    out_b[c][at, ks] = value.astype(BF16)

    if last:
        gram[...] = jnp.zeros_like(gram)
        for n in range(3):
            gram[n : n + 1, :] = jnp.sum(acc[n], axis=0, keepdims=True)


def add_tile(acc, n, value):
    value = sum(value[r : r + 8] for r in range(0, value.shape[0], 8))
    acc[n] += sum(value[:, k : k + 128] for k in range(0, value.shape[1], 128))


def local_first(advect, v, vb, recv, two, tables, sizes):
    shape = two.shape
    args = [advect, *v, *vb, *recv, two, tables[3]]
    part, *part_b = kernel_call(
        functools.partial(local_kernel, (len(v), len(vb), len(recv), len(sizes)), False, False),
        "local_first",
        args,
        [IN_SMEM] + [IN_VMEM] * (len(args) - 1),
        [pltpu.VMEM(shape, F32)] + [pltpu.VMEM((n,) + shape[1:], BF16) for n in sizes],
        scratch=[pltpu.VMEM(shape, F32)],
    )
    return part, part_b


def local_last(advect, v, vb, recv, two, tables, u0, paired):
    shape = two.shape
    args = [advect, *v, *vb, *recv, two, tables[3], u0]
    return kernel_call(
        functools.partial(local_kernel, (len(v), len(vb), len(recv)), True, paired),
        "local_last",
        args,
        [IN_SMEM] + [IN_VMEM] * (len(args) - 1),
        [pltpu.VMEM(shape, F32), pltpu.VMEM(shape[1:], F32), pltpu.VMEM((8, 128), F32)],
        scratch=[pltpu.VMEM(shape, F32), pltpu.VMEM((3, 8, 128), F32)],
    )


def added(planes, c, at):
    near = planes[0][c][at, :].astype(F32)
    for plane in planes[1:]:
        near += plane[c][at, :].astype(F32)
    return near


def first_kernel(groups, sides, part, *refs):
    take, take_list = taker(refs)
    planes = [channels(take_list(groups)) for _ in range(sides)]
    out, out_b = take(), channels(refs[-part.shape[0] :])
    chans, modes_m, modes_k = part.shape

    @pl.loop(0, modes_m // BAND)
    def _(i):
        row0 = pl.multiple_of(i * BAND, BAND)
        at = pl.ds(row0, BAND)
        inv = inverse_divisor(row0, BAND, modes_m, modes_k, own_plane()) * F32(RADIAL_GAIN)
        for c in range(chans):
            value = part[c, at, :] + added(planes, c, at) * inv
            out[c, at, :] = value
            out_b[c][at, :] = value.astype(BF16)


def first_image(part, sides):
    args = [part, *(x for side in sides for x in side)]
    return kernel_call(
        functools.partial(first_kernel, len(sides[0]), len(sides)),
        "first_image",
        args,
        [IN_VMEM] * len(args),
        [pltpu.VMEM(part.shape, F32)]
        + [pltpu.VMEM((1,) + part.shape[1:], BF16)] * part.shape[0],
    )


def second_kernel(first, sides, done, scale, u0, u1, part, before, *refs):
    take, take_list = taker(refs)
    planes = [channels([take()]) for _ in range(sides)]
    out, gram, acc = take_list(3)
    count, modes_m, _ = out.shape
    acc[...] = jnp.zeros_like(acc)

    @pl.loop(0, modes_m // BAND)
    def _(i):
        at = pl.ds(pl.multiple_of(i * BAND, BAND), BAND)
        for g in range(count):
            x2 = part[first + g, at, :] + added(planes, g, at) * scale[at, :]
            out[g, at, :] = x2
            for n, x in enumerate((u0[first + g, at, :], u1[first + g, at, :], x2)):
                add_tile(acc, n, x * x2)

    rows = [jnp.sum(acc[n], axis=0, keepdims=True) for n in range(3)]
    total = before[...] + jnp.concatenate([jnp.zeros((3, 128), F32), *rows, jnp.zeros((2, 128), F32)], axis=0)
    if done:
        total = jnp.sum(total, axis=1, keepdims=True)
        total = jnp.sum(jnp.where(on_diagonal(), total, F32(0.0)), axis=0, keepdims=True)
    gram[...] = jnp.broadcast_to(total, gram.shape)


def on_diagonal():
    rows, lanes = (lax.broadcasted_iota(jnp.int32, (8, 128), n) for n in (0, 1))
    return rows == lanes


def second_image(first, scale, u0, u1, part, before, planes, done):
    tile = (1, 128) if done else (8, 128)
    args = [scale, u0, u1, part, before, *planes]
    return kernel_call(
        functools.partial(second_kernel, first, len(planes), done),
        "second_image",
        args,
        [IN_VMEM] * len(args),
        [pltpu.VMEM(planes[0].shape, F32), pltpu.VMEM(tile, F32)],
        scratch=[pltpu.VMEM((3, 8, 128), F32)],
    )


def combine_kernel(cells, counts, grams, *refs):
    take, take_list = taker(refs)
    u0, u1, u2 = (channels(take_list(n)) for n in counts)
    out, hess, held, sems = take_list(4)
    chans, modes_m, modes_k = out.shape
    g = jnp.sum(grams[...], axis=0, keepdims=True) * F32(1.0 / cells)
    g = jnp.sum(jnp.where(on_diagonal(), g, F32(0.0)), axis=1, keepdims=True)
    g = jnp.broadcast_to(g, (8, 128))
    g00, g01, g11, g02, g12, g22 = (g[n : n + 1, :] for n in range(6))
    per_g00 = F32(1.0) / g00
    h11 = g01 * per_g00
    q = g11 - h11 * g01
    per_q = F32(1.0) / q
    w0 = g02 - h11 * g01
    w1 = g12 - h11 * g11
    ww = g22 - F32(2.0) * h11 * g12 + h11 * h11 * g11
    h22 = (w1 - h11 * w0) * per_q
    square = (ww - w0 * w0 * per_g00) * per_q - h22 * h22
    c2 = F32(1.0) / jnp.sqrt(q * square)
    c1 = -(h11 + h22) * c2
    c0 = (h11 * h22 - w0 * per_g00) * c2
    wide = [jnp.concatenate([x] * (modes_k // 128), axis=1) for x in (c0, c1, c2)]
    copies = []
    for c in range(chans):
        for r in range(0, modes_m, ROWS):

            @pl.loop(r // BAND, (r + ROWS) // BAND)
            def _(i):
                at = pl.ds(pl.multiple_of(i * BAND, BAND), BAND)
                held[c, at, :] = wide[0] * u0[c][at, :] + wide[1] * u1[c][at, :] + wide[2] * u2[c][at, :]

            rows = pl.ds(r, ROWS)
            copy = pltpu.make_async_copy(held.at[c, rows], out.at[c, rows], sems.at[len(copies)])
            copy.start()
            copies.append(copy)
    n0, s = jnp.sqrt(g00), jnp.sqrt(q)
    for n, value in enumerate((n0, h11, s / n0, w0 / (s * n0), h22, jnp.sqrt(square))):
        hess[n] = value[0, 0]
    for copy in copies:
        copy.wait()


def combine(cells, shape, grams, u0, u1, u2):
    chans, modes_m, modes_k = shape
    args = [grams, *u0, *u1, *u2]
    return kernel_call(
        functools.partial(combine_kernel, cells, (len(u0), len(u1), len(u2))),
        "combine",
        args,
        [IN_VMEM] * len(args),
        [jax.ShapeDtypeStruct(shape, F32), jax.ShapeDtypeStruct((6,), F32)],
        out_specs=[IN_HBM, IN_SMEM],
        scratch=[
            pltpu.VMEM(shape, F32),
            pltpu.SemaphoreType.DMA((chans * (modes_m // ROWS),)),
        ],
    )


def shifted(value, axis, steps):
    count = lax.axis_size(axis)
    return lax.ppermute(value, axis, [(i, (i + steps) % count) for i in range(count)])


def neighbour_planes(value, axis):
    count = lax.axis_size(axis)
    if count == 2:
        return [lax.ppermute(value, axis, [(0, 1), (1, 0)])]
    up = [(i, i + 1) for i in range(count - 1)]
    return [lax.ppermute(value, axis, up), lax.ppermute(value, axis, [(b, a) for a, b in up])]


def on_device(start_vector, coupling, advect):
    _, chans, rows_here, modes_m, modes_k = start_vector.shape
    assert rows_here == 1
    start = start_vector.reshape(chans, modes_m, modes_k)
    couple = coupling.reshape(chans, chans, modes_m, modes_k)
    devices = lax.axis_size("seg") * lax.axis_size("rad")
    cells = float(devices * start.size)
    paired = lax.axis_size("rad") == 2

    sizes = (chans - 1, 1) if paired else (1,) * chans

    u0, u0b, pieces = take_start(start)
    near_one = neighbour_planes(u0b, "rad")
    next_one = [shifted(x, "seg", -1) for x in pieces]
    two, tables = transform([u0b], couple)
    part, part_b = local_first(advect, [u0], [u0b], next_one, two, tables, sizes)
    if paired:
        near_two = [neighbour_planes(x, "rad") for x in part_b]
    u1, *u1b = first_image(part, [[x] for x in near_one])
    if not paired:
        near_two = [neighbour_planes(x, "rad") for x in u1b]
    next_two = [shifted(x, "seg", -1) for x in u1b]
    two, _ = transform(u1b, couple, tables)
    part, scale, gram = local_last(advect, [u1], u1b, next_two, two, tables, u0, paired)
    u2, first = [], 0
    for size, planes in zip(sizes, near_two):
        field, gram = second_image(first, scale, u0, u1, part, gram, planes, first + size == chans)
        first += size
        u2.append(field)
    grams = lax.all_gather(gram, ("seg", "rad"), axis=0, tiled=True)
    basis, hess = combine(cells, start.shape, grams, [u0], [u1], u2)
    return basis.reshape(start_vector.shape), hess


def solution(mesh):
    return jax.shard_map(
        on_device,
        mesh=mesh,
        in_specs=(
            P("seg", None, "rad", None, None),
            P("seg", None, None, "rad", None, None),
            P("rad"),
        ),
        out_specs=(P("seg", None, "rad", None, None), P()),
        check_vma=False,
    )
```

```python
import functools
import math

import jax
import jax.numpy as jnp
from jax import lax
from jax.experimental import pallas as pl
from jax.experimental.pallas import tpu as pltpu
from jax.sharding import PartitionSpec as P

RADIAL_ALL = 256
WINDOW_START = 124
RADIAL_GAIN = 0.25
VISC_AXIAL = 4.0
VISC_TURN = 0.05

F32 = jnp.float32
BF16 = jnp.bfloat16
VMEM_LIMIT = 8 * 1024 * 1024
TRANSFORM_LIMIT = 22 * 1024 * 1024
ROWS = 128
COLS = 256
BAND = 16
LONG = 10**11
EARLY_ROWS = 640
LATE_ROWS = 128

IN_SMEM = pl.BlockSpec(memory_space=pltpu.SMEM)
IN_VMEM = pl.BlockSpec(memory_space=pltpu.VMEM)
IN_HBM = pl.BlockSpec(memory_space=pltpu.HBM)


def kernel_call(body, name, args, in_specs, outs, out_specs=None, scratch=(), limit=VMEM_LIMIT, flops=1000):
    held = [
        a if s is IN_SMEM else pltpu.with_memory_space_constraint(a, s.memory_space)
        for a, s in zip(args, in_specs)
    ]
    more = {} if out_specs is None else {"out_specs": out_specs}
    return pl.pallas_call(
        body,
        out_shape=outs,
        in_specs=in_specs,
        scratch_shapes=list(scratch),
        compiler_params=pltpu.CompilerParams(vmem_limit_bytes=limit),
        cost_estimate=pl.CostEstimate(flops=flops, bytes_accessed=1000, transcendentals=0),
        name=name,
        **more,
    )(*held)


def sine_turns(y):
    x = y * F32(2.0 * math.pi)
    x2 = x * x
    acc = F32(1.0 / 6227020800.0)
    for c in (-1.0 / 39916800.0, 1.0 / 362880.0, -1.0 / 5040.0, 1.0 / 120.0, -1.0 / 6.0, 1.0):
        acc = acc * x2 + F32(c)
    return acc * x


def trig_block(row0, rows, cols, mode_axis, count, weighted):
    half = count // 2
    r = lax.broadcasted_iota(jnp.int32, (rows, cols), 0) + row0
    c = lax.broadcasted_iota(jnp.int32, (rows, cols), 1)
    mode, point = (r, c) if mode_axis == 0 else (c, r)
    is_cos = mode <= half
    freq = jnp.where(is_cos, mode, mode - half).astype(F32)
    phase = freq * point.astype(F32) - jnp.where(is_cos, F32(0.0), F32(count // 4))
    phase = phase - F32(count) * jnp.floor(phase * F32(1.0 / count))
    value = -sine_turns(F32(0.25) - jnp.abs(phase * F32(1.0 / count) - F32(0.5)))
    if weighted:
        edge = (mode == 0) | (mode == half)
        value = value * jnp.where(edge, F32(1.0 / count), F32(2.0 / count))
    return value.astype(BF16)


def fill_table(ref, mode_axis, weighted):
    count = ref.shape[0]

    @pl.loop(0, count // ROWS)
    def _(i):
        at = pl.multiple_of(i * ROWS, ROWS)
        ref[pl.ds(at, ROWS), :] = trig_block(at, ROWS, count, mode_axis, count, weighted)


def taker(refs):
    refs = list(refs)

    def take(count=None):
        if count is None:
            return refs.pop(0)
        out, refs[:count] = refs[:count], []
        return out

    return take


def segments(modes_m, groups):
    ends, total = {modes_m}, 0
    for group in groups:
        total += group.shape[0]
        ends.add(total % modes_m or modes_m)
    ends = sorted(ends)
    return list(zip([0] + ends[:-1], ends))


def band(groups, row, shift):
    for group in groups:
        if row < group.shape[0]:
            return group, pl.ds(pl.multiple_of(shift + row, BAND), BAND)
        row -= group.shape[0]


def read(groups, row, shift):
    group, at = band(groups, row, shift)
    return group[at, :]


def write(groups, row, shift, value):
    group, at = band(groups, row, shift)
    group[at, :] = value.astype(group.dtype)


def for_bands(lo, hi, body):
    @pl.loop(0, (hi - lo) // BAND)
    def _(i):
        body(pl.multiple_of(i * BAND, BAND))


def take_kernel(first, v, *refs):
    take = taker(refs)
    early = [] if first == 0 else [take()]
    field, rounded = take(), take()
    pieces, sems = take(len(refs) - len(early) - 3), take()
    count = field.shape[0]
    copies = []
    for n, r in enumerate(range(0, count, ROWS)):
        copies.append(
            pltpu.make_async_copy(v.at[pl.ds(first + r, ROWS)], field.at[pl.ds(r, ROWS)], sems.at[n])
        )
        copies[n].start()

    def lay(row, value):
        for n, piece in enumerate(pieces):
            at = row - n * piece.shape[0]
            if 0 <= at < piece.shape[0]:
                piece[at : at + ROWS, :] = value

    for r in range(0, first, ROWS):
        lay(r, early[0][r : r + ROWS, :])
    for n, r in enumerate(range(0, count, ROWS)):
        copies[n].wait()
        value = field[r : r + ROWS, :].astype(BF16)
        rounded[r : r + ROWS, :] = value
        lay(first + r, value)


def take_rows(v, first, count, early=(), pieces=0):
    rows, modes_k = v.shape
    shapes = [pltpu.VMEM((count, modes_k), F32), pltpu.VMEM((count, modes_k), BF16)]
    field, rounded, *by_channel = kernel_call(
        functools.partial(take_kernel, first),
        "take_rows",
        [v, *early],
        [IN_HBM] + [IN_VMEM] * len(early),
        shapes + [pltpu.VMEM((rows // max(pieces, 1), modes_k), BF16)] * pieces,
        scratch=[pltpu.SemaphoreType.DMA((count // ROWS,))],
    )
    return field, rounded, by_channel


def transform_kernel(build, *refs):
    take = taker(refs)
    chans = len(refs) - (14 if build else 13)
    x = take(chans)
    couple_far = take()
    tables_far = None if build else take(3)
    out = take()
    if build:
        tables_far, anal_m = take(3), take()
    one, phys, mixed, couple, synth_k, synth_mt, anal_kt, sems = take(8)
    near = (synth_k, synth_mt, anal_kt)
    _, modes_m, modes_k = out.shape
    load = pltpu.make_async_copy(couple_far, couple, sems.at[3])
    ends = [(n, f) if build else (f, n) for n, f in zip(near, tables_far)]
    moves = [pltpu.make_async_copy(src, dst, sems.at[i]) for i, (src, dst) in enumerate(ends)]
    if not build:
        for move in moves[:2]:
            move.start()
    load.start()
    if not build:
        moves[2].start()

    def ready(i, mode_axis, weighted):
        if build:
            fill_table(near[i], mode_axis, weighted)
            moves[i].start()
        else:
            moves[i].wait()

    ready(0, 0, False)
    for c in range(chans):

        @pl.loop(0, modes_m // ROWS)
        def _(i):
            at = pl.ds(pl.multiple_of(i * ROWS, ROWS), ROWS)
            one[c, at, :] = jnp.dot(x[c][at, :], synth_k[...], preferred_element_type=F32).astype(BF16)

    ready(1, 1, False)
    load.wait()

    @pl.loop(0, modes_k // COLS)
    def _(z):
        zs = pl.ds(pl.multiple_of(z * COLS, COLS), COLS)
        for j in range(chans):
            phys[j] = jnp.dot(synth_mt[...], one[j, :, zs], preferred_element_type=F32)

        @pl.loop(0, modes_m // BAND)
        def _(i):
            ts = pl.ds(pl.multiple_of(i * BAND, BAND), BAND)
            parts = [phys[j, ts, :] for j in range(chans)]
            for c in range(chans):
                total = couple[c, 0, ts, zs].astype(F32) * parts[0]
                for j in range(1, chans):
                    total += couple[c, j, ts, zs].astype(F32) * parts[j]
                mixed[c, ts, zs] = total.astype(BF16)

    ready(2, 1, True)
    for c in range(chans):

        @pl.loop(0, modes_m // ROWS)
        def _(i):
            at = pl.ds(pl.multiple_of(i * ROWS, ROWS), ROWS)
            out[c, at, :] = jnp.dot(mixed[c, at, :], anal_kt[...], preferred_element_type=F32).astype(BF16)

    if build:
        fill_table(anal_m, 0, True)
        for move in moves:
            move.wait()


def transform(x, couple, tables=None):
    chans, _, modes_m, modes_k = couple.shape
    shape = (chans, modes_m, modes_k)
    sizes = [(modes_k, modes_k), (modes_m, modes_m), (modes_k, modes_k)]
    build = tables is None
    far = [] if build else list(tables[:3])
    outs, out_specs = [pltpu.VMEM(shape, BF16)], [IN_VMEM]
    if build:
        outs += [pltpu.HBM(n, BF16) for n in sizes] + [pltpu.VMEM((modes_m, modes_m), BF16)]
        out_specs += [IN_HBM] * 3 + [IN_VMEM]
    result = kernel_call(
        functools.partial(transform_kernel, build),
        "transform",
        [*x, couple, *far],
        [IN_VMEM] * chans + [IN_HBM] * (1 + len(far)),
        outs,
        out_specs=out_specs,
        scratch=[
            pltpu.VMEM(shape, BF16),
            pltpu.VMEM((chans, modes_m, COLS), F32),
            pltpu.VMEM(shape, BF16),
            pltpu.VMEM(couple.shape, BF16),
            *[pltpu.VMEM(n, BF16) for n in sizes],
            pltpu.SemaphoreType.DMA((4,)),
        ],
        limit=TRANSFORM_LIMIT,
    )
    return result[0], (result[1:] if build else tables)


def own_plane():
    return WINDOW_START + lax.axis_index("rad")


def paired_plane():
    return WINDOW_START + 1 - lax.axis_index("rad")


def inverse_divisor(row0, modes_m, modes_k, plane):
    m = lax.broadcasted_iota(jnp.int32, (BAND, 1), 0) + row0
    k = lax.broadcasted_iota(jnp.int32, (1, modes_k), 1)
    fm = jnp.where(m <= modes_m // 2, m, m - modes_m // 2).astype(F32) / F32(modes_m // 2)
    fk = jnp.where(k <= modes_k // 2, k, k - modes_k // 2).astype(F32) / F32(modes_k // 2)
    radius = (jnp.full((1, 1), plane, jnp.int32).astype(F32) + F32(0.5)) / F32(RADIAL_ALL)
    turning = F32(VISC_TURN) * fm * fm / (radius * radius)
    return F32(1.0) / (F32(1.0) + F32(VISC_AXIAL) * fk * fk + turning)


def add_tile(acc, n, value):
    value = sum(value[r : r + 8] for r in range(0, value.shape[0], 8))
    acc[n] += sum(value[:, k : k + 128] for k in range(0, value.shape[1], 128))


def local_kernel(counts, last, paired, advect, *refs):
    take = taker(refs)
    v, vb, recv = (take(n) for n in counts[:3])
    two, anal_m = take(), take()
    if last:
        u0, out_b = take(counts[3]), []
        out, scale, gram, spec, acc = take(5)
        acc[...] = jnp.zeros_like(acc)
    else:
        out, out_b, spec = take(), take(counts[3]), take()
    chans, modes_m, modes_k = two.shape
    half = modes_k // 2
    for c in range(chans):
        spec[c] = jnp.dot(anal_m[...], two[c], preferred_element_type=F32)
    wave = lax.broadcasted_iota(jnp.int32, (1, half), 1).astype(F32) * advect[0]

    def step(lo, shift):
        at = pl.ds(pl.multiple_of(shift + lo, BAND), BAND)
        inv = inverse_divisor(shift + lo, modes_m, modes_k, own_plane())
        if last:
            scale[at, :] = inv * F32(RADIAL_GAIN)
            if paired:
                mate = inverse_divisor(shift + lo, modes_m, modes_k, paired_plane()) * F32(RADIAL_GAIN**2)
        for c in range(chans):
            row = c * modes_m + lo
            own = read(v, row, shift)
            drift = jnp.concatenate([-wave * own[:, half:], wave * own[:, :half]], axis=1)
            mid = F32(-2.0 * RADIAL_GAIN) * read(vb, row, shift).astype(F32)
            total = own + spec[c, at, :] + drift + mid
            if last:
                x0 = read(u0, row, shift)
                if paired:
                    total += mate * x0
                for n, (a, b) in enumerate(((x0, x0), (x0, own), (own, own))):
                    add_tile(acc, n, a * b)
            value = total * inv - read(recv, row, shift).astype(F32)
            write([out], row, shift, value)
            if not last:
                write(out_b, row, shift, value)

    for lo, hi in segments(modes_m, [*v, *(u0 if last else out_b)]):
        for_bands(lo, hi, functools.partial(step, lo))

    if last:
        gram[...] = jnp.zeros_like(gram)
        for n in range(3):
            gram[n : n + 1, :] = jnp.sum(acc[n], axis=0, keepdims=True)


def local_first(advect, v, vb, recv, two, tables, sizes):
    chans, modes_m, modes_k = two.shape
    args = [advect, *v, *vb, *recv, two, tables[3]]
    part, *part_b = kernel_call(
        functools.partial(local_kernel, (len(v), len(vb), len(recv), len(sizes)), False, False),
        "local_first",
        args,
        [IN_SMEM] + [IN_VMEM] * (len(args) - 1),
        [pltpu.VMEM((chans * modes_m, modes_k), F32)] + [pltpu.VMEM((n, modes_k), BF16) for n in sizes],
        scratch=[pltpu.VMEM(two.shape, F32)],
    )
    return part, part_b


def local_last(advect, v, vb, recv, two, tables, u0, paired):
    chans, modes_m, modes_k = two.shape
    args = [advect, *v, *vb, *recv, two, tables[3], *u0]
    return kernel_call(
        functools.partial(local_kernel, (len(v), len(vb), len(recv), len(u0)), True, paired),
        "local_last",
        args,
        [IN_SMEM] + [IN_VMEM] * (len(args) - 1),
        [
            pltpu.VMEM((chans * modes_m, modes_k), F32),
            pltpu.VMEM((modes_m, modes_k), F32),
            pltpu.VMEM((8, 128), F32),
        ],
        scratch=[pltpu.VMEM(two.shape, F32), pltpu.VMEM((3, 8, 128), F32)],
    )


def added(sides, row, shift):
    return functools.reduce(lambda a, b: a + b, [read(s, row, shift).astype(F32) for s in sides])


def first_kernel(groups, count, part, *refs):
    take = taker(refs)
    sides = [take(groups) for _ in range(count)]
    out, out_b = take(), take(len(refs) - groups * count - 1)
    chans, (modes_m, modes_k) = len(out_b), out_b[0].shape

    def step(lo, shift):
        inv = inverse_divisor(shift + lo, modes_m, modes_k, own_plane()) * F32(RADIAL_GAIN)
        for c in range(chans):
            row = c * modes_m + lo
            value = read([part], row, shift) + added(sides, row, shift) * inv
            write([out], row, shift, value)
            write(out_b, row, shift, value)

    for lo, hi in segments(modes_m, sides[0]):
        for_bands(lo, hi, functools.partial(step, lo))


def first_image(part, sides, chans):
    rows, modes_k = part.shape
    args = [part, *(x for side in sides for x in side)]
    return kernel_call(
        functools.partial(first_kernel, len(sides[0]), len(sides)),
        "first_image",
        args,
        [IN_VMEM] * len(args),
        [pltpu.VMEM(part.shape, F32)] + [pltpu.VMEM((rows // chans, modes_k), BF16)] * chans,
        flops=LONG,
    )


def on_diagonal():
    rows, lanes = (lax.broadcasted_iota(jnp.int32, (8, 128), n) for n in (0, 1))
    return rows == lanes


def second_kernel(first, counts, done, scale, u1, part, before, *refs):
    take = taker(refs)
    u0, planes = take(counts[0]), take(counts[1])
    out, gram, acc = take(3)
    modes_m = scale.shape[0]
    acc[...] = jnp.zeros_like(acc)

    def step(row, shift):
        at = pl.ds(pl.multiple_of(shift + row % modes_m, BAND), BAND)
        near = added([[p] for p in planes], row - first, shift)
        x2 = read([part], row, shift) + near * scale[at, :]
        write([out], row - first, shift, x2)
        for n, x in enumerate((read(u0, row, shift), read([u1], row, shift), x2)):
            add_tile(acc, n, x * x2)

    starts = {first, *range(0, first + out.shape[0], modes_m)}
    total = 0
    for group in u0:
        starts.add(total)
        total += group.shape[0]
    starts = [r for r in sorted(starts) if first <= r < first + out.shape[0]]
    for lo, hi in zip(starts, starts[1:] + [first + out.shape[0]]):
        for_bands(lo, hi, functools.partial(step, lo))

    rows = [jnp.sum(acc[n], axis=0, keepdims=True) for n in range(3)]
    total = before[...] + jnp.concatenate([jnp.zeros((3, 128), F32), *rows, jnp.zeros((2, 128), F32)], axis=0)
    if done:
        total = jnp.sum(total, axis=1, keepdims=True)
        total = jnp.sum(jnp.where(on_diagonal(), total, F32(0.0)), axis=0, keepdims=True)
    gram[...] = jnp.broadcast_to(total, gram.shape)


def second_image(first, scale, u0, u1, part, before, planes, slots=None):
    done = slots is not None
    tile = (slots, 128) if done else (8, 128)
    args = [scale, u1, part, before, *u0, *planes]
    return kernel_call(
        functools.partial(second_kernel, first, (len(u0), len(planes)), done),
        "second_image",
        args,
        [IN_VMEM] * len(args),
        [pltpu.VMEM(planes[0].shape, F32), pltpu.VMEM(tile, F32)],
        scratch=[pltpu.VMEM((3, 8, 128), F32)],
    )


def combine_kernel(cells, counts, grams, u1, *refs):
    take = taker(refs)
    u0, u2 = take(counts[0]), take(counts[1])
    out, hess, held, sems = take(4)
    total, modes_k = out.shape
    g = jnp.sum(grams[...], axis=0, keepdims=True) * F32(1.0 / cells)
    g = jnp.sum(jnp.where(on_diagonal(), g, F32(0.0)), axis=1, keepdims=True)
    g = jnp.broadcast_to(g, (8, 128))
    g00, g01, g11, g02, g12, g22 = (g[n : n + 1, :] for n in range(6))
    per_g00 = F32(1.0) / g00
    h11 = g01 * per_g00
    q = g11 - h11 * g01
    per_q = F32(1.0) / q
    w0 = g02 - h11 * g01
    w1 = g12 - h11 * g11
    ww = g22 - F32(2.0) * h11 * g12 + h11 * h11 * g11
    h22 = (w1 - h11 * w0) * per_q
    square = (ww - w0 * w0 * per_g00) * per_q - h22 * h22
    c2 = F32(1.0) / jnp.sqrt(q * square)
    c1 = -(h11 + h22) * c2
    c0 = (h11 * h22 - w0 * per_g00) * c2
    wide = [jnp.concatenate([x] * (modes_k // 128), axis=1) for x in (c0, c1, c2)]

    def step(row, shift):
        value = wide[0] * read(u0, row, shift) + wide[1] * read([u1], row, shift)
        write([held], row, shift, value + wide[2] * read(u2, row, shift))

    copies = []
    for r in range(0, total, ROWS):
        for_bands(r, r + ROWS, functools.partial(step, r))
        at = pl.ds(r, ROWS)
        copies.append(pltpu.make_async_copy(held.at[at], out.at[at], sems.at[len(copies)]))
        copies[-1].start()
    n0, s = jnp.sqrt(g00), jnp.sqrt(q)
    for n, value in enumerate((n0, h11, s / n0, w0 / (s * n0), h22, jnp.sqrt(square))):
        hess[n] = value[0, 0]
    for copy in copies:
        copy.wait()


def combine(cells, grams, u0, u1, u2):
    args = [grams, u1, *u0, *u2]
    return kernel_call(
        functools.partial(combine_kernel, cells, (len(u0), len(u2))),
        "combine",
        args,
        [IN_VMEM] * len(args),
        [jax.ShapeDtypeStruct(u1.shape, F32), jax.ShapeDtypeStruct((6,), F32)],
        out_specs=[IN_HBM, IN_SMEM],
        scratch=[pltpu.VMEM(u1.shape, F32), pltpu.SemaphoreType.DMA((u1.shape[0] // ROWS,))],
    )


def shifted(value, axis, steps):
    count = lax.axis_size(axis)
    return lax.ppermute(value, axis, [(i, (i + steps) % count) for i in range(count)])


def neighbour_planes(value, axis):
    count = lax.axis_size(axis)
    if count == 2:
        return [lax.ppermute(value, axis, [(0, 1), (1, 0)])]
    up = [(i, i + 1) for i in range(count - 1)]
    return [lax.ppermute(value, axis, up), lax.ppermute(value, axis, [(b, a) for a, b in up])]


def on_device(start_vector, coupling, advect):
    _, chans, rows_here, modes_m, modes_k = start_vector.shape
    assert rows_here == 1
    rows = chans * modes_m
    start = start_vector.reshape(rows, modes_k)
    couple = coupling.reshape(chans, chans, modes_m, modes_k)
    devices = lax.axis_size("seg") * lax.axis_size("rad")
    cells = float(devices * start.size)
    paired = lax.axis_size("rad") == 2

    early = EARLY_ROWS
    sizes = (rows - LATE_ROWS, LATE_ROWS) if paired else (modes_m,) * chans

    u0, u0b, near_one, pieces = [], [], [], None
    for first, size, parts in ((0, early, 0), (early, rows - early, chans)):
        field, rounded, pieces = take_rows(start, first, size, u0b, parts)
        u0.append(field)
        u0b.append(rounded)
        near_one.append(neighbour_planes(rounded, "rad"))
    next_one = [shifted(x, "seg", -1) for x in pieces]
    two, tables = transform(pieces, couple)
    part, part_b = local_first(advect, u0, pieces, next_one, two, tables, sizes)
    if paired:
        near_two = [neighbour_planes(x, "rad") for x in part_b]
    u1, *u1b = first_image(part, list(zip(*near_one)), chans)
    if not paired:
        near_two = [neighbour_planes(x, "rad") for x in u1b]
    next_two = [shifted(x, "seg", -1) for x in u1b]
    two, _ = transform(u1b, couple, tables)
    part, scale, gram = local_last(advect, [u1], u1b, next_two, two, tables, u0, paired)
    u2, first = [], 0
    for size, planes in zip(sizes, near_two):
        slots = devices if first + size == rows else None
        field, gram = second_image(first, scale, u0, u1, part, gram, planes, slots)
        first += size
        u2.append(field)
    grams = lax.all_to_all(gram, ("seg", "rad"), 0, 0)
    basis, hess = combine(cells, grams, u0, u1, u2)
    return basis.reshape(start_vector.shape), hess


def solution(mesh):
    return jax.shard_map(
        on_device,
        mesh=mesh,
        in_specs=(
            P("seg", None, "rad", None, None),
            P("seg", None, None, "rad", None, None),
            P("rad"),
        ),
        out_specs=(P("seg", None, "rad", None, None), P()),
        check_vma=False,
    )
```

```python
import functools
import math

import jax
import jax.numpy as jnp
from jax import lax
from jax.experimental import pallas as pl
from jax.experimental.pallas import tpu as pltpu
from jax.sharding import PartitionSpec as P

RADIAL_ALL = 256
WINDOW_START = 124
RADIAL_GAIN = 0.25
VISC_AXIAL = 4.0
VISC_TURN = 0.05

F32 = jnp.float32
BF16 = jnp.bfloat16
VMEM_LIMIT = 8 * 1024 * 1024
TRANSFORM_LIMIT = 22 * 1024 * 1024
ROWS = 128
COLS = 256
BAND = 16
LONG = 10**11
MEDIUM = 15 * 10**9
CHUNK = 64
EARLY_ROWS = 128
LATE_ROWS = 128

IN_SMEM = pl.BlockSpec(memory_space=pltpu.SMEM)
IN_VMEM = pl.BlockSpec(memory_space=pltpu.VMEM)
IN_HBM = pl.BlockSpec(memory_space=pltpu.HBM)


def kernel_call(body, name, args, in_specs, outs, out_specs=None, scratch=(), limit=VMEM_LIMIT, flops=1000):
    held = [
        a if s is IN_SMEM else pltpu.with_memory_space_constraint(a, s.memory_space)
        for a, s in zip(args, in_specs)
    ]
    more = {} if out_specs is None else {"out_specs": out_specs}
    return pl.pallas_call(
        body,
        out_shape=outs,
        in_specs=in_specs,
        scratch_shapes=list(scratch),
        compiler_params=pltpu.CompilerParams(vmem_limit_bytes=limit),
        cost_estimate=pl.CostEstimate(flops=flops, bytes_accessed=1000, transcendentals=0),
        name=name,
        **more,
    )(*held)


def sine_turns(y):
    x = y * F32(2.0 * math.pi)
    x2 = x * x
    acc = F32(1.0 / 6227020800.0)
    for c in (-1.0 / 39916800.0, 1.0 / 362880.0, -1.0 / 5040.0, 1.0 / 120.0, -1.0 / 6.0, 1.0):
        acc = acc * x2 + F32(c)
    return acc * x


def trig_block(row0, rows, cols, mode_axis, count, weighted):
    half = count // 2
    r = lax.broadcasted_iota(jnp.int32, (rows, cols), 0) + row0
    c = lax.broadcasted_iota(jnp.int32, (rows, cols), 1)
    mode, point = (r, c) if mode_axis == 0 else (c, r)
    is_cos = mode <= half
    freq = jnp.where(is_cos, mode, mode - half).astype(F32)
    phase = freq * point.astype(F32) - jnp.where(is_cos, F32(0.0), F32(count // 4))
    phase = phase - F32(count) * jnp.floor(phase * F32(1.0 / count))
    value = -sine_turns(F32(0.25) - jnp.abs(phase * F32(1.0 / count) - F32(0.5)))
    if weighted:
        edge = (mode == 0) | (mode == half)
        value = value * jnp.where(edge, F32(1.0 / count), F32(2.0 / count))
    return value.astype(BF16)


def fill_table(ref, mode_axis, weighted):
    count = ref.shape[0]

    @pl.loop(0, count // ROWS)
    def _(i):
        at = pl.multiple_of(i * ROWS, ROWS)
        ref[pl.ds(at, ROWS), :] = trig_block(at, ROWS, count, mode_axis, count, weighted)


def taker(refs):
    refs = list(refs)

    def take(count=None):
        if count is None:
            return refs.pop(0)
        out, refs[:count] = refs[:count], []
        return out

    return take


def segments(modes_m, groups):
    ends, total = {modes_m}, 0
    for group in groups:
        total += group.shape[0]
        ends.add(total % modes_m or modes_m)
    ends = sorted(ends)
    return list(zip([0] + ends[:-1], ends))


def starts_of(groups):
    return [sum(g.shape[0] for g in groups[:n]) for n in range(len(groups))]


def band(groups, row, shift):
    for group in groups:
        if row < group.shape[0]:
            return group, pl.ds(pl.multiple_of(shift + row, BAND), BAND)
        row -= group.shape[0]


def read(groups, row, shift):
    group, at = band(groups, row, shift)
    return group[at, :]


def write(groups, row, shift, value):
    group, at = band(groups, row, shift)
    group[at, :] = value.astype(group.dtype)


def for_bands(lo, hi, body):
    @pl.loop(0, (hi - lo) // BAND)
    def _(i):
        body(pl.multiple_of(i * BAND, BAND))


def take_kernel(first, v, *refs):
    take = taker(refs)
    early = [] if first == 0 else [take()]
    field, rounded = take(), take()
    pieces, sems = take(len(refs) - len(early) - 3), take()
    count = field.shape[0]
    copies = []
    for n, r in enumerate(range(0, count, ROWS)):
        copies.append(
            pltpu.make_async_copy(v.at[pl.ds(first + r, ROWS)], field.at[pl.ds(r, ROWS)], sems.at[n])
        )
        copies[n].start()

    def lay(row, value):
        for n, piece in enumerate(pieces):
            at = row - n * piece.shape[0]
            if 0 <= at < piece.shape[0]:
                piece[at : at + ROWS, :] = value

    for r in range(0, first, ROWS):
        lay(r, early[0][r : r + ROWS, :])
    for n, r in enumerate(range(0, count, ROWS)):
        copies[n].wait()
        value = field[r : r + ROWS, :].astype(BF16)
        rounded[r : r + ROWS, :] = value
        lay(first + r, value)


def take_rows(v, first, count, early=(), pieces=0):
    rows, modes_k = v.shape
    shapes = [pltpu.VMEM((count, modes_k), F32), pltpu.VMEM((count, modes_k), BF16)]
    field, rounded, *by_channel = kernel_call(
        functools.partial(take_kernel, first),
        "take_rows",
        [v, *early],
        [IN_HBM] + [IN_VMEM] * len(early),
        shapes + [pltpu.VMEM((rows // max(pieces, 1), modes_k), BF16)] * pieces,
        scratch=[pltpu.SemaphoreType.DMA((count // ROWS,))],
    )
    return field, rounded, by_channel


def transform_kernel(build, awaited, *refs):
    take = taker(refs)
    chans = len(refs) - awaited - (14 if build else 13)
    x = take(chans)
    take(awaited)
    couple_far = take()
    tables_far = None if build else take(3)
    out = take()
    if build:
        tables_far, anal_m = take(3), take()
    one, phys, mixed, couple, synth_k, synth_mt, anal_kt, sems = take(8)
    near = (synth_k, synth_mt, anal_kt)
    _, modes_m, modes_k = out.shape
    load = pltpu.make_async_copy(couple_far, couple, sems.at[3])
    ends = [(n, f) if build else (f, n) for n, f in zip(near, tables_far)]
    moves = [pltpu.make_async_copy(src, dst, sems.at[i]) for i, (src, dst) in enumerate(ends)]
    if not build:
        for move in moves[:2]:
            move.start()
    load.start()
    if not build:
        moves[2].start()

    def ready(i, mode_axis, weighted):
        if build:
            fill_table(near[i], mode_axis, weighted)
            moves[i].start()
        else:
            moves[i].wait()

    ready(0, 0, False)
    for c in range(chans):

        @pl.loop(0, modes_m // ROWS)
        def _(i):
            at = pl.ds(pl.multiple_of(i * ROWS, ROWS), ROWS)
            one[c, at, :] = jnp.dot(x[c][at, :], synth_k[...], preferred_element_type=F32).astype(BF16)

    ready(1, 1, False)
    load.wait()

    @pl.loop(0, modes_k // COLS)
    def _(z):
        zs = pl.ds(pl.multiple_of(z * COLS, COLS), COLS)
        for j in range(chans):
            phys[j] = jnp.dot(synth_mt[...], one[j, :, zs], preferred_element_type=F32)

        @pl.loop(0, modes_m // BAND)
        def _(i):
            ts = pl.ds(pl.multiple_of(i * BAND, BAND), BAND)
            parts = [phys[j, ts, :] for j in range(chans)]
            for c in range(chans):
                total = couple[c, 0, ts, zs].astype(F32) * parts[0]
                for j in range(1, chans):
                    total += couple[c, j, ts, zs].astype(F32) * parts[j]
                mixed[c, ts, zs] = total.astype(BF16)

    ready(2, 1, True)
    for c in range(chans):

        @pl.loop(0, modes_m // ROWS)
        def _(i):
            at = pl.ds(pl.multiple_of(i * ROWS, ROWS), ROWS)
            out[c, at, :] = jnp.dot(mixed[c, at, :], anal_kt[...], preferred_element_type=F32).astype(BF16)

    if build:
        fill_table(anal_m, 0, True)
        for move in moves:
            move.wait()


def transform(x, couple, tables=None, awaited=()):
    chans, _, modes_m, modes_k = couple.shape
    shape = (chans, modes_m, modes_k)
    sizes = [(modes_k, modes_k), (modes_m, modes_m), (modes_k, modes_k)]
    build = tables is None
    far = [] if build else list(tables[:3])
    outs, out_specs = [pltpu.VMEM(shape, BF16)], [IN_VMEM]
    if build:
        outs += [pltpu.HBM(n, BF16) for n in sizes] + [pltpu.VMEM((modes_m, modes_m), BF16)]
        out_specs += [IN_HBM] * 3 + [IN_VMEM]
    result = kernel_call(
        functools.partial(transform_kernel, build, len(awaited)),
        "transform",
        [*x, *awaited, couple, *far],
        [IN_VMEM] * (chans + len(awaited)) + [IN_HBM] * (1 + len(far)),
        outs,
        out_specs=out_specs,
        scratch=[
            pltpu.VMEM(shape, BF16),
            pltpu.VMEM((chans, modes_m, COLS), F32),
            pltpu.VMEM(shape, BF16),
            pltpu.VMEM(couple.shape, BF16),
            *[pltpu.VMEM(n, BF16) for n in sizes],
            pltpu.SemaphoreType.DMA((4,)),
        ],
        limit=TRANSFORM_LIMIT,
        flops=MEDIUM if awaited else 1000,
    )
    return result[0], (result[1:] if build else tables)


def own_plane():
    return WINDOW_START + lax.axis_index("rad")


def paired_plane():
    return WINDOW_START + 1 - lax.axis_index("rad")


def inverse_divisor(row0, modes_m, modes_k, plane):
    m = lax.broadcasted_iota(jnp.int32, (BAND, 1), 0) + row0
    k = lax.broadcasted_iota(jnp.int32, (1, modes_k), 1)
    fm = jnp.where(m <= modes_m // 2, m, m - modes_m // 2).astype(F32) / F32(modes_m // 2)
    fk = jnp.where(k <= modes_k // 2, k, k - modes_k // 2).astype(F32) / F32(modes_k // 2)
    radius = (jnp.full((1, 1), plane, jnp.int32).astype(F32) + F32(0.5)) / F32(RADIAL_ALL)
    turning = F32(VISC_TURN) * fm * fm / (radius * radius)
    return F32(1.0) / (F32(1.0) + F32(VISC_AXIAL) * fk * fk + turning)


def add_tile(acc, n, value):
    value = sum(value[r : r + 8] for r in range(0, value.shape[0], 8))
    acc[n] += sum(value[:, k : k + 128] for k in range(0, value.shape[1], 128))


def local_kernel(counts, last, paired, advect, *refs):
    take = taker(refs)
    v, vb, recv = (take(n) for n in counts[:3])
    two, anal_m = take(), take()
    if last:
        u0, out_b = take(counts[3]), []
        out, scale, gram, spec, acc = take(5)
        acc[...] = jnp.zeros_like(acc)
    else:
        out, out_b, spec = take(), take(counts[3]), take()
    chans, modes_m, modes_k = two.shape
    half = modes_k // 2
    for c in range(chans):
        spec[c] = jnp.dot(anal_m[...], two[c], preferred_element_type=F32)
    wave = lax.broadcasted_iota(jnp.int32, (1, half), 1).astype(F32) * advect[0]

    def step(lo, shift):
        at = pl.ds(pl.multiple_of(shift + lo, BAND), BAND)
        inv = inverse_divisor(shift + lo, modes_m, modes_k, own_plane())
        if last:
            scale[at, :] = inv * F32(RADIAL_GAIN)
            if paired:
                mate = inverse_divisor(shift + lo, modes_m, modes_k, paired_plane()) * F32(RADIAL_GAIN**2)
        for c in range(chans):
            row = c * modes_m + lo
            own = read(v, row, shift)
            drift = jnp.concatenate([-wave * own[:, half:], wave * own[:, :half]], axis=1)
            mid = F32(-2.0 * RADIAL_GAIN) * read(vb, row, shift).astype(F32)
            total = own + spec[c, at, :] + drift + mid
            if last:
                x0 = read(u0, row, shift)
                if paired:
                    total += mate * x0
                for n, (a, b) in enumerate(((x0, x0), (x0, own), (own, own))):
                    add_tile(acc, n, a * b)
            value = total * inv - read(recv, row, shift).astype(F32)
            write([out], row, shift, value)
            if not last:
                write(out_b, row, shift, value)

    for lo, hi in segments(modes_m, [*v, *(u0 if last else out_b)]):
        for_bands(lo, hi, functools.partial(step, lo))

    if last:
        gram[...] = jnp.zeros_like(gram)
        for n in range(3):
            gram[n : n + 1, :] = jnp.sum(acc[n], axis=0, keepdims=True)


def local_first(advect, v, vb, recv, two, tables, sizes):
    chans, modes_m, modes_k = two.shape
    args = [advect, *v, *vb, *recv, two, tables[3]]
    part, *part_b = kernel_call(
        functools.partial(local_kernel, (len(v), len(vb), len(recv), len(sizes)), False, False),
        "local_first",
        args,
        [IN_SMEM] + [IN_VMEM] * (len(args) - 1),
        [pltpu.VMEM((chans * modes_m, modes_k), F32)] + [pltpu.VMEM((n, modes_k), BF16) for n in sizes],
        scratch=[pltpu.VMEM(two.shape, F32)],
    )
    return part, part_b


def local_last(advect, v, vb, recv, two, tables, u0, paired):
    chans, modes_m, modes_k = two.shape
    args = [advect, *v, *vb, *recv, two, tables[3], *u0]
    return kernel_call(
        functools.partial(local_kernel, (len(v), len(vb), len(recv), len(u0)), True, paired),
        "local_last",
        args,
        [IN_SMEM] + [IN_VMEM] * (len(args) - 1),
        [
            pltpu.VMEM((chans * modes_m, modes_k), F32),
            pltpu.VMEM((modes_m, modes_k), F32),
            pltpu.VMEM((8, 128), F32),
        ],
        scratch=[pltpu.VMEM(two.shape, F32), pltpu.VMEM((3, 8, 128), F32)],
    )


def added(sides, row, shift):
    return functools.reduce(lambda a, b: a + b, [read(s, row, shift).astype(F32) for s in sides])


def first_kernel(groups, count, part, *refs):
    take = taker(refs)
    sides = [take(groups) for _ in range(count)]
    out, out_b = take(), take(len(refs) - groups * count - 1)
    chans, (modes_m, modes_k) = len(out_b), out_b[0].shape

    def step(lo, shift):
        inv = inverse_divisor(shift + lo, modes_m, modes_k, own_plane()) * F32(RADIAL_GAIN)
        for c in range(chans):
            row = c * modes_m + lo
            value = read([part], row, shift) + added(sides, row, shift) * inv
            write([out], row, shift, value)
            write(out_b, row, shift, value)

    for lo, hi in segments(modes_m, sides[0]):
        for_bands(lo, hi, functools.partial(step, lo))


def first_image(part, sides, chans):
    rows, modes_k = part.shape
    args = [part, *(x for side in sides for x in side)]
    return kernel_call(
        functools.partial(first_kernel, len(sides[0]), len(sides)),
        "first_image",
        args,
        [IN_VMEM] * len(args),
        [pltpu.VMEM(part.shape, F32)] + [pltpu.VMEM((rows // chans, modes_k), BF16)] * chans,
        flops=LONG,
    )


def on_diagonal():
    rows, lanes = (lax.broadcasted_iota(jnp.int32, (8, 128), n) for n in (0, 1))
    return rows == lanes


def second_kernel(first, counts, done, scale, u1, part, before, *refs):
    take = taker(refs)
    u0, planes = take(counts[0]), take(counts[1])
    out, gram, acc = take(3)
    modes_m = scale.shape[0]
    acc[...] = jnp.zeros_like(acc)

    def step(row, shift):
        at = pl.ds(pl.multiple_of(shift + row % modes_m, BAND), BAND)
        near = added([[p] for p in planes], row - first, shift)
        x2 = read([part], row, shift) + near * scale[at, :]
        write([out], row - first, shift, x2)
        for n, x in enumerate((read(u0, row, shift), read([u1], row, shift), x2)):
            add_tile(acc, n, x * x2)

    end = first + out.shape[0]
    starts = {first, *starts_of(u0), *range(0, end, modes_m)}
    starts = [r for r in sorted(starts) if first <= r < end]
    for lo, hi in zip(starts, starts[1:] + [end]):
        for_bands(lo, hi, functools.partial(step, lo))

    rows = [jnp.sum(acc[n], axis=0, keepdims=True) for n in range(3)]
    total = before[...] + jnp.concatenate([jnp.zeros((3, 128), F32), *rows, jnp.zeros((2, 128), F32)], axis=0)
    if done:
        total = jnp.sum(total, axis=1, keepdims=True)
        total = jnp.sum(jnp.where(on_diagonal(), total, F32(0.0)), axis=0, keepdims=True)
    gram[...] = jnp.broadcast_to(total, gram.shape)


def second_image(first, scale, u0, u1, part, before, planes, slots=None):
    done = slots is not None
    tile = (slots, 128) if done else (8, 128)
    args = [scale, u1, part, before, *u0, *planes]
    return kernel_call(
        functools.partial(second_kernel, first, (len(u0), len(planes)), done),
        "second_image",
        args,
        [IN_VMEM] * len(args),
        [pltpu.VMEM(planes[0].shape, F32), pltpu.VMEM(tile, F32)],
        scratch=[pltpu.VMEM((3, 8, 128), F32)],
    )


def combine_kernel(cells, counts, grams, u1, *refs):
    take = taker(refs)
    u0, u2 = take(counts[0]), take(counts[1])
    out, hess, held, sems = take(4)
    total, modes_k = out.shape
    g = jnp.sum(grams[...], axis=0, keepdims=True) * F32(1.0 / cells)
    g = jnp.sum(jnp.where(on_diagonal(), g, F32(0.0)), axis=1, keepdims=True)
    g = jnp.broadcast_to(g, (8, 128))
    g00, g01, g11, g02, g12, g22 = (g[n : n + 1, :] for n in range(6))
    per_g00 = F32(1.0) / g00
    h11 = g01 * per_g00
    q = g11 - h11 * g01
    per_q = F32(1.0) / q
    w0 = g02 - h11 * g01
    w1 = g12 - h11 * g11
    ww = g22 - F32(2.0) * h11 * g12 + h11 * h11 * g11
    h22 = (w1 - h11 * w0) * per_q
    square = (ww - w0 * w0 * per_g00) * per_q - h22 * h22
    c2 = F32(1.0) / jnp.sqrt(q * square)
    c1 = -(h11 + h22) * c2
    c0 = (h11 * h22 - w0 * per_g00) * c2
    wide = [jnp.concatenate([x] * (modes_k // 128), axis=1) for x in (c0, c1, c2)]

    def copy_out(n):
        at = pl.ds(pl.multiple_of(n * CHUNK, CHUNK), CHUNK)
        return pltpu.make_async_copy(held.at[at], out.at[at], sems.at[n])

    def step(first, n):
        for r in range(0, CHUNK, BAND):
            row, shift = first + r, pl.multiple_of(n * CHUNK, CHUNK)
            value = wide[0] * read(u0, row, shift) + wide[1] * read([u1], row, shift)
            write([held], row, shift, value + wide[2] * read(u2, row, shift))
        copy_out(n + first // CHUNK).start()

    starts = sorted({*starts_of(u0), *starts_of(u2)})
    for first, end in zip(starts, starts[1:] + [total]):
        pl.loop(0, (end - first) // CHUNK)(functools.partial(step, first))
    n0, s = jnp.sqrt(g00), jnp.sqrt(q)
    for n, value in enumerate((n0, h11, s / n0, w0 / (s * n0), h22, jnp.sqrt(square))):
        hess[n] = value[0, 0]
    pl.loop(0, total // CHUNK)(lambda n: copy_out(n).wait())


def combine(cells, grams, u0, u1, u2):
    args = [grams, u1, *u0, *u2]
    return kernel_call(
        functools.partial(combine_kernel, cells, (len(u0), len(u2))),
        "combine",
        args,
        [IN_VMEM] * len(args),
        [jax.ShapeDtypeStruct(u1.shape, F32), jax.ShapeDtypeStruct((6,), F32)],
        out_specs=[IN_HBM, IN_SMEM],
        scratch=[pltpu.VMEM(u1.shape, F32), pltpu.SemaphoreType.DMA((u1.shape[0] // CHUNK,))],
    )


def shifted(value, axis, steps):
    count = lax.axis_size(axis)
    return lax.ppermute(value, axis, [(i, (i + steps) % count) for i in range(count)])


def neighbour_planes(value, axis):
    count = lax.axis_size(axis)
    if count == 2:
        return [lax.ppermute(value, axis, [(0, 1), (1, 0)])]
    up = [(i, i + 1) for i in range(count - 1)]
    return [lax.ppermute(value, axis, up), lax.ppermute(value, axis, [(b, a) for a, b in up])]


def on_device(start_vector, coupling, advect):
    _, chans, rows_here, modes_m, modes_k = start_vector.shape
    assert rows_here == 1
    rows = chans * modes_m
    start = start_vector.reshape(rows, modes_k)
    couple = coupling.reshape(chans, chans, modes_m, modes_k)
    devices = lax.axis_size("seg") * lax.axis_size("rad")
    cells = float(devices * start.size)
    paired = lax.axis_size("rad") == 2

    early = EARLY_ROWS
    sizes = (rows - LATE_ROWS, LATE_ROWS) if paired else (modes_m,) * chans

    u0, u0b, near_one, pieces = [], [], [], None
    for first, size, parts in ((0, early, 0), (early, rows - early, chans)):
        field, rounded, pieces = take_rows(start, first, size, u0b, parts)
        u0.append(field)
        u0b.append(rounded)
        near_one.append(neighbour_planes(rounded, "rad"))
    next_one = [shifted(x, "seg", -1) for x in pieces]
    two, tables = transform(pieces, couple, awaited=near_one[0])
    part, part_b = local_first(advect, u0, pieces, next_one, two, tables, sizes)
    if paired:
        near_two = [neighbour_planes(x, "rad") for x in part_b]
    u1, *u1b = first_image(part, list(zip(*near_one)), chans)
    if not paired:
        near_two = [neighbour_planes(x, "rad") for x in u1b]
    next_two = [shifted(x, "seg", -1) for x in u1b]
    two, _ = transform(u1b, couple, tables)
    part, scale, gram = local_last(advect, [u1], u1b, next_two, two, tables, u0, paired)
    u2, first = [], 0
    for size, planes in zip(sizes, near_two):
        slots = devices if first + size == rows else None
        field, gram = second_image(first, scale, u0, u1, part, gram, planes, slots)
        first += size
        u2.append(field)
    grams = lax.all_to_all(gram, ("seg", "rad"), 0, 0)
    basis, hess = combine(cells, grams, u0, u1, u2)
    return basis.reshape(start_vector.shape), hess


def solution(mesh):
    return jax.shard_map(
        on_device,
        mesh=mesh,
        in_specs=(
            P("seg", None, "rad", None, None),
            P("seg", None, None, "rad", None, None),
            P("rad"),
        ),
        out_specs=(P("seg", None, "rad", None, None), P()),
        check_vma=False,
    )
```

```python
import functools
import math

import jax
import jax.numpy as jnp
from jax import lax
from jax.experimental import pallas as pl
from jax.experimental.pallas import tpu as pltpu
from jax.sharding import PartitionSpec as P

RADIAL_ALL = 256
WINDOW_START = 124
RADIAL_GAIN = 0.25
VISC_AXIAL = 4.0
VISC_TURN = 0.05

F32 = jnp.float32
BF16 = jnp.bfloat16
VMEM_LIMIT = 8 * 1024 * 1024
TRANSFORM_LIMIT = 22 * 1024 * 1024
ROWS = 128
COLS = 256
BAND = 16
LONG = 10**11
MEDIUM = 15 * 10**9
CHUNK = 64
EARLY_ROWS = 128
LATE_ROWS = 128

IN_SMEM = pl.BlockSpec(memory_space=pltpu.SMEM)
IN_VMEM = pl.BlockSpec(memory_space=pltpu.VMEM)
IN_HBM = pl.BlockSpec(memory_space=pltpu.HBM)


def kernel_call(body, name, args, in_specs, outs, out_specs=None, scratch=(), limit=VMEM_LIMIT, flops=1000):
    held = [
        a if s is IN_SMEM else pltpu.with_memory_space_constraint(a, s.memory_space)
        for a, s in zip(args, in_specs)
    ]
    more = {} if out_specs is None else {"out_specs": out_specs}
    return pl.pallas_call(
        body,
        out_shape=outs,
        in_specs=in_specs,
        scratch_shapes=list(scratch),
        compiler_params=pltpu.CompilerParams(vmem_limit_bytes=limit),
        cost_estimate=pl.CostEstimate(flops=flops, bytes_accessed=1000, transcendentals=0),
        name=name,
        **more,
    )(*held)


def sine_turns(y):
    x = y * F32(2.0 * math.pi)
    x2 = x * x
    acc = F32(1.0 / 6227020800.0)
    for c in (-1.0 / 39916800.0, 1.0 / 362880.0, -1.0 / 5040.0, 1.0 / 120.0, -1.0 / 6.0, 1.0):
        acc = acc * x2 + F32(c)
    return acc * x


def trig_block(row0, rows, cols, mode_axis, count, weighted):
    half = count // 2
    r = lax.broadcasted_iota(jnp.int32, (rows, cols), 0) + row0
    c = lax.broadcasted_iota(jnp.int32, (rows, cols), 1)
    mode, point = (r, c) if mode_axis == 0 else (c, r)
    is_cos = mode <= half
    freq = jnp.where(is_cos, mode, mode - half).astype(F32)
    phase = freq * point.astype(F32) - jnp.where(is_cos, F32(0.0), F32(count // 4))
    phase = phase - F32(count) * jnp.floor(phase * F32(1.0 / count))
    value = -sine_turns(F32(0.25) - jnp.abs(phase * F32(1.0 / count) - F32(0.5)))
    if weighted:
        edge = (mode == 0) | (mode == half)
        value = value * jnp.where(edge, F32(1.0 / count), F32(2.0 / count))
    return value.astype(BF16)


def fill_table(ref, mode_axis, weighted):
    count = ref.shape[0]

    @pl.loop(0, count // ROWS)
    def _(i):
        at = pl.multiple_of(i * ROWS, ROWS)
        ref[pl.ds(at, ROWS), :] = trig_block(at, ROWS, count, mode_axis, count, weighted)


def taker(refs):
    refs = list(refs)

    def take(count=None):
        if count is None:
            return refs.pop(0)
        out, refs[:count] = refs[:count], []
        return out

    return take


def segments(modes_m, groups):
    ends, total = {modes_m}, 0
    for group in groups:
        total += group.shape[0]
        ends.add(total % modes_m or modes_m)
    ends = sorted(ends)
    return list(zip([0] + ends[:-1], ends))


def starts_of(groups):
    return [sum(g.shape[0] for g in groups[:n]) for n in range(len(groups))]


def band(groups, row, shift):
    for group in groups:
        if row < group.shape[0]:
            return group, pl.ds(pl.multiple_of(shift + row, BAND), BAND)
        row -= group.shape[0]


def read(groups, row, shift):
    group, at = band(groups, row, shift)
    return group[at, :]


def write(groups, row, shift, value):
    group, at = band(groups, row, shift)
    group[at, :] = value.astype(group.dtype)


def for_bands(lo, hi, body):
    @pl.loop(0, (hi - lo) // BAND)
    def _(i):
        body(pl.multiple_of(i * BAND, BAND))


def take_kernel(first, v, *refs):
    take = taker(refs)
    early = [] if first == 0 else [take()]
    field, rounded = take(), take()
    pieces, sems = take(len(refs) - len(early) - 3), take()
    count = field.shape[0]
    copies = []
    for n, r in enumerate(range(0, count, ROWS)):
        copies.append(
            pltpu.make_async_copy(v.at[pl.ds(first + r, ROWS)], field.at[pl.ds(r, ROWS)], sems.at[n])
        )
        copies[n].start()

    def lay(row, value):
        for n, piece in enumerate(pieces):
            at = row - n * piece.shape[0]
            if 0 <= at < piece.shape[0]:
                piece[at : at + ROWS, :] = value

    for r in range(0, first, ROWS):
        lay(r, early[0][r : r + ROWS, :])
    for n, r in enumerate(range(0, count, ROWS)):
        copies[n].wait()
        value = field[r : r + ROWS, :].astype(BF16)
        rounded[r : r + ROWS, :] = value
        lay(first + r, value)


def take_rows(v, first, count, early=(), pieces=0):
    rows, modes_k = v.shape
    shapes = [pltpu.VMEM((count, modes_k), F32), pltpu.VMEM((count, modes_k), BF16)]
    field, rounded, *by_channel = kernel_call(
        functools.partial(take_kernel, first),
        "take_rows",
        [v, *early],
        [IN_HBM] + [IN_VMEM] * len(early),
        shapes + [pltpu.VMEM((rows // max(pieces, 1), modes_k), BF16)] * pieces,
        scratch=[pltpu.SemaphoreType.DMA((count // ROWS,))],
    )
    return field, rounded, by_channel


def transform_kernel(build, awaited, *refs):
    take = taker(refs)
    chans = len(refs) - awaited - (14 if build else 13)
    x = take(chans)
    take(awaited)
    couple_far = take()
    tables_far = None if build else take(3)
    out = take()
    if build:
        tables_far, anal_m = take(3), take()
    one, phys, mixed, couple, synth_k, synth_mt, anal_kt, sems = take(8)
    near = (synth_k, synth_mt, anal_kt)
    _, modes_m, modes_k = out.shape
    load = pltpu.make_async_copy(couple_far, couple, sems.at[3])
    ends = [(n, f) if build else (f, n) for n, f in zip(near, tables_far)]
    moves = [pltpu.make_async_copy(src, dst, sems.at[i]) for i, (src, dst) in enumerate(ends)]
    if not build:
        for move in moves[:2]:
            move.start()
    load.start()
    if not build:
        moves[2].start()

    def ready(i, mode_axis, weighted):
        if build:
            fill_table(near[i], mode_axis, weighted)
            moves[i].start()
        else:
            moves[i].wait()

    ready(0, 0, False)
    for c in range(chans):

        @pl.loop(0, modes_m // ROWS)
        def _(i):
            at = pl.ds(pl.multiple_of(i * ROWS, ROWS), ROWS)
            one[c, at, :] = jnp.dot(x[c][at, :], synth_k[...], preferred_element_type=F32).astype(BF16)

    ready(1, 1, False)
    load.wait()

    @pl.loop(0, modes_k // COLS)
    def _(z):
        zs = pl.ds(pl.multiple_of(z * COLS, COLS), COLS)
        for j in range(chans):
            phys[j] = jnp.dot(synth_mt[...], one[j, :, zs], preferred_element_type=F32)

        @pl.loop(0, modes_m // BAND)
        def _(i):
            ts = pl.ds(pl.multiple_of(i * BAND, BAND), BAND)
            parts = [phys[j, ts, :] for j in range(chans)]
            for c in range(chans):
                total = couple[c, 0, ts, zs].astype(F32) * parts[0]
                for j in range(1, chans):
                    total += couple[c, j, ts, zs].astype(F32) * parts[j]
                mixed[c, ts, zs] = total.astype(BF16)

    ready(2, 1, True)
    for c in range(chans):

        @pl.loop(0, modes_m // ROWS)
        def _(i):
            at = pl.ds(pl.multiple_of(i * ROWS, ROWS), ROWS)
            out[c, at, :] = jnp.dot(mixed[c, at, :], anal_kt[...], preferred_element_type=F32).astype(BF16)

    if build:
        fill_table(anal_m, 0, True)
        for move in moves:
            move.wait()


def transform(x, couple, tables=None, awaited=()):
    chans, _, modes_m, modes_k = couple.shape
    shape = (chans, modes_m, modes_k)
    sizes = [(modes_k, modes_k), (modes_m, modes_m), (modes_k, modes_k)]
    build = tables is None
    far = [] if build else list(tables[:3])
    outs, out_specs = [pltpu.VMEM(shape, BF16)], [IN_VMEM]
    if build:
        outs += [pltpu.HBM(n, BF16) for n in sizes] + [pltpu.VMEM((modes_m, modes_m), BF16)]
        out_specs += [IN_HBM] * 3 + [IN_VMEM]
    result = kernel_call(
        functools.partial(transform_kernel, build, len(awaited)),
        "transform",
        [*x, *awaited, couple, *far],
        [IN_VMEM] * (chans + len(awaited)) + [IN_HBM] * (1 + len(far)),
        outs,
        out_specs=out_specs,
        scratch=[
            pltpu.VMEM(shape, BF16),
            pltpu.VMEM((chans, modes_m, COLS), F32),
            pltpu.VMEM(shape, BF16),
            pltpu.VMEM(couple.shape, BF16),
            *[pltpu.VMEM(n, BF16) for n in sizes],
            pltpu.SemaphoreType.DMA((4,)),
        ],
        limit=TRANSFORM_LIMIT,
        flops=MEDIUM if awaited else 1000,
    )
    return result[0], (result[1:] if build else tables)


def own_plane():
    return WINDOW_START + lax.axis_index("rad")


def paired_plane():
    return WINDOW_START + 1 - lax.axis_index("rad")


def inverse_divisor(row0, modes_m, modes_k, plane):
    m = lax.broadcasted_iota(jnp.int32, (BAND, 1), 0) + row0
    k = lax.broadcasted_iota(jnp.int32, (1, modes_k), 1)
    fm = jnp.where(m <= modes_m // 2, m, m - modes_m // 2).astype(F32) / F32(modes_m // 2)
    fk = jnp.where(k <= modes_k // 2, k, k - modes_k // 2).astype(F32) / F32(modes_k // 2)
    radius = (jnp.full((1, 1), plane, jnp.int32).astype(F32) + F32(0.5)) / F32(RADIAL_ALL)
    turning = F32(VISC_TURN) * fm * fm / (radius * radius)
    return F32(1.0) / (F32(1.0) + F32(VISC_AXIAL) * fk * fk + turning)


def add_tile(acc, n, value):
    value = sum(value[r : r + 8] for r in range(0, value.shape[0], 8))
    acc[n] += sum(value[:, k : k + 128] for k in range(0, value.shape[1], 128))


def local_kernel(counts, last, paired, advect, *refs):
    take = taker(refs)
    v, vb, recv = (take(n) for n in counts[:3])
    two, anal_m = take(), take()
    if last:
        u0, out_b = take(counts[3]), []
        out, scale, gram, spec, acc = take(5)
        acc[...] = jnp.zeros_like(acc)
    else:
        out, out_b, spec = take(), take(counts[3]), take()
    chans, modes_m, modes_k = two.shape
    half = modes_k // 2
    for c in range(chans):
        spec[c] = jnp.dot(anal_m[...], two[c], preferred_element_type=F32)
    wave = lax.broadcasted_iota(jnp.int32, (1, half), 1).astype(F32) * advect[0]

    def step(lo, shift):
        at = pl.ds(pl.multiple_of(shift + lo, BAND), BAND)
        inv = inverse_divisor(shift + lo, modes_m, modes_k, own_plane())
        if last:
            scale[at, :] = inv * F32(RADIAL_GAIN)
            if paired:
                mate = inverse_divisor(shift + lo, modes_m, modes_k, paired_plane()) * F32(RADIAL_GAIN**2)
        for c in range(chans):
            row = c * modes_m + lo
            own = read(v, row, shift)
            drift = jnp.concatenate([-wave * own[:, half:], wave * own[:, :half]], axis=1)
            mid = F32(-2.0 * RADIAL_GAIN) * read(vb, row, shift).astype(F32)
            total = own + spec[c, at, :] + drift + mid
            if last:
                x0 = read(u0, row, shift)
                if paired:
                    total += mate * x0
                for n, (a, b) in enumerate(((x0, x0), (x0, own), (own, own))):
                    add_tile(acc, n, a * b)
            value = total * inv - read(recv, row, shift).astype(F32)
            write([out], row, shift, value)
            if not last:
                write(out_b, row, shift, value)

    for lo, hi in segments(modes_m, [*v, *(u0 if last else out_b)]):
        for_bands(lo, hi, functools.partial(step, lo))

    if last:
        gram[...] = jnp.zeros_like(gram)
        for n in range(3):
            gram[n : n + 1, :] = jnp.sum(acc[n], axis=0, keepdims=True)


def local_first(advect, v, vb, recv, two, tables, sizes):
    chans, modes_m, modes_k = two.shape
    args = [advect, *v, *vb, *recv, two, tables[3]]
    part, *part_b = kernel_call(
        functools.partial(local_kernel, (len(v), len(vb), len(recv), len(sizes)), False, False),
        "local_first",
        args,
        [IN_SMEM] + [IN_VMEM] * (len(args) - 1),
        [pltpu.VMEM((chans * modes_m, modes_k), F32)] + [pltpu.VMEM((n, modes_k), BF16) for n in sizes],
        scratch=[pltpu.VMEM(two.shape, F32)],
    )
    return part, part_b


def local_last(advect, v, vb, recv, two, tables, u0, paired):
    chans, modes_m, modes_k = two.shape
    args = [advect, *v, *vb, *recv, two, tables[3], *u0]
    return kernel_call(
        functools.partial(local_kernel, (len(v), len(vb), len(recv), len(u0)), True, paired),
        "local_last",
        args,
        [IN_SMEM] + [IN_VMEM] * (len(args) - 1),
        [
            pltpu.VMEM((chans * modes_m, modes_k), F32),
            pltpu.VMEM((modes_m, modes_k), F32),
            pltpu.VMEM((8, 128), F32),
        ],
        scratch=[pltpu.VMEM(two.shape, F32), pltpu.VMEM((3, 8, 128), F32)],
    )


def added(sides, row, shift):
    return functools.reduce(lambda a, b: a + b, [read(s, row, shift).astype(F32) for s in sides])


def first_kernel(groups, count, part, *refs):
    take = taker(refs)
    sides = [take(groups) for _ in range(count)]
    out, out_b = take(), take(len(refs) - groups * count - 1)
    chans, (modes_m, modes_k) = len(out_b), out_b[0].shape

    def step(lo, shift):
        inv = inverse_divisor(shift + lo, modes_m, modes_k, own_plane()) * F32(RADIAL_GAIN)
        for c in range(chans):
            row = c * modes_m + lo
            value = read([part], row, shift) + added(sides, row, shift) * inv
            write([out], row, shift, value)
            write(out_b, row, shift, value)

    for lo, hi in segments(modes_m, sides[0]):
        for_bands(lo, hi, functools.partial(step, lo))


def first_image(part, sides, chans):
    rows, modes_k = part.shape
    args = [part, *(x for side in sides for x in side)]
    return kernel_call(
        functools.partial(first_kernel, len(sides[0]), len(sides)),
        "first_image",
        args,
        [IN_VMEM] * len(args),
        [pltpu.VMEM(part.shape, F32)] + [pltpu.VMEM((rows // chans, modes_k), BF16)] * chans,
        flops=LONG,
    )


def on_diagonal():
    rows, lanes = (lax.broadcasted_iota(jnp.int32, (8, 128), n) for n in (0, 1))
    return rows == lanes


def second_kernel(first, counts, done, scale, u1, part, before, *refs):
    take = taker(refs)
    u0, planes = take(counts[0]), take(counts[1])
    out, gram, acc = take(3)
    modes_m = scale.shape[0]
    acc[...] = jnp.zeros_like(acc)

    def step(row, shift):
        at = pl.ds(pl.multiple_of(shift + row % modes_m, BAND), BAND)
        near = added([[p] for p in planes], row - first, shift)
        x2 = read([part], row, shift) + near * scale[at, :]
        write([out], row - first, shift, x2)
        for n, x in enumerate((read(u0, row, shift), read([u1], row, shift), x2)):
            add_tile(acc, n, x * x2)

    end = first + out.shape[0]
    starts = {first, *starts_of(u0), *range(0, end, modes_m)}
    starts = [r for r in sorted(starts) if first <= r < end]
    for lo, hi in zip(starts, starts[1:] + [end]):
        for_bands(lo, hi, functools.partial(step, lo))

    rows = [jnp.sum(acc[n], axis=0, keepdims=True) for n in range(3)]
    total = before[...] + jnp.concatenate([jnp.zeros((3, 128), F32), *rows, jnp.zeros((2, 128), F32)], axis=0)
    if done:
        total = jnp.sum(total, axis=1, keepdims=True)
        total = jnp.sum(jnp.where(on_diagonal(), total, F32(0.0)), axis=0, keepdims=True)
    gram[...] = jnp.broadcast_to(total, gram.shape)


def second_image(first, scale, u0, u1, part, before, planes, slots=None):
    done = slots is not None
    tile = (slots, 128) if done else (8, 128)
    args = [scale, u1, part, before, *u0, *planes]
    return kernel_call(
        functools.partial(second_kernel, first, (len(u0), len(planes)), done),
        "second_image",
        args,
        [IN_VMEM] * len(args),
        [pltpu.VMEM(planes[0].shape, F32), pltpu.VMEM(tile, F32)],
        scratch=[pltpu.VMEM((3, 8, 128), F32)],
    )


def combine_kernel(cells, counts, grams, u1, *refs):
    take = taker(refs)
    u0, u2 = take(counts[0]), take(counts[1])
    out, hess, held, sems = take(4)
    total, modes_k = out.shape
    g = jnp.sum(grams[...], axis=0, keepdims=True) * F32(1.0 / cells)
    g = jnp.sum(jnp.where(on_diagonal(), g, F32(0.0)), axis=1, keepdims=True)
    g = jnp.broadcast_to(g, (8, 128))
    g00, g01, g11, g02, g12, g22 = (g[n : n + 1, :] for n in range(6))
    per_g00 = F32(1.0) / g00
    h11 = g01 * per_g00
    q = g11 - h11 * g01
    per_q = F32(1.0) / q
    w0 = g02 - h11 * g01
    w1 = g12 - h11 * g11
    ww = g22 - F32(2.0) * h11 * g12 + h11 * h11 * g11
    h22 = (w1 - h11 * w0) * per_q
    ratio = w0 * per_g00
    square = (ww - w0 * ratio) * per_q - h22 * h22
    c2 = F32(1.0) / jnp.sqrt(q * square)
    c1 = -(h11 + h22) * c2
    c0 = (h11 * h22 - ratio) * c2
    wide = [jnp.concatenate([x] * (modes_k // 128), axis=1) for x in (c0, c1, c2)]

    def copy_out(n):
        at = pl.ds(pl.multiple_of(n * CHUNK, CHUNK), CHUNK)
        return pltpu.make_async_copy(held.at[at], out.at[at], sems.at[n])

    def step(first, n):
        for r in range(0, CHUNK, BAND):
            row, shift = first + r, pl.multiple_of(n * CHUNK, CHUNK)
            value = wide[0] * read(u0, row, shift) + wide[1] * read([u1], row, shift)
            write([held], row, shift, value + wide[2] * read(u2, row, shift))
        copy_out(n + first // CHUNK).start()

    starts = sorted({*starts_of(u0), *starts_of(u2)})
    for first, end in zip(starts, starts[1:] + [total]):
        pl.loop(0, (end - first) // CHUNK)(functools.partial(step, first))
    n0, s = jnp.sqrt(g00), jnp.sqrt(q)
    for n, value in enumerate((n0, h11, s / n0, w0 / (s * n0), h22, jnp.sqrt(square))):
        hess[n] = value[0, 0]
    pl.loop(0, total // CHUNK)(lambda n: copy_out(n).wait())


def combine(cells, grams, u0, u1, u2):
    args = [grams, u1, *u0, *u2]
    return kernel_call(
        functools.partial(combine_kernel, cells, (len(u0), len(u2))),
        "combine",
        args,
        [IN_VMEM] * len(args),
        [jax.ShapeDtypeStruct(u1.shape, F32), jax.ShapeDtypeStruct((6,), F32)],
        out_specs=[IN_HBM, IN_SMEM],
        scratch=[pltpu.VMEM(u1.shape, F32), pltpu.SemaphoreType.DMA((u1.shape[0] // CHUNK,))],
    )


def shifted(value, axis, steps):
    count = lax.axis_size(axis)
    return lax.ppermute(value, axis, [(i, (i + steps) % count) for i in range(count)])


def neighbour_planes(value, axis):
    count = lax.axis_size(axis)
    if count == 2:
        return [lax.ppermute(value, axis, [(0, 1), (1, 0)])]
    up = [(i, i + 1) for i in range(count - 1)]
    return [lax.ppermute(value, axis, up), lax.ppermute(value, axis, [(b, a) for a, b in up])]


def on_device(start_vector, coupling, advect):
    _, chans, rows_here, modes_m, modes_k = start_vector.shape
    assert rows_here == 1
    rows = chans * modes_m
    start = start_vector.reshape(rows, modes_k)
    couple = coupling.reshape(chans, chans, modes_m, modes_k)
    devices = lax.axis_size("seg") * lax.axis_size("rad")
    cells = float(devices * start.size)
    paired = lax.axis_size("rad") == 2

    early = EARLY_ROWS
    sizes = (rows - LATE_ROWS, LATE_ROWS) if paired else (modes_m,) * chans

    u0, u0b, near_one, pieces = [], [], [], None
    for first, size, parts in ((0, early, 0), (early, rows - early, chans)):
        field, rounded, pieces = take_rows(start, first, size, u0b, parts)
        u0.append(field)
        u0b.append(rounded)
        near_one.append(neighbour_planes(rounded, "rad"))
    next_one = [shifted(x, "seg", -1) for x in pieces]
    two, tables = transform(pieces, couple, awaited=near_one[0])
    part, part_b = local_first(advect, u0, pieces, next_one, two, tables, sizes)
    if paired:
        near_two = [neighbour_planes(x, "rad") for x in part_b]
    u1, *u1b = first_image(part, list(zip(*near_one)), chans)
    if not paired:
        near_two = [neighbour_planes(x, "rad") for x in u1b]
    next_two = [shifted(x, "seg", -1) for x in u1b]
    two, _ = transform(u1b, couple, tables)
    part, scale, gram = local_last(advect, [u1], u1b, next_two, two, tables, u0, paired)
    u2, first = [], 0
    for size, planes in zip(sizes, near_two):
        slots = devices if first + size == rows else None
        field, gram = second_image(first, scale, u0, u1, part, gram, planes, slots)
        first += size
        u2.append(field)
    grams = lax.all_to_all(gram, ("rad", "seg"), 0, 0)
    basis, hess = combine(cells, grams, u0, u1, u2)
    return basis.reshape(start_vector.shape), hess


def solution(mesh):
    return jax.shard_map(
        on_device,
        mesh=mesh,
        in_specs=(
            P("seg", None, "rad", None, None),
            P("seg", None, None, "rad", None, None),
            P("rad"),
        ),
        out_specs=(P("seg", None, "rad", None, None), P()),
        check_vma=False,
    )
```

```python
import functools
import math

import jax
import jax.numpy as jnp
from jax import lax
from jax.experimental import pallas as pl
from jax.experimental.pallas import tpu as pltpu
from jax.sharding import PartitionSpec as P

RADIAL_ALL = 256
WINDOW_START = 124
RADIAL_GAIN = 0.25
VISC_AXIAL = 4.0
VISC_TURN = 0.05

F32 = jnp.float32
BF16 = jnp.bfloat16
VMEM_LIMIT = 8 * 1024 * 1024
TRANSFORM_LIMIT = 22 * 1024 * 1024
ROWS = 128
COLS = 256
BAND = 16
LONG = 10**11
MEDIUM = 15 * 10**9
CHUNK = 64
NEAR = 8
EARLY_ROWS = 128
LATE_ROWS = 128

IN_SMEM = pl.BlockSpec(memory_space=pltpu.SMEM)
IN_VMEM = pl.BlockSpec(memory_space=pltpu.VMEM)
IN_HBM = pl.BlockSpec(memory_space=pltpu.HBM)


def kernel_call(body, name, args, in_specs, outs, out_specs=None, scratch=(), limit=VMEM_LIMIT, flops=1000):
    held = [
        a if s is IN_SMEM else pltpu.with_memory_space_constraint(a, s.memory_space)
        for a, s in zip(args, in_specs)
    ]
    more = {} if out_specs is None else {"out_specs": out_specs}
    return pl.pallas_call(
        body,
        out_shape=outs,
        in_specs=in_specs,
        scratch_shapes=list(scratch),
        compiler_params=pltpu.CompilerParams(vmem_limit_bytes=limit),
        cost_estimate=pl.CostEstimate(flops=flops, bytes_accessed=1000, transcendentals=0),
        name=name,
        **more,
    )(*held)


def sine_turns(y):
    x = y * F32(2.0 * math.pi)
    x2 = x * x
    acc = F32(1.0 / 6227020800.0)
    for c in (-1.0 / 39916800.0, 1.0 / 362880.0, -1.0 / 5040.0, 1.0 / 120.0, -1.0 / 6.0, 1.0):
        acc = acc * x2 + F32(c)
    return acc * x


def trig_block(row0, rows, cols, mode_axis, count, weighted):
    half = count // 2
    r = lax.broadcasted_iota(jnp.int32, (rows, cols), 0) + row0
    c = lax.broadcasted_iota(jnp.int32, (rows, cols), 1)
    mode, point = (r, c) if mode_axis == 0 else (c, r)
    is_cos = mode <= half
    freq = jnp.where(is_cos, mode, mode - half).astype(F32)
    phase = freq * point.astype(F32) - jnp.where(is_cos, F32(0.0), F32(count // 4))
    phase = phase - F32(count) * jnp.floor(phase * F32(1.0 / count))
    value = -sine_turns(F32(0.25) - jnp.abs(phase * F32(1.0 / count) - F32(0.5)))
    if weighted:
        edge = (mode == 0) | (mode == half)
        value = value * jnp.where(edge, F32(1.0 / count), F32(2.0 / count))
    return value.astype(BF16)


def fill_table(ref, mode_axis, weighted):
    count = ref.shape[0]

    @pl.loop(0, count // ROWS)
    def _(i):
        at = pl.multiple_of(i * ROWS, ROWS)
        ref[pl.ds(at, ROWS), :] = trig_block(at, ROWS, count, mode_axis, count, weighted)


def taker(refs):
    refs = list(refs)

    def take(count=None):
        if count is None:
            return refs.pop(0)
        out, refs[:count] = refs[:count], []
        return out

    return take


def segments(modes_m, groups):
    ends, total = {modes_m}, 0
    for group in groups:
        total += group.shape[0]
        ends.add(total % modes_m or modes_m)
    ends = sorted(ends)
    return list(zip([0] + ends[:-1], ends))


def starts_of(groups):
    return [sum(g.shape[0] for g in groups[:n]) for n in range(len(groups))]


def band(groups, row, shift):
    for group in groups:
        if row < group.shape[0]:
            return group, pl.ds(pl.multiple_of(shift + row, BAND), BAND)
        row -= group.shape[0]


def read(groups, row, shift):
    group, at = band(groups, row, shift)
    return group[at, :]


def write(groups, row, shift, value):
    group, at = band(groups, row, shift)
    group[at, :] = value.astype(group.dtype)


def for_bands(lo, hi, body):
    @pl.loop(0, (hi - lo) // BAND)
    def _(i):
        body(pl.multiple_of(i * BAND, BAND))


def take_kernel(first, v, *refs):
    take = taker(refs)
    early = [] if first == 0 else [take()]
    field, rounded = take(), take()
    pieces, sems = take(len(refs) - len(early) - 3), take()
    count = field.shape[0]
    copies = []
    for n, r in enumerate(range(0, count, ROWS)):
        copies.append(
            pltpu.make_async_copy(v.at[pl.ds(first + r, ROWS)], field.at[pl.ds(r, ROWS)], sems.at[n])
        )
        copies[n].start()

    def lay(row, value):
        for n, piece in enumerate(pieces):
            at = row - n * piece.shape[0]
            if 0 <= at < piece.shape[0]:
                piece[at : at + ROWS, :] = value

    for r in range(0, first, ROWS):
        lay(r, early[0][r : r + ROWS, :])
    for n, r in enumerate(range(0, count, ROWS)):
        copies[n].wait()
        value = field[r : r + ROWS, :].astype(BF16)
        rounded[r : r + ROWS, :] = value
        lay(first + r, value)


def take_rows(v, first, count, early=(), pieces=0):
    rows, modes_k = v.shape
    shapes = [pltpu.VMEM((count, modes_k), F32), pltpu.VMEM((count, modes_k), BF16)]
    field, rounded, *by_channel = kernel_call(
        functools.partial(take_kernel, first),
        "take_rows",
        [v, *early],
        [IN_HBM] + [IN_VMEM] * len(early),
        shapes + [pltpu.VMEM((rows // max(pieces, 1), modes_k), BF16)] * pieces,
        scratch=[pltpu.SemaphoreType.DMA((count // ROWS,))],
    )
    return field, rounded, by_channel


def transform_kernel(build, awaited, *refs):
    take = taker(refs)
    chans = len(refs) - awaited - (14 if build else 13)
    x = take(chans)
    take(awaited)
    couple_far = take()
    tables_far = None if build else take(3)
    out = take()
    if build:
        tables_far, anal_m = take(3), take()
    one, phys, mixed, couple, synth_k, synth_mt, anal_kt, sems = take(8)
    near = (synth_k, synth_mt, anal_kt)
    _, modes_m, modes_k = out.shape
    load = pltpu.make_async_copy(couple_far, couple, sems.at[3])
    ends = [(n, f) if build else (f, n) for n, f in zip(near, tables_far)]
    moves = [pltpu.make_async_copy(src, dst, sems.at[i]) for i, (src, dst) in enumerate(ends)]
    if not build:
        for move in moves[:2]:
            move.start()
    load.start()
    if not build:
        moves[2].start()

    def ready(i, mode_axis, weighted):
        if build:
            fill_table(near[i], mode_axis, weighted)
            moves[i].start()
        else:
            moves[i].wait()

    ready(0, 0, False)
    for c in range(chans):

        @pl.loop(0, modes_m // ROWS)
        def _(i):
            at = pl.ds(pl.multiple_of(i * ROWS, ROWS), ROWS)
            one[c, at, :] = jnp.dot(x[c][at, :], synth_k[...], preferred_element_type=F32).astype(BF16)

    ready(1, 1, False)
    load.wait()

    @pl.loop(0, modes_k // COLS)
    def _(z):
        zs = pl.ds(pl.multiple_of(z * COLS, COLS), COLS)
        for j in range(chans):
            phys[j] = jnp.dot(synth_mt[...], one[j, :, zs], preferred_element_type=F32)

        @pl.loop(0, modes_m // BAND)
        def _(i):
            ts = pl.ds(pl.multiple_of(i * BAND, BAND), BAND)
            parts = [phys[j, ts, :] for j in range(chans)]
            for c in range(chans):
                total = couple[c, 0, ts, zs].astype(F32) * parts[0]
                for j in range(1, chans):
                    total += couple[c, j, ts, zs].astype(F32) * parts[j]
                mixed[c, ts, zs] = total.astype(BF16)

    ready(2, 1, True)
    for c in range(chans):

        @pl.loop(0, modes_m // ROWS)
        def _(i):
            at = pl.ds(pl.multiple_of(i * ROWS, ROWS), ROWS)
            out[c, at, :] = jnp.dot(mixed[c, at, :], anal_kt[...], preferred_element_type=F32).astype(BF16)

    if build:
        fill_table(anal_m, 0, True)
        for move in moves:
            move.wait()


def transform(x, couple, tables=None, awaited=()):
    chans, _, modes_m, modes_k = couple.shape
    shape = (chans, modes_m, modes_k)
    sizes = [(modes_k, modes_k), (modes_m, modes_m), (modes_k, modes_k)]
    build = tables is None
    far = [] if build else list(tables[:3])
    outs, out_specs = [pltpu.VMEM(shape, BF16)], [IN_VMEM]
    if build:
        outs += [pltpu.HBM(n, BF16) for n in sizes] + [pltpu.VMEM((modes_m, modes_m), BF16)]
        out_specs += [IN_HBM] * 3 + [IN_VMEM]
    result = kernel_call(
        functools.partial(transform_kernel, build, len(awaited)),
        "transform",
        [*x, *awaited, couple, *far],
        [IN_VMEM] * (chans + len(awaited)) + [IN_HBM] * (1 + len(far)),
        outs,
        out_specs=out_specs,
        scratch=[
            pltpu.VMEM(shape, BF16),
            pltpu.VMEM((chans, modes_m, COLS), F32),
            pltpu.VMEM(shape, BF16),
            pltpu.VMEM(couple.shape, BF16),
            *[pltpu.VMEM(n, BF16) for n in sizes],
            pltpu.SemaphoreType.DMA((4,)),
        ],
        limit=TRANSFORM_LIMIT,
        flops=MEDIUM if awaited else 1000,
    )
    return result[0], (result[1:] if build else tables)


def own_plane():
    return WINDOW_START + lax.axis_index("rad")


def paired_plane():
    return WINDOW_START + 1 - lax.axis_index("rad")


def inverse_divisor(row0, modes_m, modes_k, plane):
    m = lax.broadcasted_iota(jnp.int32, (BAND, 1), 0) + row0
    k = lax.broadcasted_iota(jnp.int32, (1, modes_k), 1)
    fm = jnp.where(m <= modes_m // 2, m, m - modes_m // 2).astype(F32) / F32(modes_m // 2)
    fk = jnp.where(k <= modes_k // 2, k, k - modes_k // 2).astype(F32) / F32(modes_k // 2)
    radius = (jnp.full((1, 1), plane, jnp.int32).astype(F32) + F32(0.5)) / F32(RADIAL_ALL)
    turning = F32(VISC_TURN) * fm * fm / (radius * radius)
    return F32(1.0) / (F32(1.0) + F32(VISC_AXIAL) * fk * fk + turning)


def add_tile(acc, n, value):
    value = sum(value[r : r + 8] for r in range(0, value.shape[0], 8))
    acc[n] += sum(value[:, k : k + 128] for k in range(0, value.shape[1], 128))


def local_kernel(counts, last, paired, advect, *refs):
    take = taker(refs)
    v, vb, recv = (take(n) for n in counts[:3])
    two, anal_m = take(), take()
    if last:
        u0, out_b = take(counts[3]), []
        out, scale, gram, spec, acc = take(5)
        acc[...] = jnp.zeros_like(acc)
    else:
        out, out_b, spec = take(), take(counts[3]), take()
    chans, modes_m, modes_k = two.shape
    half = modes_k // 2
    for c in range(chans):
        spec[c] = jnp.dot(anal_m[...], two[c], preferred_element_type=F32)
    wave = lax.broadcasted_iota(jnp.int32, (1, half), 1).astype(F32) * advect[0]

    def step(lo, shift):
        at = pl.ds(pl.multiple_of(shift + lo, BAND), BAND)
        inv = inverse_divisor(shift + lo, modes_m, modes_k, own_plane())
        if last:
            scale[at, :] = inv * F32(RADIAL_GAIN)
            if paired:
                mate = inverse_divisor(shift + lo, modes_m, modes_k, paired_plane()) * F32(RADIAL_GAIN**2)
        for c in range(chans):
            row = c * modes_m + lo
            own = read(v, row, shift)
            drift = jnp.concatenate([-wave * own[:, half:], wave * own[:, :half]], axis=1)
            mid = F32(-2.0 * RADIAL_GAIN) * read(vb, row, shift).astype(F32)
            total = own + spec[c, at, :] + drift + mid
            if last:
                x0 = read(u0, row, shift)
                if paired:
                    total += mate * x0
                for n, (a, b) in enumerate(((x0, x0), (x0, own), (own, own))):
                    add_tile(acc, n, a * b)
            value = total * inv - read(recv, row, shift).astype(F32)
            write([out], row, shift, value)
            if not last:
                write(out_b, row, shift, value)

    for lo, hi in segments(modes_m, [*v, *(u0 if last else out_b)]):
        for_bands(lo, hi, functools.partial(step, lo))

    if last:
        gram[...] = jnp.zeros_like(gram)
        for n in range(3):
            gram[n : n + 1, :] = jnp.sum(acc[n], axis=0, keepdims=True)


def local_first(advect, v, vb, recv, two, tables, sizes):
    chans, modes_m, modes_k = two.shape
    args = [advect, *v, *vb, *recv, two, tables[3]]
    part, *part_b = kernel_call(
        functools.partial(local_kernel, (len(v), len(vb), len(recv), len(sizes)), False, False),
        "local_first",
        args,
        [IN_SMEM] + [IN_VMEM] * (len(args) - 1),
        [pltpu.VMEM((chans * modes_m, modes_k), F32)] + [pltpu.VMEM((n, modes_k), BF16) for n in sizes],
        scratch=[pltpu.VMEM(two.shape, F32)],
    )
    return part, part_b


def local_last(advect, v, vb, recv, two, tables, u0, paired):
    chans, modes_m, modes_k = two.shape
    args = [advect, *v, *vb, *recv, two, tables[3], *u0]
    return kernel_call(
        functools.partial(local_kernel, (len(v), len(vb), len(recv), len(u0)), True, paired),
        "local_last",
        args,
        [IN_SMEM] + [IN_VMEM] * (len(args) - 1),
        [
            pltpu.VMEM((chans * modes_m, modes_k), F32),
            pltpu.VMEM((modes_m, modes_k), F32),
            pltpu.VMEM((8, 128), F32),
        ],
        scratch=[pltpu.VMEM(two.shape, F32), pltpu.VMEM((3, 8, 128), F32)],
    )


def added(sides, row, shift):
    return functools.reduce(lambda a, b: a + b, [read(s, row, shift).astype(F32) for s in sides])


def first_kernel(groups, count, part, *refs):
    take = taker(refs)
    sides = [take(groups) for _ in range(count)]
    out, out_b = take(), take(len(refs) - groups * count - 1)
    chans, (modes_m, modes_k) = len(out_b), out_b[0].shape

    def step(lo, shift):
        inv = inverse_divisor(shift + lo, modes_m, modes_k, own_plane()) * F32(RADIAL_GAIN)
        for c in range(chans):
            row = c * modes_m + lo
            value = read([part], row, shift) + added(sides, row, shift) * inv
            write([out], row, shift, value)
            write(out_b, row, shift, value)

    for lo, hi in segments(modes_m, sides[0]):
        for_bands(lo, hi, functools.partial(step, lo))


def first_image(part, sides, chans):
    rows, modes_k = part.shape
    args = [part, *(x for side in sides for x in side)]
    return kernel_call(
        functools.partial(first_kernel, len(sides[0]), len(sides)),
        "first_image",
        args,
        [IN_VMEM] * len(args),
        [pltpu.VMEM(part.shape, F32)] + [pltpu.VMEM((rows // chans, modes_k), BF16)] * chans,
        flops=LONG,
    )


def on_diagonal():
    rows, lanes = (lax.broadcasted_iota(jnp.int32, (8, 128), n) for n in (0, 1))
    return rows == lanes


def second_kernel(first, counts, done, scale, u1, part, before, *refs):
    take = taker(refs)
    u0, planes = take(counts[0]), take(counts[1])
    out, gram, acc = take(3)
    modes_m = scale.shape[0]
    acc[...] = jnp.zeros_like(acc)

    def step(row, shift):
        at = pl.ds(pl.multiple_of(shift + row % modes_m, BAND), BAND)
        near = added([[p] for p in planes], row - first, shift)
        x2 = read([part], row, shift) + near * scale[at, :]
        write([out], row - first, shift, x2)
        for n, x in enumerate((read(u0, row, shift), read([u1], row, shift), x2)):
            add_tile(acc, n, x * x2)

    end = first + out.shape[0]
    starts = {first, *starts_of(u0), *range(0, end, modes_m)}
    starts = [r for r in sorted(starts) if first <= r < end]
    for lo, hi in zip(starts, starts[1:] + [end]):
        for_bands(lo, hi, functools.partial(step, lo))

    rows = [jnp.sum(acc[n], axis=0, keepdims=True) for n in range(3)]
    total = before[...] + jnp.concatenate([jnp.zeros((3, 128), F32), *rows, jnp.zeros((2, 128), F32)], axis=0)
    if done:
        total = jnp.sum(total, axis=1, keepdims=True)
        total = jnp.sum(jnp.where(on_diagonal(), total, F32(0.0)), axis=0, keepdims=True)
    gram[...] = jnp.broadcast_to(total, gram.shape)


def second_image(first, scale, u0, u1, part, before, planes, slots=None):
    done = slots is not None
    tile = (slots, 128) if done else (8, 128)
    args = [scale, u1, part, before, *u0, *planes]
    return kernel_call(
        functools.partial(second_kernel, first, (len(u0), len(planes)), done),
        "second_image",
        args,
        [IN_VMEM] * len(args),
        [pltpu.VMEM(planes[0].shape, F32), pltpu.VMEM(tile, F32)],
        scratch=[pltpu.VMEM((3, 8, 128), F32)],
    )


def combine_kernel(cells, counts, grams, u1, *refs):
    take = taker(refs)
    u0, u2 = take(counts[0]), take(counts[1])
    out, hess, held, sems = take(4)
    total, modes_k = out.shape
    g = jnp.sum(grams[...], axis=0, keepdims=True) * F32(1.0 / cells)
    g = jnp.sum(jnp.where(on_diagonal(), g, F32(0.0)), axis=1, keepdims=True)
    g = jnp.broadcast_to(g, (8, 128))
    g00, g01, g11, g02, g12, g22 = (g[n : n + 1, :] for n in range(6))
    per_g00 = F32(1.0) / g00
    h11 = g01 * per_g00
    q = g11 - h11 * g01
    per_q = F32(1.0) / q
    w0 = g02 - h11 * g01
    w1 = g12 - h11 * g11
    ww = g22 - F32(2.0) * h11 * g12 + h11 * h11 * g11
    h22 = (w1 - h11 * w0) * per_q
    ratio = w0 * per_g00
    square = (ww - w0 * ratio) * per_q - h22 * h22
    c2 = F32(1.0) / jnp.sqrt(q * square)
    c1 = -(h11 + h22) * c2
    c0 = (h11 * h22 - ratio) * c2
    wide = [jnp.concatenate([x] * (modes_k // 128), axis=1) for x in (c0, c1, c2)]

    def copy_out(n):
        at = pl.ds(pl.multiple_of(n * CHUNK, CHUNK), CHUNK)
        return pltpu.make_async_copy(held.at[at], out.at[at], sems.at[n])

    def step(first, n):
        for r in range(0, CHUNK, BAND):
            row, shift = first + r, pl.multiple_of(n * CHUNK, CHUNK)
            value = wide[0] * read(u0, row, shift) + wide[1] * read([u1], row, shift)
            write([held], row, shift, value + wide[2] * read(u2, row, shift))
        copy_out(n + first // CHUNK).start()

    starts = sorted({*starts_of(u0), *starts_of(u2)})
    for first, end in zip(starts, starts[1:] + [total]):
        pl.loop(0, (end - first) // CHUNK)(functools.partial(step, first))
    n0, s = jnp.sqrt(g00), jnp.sqrt(q)
    for n, value in enumerate((n0, h11, s / n0, w0 / (s * n0), h22, jnp.sqrt(square))):
        hess[n] = value[0, 0]
    pl.loop(0, total // CHUNK)(lambda n: copy_out(n).wait())


def combine(cells, grams, u0, u1, u2):
    args = [grams, u1, *u0, *u2]
    return kernel_call(
        functools.partial(combine_kernel, cells, (len(u0), len(u2))),
        "combine",
        args,
        [IN_VMEM] * len(args),
        [jax.ShapeDtypeStruct(u1.shape, F32), jax.ShapeDtypeStruct((6,), F32)],
        out_specs=[IN_HBM, IN_SMEM],
        scratch=[pltpu.VMEM(u1.shape, F32), pltpu.SemaphoreType.DMA((u1.shape[0] // CHUNK,))],
    )


def shifted(value, axis, steps):
    count = lax.axis_size(axis)
    return lax.ppermute(value, axis, [(i, (i + steps) % count) for i in range(count)])


def neighbour_planes(value, axis):
    count = lax.axis_size(axis)
    if count == 2:
        return [lax.ppermute(value, axis, [(0, 1), (1, 0)])]
    up = [(i, i + 1) for i in range(count - 1)]
    return [lax.ppermute(value, axis, up), lax.ppermute(value, axis, [(b, a) for a, b in up])]


def group_of(devices):
    return NEAR if devices % NEAR == 0 else devices


def resum_kernel(rows, out):
    out[...] = jnp.broadcast_to(jnp.sum(rows[...], axis=0, keepdims=True), out.shape)


def gathered(rows, axes, devices):
    near, far = rows.shape[0], devices // rows.shape[0]
    groups = [[g * near + i for i in range(near)] for g in range(far)]
    rows = lax.all_to_all(rows, axes, 0, 0, axis_index_groups=groups)
    if far == 1:
        return rows
    rows = kernel_call(resum_kernel, "resum", [rows], [IN_VMEM], pltpu.VMEM((far, rows.shape[1]), F32))
    return lax.all_to_all(rows, axes, 0, 0, axis_index_groups=[list(g) for g in zip(*groups)])


def on_device(start_vector, coupling, advect):
    _, chans, rows_here, modes_m, modes_k = start_vector.shape
    assert rows_here == 1
    rows = chans * modes_m
    start = start_vector.reshape(rows, modes_k)
    couple = coupling.reshape(chans, chans, modes_m, modes_k)
    devices = lax.axis_size("seg") * lax.axis_size("rad")
    cells = float(devices * start.size)
    paired = lax.axis_size("rad") == 2

    early = EARLY_ROWS
    sizes = (rows - LATE_ROWS, LATE_ROWS) if paired else (modes_m,) * chans

    u0, u0b, near_one, pieces = [], [], [], None
    for first, size, parts in ((0, early, 0), (early, rows - early, chans)):
        field, rounded, pieces = take_rows(start, first, size, u0b, parts)
        u0.append(field)
        u0b.append(rounded)
        near_one.append(neighbour_planes(rounded, "rad"))
    next_one = [shifted(x, "seg", -1) for x in pieces]
    two, tables = transform(pieces, couple, awaited=near_one[0])
    part, part_b = local_first(advect, u0, pieces, next_one, two, tables, sizes)
    if paired:
        near_two = [neighbour_planes(x, "rad") for x in part_b]
    u1, *u1b = first_image(part, list(zip(*near_one)), chans)
    if not paired:
        near_two = [neighbour_planes(x, "rad") for x in u1b]
    next_two = [shifted(x, "seg", -1) for x in u1b]
    two, _ = transform(u1b, couple, tables)
    part, scale, gram = local_last(advect, [u1], u1b, next_two, two, tables, u0, paired)
    u2, first = [], 0
    for size, planes in zip(sizes, near_two):
        slots = group_of(devices) if first + size == rows else None
        field, gram = second_image(first, scale, u0, u1, part, gram, planes, slots)
        first += size
        u2.append(field)
    grams = gathered(gram, ("seg", "rad"), devices)
    basis, hess = combine(cells, grams, u0, u1, u2)
    return basis.reshape(start_vector.shape), hess


def solution(mesh):
    return jax.shard_map(
        on_device,
        mesh=mesh,
        in_specs=(
            P("seg", None, "rad", None, None),
            P("seg", None, None, "rad", None, None),
            P("rad"),
        ),
        out_specs=(P("seg", None, "rad", None, None), P()),
        check_vma=False,
    )
```

```python
import functools
import math

import jax
import jax.numpy as jnp
from jax import lax
from jax.experimental import pallas as pl
from jax.experimental.pallas import tpu as pltpu
from jax.sharding import PartitionSpec as P

RADIAL_ALL = 256
WINDOW_START = 124
RADIAL_GAIN = 0.25
VISC_AXIAL = 4.0
VISC_TURN = 0.05

F32 = jnp.float32
BF16 = jnp.bfloat16
VMEM_LIMIT = 8 * 1024 * 1024
TRANSFORM_LIMIT = 22 * 1024 * 1024
ROWS = 128
COLS = 256
BAND = 16
LONG = 10**11
MEDIUM = 15 * 10**9
CHUNK = 64
EARLY_ROWS = 128
LATE_ROWS = 128

IN_SMEM = pl.BlockSpec(memory_space=pltpu.SMEM)
IN_VMEM = pl.BlockSpec(memory_space=pltpu.VMEM)
IN_HBM = pl.BlockSpec(memory_space=pltpu.HBM)


def kernel_call(body, name, args, in_specs, outs, out_specs=None, scratch=(), limit=VMEM_LIMIT, flops=1000):
    held = [
        a if s is IN_SMEM else pltpu.with_memory_space_constraint(a, s.memory_space)
        for a, s in zip(args, in_specs)
    ]
    more = {} if out_specs is None else {"out_specs": out_specs}
    return pl.pallas_call(
        body,
        out_shape=outs,
        in_specs=in_specs,
        scratch_shapes=list(scratch),
        compiler_params=pltpu.CompilerParams(vmem_limit_bytes=limit),
        cost_estimate=pl.CostEstimate(flops=flops, bytes_accessed=1000, transcendentals=0),
        name=name,
        **more,
    )(*held)


def sine_turns(y):
    x = y * F32(2.0 * math.pi)
    x2 = x * x
    acc = F32(1.0 / 6227020800.0)
    for c in (-1.0 / 39916800.0, 1.0 / 362880.0, -1.0 / 5040.0, 1.0 / 120.0, -1.0 / 6.0, 1.0):
        acc = acc * x2 + F32(c)
    return acc * x


def trig_block(row0, rows, cols, mode_axis, count, weighted):
    half = count // 2
    r = lax.broadcasted_iota(jnp.int32, (rows, cols), 0) + row0
    c = lax.broadcasted_iota(jnp.int32, (rows, cols), 1)
    mode, point = (r, c) if mode_axis == 0 else (c, r)
    is_cos = mode <= half
    freq = jnp.where(is_cos, mode, mode - half).astype(F32)
    phase = freq * point.astype(F32) - jnp.where(is_cos, F32(0.0), F32(count // 4))
    phase = phase - F32(count) * jnp.floor(phase * F32(1.0 / count))
    value = -sine_turns(F32(0.25) - jnp.abs(phase * F32(1.0 / count) - F32(0.5)))
    if weighted:
        edge = (mode == 0) | (mode == half)
        value = value * jnp.where(edge, F32(1.0 / count), F32(2.0 / count))
    return value.astype(BF16)


def fill_table(ref, mode_axis, weighted):
    count = ref.shape[0]

    @pl.loop(0, count // ROWS)
    def _(i):
        at = pl.multiple_of(i * ROWS, ROWS)
        ref[pl.ds(at, ROWS), :] = trig_block(at, ROWS, count, mode_axis, count, weighted)


def taker(refs):
    refs = list(refs)

    def take(count=None):
        if count is None:
            return refs.pop(0)
        out, refs[:count] = refs[:count], []
        return out

    return take


def segments(modes_m, groups):
    ends, total = {modes_m}, 0
    for group in groups:
        total += group.shape[0]
        ends.add(total % modes_m or modes_m)
    ends = sorted(ends)
    return list(zip([0] + ends[:-1], ends))


def starts_of(groups):
    return [sum(g.shape[0] for g in groups[:n]) for n in range(len(groups))]


def band(groups, row, shift):
    for group in groups:
        if row < group.shape[0]:
            return group, pl.ds(pl.multiple_of(shift + row, BAND), BAND)
        row -= group.shape[0]


def read(groups, row, shift):
    group, at = band(groups, row, shift)
    return group[at, :]


def write(groups, row, shift, value):
    group, at = band(groups, row, shift)
    group[at, :] = value.astype(group.dtype)


def for_bands(lo, hi, body):
    @pl.loop(0, (hi - lo) // BAND)
    def _(i):
        body(pl.multiple_of(i * BAND, BAND))


def take_kernel(first, v, *refs):
    take = taker(refs)
    early = [] if first == 0 else [take()]
    field, rounded = take(), take()
    pieces, sems = take(len(refs) - len(early) - 3), take()
    count = field.shape[0]
    copies = []
    for n, r in enumerate(range(0, count, ROWS)):
        copies.append(
            pltpu.make_async_copy(v.at[pl.ds(first + r, ROWS)], field.at[pl.ds(r, ROWS)], sems.at[n])
        )
        copies[n].start()

    def lay(row, value):
        for n, piece in enumerate(pieces):
            at = row - n * piece.shape[0]
            if 0 <= at < piece.shape[0]:
                piece[at : at + ROWS, :] = value

    for r in range(0, first, ROWS):
        lay(r, early[0][r : r + ROWS, :])
    for n, r in enumerate(range(0, count, ROWS)):
        copies[n].wait()
        value = field[r : r + ROWS, :].astype(BF16)
        rounded[r : r + ROWS, :] = value
        lay(first + r, value)


def take_rows(v, first, count, early=(), pieces=0):
    rows, modes_k = v.shape
    shapes = [pltpu.VMEM((count, modes_k), F32), pltpu.VMEM((count, modes_k), BF16)]
    field, rounded, *by_channel = kernel_call(
        functools.partial(take_kernel, first),
        "take_rows",
        [v, *early],
        [IN_HBM] + [IN_VMEM] * len(early),
        shapes + [pltpu.VMEM((rows // max(pieces, 1), modes_k), BF16)] * pieces,
        scratch=[pltpu.SemaphoreType.DMA((count // ROWS,))],
    )
    return field, rounded, by_channel


def transform_kernel(build, awaited, *refs):
    take = taker(refs)
    chans = len(refs) - awaited - (14 if build else 13)
    x = take(chans)
    take(awaited)
    couple_far = take()
    tables_far = None if build else take(3)
    out = take()
    if build:
        tables_far, anal_m = take(3), take()
    one, phys, mixed, couple, synth_k, synth_mt, anal_kt, sems = take(8)
    near = (synth_k, synth_mt, anal_kt)
    _, modes_m, modes_k = out.shape
    load = pltpu.make_async_copy(couple_far, couple, sems.at[3])
    ends = [(n, f) if build else (f, n) for n, f in zip(near, tables_far)]
    moves = [pltpu.make_async_copy(src, dst, sems.at[i]) for i, (src, dst) in enumerate(ends)]
    if not build:
        for move in moves[:2]:
            move.start()
    load.start()
    if not build:
        moves[2].start()

    def ready(i, mode_axis, weighted):
        if build:
            fill_table(near[i], mode_axis, weighted)
            moves[i].start()
        else:
            moves[i].wait()

    ready(0, 0, False)
    for c in range(chans):

        @pl.loop(0, modes_m // ROWS)
        def _(i):
            at = pl.ds(pl.multiple_of(i * ROWS, ROWS), ROWS)
            one[c, at, :] = jnp.dot(x[c][at, :], synth_k[...], preferred_element_type=F32).astype(BF16)

    ready(1, 1, False)
    load.wait()

    @pl.loop(0, modes_k // COLS)
    def _(z):
        zs = pl.ds(pl.multiple_of(z * COLS, COLS), COLS)
        for j in range(chans):
            phys[j] = jnp.dot(synth_mt[...], one[j, :, zs], preferred_element_type=F32)

        @pl.loop(0, modes_m // BAND)
        def _(i):
            ts = pl.ds(pl.multiple_of(i * BAND, BAND), BAND)
            parts = [phys[j, ts, :] for j in range(chans)]
            for c in range(chans):
                total = couple[c, 0, ts, zs].astype(F32) * parts[0]
                for j in range(1, chans):
                    total += couple[c, j, ts, zs].astype(F32) * parts[j]
                mixed[c, ts, zs] = total.astype(BF16)

    ready(2, 1, True)
    for c in range(chans):

        @pl.loop(0, modes_m // ROWS)
        def _(i):
            at = pl.ds(pl.multiple_of(i * ROWS, ROWS), ROWS)
            out[c, at, :] = jnp.dot(mixed[c, at, :], anal_kt[...], preferred_element_type=F32).astype(BF16)

    if build:
        fill_table(anal_m, 0, True)
        for move in moves:
            move.wait()


def transform(x, couple, tables=None, awaited=()):
    chans, _, modes_m, modes_k = couple.shape
    shape = (chans, modes_m, modes_k)
    sizes = [(modes_k, modes_k), (modes_m, modes_m), (modes_k, modes_k)]
    build = tables is None
    far = [] if build else list(tables[:3])
    outs, out_specs = [pltpu.VMEM(shape, BF16)], [IN_VMEM]
    if build:
        outs += [pltpu.HBM(n, BF16) for n in sizes] + [pltpu.VMEM((modes_m, modes_m), BF16)]
        out_specs += [IN_HBM] * 3 + [IN_VMEM]
    result = kernel_call(
        functools.partial(transform_kernel, build, len(awaited)),
        "transform",
        [*x, *awaited, couple, *far],
        [IN_VMEM] * (chans + len(awaited)) + [IN_HBM] * (1 + len(far)),
        outs,
        out_specs=out_specs,
        scratch=[
            pltpu.VMEM(shape, BF16),
            pltpu.VMEM((chans, modes_m, COLS), F32),
            pltpu.VMEM(shape, BF16),
            pltpu.VMEM(couple.shape, BF16),
            *[pltpu.VMEM(n, BF16) for n in sizes],
            pltpu.SemaphoreType.DMA((4,)),
        ],
        limit=TRANSFORM_LIMIT,
        flops=MEDIUM if awaited else 1000,
    )
    return result[0], (result[1:] if build else tables)


def own_plane():
    return WINDOW_START + lax.axis_index("rad")


def paired_plane():
    return WINDOW_START + 1 - lax.axis_index("rad")


def inverse_divisor(row0, modes_m, modes_k, plane):
    m = lax.broadcasted_iota(jnp.int32, (BAND, 1), 0) + row0
    k = lax.broadcasted_iota(jnp.int32, (1, modes_k), 1)
    fm = jnp.where(m <= modes_m // 2, m, m - modes_m // 2).astype(F32) / F32(modes_m // 2)
    fk = jnp.where(k <= modes_k // 2, k, k - modes_k // 2).astype(F32) / F32(modes_k // 2)
    radius = (jnp.full((1, 1), plane, jnp.int32).astype(F32) + F32(0.5)) / F32(RADIAL_ALL)
    turning = F32(VISC_TURN) * fm * fm / (radius * radius)
    return F32(1.0) / (F32(1.0) + F32(VISC_AXIAL) * fk * fk + turning)


def add_tile(acc, n, value):
    value = sum(value[r : r + 8] for r in range(0, value.shape[0], 8))
    acc[n] += sum(value[:, k : k + 128] for k in range(0, value.shape[1], 128))


def local_kernel(counts, last, paired, advect, *refs):
    take = taker(refs)
    v, vb, recv = (take(n) for n in counts[:3])
    two, anal_m = take(), take()
    if last:
        u0, out_b = take(counts[3]), []
        out, scale, gram, spec, acc = take(5)
        acc[...] = jnp.zeros_like(acc)
    else:
        out, out_b, spec = take(), take(counts[3]), take()
    chans, modes_m, modes_k = two.shape
    half = modes_k // 2
    for c in range(chans):
        spec[c] = jnp.dot(anal_m[...], two[c], preferred_element_type=F32)
    wave = lax.broadcasted_iota(jnp.int32, (1, half), 1).astype(F32) * advect[0]

    def step(lo, shift):
        at = pl.ds(pl.multiple_of(shift + lo, BAND), BAND)
        inv = inverse_divisor(shift + lo, modes_m, modes_k, own_plane())
        if last:
            scale[at, :] = inv * F32(RADIAL_GAIN)
            if paired:
                mate = inverse_divisor(shift + lo, modes_m, modes_k, paired_plane()) * F32(RADIAL_GAIN**2)
        for c in range(chans):
            row = c * modes_m + lo
            own = read(v, row, shift)
            drift = jnp.concatenate([-wave * own[:, half:], wave * own[:, :half]], axis=1)
            mid = F32(-2.0 * RADIAL_GAIN) * read(vb, row, shift).astype(F32)
            total = own + spec[c, at, :] + drift + mid
            if last:
                x0 = read(u0, row, shift)
                if paired:
                    total += mate * x0
                for n, (a, b) in enumerate(((x0, x0), (x0, own), (own, own))):
                    add_tile(acc, n, a * b)
            value = total * inv - read(recv, row, shift).astype(F32)
            write([out], row, shift, value)
            if not last:
                write(out_b, row, shift, value)

    for lo, hi in segments(modes_m, [*v, *(u0 if last else out_b)]):
        for_bands(lo, hi, functools.partial(step, lo))

    if last:
        gram[...] = jnp.zeros_like(gram)
        for n in range(3):
            gram[n : n + 1, :] = jnp.sum(acc[n], axis=0, keepdims=True)


def local_first(advect, v, vb, recv, two, tables, sizes):
    chans, modes_m, modes_k = two.shape
    args = [advect, *v, *vb, *recv, two, tables[3]]
    part, *part_b = kernel_call(
        functools.partial(local_kernel, (len(v), len(vb), len(recv), len(sizes)), False, False),
        "local_first",
        args,
        [IN_SMEM] + [IN_VMEM] * (len(args) - 1),
        [pltpu.VMEM((chans * modes_m, modes_k), F32)] + [pltpu.VMEM((n, modes_k), BF16) for n in sizes],
        scratch=[pltpu.VMEM(two.shape, F32)],
    )
    return part, part_b


def local_last(advect, v, vb, recv, two, tables, u0, paired):
    chans, modes_m, modes_k = two.shape
    args = [advect, *v, *vb, *recv, two, tables[3], *u0]
    return kernel_call(
        functools.partial(local_kernel, (len(v), len(vb), len(recv), len(u0)), True, paired),
        "local_last",
        args,
        [IN_SMEM] + [IN_VMEM] * (len(args) - 1),
        [
            pltpu.VMEM((chans * modes_m, modes_k), F32),
            pltpu.VMEM((modes_m, modes_k), F32),
            pltpu.VMEM((8, 128), F32),
        ],
        scratch=[pltpu.VMEM(two.shape, F32), pltpu.VMEM((3, 8, 128), F32)],
    )


def added(sides, row, shift):
    return functools.reduce(lambda a, b: a + b, [read(s, row, shift).astype(F32) for s in sides])


def first_kernel(groups, count, part, *refs):
    take = taker(refs)
    sides = [take(groups) for _ in range(count)]
    out, out_b = take(), take(len(refs) - groups * count - 1)
    chans, (modes_m, modes_k) = len(out_b), out_b[0].shape

    def step(lo, shift):
        inv = inverse_divisor(shift + lo, modes_m, modes_k, own_plane()) * F32(RADIAL_GAIN)
        for c in range(chans):
            row = c * modes_m + lo
            value = read([part], row, shift) + added(sides, row, shift) * inv
            write([out], row, shift, value)
            write(out_b, row, shift, value)

    for lo, hi in segments(modes_m, sides[0]):
        for_bands(lo, hi, functools.partial(step, lo))


def first_image(part, sides, chans):
    rows, modes_k = part.shape
    args = [part, *(x for side in sides for x in side)]
    return kernel_call(
        functools.partial(first_kernel, len(sides[0]), len(sides)),
        "first_image",
        args,
        [IN_VMEM] * len(args),
        [pltpu.VMEM(part.shape, F32)] + [pltpu.VMEM((rows // chans, modes_k), BF16)] * chans,
        flops=LONG,
    )


def on_diagonal():
    rows, lanes = (lax.broadcasted_iota(jnp.int32, (8, 128), n) for n in (0, 1))
    return rows == lanes


def second_kernel(first, counts, done, scale, u1, part, before, *refs):
    take = taker(refs)
    u0, planes = take(counts[0]), take(counts[1])
    out, gram, acc = take(3)
    modes_m = scale.shape[0]
    acc[...] = jnp.zeros_like(acc)

    def step(row, shift):
        at = pl.ds(pl.multiple_of(shift + row % modes_m, BAND), BAND)
        near = added([[p] for p in planes], row - first, shift)
        x2 = read([part], row, shift) + near * scale[at, :]
        write([out], row - first, shift, x2)
        for n, x in enumerate((read(u0, row, shift), read([u1], row, shift), x2)):
            add_tile(acc, n, x * x2)

    end = first + out.shape[0]
    starts = {first, *starts_of(u0), *range(0, end, modes_m)}
    starts = [r for r in sorted(starts) if first <= r < end]
    for lo, hi in zip(starts, starts[1:] + [end]):
        for_bands(lo, hi, functools.partial(step, lo))

    rows = [jnp.sum(acc[n], axis=0, keepdims=True) for n in range(3)]
    total = before[...] + jnp.concatenate([jnp.zeros((3, 128), F32), *rows, jnp.zeros((2, 128), F32)], axis=0)
    if done:
        total = jnp.sum(total, axis=1, keepdims=True)
        total = jnp.sum(jnp.where(on_diagonal(), total, F32(0.0)), axis=0, keepdims=True)
    gram[...] = jnp.broadcast_to(total, gram.shape)


def second_image(first, scale, u0, u1, part, before, planes, slots=None):
    done = slots is not None
    tile = (slots, 128) if done else (8, 128)
    args = [scale, u1, part, before, *u0, *planes]
    return kernel_call(
        functools.partial(second_kernel, first, (len(u0), len(planes)), done),
        "second_image",
        args,
        [IN_VMEM] * len(args),
        [pltpu.VMEM(planes[0].shape, F32), pltpu.VMEM(tile, F32)],
        scratch=[pltpu.VMEM((3, 8, 128), F32)],
    )


def combine_kernel(cells, counts, grams, u1, *refs):
    take = taker(refs)
    u0, u2 = take(counts[0]), take(counts[1])
    out, hess, held, sems = take(4)
    total, modes_k = out.shape
    g = jnp.sum(grams[...], axis=0, keepdims=True) * F32(1.0 / cells)
    g = jnp.sum(jnp.where(on_diagonal(), g, F32(0.0)), axis=1, keepdims=True)
    g = jnp.broadcast_to(g, (8, 128))
    g00, g01, g11, g02, g12, g22 = (g[n : n + 1, :] for n in range(6))
    per_g00 = F32(1.0) / g00
    h11 = g01 * per_g00
    q = g11 - h11 * g01
    per_q = F32(1.0) / q
    w0 = g02 - h11 * g01
    w1 = g12 - h11 * g11
    ww = g22 - F32(2.0) * h11 * g12 + h11 * h11 * g11
    h22 = (w1 - h11 * w0) * per_q
    ratio = w0 * per_g00
    square = (ww - w0 * ratio) * per_q - h22 * h22
    c2 = F32(1.0) / jnp.sqrt(q * square)
    c1 = -(h11 + h22) * c2
    c0 = (h11 * h22 - ratio) * c2
    wide = [jnp.concatenate([x] * (modes_k // 128), axis=1) for x in (c0, c1, c2)]

    def copy_out(n):
        at = pl.ds(pl.multiple_of(n * CHUNK, CHUNK), CHUNK)
        return pltpu.make_async_copy(held.at[at], out.at[at], sems.at[n])

    def step(first, n):
        for r in range(0, CHUNK, BAND):
            row, shift = first + r, pl.multiple_of(n * CHUNK, CHUNK)
            value = wide[0] * read(u0, row, shift) + wide[1] * read([u1], row, shift)
            write([held], row, shift, value + wide[2] * read(u2, row, shift))
        copy_out(n + first // CHUNK).start()

    starts = sorted({*starts_of(u0), *starts_of(u2)})
    for first, end in zip(starts, starts[1:] + [total]):
        pl.loop(0, (end - first) // CHUNK)(functools.partial(step, first))
    n0, s = jnp.sqrt(g00), jnp.sqrt(q)
    for n, value in enumerate((n0, h11, s / n0, w0 / (s * n0), h22, jnp.sqrt(square))):
        hess[n] = value[0, 0]
    pl.loop(0, total // CHUNK)(lambda n: copy_out(n).wait())


def combine(cells, grams, u0, u1, u2):
    args = [grams, u1, *u0, *u2]
    return kernel_call(
        functools.partial(combine_kernel, cells, (len(u0), len(u2))),
        "combine",
        args,
        [IN_VMEM] * len(args),
        [jax.ShapeDtypeStruct(u1.shape, F32), jax.ShapeDtypeStruct((6,), F32)],
        out_specs=[IN_HBM, IN_SMEM],
        scratch=[pltpu.VMEM(u1.shape, F32), pltpu.SemaphoreType.DMA((u1.shape[0] // CHUNK,))],
    )


def shifted(value, axis, steps):
    count = lax.axis_size(axis)
    return lax.ppermute(value, axis, [(i, (i + steps) % count) for i in range(count)])


def neighbour_planes(value, axis):
    count = lax.axis_size(axis)
    if count == 2:
        return [lax.ppermute(value, axis, [(0, 1), (1, 0)])]
    up = [(i, i + 1) for i in range(count - 1)]
    return [lax.ppermute(value, axis, up), lax.ppermute(value, axis, [(b, a) for a, b in up])]


def summed(row, axes, devices):
    step = 1
    while step < devices and devices % (2 * step) == 0:
        groups = [[i, i + step] for i in range(devices) if i // step % 2 == 0]
        row = lax.psum(row, axes, axis_index_groups=groups)
        step *= 2
    if step < devices:
        row = lax.psum(row, axes, axis_index_groups=[list(range(i, devices, step)) for i in range(step)])
    return row


def on_device(start_vector, coupling, advect):
    _, chans, rows_here, modes_m, modes_k = start_vector.shape
    assert rows_here == 1
    rows = chans * modes_m
    start = start_vector.reshape(rows, modes_k)
    couple = coupling.reshape(chans, chans, modes_m, modes_k)
    devices = lax.axis_size("seg") * lax.axis_size("rad")
    cells = float(devices * start.size)
    paired = lax.axis_size("rad") == 2

    early = EARLY_ROWS
    sizes = (rows - LATE_ROWS, LATE_ROWS) if paired else (modes_m,) * chans

    u0, u0b, near_one, pieces = [], [], [], None
    for first, size, parts in ((0, early, 0), (early, rows - early, chans)):
        field, rounded, pieces = take_rows(start, first, size, u0b, parts)
        u0.append(field)
        u0b.append(rounded)
        near_one.append(neighbour_planes(rounded, "rad"))
    next_one = [shifted(x, "seg", -1) for x in pieces]
    two, tables = transform(pieces, couple, awaited=near_one[0])
    part, part_b = local_first(advect, u0, pieces, next_one, two, tables, sizes)
    if paired:
        near_two = [neighbour_planes(x, "rad") for x in part_b]
    u1, *u1b = first_image(part, list(zip(*near_one)), chans)
    if not paired:
        near_two = [neighbour_planes(x, "rad") for x in u1b]
    next_two = [shifted(x, "seg", -1) for x in u1b]
    two, _ = transform(u1b, couple, tables)
    part, scale, gram = local_last(advect, [u1], u1b, next_two, two, tables, u0, paired)
    u2, first = [], 0
    for size, planes in zip(sizes, near_two):
        slots = 1 if first + size == rows else None
        field, gram = second_image(first, scale, u0, u1, part, gram, planes, slots)
        first += size
        u2.append(field)
    grams = summed(gram, ("seg", "rad"), devices)
    basis, hess = combine(cells, grams, u0, u1, u2)
    return basis.reshape(start_vector.shape), hess


def solution(mesh):
    return jax.shard_map(
        on_device,
        mesh=mesh,
        in_specs=(
            P("seg", None, "rad", None, None),
            P("seg", None, None, "rad", None, None),
            P("rad"),
        ),
        out_specs=(P("seg", None, "rad", None, None), P()),
        check_vma=False,
    )
```

```python
import functools
import math

import jax
import jax.numpy as jnp
from jax import lax
from jax.experimental import pallas as pl
from jax.experimental.pallas import tpu as pltpu
from jax.sharding import PartitionSpec as P

RADIAL_ALL = 256
WINDOW_START = 124
RADIAL_GAIN = 0.25
VISC_AXIAL = 4.0
VISC_TURN = 0.05

F32 = jnp.float32
BF16 = jnp.bfloat16
VMEM_LIMIT = 8 * 1024 * 1024
TRANSFORM_LIMIT = 22 * 1024 * 1024
ROWS = 128
COLS = 256
BAND = 16
LONG = 10**11
MEDIUM = 15 * 10**9
CHUNK = 64
EARLY_ROWS = 128
LATE_ROWS = 128

IN_SMEM = pl.BlockSpec(memory_space=pltpu.SMEM)
IN_VMEM = pl.BlockSpec(memory_space=pltpu.VMEM)
IN_HBM = pl.BlockSpec(memory_space=pltpu.HBM)


def kernel_call(body, name, args, in_specs, outs, out_specs=None, scratch=(), limit=VMEM_LIMIT, flops=1000):
    held = [
        a if s is IN_SMEM else pltpu.with_memory_space_constraint(a, s.memory_space)
        for a, s in zip(args, in_specs)
    ]
    more = {} if out_specs is None else {"out_specs": out_specs}
    return pl.pallas_call(
        body,
        out_shape=outs,
        in_specs=in_specs,
        scratch_shapes=list(scratch),
        compiler_params=pltpu.CompilerParams(vmem_limit_bytes=limit),
        cost_estimate=pl.CostEstimate(flops=flops, bytes_accessed=1000, transcendentals=0),
        name=name,
        **more,
    )(*held)


def sine_turns(y):
    x = y * F32(2.0 * math.pi)
    x2 = x * x
    acc = F32(1.0 / 6227020800.0)
    for c in (-1.0 / 39916800.0, 1.0 / 362880.0, -1.0 / 5040.0, 1.0 / 120.0, -1.0 / 6.0, 1.0):
        acc = acc * x2 + F32(c)
    return acc * x


def trig_block(row0, rows, cols, mode_axis, count, weighted):
    half = count // 2
    r = lax.broadcasted_iota(jnp.int32, (rows, cols), 0) + row0
    c = lax.broadcasted_iota(jnp.int32, (rows, cols), 1)
    mode, point = (r, c) if mode_axis == 0 else (c, r)
    is_cos = mode <= half
    freq = jnp.where(is_cos, mode, mode - half).astype(F32)
    phase = freq * point.astype(F32) - jnp.where(is_cos, F32(0.0), F32(count // 4))
    phase = phase - F32(count) * jnp.floor(phase * F32(1.0 / count))
    value = -sine_turns(F32(0.25) - jnp.abs(phase * F32(1.0 / count) - F32(0.5)))
    if weighted:
        edge = (mode == 0) | (mode == half)
        value = value * jnp.where(edge, F32(1.0 / count), F32(2.0 / count))
    return value.astype(BF16)


def fill_table(ref, mode_axis, weighted):
    count = ref.shape[0]

    @pl.loop(0, count // ROWS)
    def _(i):
        at = pl.multiple_of(i * ROWS, ROWS)
        ref[pl.ds(at, ROWS), :] = trig_block(at, ROWS, count, mode_axis, count, weighted)


def taker(refs):
    refs = list(refs)

    def take(count=None):
        if count is None:
            return refs.pop(0)
        out, refs[:count] = refs[:count], []
        return out

    return take


def segments(modes_m, groups):
    ends, total = {modes_m}, 0
    for group in groups:
        total += group.shape[0]
        ends.add(total % modes_m or modes_m)
    ends = sorted(ends)
    return list(zip([0] + ends[:-1], ends))


def starts_of(groups):
    return [sum(g.shape[0] for g in groups[:n]) for n in range(len(groups))]


def band(groups, row, shift):
    for group in groups:
        if row < group.shape[0]:
            return group, pl.ds(pl.multiple_of(shift + row, BAND), BAND)
        row -= group.shape[0]


def read(groups, row, shift):
    group, at = band(groups, row, shift)
    return group[at, :]


def write(groups, row, shift, value):
    group, at = band(groups, row, shift)
    group[at, :] = value.astype(group.dtype)


def for_bands(lo, hi, body):
    @pl.loop(0, (hi - lo) // BAND)
    def _(i):
        body(pl.multiple_of(i * BAND, BAND))


def take_kernel(first, v, *refs):
    take = taker(refs)
    early = [] if first == 0 else [take()]
    field, rounded = take(), take()
    pieces, sems = take(len(refs) - len(early) - 3), take()
    count = field.shape[0]
    copies = []
    for n, r in enumerate(range(0, count, ROWS)):
        copies.append(
            pltpu.make_async_copy(v.at[pl.ds(first + r, ROWS)], field.at[pl.ds(r, ROWS)], sems.at[n])
        )
        copies[n].start()

    def lay(row, value):
        for n, piece in enumerate(pieces):
            at = row - n * piece.shape[0]
            if 0 <= at < piece.shape[0]:
                piece[at : at + ROWS, :] = value

    for r in range(0, first, ROWS):
        lay(r, early[0][r : r + ROWS, :])
    for n, r in enumerate(range(0, count, ROWS)):
        copies[n].wait()
        value = field[r : r + ROWS, :].astype(BF16)
        rounded[r : r + ROWS, :] = value
        lay(first + r, value)


def take_rows(v, first, count, early=(), pieces=0):
    rows, modes_k = v.shape
    shapes = [pltpu.VMEM((count, modes_k), F32), pltpu.VMEM((count, modes_k), BF16)]
    field, rounded, *by_channel = kernel_call(
        functools.partial(take_kernel, first),
        "take_rows",
        [v, *early],
        [IN_HBM] + [IN_VMEM] * len(early),
        shapes + [pltpu.VMEM((rows // max(pieces, 1), modes_k), BF16)] * pieces,
        scratch=[pltpu.SemaphoreType.DMA((count // ROWS,))],
    )
    return field, rounded, by_channel


def transform_kernel(build, awaited, *refs):
    take = taker(refs)
    chans = len(refs) - awaited - (14 if build else 13)
    x = take(chans)
    take(awaited)
    couple_far = take()
    tables_far = None if build else take(3)
    out = take()
    if build:
        tables_far, anal_m = take(3), take()
    one, phys, mixed, couple, synth_k, synth_mt, anal_kt, sems = take(8)
    near = (synth_k, synth_mt, anal_kt)
    _, modes_m, modes_k = out.shape
    load = pltpu.make_async_copy(couple_far, couple, sems.at[3])
    ends = [(n, f) if build else (f, n) for n, f in zip(near, tables_far)]
    moves = [pltpu.make_async_copy(src, dst, sems.at[i]) for i, (src, dst) in enumerate(ends)]
    if not build:
        for move in moves[:2]:
            move.start()
    load.start()
    if not build:
        moves[2].start()

    def ready(i, mode_axis, weighted):
        if build:
            fill_table(near[i], mode_axis, weighted)
            moves[i].start()
        else:
            moves[i].wait()

    ready(0, 0, False)
    for c in range(chans):

        @pl.loop(0, modes_m // ROWS)
        def _(i):
            at = pl.ds(pl.multiple_of(i * ROWS, ROWS), ROWS)
            one[c, at, :] = jnp.dot(x[c][at, :], synth_k[...], preferred_element_type=F32).astype(BF16)

    ready(1, 1, False)
    load.wait()

    @pl.loop(0, modes_k // COLS)
    def _(z):
        zs = pl.ds(pl.multiple_of(z * COLS, COLS), COLS)
        for j in range(chans):
            phys[j] = jnp.dot(synth_mt[...], one[j, :, zs], preferred_element_type=F32)

        @pl.loop(0, modes_m // BAND)
        def _(i):
            ts = pl.ds(pl.multiple_of(i * BAND, BAND), BAND)
            parts = [phys[j, ts, :] for j in range(chans)]
            for c in range(chans):
                total = couple[c, 0, ts, zs].astype(F32) * parts[0]
                for j in range(1, chans):
                    total += couple[c, j, ts, zs].astype(F32) * parts[j]
                mixed[c, ts, zs] = total.astype(BF16)

    ready(2, 1, True)
    for c in range(chans):

        @pl.loop(0, modes_m // ROWS)
        def _(i):
            at = pl.ds(pl.multiple_of(i * ROWS, ROWS), ROWS)
            out[c, at, :] = jnp.dot(mixed[c, at, :], anal_kt[...], preferred_element_type=F32).astype(BF16)

    if build:
        fill_table(anal_m, 0, True)
        for move in moves:
            move.wait()


def transform(x, couple, tables=None, awaited=()):
    chans, _, modes_m, modes_k = couple.shape
    shape = (chans, modes_m, modes_k)
    sizes = [(modes_k, modes_k), (modes_m, modes_m), (modes_k, modes_k)]
    build = tables is None
    far = [] if build else list(tables[:3])
    outs, out_specs = [pltpu.VMEM(shape, BF16)], [IN_VMEM]
    if build:
        outs += [pltpu.HBM(n, BF16) for n in sizes] + [pltpu.VMEM((modes_m, modes_m), BF16)]
        out_specs += [IN_HBM] * 3 + [IN_VMEM]
    result = kernel_call(
        functools.partial(transform_kernel, build, len(awaited)),
        "transform",
        [*x, *awaited, couple, *far],
        [IN_VMEM] * (chans + len(awaited)) + [IN_HBM] * (1 + len(far)),
        outs,
        out_specs=out_specs,
        scratch=[
            pltpu.VMEM(shape, BF16),
            pltpu.VMEM((chans, modes_m, COLS), F32),
            pltpu.VMEM(shape, BF16),
            pltpu.VMEM(couple.shape, BF16),
            *[pltpu.VMEM(n, BF16) for n in sizes],
            pltpu.SemaphoreType.DMA((4,)),
        ],
        limit=TRANSFORM_LIMIT,
        flops=MEDIUM if awaited else 1000,
    )
    return result[0], (result[1:] if build else tables)


def own_plane():
    return WINDOW_START + lax.axis_index("rad")


def paired_plane():
    return WINDOW_START + 1 - lax.axis_index("rad")


def inverse_divisor(row0, modes_m, modes_k, plane):
    m = lax.broadcasted_iota(jnp.int32, (BAND, 1), 0) + row0
    k = lax.broadcasted_iota(jnp.int32, (1, modes_k), 1)
    fm = jnp.where(m <= modes_m // 2, m, m - modes_m // 2).astype(F32) / F32(modes_m // 2)
    fk = jnp.where(k <= modes_k // 2, k, k - modes_k // 2).astype(F32) / F32(modes_k // 2)
    radius = (jnp.full((1, 1), plane, jnp.int32).astype(F32) + F32(0.5)) / F32(RADIAL_ALL)
    turning = F32(VISC_TURN) * fm * fm / (radius * radius)
    return F32(1.0) / (F32(1.0) + F32(VISC_AXIAL) * fk * fk + turning)


def add_tile(acc, n, value):
    value = sum(value[r : r + 8] for r in range(0, value.shape[0], 8))
    acc[n] += sum(value[:, k : k + 128] for k in range(0, value.shape[1], 128))


def local_kernel(counts, last, paired, advect, *refs):
    take = taker(refs)
    v, vb, recv = (take(n) for n in counts[:3])
    two, anal_m = take(), take()
    if last:
        u0, out_b = take(counts[3]), []
        out, scale, gram, spec, acc = take(5)
        acc[...] = jnp.zeros_like(acc)
    else:
        out, out_b, spec = take(), take(counts[3]), take()
    chans, modes_m, modes_k = two.shape
    half = modes_k // 2
    for c in range(chans):
        spec[c] = jnp.dot(anal_m[...], two[c], preferred_element_type=F32)
    wave = lax.broadcasted_iota(jnp.int32, (1, half), 1).astype(F32) * advect[0]

    def step(lo, shift):
        at = pl.ds(pl.multiple_of(shift + lo, BAND), BAND)
        inv = inverse_divisor(shift + lo, modes_m, modes_k, own_plane())
        if last:
            scale[at, :] = inv * F32(RADIAL_GAIN)
            if paired:
                mate = inverse_divisor(shift + lo, modes_m, modes_k, paired_plane()) * F32(RADIAL_GAIN**2)
        for c in range(chans):
            row = c * modes_m + lo
            own = read(v, row, shift)
            drift = jnp.concatenate([-wave * own[:, half:], wave * own[:, :half]], axis=1)
            mid = F32(-2.0 * RADIAL_GAIN) * read(vb, row, shift).astype(F32)
            total = own + spec[c, at, :] + drift + mid
            if last:
                x0 = read(u0, row, shift)
                if paired:
                    total += mate * x0
                for n, (a, b) in enumerate(((x0, x0), (x0, own), (own, own))):
                    add_tile(acc, n, a * b)
            value = total * inv - read(recv, row, shift).astype(F32)
            write([out], row, shift, value)
            if not last:
                write(out_b, row, shift, value)

    for lo, hi in segments(modes_m, [*v, *(u0 if last else out_b)]):
        for_bands(lo, hi, functools.partial(step, lo))

    if last:
        gram[...] = jnp.zeros_like(gram)
        for n in range(3):
            gram[n : n + 1, :] = jnp.sum(acc[n], axis=0, keepdims=True)


def local_first(advect, v, vb, recv, two, tables, sizes):
    chans, modes_m, modes_k = two.shape
    args = [advect, *v, *vb, *recv, two, tables[3]]
    part, *part_b = kernel_call(
        functools.partial(local_kernel, (len(v), len(vb), len(recv), len(sizes)), False, False),
        "local_first",
        args,
        [IN_SMEM] + [IN_VMEM] * (len(args) - 1),
        [pltpu.VMEM((chans * modes_m, modes_k), F32)] + [pltpu.VMEM((n, modes_k), BF16) for n in sizes],
        scratch=[pltpu.VMEM(two.shape, F32)],
    )
    return part, part_b


def local_last(advect, v, vb, recv, two, tables, u0, paired):
    chans, modes_m, modes_k = two.shape
    args = [advect, *v, *vb, *recv, two, tables[3], *u0]
    return kernel_call(
        functools.partial(local_kernel, (len(v), len(vb), len(recv), len(u0)), True, paired),
        "local_last",
        args,
        [IN_SMEM] + [IN_VMEM] * (len(args) - 1),
        [
            pltpu.VMEM((chans * modes_m, modes_k), F32),
            pltpu.VMEM((modes_m, modes_k), F32),
            pltpu.VMEM((8, 128), F32),
        ],
        scratch=[pltpu.VMEM(two.shape, F32), pltpu.VMEM((3, 8, 128), F32)],
    )


def added(sides, row, shift):
    return functools.reduce(lambda a, b: a + b, [read(s, row, shift).astype(F32) for s in sides])


def first_kernel(groups, count, part, *refs):
    take = taker(refs)
    sides = [take(groups) for _ in range(count)]
    out, out_b = take(), take(len(refs) - groups * count - 1)
    chans, (modes_m, modes_k) = len(out_b), out_b[0].shape

    def step(lo, shift):
        inv = inverse_divisor(shift + lo, modes_m, modes_k, own_plane()) * F32(RADIAL_GAIN)
        for c in range(chans):
            row = c * modes_m + lo
            value = read([part], row, shift) + added(sides, row, shift) * inv
            write([out], row, shift, value)
            write(out_b, row, shift, value)

    for lo, hi in segments(modes_m, sides[0]):
        for_bands(lo, hi, functools.partial(step, lo))


def first_image(part, sides, chans):
    rows, modes_k = part.shape
    args = [part, *(x for side in sides for x in side)]
    return kernel_call(
        functools.partial(first_kernel, len(sides[0]), len(sides)),
        "first_image",
        args,
        [IN_VMEM] * len(args),
        [pltpu.VMEM(part.shape, F32)] + [pltpu.VMEM((rows // chans, modes_k), BF16)] * chans,
        flops=LONG,
    )


def on_diagonal():
    rows, lanes = (lax.broadcasted_iota(jnp.int32, (8, 128), n) for n in (0, 1))
    return rows == lanes


def second_kernel(first, counts, done, scale, u1, part, before, *refs):
    take = taker(refs)
    u0, planes = take(counts[0]), take(counts[1])
    out, gram, acc = take(3)
    modes_m = scale.shape[0]
    acc[...] = jnp.zeros_like(acc)

    def step(row, shift):
        at = pl.ds(pl.multiple_of(shift + row % modes_m, BAND), BAND)
        near = added([[p] for p in planes], row - first, shift)
        x2 = read([part], row, shift) + near * scale[at, :]
        write([out], row - first, shift, x2)
        for n, x in enumerate((read(u0, row, shift), read([u1], row, shift), x2)):
            add_tile(acc, n, x * x2)

    end = first + out.shape[0]
    starts = {first, *starts_of(u0), *range(0, end, modes_m)}
    starts = [r for r in sorted(starts) if first <= r < end]
    for lo, hi in zip(starts, starts[1:] + [end]):
        for_bands(lo, hi, functools.partial(step, lo))

    rows = [jnp.sum(acc[n], axis=0, keepdims=True) for n in range(3)]
    total = before[...] + jnp.concatenate([jnp.zeros((3, 128), F32), *rows, jnp.zeros((2, 128), F32)], axis=0)
    if done:
        total = jnp.sum(total, axis=1, keepdims=True)
        total = jnp.sum(jnp.where(on_diagonal(), total, F32(0.0)), axis=0, keepdims=True)
    gram[...] = jnp.broadcast_to(total, gram.shape)


def second_image(first, scale, u0, u1, part, before, planes, slots=None):
    done = slots is not None
    tile = (slots, 128) if done else (8, 128)
    args = [scale, u1, part, before, *u0, *planes]
    return kernel_call(
        functools.partial(second_kernel, first, (len(u0), len(planes)), done),
        "second_image",
        args,
        [IN_VMEM] * len(args),
        [pltpu.VMEM(planes[0].shape, F32), pltpu.VMEM(tile, F32)],
        scratch=[pltpu.VMEM((3, 8, 128), F32)],
    )


def combine_kernel(cells, counts, grams, u1, *refs):
    take = taker(refs)
    u0, u2 = take(counts[0]), take(counts[1])
    out, hess, held, sems = take(4)
    total, modes_k = out.shape
    g = jnp.sum(grams[...], axis=0, keepdims=True) * F32(1.0 / cells)
    g = jnp.sum(jnp.where(on_diagonal(), g, F32(0.0)), axis=1, keepdims=True)
    g = jnp.broadcast_to(g, (8, 128))
    g00, g01, g11, g02, g12, g22 = (g[n : n + 1, :] for n in range(6))
    per_g00 = F32(1.0) / g00
    h11 = g01 * per_g00
    q = g11 - h11 * g01
    per_q = F32(1.0) / q
    w0 = g02 - h11 * g01
    w1 = g12 - h11 * g11
    ww = g22 - F32(2.0) * h11 * g12 + h11 * h11 * g11
    h22 = (w1 - h11 * w0) * per_q
    ratio = w0 * per_g00
    square = (ww - w0 * ratio) * per_q - h22 * h22
    c2 = F32(1.0) / jnp.sqrt(q * square)
    c1 = -(h11 + h22) * c2
    c0 = (h11 * h22 - ratio) * c2
    wide = [jnp.concatenate([x] * (modes_k // 128), axis=1) for x in (c0, c1, c2)]

    def copy_out(n):
        at = pl.ds(pl.multiple_of(n * CHUNK, CHUNK), CHUNK)
        return pltpu.make_async_copy(held.at[at], out.at[at], sems.at[n])

    def step(first, n):
        for r in range(0, CHUNK, BAND):
            row, shift = first + r, pl.multiple_of(n * CHUNK, CHUNK)
            value = wide[0] * read(u0, row, shift) + wide[1] * read([u1], row, shift)
            write([held], row, shift, value + wide[2] * read(u2, row, shift))
        copy_out(n + first // CHUNK).start()

    starts = sorted({*starts_of(u0), *starts_of(u2)})
    for first, end in zip(starts, starts[1:] + [total]):
        pl.loop(0, (end - first) // CHUNK)(functools.partial(step, first))
    n0, s = jnp.sqrt(g00), jnp.sqrt(q)
    for n, value in enumerate((n0, h11, s / n0, w0 / (s * n0), h22, jnp.sqrt(square))):
        hess[n] = value[0, 0]
    pl.loop(0, total // CHUNK)(lambda n: copy_out(n).wait())


def combine(cells, grams, u0, u1, u2):
    args = [grams, u1, *u0, *u2]
    return kernel_call(
        functools.partial(combine_kernel, cells, (len(u0), len(u2))),
        "combine",
        args,
        [IN_VMEM] * len(args),
        [jax.ShapeDtypeStruct(u1.shape, F32), jax.ShapeDtypeStruct((6,), F32)],
        out_specs=[IN_HBM, IN_SMEM],
        scratch=[pltpu.VMEM(u1.shape, F32), pltpu.SemaphoreType.DMA((u1.shape[0] // CHUNK,))],
    )


def shifted(value, axis, steps):
    count = lax.axis_size(axis)
    return lax.ppermute(value, axis, [(i, (i + steps) % count) for i in range(count)])


def neighbour_planes(value, axis):
    count = lax.axis_size(axis)
    if count == 2:
        return [lax.ppermute(value, axis, [(0, 1), (1, 0)])]
    up = [(i, i + 1) for i in range(count - 1)]
    return [lax.ppermute(value, axis, up), lax.ppermute(value, axis, [(b, a) for a, b in up])]


def on_device(start_vector, coupling, advect):
    _, chans, rows_here, modes_m, modes_k = start_vector.shape
    assert rows_here == 1
    rows = chans * modes_m
    start = start_vector.reshape(rows, modes_k)
    couple = coupling.reshape(chans, chans, modes_m, modes_k)
    devices = lax.axis_size("seg") * lax.axis_size("rad")
    cells = float(devices * start.size)
    paired = lax.axis_size("rad") == 2

    early = EARLY_ROWS
    sizes = (rows - LATE_ROWS, LATE_ROWS) if paired else (modes_m,) * chans

    u0, u0b, near_one, pieces = [], [], [], None
    for first, size, parts in ((0, early, 0), (early, rows - early, chans)):
        field, rounded, pieces = take_rows(start, first, size, u0b, parts)
        u0.append(field)
        u0b.append(rounded)
        near_one.append(neighbour_planes(rounded, "rad"))
    next_one = [shifted(x, "seg", -1) for x in pieces]
    two, tables = transform(pieces, couple, awaited=near_one[0])
    part, part_b = local_first(advect, u0, pieces, next_one, two, tables, sizes)
    if paired:
        near_two = [neighbour_planes(x, "rad") for x in part_b]
    u1, *u1b = first_image(part, list(zip(*near_one)), chans)
    if not paired:
        near_two = [neighbour_planes(x, "rad") for x in u1b]
    next_two = [shifted(x, "seg", -1) for x in u1b]
    two, _ = transform(u1b, couple, tables)
    part, scale, gram = local_last(advect, [u1], u1b, next_two, two, tables, u0, paired)
    u2, first = [], 0
    for size, planes in zip(sizes, near_two):
        slots = devices if first + size == rows else None
        field, gram = second_image(first, scale, u0, u1, part, gram, planes, slots)
        first += size
        u2.append(field)
    grams = lax.all_to_all(gram, ("seg", "rad"), 0, 0)
    basis, hess = combine(cells, grams, u0, u1, u2)
    return basis.reshape(start_vector.shape), hess


def solution(mesh):
    return jax.shard_map(
        on_device,
        mesh=mesh,
        in_specs=(
            P("seg", None, "rad", None, None),
            P("seg", None, None, "rad", None, None),
            P("rad"),
        ),
        out_specs=(P("seg", None, "rad", None, None), P()),
        check_vma=False,
    )
```

```python
import functools
import math

import jax
import jax.numpy as jnp
from jax import lax
from jax.experimental import pallas as pl
from jax.experimental.pallas import tpu as pltpu
from jax.sharding import PartitionSpec as P

RADIAL_ALL = 256
WINDOW_START = 124
RADIAL_GAIN = 0.25
VISC_AXIAL = 4.0
VISC_TURN = 0.05

F32 = jnp.float32
BF16 = jnp.bfloat16
VMEM_LIMIT = 8 * 1024 * 1024
TRANSFORM_LIMIT = 22 * 1024 * 1024
ROWS = 128
COLS = 256
BAND = 16
LONG = 10**11
MEDIUM = 15 * 10**9
HALF = 32
EARLY_ROWS = 128
LATE_ROWS = 128

IN_SMEM = pl.BlockSpec(memory_space=pltpu.SMEM)
IN_VMEM = pl.BlockSpec(memory_space=pltpu.VMEM)
IN_HBM = pl.BlockSpec(memory_space=pltpu.HBM)


def kernel_call(body, name, args, in_specs, outs, out_specs=None, scratch=(), limit=VMEM_LIMIT, flops=1000):
    held = [
        a if s is IN_SMEM else pltpu.with_memory_space_constraint(a, s.memory_space)
        for a, s in zip(args, in_specs)
    ]
    more = {} if out_specs is None else {"out_specs": out_specs}
    return pl.pallas_call(
        body,
        out_shape=outs,
        in_specs=in_specs,
        scratch_shapes=list(scratch),
        compiler_params=pltpu.CompilerParams(vmem_limit_bytes=limit),
        cost_estimate=pl.CostEstimate(flops=flops, bytes_accessed=1000, transcendentals=0),
        name=name,
        **more,
    )(*held)


def sine_turns(y):
    x = y * F32(2.0 * math.pi)
    x2 = x * x
    acc = F32(1.0 / 6227020800.0)
    for c in (-1.0 / 39916800.0, 1.0 / 362880.0, -1.0 / 5040.0, 1.0 / 120.0, -1.0 / 6.0, 1.0):
        acc = acc * x2 + F32(c)
    return acc * x


def trig_block(row0, rows, cols, mode_axis, count, weighted):
    half = count // 2
    r = lax.broadcasted_iota(jnp.int32, (rows, cols), 0) + row0
    c = lax.broadcasted_iota(jnp.int32, (rows, cols), 1)
    mode, point = (r, c) if mode_axis == 0 else (c, r)
    is_cos = mode <= half
    freq = jnp.where(is_cos, mode, mode - half).astype(F32)
    phase = freq * point.astype(F32) - jnp.where(is_cos, F32(0.0), F32(count // 4))
    phase = phase - F32(count) * jnp.floor(phase * F32(1.0 / count))
    value = -sine_turns(F32(0.25) - jnp.abs(phase * F32(1.0 / count) - F32(0.5)))
    if weighted:
        edge = (mode == 0) | (mode == half)
        value = value * jnp.where(edge, F32(1.0 / count), F32(2.0 / count))
    return value.astype(BF16)


def fill_table(ref, mode_axis, weighted):
    count = ref.shape[0]

    @pl.loop(0, count // ROWS)
    def _(i):
        at = pl.multiple_of(i * ROWS, ROWS)
        ref[pl.ds(at, ROWS), :] = trig_block(at, ROWS, count, mode_axis, count, weighted)


def taker(refs):
    refs = list(refs)

    def take(count=None):
        if count is None:
            return refs.pop(0)
        out, refs[:count] = refs[:count], []
        return out

    return take


def segments(modes_m, groups):
    ends, total = {modes_m}, 0
    for group in groups:
        total += group.shape[0]
        ends.add(total % modes_m or modes_m)
    ends = sorted(ends)
    return list(zip([0] + ends[:-1], ends))


def starts_of(groups):
    return [sum(g.shape[0] for g in groups[:n]) for n in range(len(groups))]


def band(groups, row, shift):
    for group in groups:
        if row < group.shape[0]:
            return group, pl.ds(pl.multiple_of(shift + row, BAND), BAND)
        row -= group.shape[0]


def read(groups, row, shift):
    group, at = band(groups, row, shift)
    return group[at, :]


def write(groups, row, shift, value):
    group, at = band(groups, row, shift)
    group[at, :] = value.astype(group.dtype)


def for_bands(lo, hi, body):
    @pl.loop(0, (hi - lo) // BAND)
    def _(i):
        body(pl.multiple_of(i * BAND, BAND))


def take_kernel(first, v, *refs):
    take = taker(refs)
    early = [] if first == 0 else [take()]
    field, rounded = take(), take()
    pieces, sems = take(len(refs) - len(early) - 3), take()
    count = field.shape[0]
    copies = []
    for n, r in enumerate(range(0, count, ROWS)):
        copies.append(
            pltpu.make_async_copy(v.at[pl.ds(first + r, ROWS)], field.at[pl.ds(r, ROWS)], sems.at[n])
        )
        copies[n].start(priority=n % 2)

    def lay(row, value):
        for n, piece in enumerate(pieces):
            at = row - n * piece.shape[0]
            if 0 <= at < piece.shape[0]:
                piece[at : at + ROWS, :] = value

    for r in range(0, first, ROWS):
        lay(r, early[0][r : r + ROWS, :])
    for n, r in enumerate(range(0, count, ROWS)):
        copies[n].wait()
        value = field[r : r + ROWS, :].astype(BF16)
        rounded[r : r + ROWS, :] = value
        lay(first + r, value)


def take_rows(v, first, count, early=(), pieces=0):
    rows, modes_k = v.shape
    shapes = [pltpu.VMEM((count, modes_k), F32), pltpu.VMEM((count, modes_k), BF16)]
    field, rounded, *by_channel = kernel_call(
        functools.partial(take_kernel, first),
        "take_rows",
        [v, *early],
        [IN_HBM] + [IN_VMEM] * len(early),
        shapes + [pltpu.VMEM((rows // max(pieces, 1), modes_k), BF16)] * pieces,
        scratch=[pltpu.SemaphoreType.DMA((count // ROWS,))],
    )
    return field, rounded, by_channel


def transform_kernel(build, awaited, *refs):
    take = taker(refs)
    chans = len(refs) - awaited - (14 if build else 13)
    x = take(chans)
    take(awaited)
    couple_far = take()
    tables_far = None if build else take(3)
    out = take()
    if build:
        tables_far, anal_m = take(3), take()
    one, phys, mixed, couple, synth_k, synth_mt, anal_kt, sems = take(8)
    near = (synth_k, synth_mt, anal_kt)
    _, modes_m, modes_k = out.shape
    load = pltpu.make_async_copy(couple_far, couple, sems.at[3])
    ends = [(n, f) if build else (f, n) for n, f in zip(near, tables_far)]
    moves = [pltpu.make_async_copy(src, dst, sems.at[i]) for i, (src, dst) in enumerate(ends)]
    if not build:
        for move in moves[:2]:
            move.start()
    load.start()
    if not build:
        moves[2].start()

    def ready(i, mode_axis, weighted):
        if build:
            fill_table(near[i], mode_axis, weighted)
            moves[i].start()
        else:
            moves[i].wait()

    ready(0, 0, False)
    for c in range(chans):

        @pl.loop(0, modes_m // ROWS)
        def _(i):
            at = pl.ds(pl.multiple_of(i * ROWS, ROWS), ROWS)
            one[c, at, :] = jnp.dot(x[c][at, :], synth_k[...], preferred_element_type=F32).astype(BF16)

    ready(1, 1, False)
    load.wait()

    @pl.loop(0, modes_k // COLS)
    def _(z):
        zs = pl.ds(pl.multiple_of(z * COLS, COLS), COLS)
        for j in range(chans):
            phys[j] = jnp.dot(synth_mt[...], one[j, :, zs], preferred_element_type=F32)

        @pl.loop(0, modes_m // BAND)
        def _(i):
            ts = pl.ds(pl.multiple_of(i * BAND, BAND), BAND)
            parts = [phys[j, ts, :] for j in range(chans)]
            for c in range(chans):
                total = couple[c, 0, ts, zs].astype(F32) * parts[0]
                for j in range(1, chans):
                    total += couple[c, j, ts, zs].astype(F32) * parts[j]
                mixed[c, ts, zs] = total.astype(BF16)

    ready(2, 1, True)
    for c in range(chans):

        @pl.loop(0, modes_m // ROWS)
        def _(i):
            at = pl.ds(pl.multiple_of(i * ROWS, ROWS), ROWS)
            out[c, at, :] = jnp.dot(mixed[c, at, :], anal_kt[...], preferred_element_type=F32).astype(BF16)

    if build:
        fill_table(anal_m, 0, True)
        for move in moves:
            move.wait()


def transform(x, couple, tables=None, awaited=()):
    chans, _, modes_m, modes_k = couple.shape
    shape = (chans, modes_m, modes_k)
    sizes = [(modes_k, modes_k), (modes_m, modes_m), (modes_k, modes_k)]
    build = tables is None
    far = [] if build else list(tables[:3])
    outs, out_specs = [pltpu.VMEM(shape, BF16)], [IN_VMEM]
    if build:
        outs += [pltpu.HBM(n, BF16) for n in sizes] + [pltpu.VMEM((modes_m, modes_m), BF16)]
        out_specs += [IN_HBM] * 3 + [IN_VMEM]
    result = kernel_call(
        functools.partial(transform_kernel, build, len(awaited)),
        "transform",
        [*x, *awaited, couple, *far],
        [IN_VMEM] * (chans + len(awaited)) + [IN_HBM] * (1 + len(far)),
        outs,
        out_specs=out_specs,
        scratch=[
            pltpu.VMEM(shape, BF16),
            pltpu.VMEM((chans, modes_m, COLS), F32),
            pltpu.VMEM(shape, BF16),
            pltpu.VMEM(couple.shape, BF16),
            *[pltpu.VMEM(n, BF16) for n in sizes],
            pltpu.SemaphoreType.DMA((4,)),
        ],
        limit=TRANSFORM_LIMIT,
        flops=MEDIUM if awaited else 1000,
    )
    return result[0], (result[1:] if build else tables)


def own_plane():
    return WINDOW_START + lax.axis_index("rad")


def paired_plane():
    return WINDOW_START + 1 - lax.axis_index("rad")


def inverse_divisor(row0, modes_m, modes_k, plane):
    m = lax.broadcasted_iota(jnp.int32, (BAND, 1), 0) + row0
    k = lax.broadcasted_iota(jnp.int32, (1, modes_k), 1)
    fm = jnp.where(m <= modes_m // 2, m, m - modes_m // 2).astype(F32) / F32(modes_m // 2)
    fk = jnp.where(k <= modes_k // 2, k, k - modes_k // 2).astype(F32) / F32(modes_k // 2)
    radius = (jnp.full((1, 1), plane, jnp.int32).astype(F32) + F32(0.5)) / F32(RADIAL_ALL)
    turning = F32(VISC_TURN) * fm * fm / (radius * radius)
    return F32(1.0) / (F32(1.0) + F32(VISC_AXIAL) * fk * fk + turning)


def add_tile(acc, n, value):
    value = sum(value[r : r + 8] for r in range(0, value.shape[0], 8))
    acc[n] += sum(value[:, k : k + 128] for k in range(0, value.shape[1], 128))


def local_kernel(counts, last, paired, advect, *refs):
    take = taker(refs)
    v, vb, recv = (take(n) for n in counts[:3])
    two, anal_m = take(), take()
    if last:
        u0, out_b = take(counts[3]), []
        out, scale, gram, spec, acc = take(5)
        acc[...] = jnp.zeros_like(acc)
    else:
        out, out_b, spec = take(), take(counts[3]), take()
    chans, modes_m, modes_k = two.shape
    half = modes_k // 2
    for c in range(chans):
        spec[c] = jnp.dot(anal_m[...], two[c], preferred_element_type=F32)
    wave = lax.broadcasted_iota(jnp.int32, (1, half), 1).astype(F32) * advect[0]

    def step(lo, shift):
        at = pl.ds(pl.multiple_of(shift + lo, BAND), BAND)
        inv = inverse_divisor(shift + lo, modes_m, modes_k, own_plane())
        if last:
            scale[at, :] = inv * F32(RADIAL_GAIN)
            if paired:
                mate = inverse_divisor(shift + lo, modes_m, modes_k, paired_plane()) * F32(RADIAL_GAIN**2)
        for c in range(chans):
            row = c * modes_m + lo
            own = read(v, row, shift)
            drift = jnp.concatenate([-wave * own[:, half:], wave * own[:, :half]], axis=1)
            mid = F32(-2.0 * RADIAL_GAIN) * read(vb, row, shift).astype(F32)
            total = own + spec[c, at, :] + drift + mid
            if last:
                x0 = read(u0, row, shift)
                if paired:
                    total += mate * x0
                for n, (a, b) in enumerate(((x0, x0), (x0, own), (own, own))):
                    add_tile(acc, n, a * b)
            value = total * inv - read(recv, row, shift).astype(F32)
            write([out], row, shift, value)
            if not last:
                write(out_b, row, shift, value)

    for lo, hi in segments(modes_m, [*v, *(u0 if last else out_b)]):
        for_bands(lo, hi, functools.partial(step, lo))

    if last:
        gram[...] = jnp.zeros_like(gram)
        for n in range(3):
            gram[n : n + 1, :] = jnp.sum(acc[n], axis=0, keepdims=True)


def local_first(advect, v, vb, recv, two, tables, sizes):
    chans, modes_m, modes_k = two.shape
    args = [advect, *v, *vb, *recv, two, tables[3]]
    part, *part_b = kernel_call(
        functools.partial(local_kernel, (len(v), len(vb), len(recv), len(sizes)), False, False),
        "local_first",
        args,
        [IN_SMEM] + [IN_VMEM] * (len(args) - 1),
        [pltpu.VMEM((chans * modes_m, modes_k), F32)] + [pltpu.VMEM((n, modes_k), BF16) for n in sizes],
        scratch=[pltpu.VMEM(two.shape, F32)],
    )
    return part, part_b


def local_last(advect, v, vb, recv, two, tables, u0, paired):
    chans, modes_m, modes_k = two.shape
    args = [advect, *v, *vb, *recv, two, tables[3], *u0]
    return kernel_call(
        functools.partial(local_kernel, (len(v), len(vb), len(recv), len(u0)), True, paired),
        "local_last",
        args,
        [IN_SMEM] + [IN_VMEM] * (len(args) - 1),
        [
            pltpu.VMEM((chans * modes_m, modes_k), F32),
            pltpu.VMEM((modes_m, modes_k), F32),
            pltpu.VMEM((8, 128), F32),
        ],
        scratch=[pltpu.VMEM(two.shape, F32), pltpu.VMEM((3, 8, 128), F32)],
    )


def added(sides, row, shift):
    return functools.reduce(lambda a, b: a + b, [read(s, row, shift).astype(F32) for s in sides])


def first_kernel(groups, count, part, *refs):
    take = taker(refs)
    sides = [take(groups) for _ in range(count)]
    out, out_b = take(), take(len(refs) - groups * count - 1)
    chans, (modes_m, modes_k) = len(out_b), out_b[0].shape

    def step(lo, shift):
        inv = inverse_divisor(shift + lo, modes_m, modes_k, own_plane()) * F32(RADIAL_GAIN)
        for c in range(chans):
            row = c * modes_m + lo
            value = read([part], row, shift) + added(sides, row, shift) * inv
            write([out], row, shift, value)
            write(out_b, row, shift, value)

    for lo, hi in segments(modes_m, sides[0]):
        for_bands(lo, hi, functools.partial(step, lo))


def first_image(part, sides, chans):
    rows, modes_k = part.shape
    args = [part, *(x for side in sides for x in side)]
    return kernel_call(
        functools.partial(first_kernel, len(sides[0]), len(sides)),
        "first_image",
        args,
        [IN_VMEM] * len(args),
        [pltpu.VMEM(part.shape, F32)] + [pltpu.VMEM((rows // chans, modes_k), BF16)] * chans,
        flops=LONG,
    )


def on_diagonal():
    rows, lanes = (lax.broadcasted_iota(jnp.int32, (8, 128), n) for n in (0, 1))
    return rows == lanes


def second_kernel(first, counts, done, scale, u1, part, before, *refs):
    take = taker(refs)
    u0, planes = take(counts[0]), take(counts[1])
    out, gram, acc = take(3)
    modes_m = scale.shape[0]
    acc[...] = jnp.zeros_like(acc)

    def step(row, shift):
        at = pl.ds(pl.multiple_of(shift + row % modes_m, BAND), BAND)
        near = added([[p] for p in planes], row - first, shift)
        x2 = read([part], row, shift) + near * scale[at, :]
        write([out], row - first, shift, x2)
        for n, x in enumerate((read(u0, row, shift), read([u1], row, shift), x2)):
            add_tile(acc, n, x * x2)

    end = first + out.shape[0]
    starts = {first, *starts_of(u0), *range(0, end, modes_m)}
    starts = [r for r in sorted(starts) if first <= r < end]
    for lo, hi in zip(starts, starts[1:] + [end]):
        for_bands(lo, hi, functools.partial(step, lo))

    rows = [jnp.sum(acc[n], axis=0, keepdims=True) for n in range(3)]
    total = before[...] + jnp.concatenate([jnp.zeros((3, 128), F32), *rows, jnp.zeros((2, 128), F32)], axis=0)
    if done:
        total = jnp.sum(total, axis=1, keepdims=True)
        total = jnp.sum(jnp.where(on_diagonal(), total, F32(0.0)), axis=0, keepdims=True)
    gram[...] = jnp.broadcast_to(total, gram.shape)


def second_image(first, scale, u0, u1, part, before, planes, slots=None):
    done = slots is not None
    tile = (slots, 128) if done else (8, 128)
    args = [scale, u1, part, before, *u0, *planes]
    return kernel_call(
        functools.partial(second_kernel, first, (len(u0), len(planes)), done),
        "second_image",
        args,
        [IN_VMEM] * len(args),
        [pltpu.VMEM(planes[0].shape, F32), pltpu.VMEM(tile, F32)],
        scratch=[pltpu.VMEM((3, 8, 128), F32)],
    )


def combine_kernel(cells, counts, grams, u1, *refs):
    take = taker(refs)
    u0, u2 = take(counts[0]), take(counts[1])
    out, hess, held, sems = take(4)
    total, modes_k = out.shape
    g = jnp.sum(grams[...], axis=0, keepdims=True) * F32(1.0 / cells)
    g = jnp.sum(jnp.where(on_diagonal(), g, F32(0.0)), axis=1, keepdims=True)
    g = jnp.broadcast_to(g, (8, 128))
    g00, g01, g11, g02, g12, g22 = (g[n : n + 1, :] for n in range(6))
    per_g00 = F32(1.0) / g00
    h11 = g01 * per_g00
    q = g11 - h11 * g01
    per_q = F32(1.0) / q
    w0 = g02 - h11 * g01
    w1 = g12 - h11 * g11
    ww = g22 - F32(2.0) * h11 * g12 + h11 * h11 * g11
    h22 = (w1 - h11 * w0) * per_q
    ratio = w0 * per_g00
    square = (ww - w0 * ratio) * per_q - h22 * h22
    c2 = F32(1.0) / jnp.sqrt(q * square)
    c1 = -(h11 + h22) * c2
    c0 = (h11 * h22 - ratio) * c2
    wide = [jnp.concatenate([x] * (modes_k // 128), axis=1) for x in (c0, c1, c2)]

    def copy_out(n):
        at = pl.ds(pl.multiple_of(n * HALF, HALF), HALF)
        return pltpu.make_async_copy(held.at[at], out.at[at], sems.at[n])

    def step(first, n):
        for half in range(2):
            for r in range(0, HALF, BAND):
                row, shift = first + half * HALF + r, pl.multiple_of(n * 2 * HALF, 2 * HALF)
                value = wide[0] * read(u0, row, shift) + wide[1] * read([u1], row, shift)
                write([held], row, shift, value + wide[2] * read(u2, row, shift))
            copy_out(2 * n + half + first // HALF).start(priority=half)

    starts = sorted({*starts_of(u0), *starts_of(u2)})
    for first, end in zip(starts, starts[1:] + [total]):
        pl.loop(0, (end - first) // (2 * HALF))(functools.partial(step, first))
    n0, s = jnp.sqrt(g00), jnp.sqrt(q)
    for n, value in enumerate((n0, h11, s / n0, w0 / (s * n0), h22, jnp.sqrt(square))):
        hess[n] = value[0, 0]
    pl.loop(0, total // HALF)(lambda n: copy_out(n).wait())


def combine(cells, grams, u0, u1, u2):
    args = [grams, u1, *u0, *u2]
    return kernel_call(
        functools.partial(combine_kernel, cells, (len(u0), len(u2))),
        "combine",
        args,
        [IN_VMEM] * len(args),
        [jax.ShapeDtypeStruct(u1.shape, F32), jax.ShapeDtypeStruct((6,), F32)],
        out_specs=[IN_HBM, IN_SMEM],
        scratch=[pltpu.VMEM(u1.shape, F32), pltpu.SemaphoreType.DMA((u1.shape[0] // HALF,))],
    )


def shifted(value, axis, steps):
    count = lax.axis_size(axis)
    return lax.ppermute(value, axis, [(i, (i + steps) % count) for i in range(count)])


def neighbour_planes(value, axis):
    count = lax.axis_size(axis)
    if count == 2:
        return [lax.ppermute(value, axis, [(0, 1), (1, 0)])]
    up = [(i, i + 1) for i in range(count - 1)]
    return [lax.ppermute(value, axis, up), lax.ppermute(value, axis, [(b, a) for a, b in up])]


def on_device(start_vector, coupling, advect):
    _, chans, rows_here, modes_m, modes_k = start_vector.shape
    assert rows_here == 1
    rows = chans * modes_m
    start = start_vector.reshape(rows, modes_k)
    couple = coupling.reshape(chans, chans, modes_m, modes_k)
    devices = lax.axis_size("seg") * lax.axis_size("rad")
    cells = float(devices * start.size)
    paired = lax.axis_size("rad") == 2

    early = EARLY_ROWS
    sizes = (rows - LATE_ROWS, LATE_ROWS) if paired else (modes_m,) * chans

    u0, u0b, near_one, pieces = [], [], [], None
    for first, size, parts in ((0, early, 0), (early, rows - early, chans)):
        field, rounded, pieces = take_rows(start, first, size, u0b, parts)
        u0.append(field)
        u0b.append(rounded)
        near_one.append(neighbour_planes(rounded, "rad"))
    next_one = [shifted(x, "seg", -1) for x in pieces]
    two, tables = transform(pieces, couple, awaited=near_one[0])
    part, part_b = local_first(advect, u0, pieces, next_one, two, tables, sizes)
    if paired:
        near_two = [neighbour_planes(x, "rad") for x in part_b]
    u1, *u1b = first_image(part, list(zip(*near_one)), chans)
    if not paired:
        near_two = [neighbour_planes(x, "rad") for x in u1b]
    next_two = [shifted(x, "seg", -1) for x in u1b]
    two, _ = transform(u1b, couple, tables)
    part, scale, gram = local_last(advect, [u1], u1b, next_two, two, tables, u0, paired)
    u2, first = [], 0
    for size, planes in zip(sizes, near_two):
        slots = devices if first + size == rows else None
        field, gram = second_image(first, scale, u0, u1, part, gram, planes, slots)
        first += size
        u2.append(field)
    grams = lax.all_to_all(gram, ("seg", "rad"), 0, 0)
    basis, hess = combine(cells, grams, u0, u1, u2)
    return basis.reshape(start_vector.shape), hess


def solution(mesh):
    return jax.shard_map(
        on_device,
        mesh=mesh,
        in_specs=(
            P("seg", None, "rad", None, None),
            P("seg", None, None, "rad", None, None),
            P("rad"),
        ),
        out_specs=(P("seg", None, "rad", None, None), P()),
        check_vma=False,
    )
```

```python
import functools
import math

import jax
import jax.numpy as jnp
from jax import lax
from jax.experimental import pallas as pl
from jax.experimental.pallas import tpu as pltpu
from jax.sharding import PartitionSpec as P

RADIAL_ALL = 256
WINDOW_START = 124
RADIAL_GAIN = 0.25
VISC_AXIAL = 4.0
VISC_TURN = 0.05

F32 = jnp.float32
BF16 = jnp.bfloat16
VMEM_LIMIT = 8 * 1024 * 1024
TRANSFORM_LIMIT = 22 * 1024 * 1024
ROWS = 128
COLS = 256
BAND = 16
LONG = 10**11
MEDIUM = 15 * 10**9
CHUNK = 64
EARLY_ROWS = 128
LATE_ROWS = 64

IN_SMEM = pl.BlockSpec(memory_space=pltpu.SMEM)
IN_VMEM = pl.BlockSpec(memory_space=pltpu.VMEM)
IN_HBM = pl.BlockSpec(memory_space=pltpu.HBM)


def kernel_call(body, name, args, in_specs, outs, out_specs=None, scratch=(), limit=VMEM_LIMIT, flops=1000):
    held = [
        a if s is IN_SMEM else pltpu.with_memory_space_constraint(a, s.memory_space)
        for a, s in zip(args, in_specs)
    ]
    more = {} if out_specs is None else {"out_specs": out_specs}
    return pl.pallas_call(
        body,
        out_shape=outs,
        in_specs=in_specs,
        scratch_shapes=list(scratch),
        compiler_params=pltpu.CompilerParams(vmem_limit_bytes=limit),
        cost_estimate=pl.CostEstimate(flops=flops, bytes_accessed=1000, transcendentals=0),
        name=name,
        **more,
    )(*held)


def sine_turns(y):
    x = y * F32(2.0 * math.pi)
    x2 = x * x
    acc = F32(1.0 / 6227020800.0)
    for c in (-1.0 / 39916800.0, 1.0 / 362880.0, -1.0 / 5040.0, 1.0 / 120.0, -1.0 / 6.0, 1.0):
        acc = acc * x2 + F32(c)
    return acc * x


def trig_block(row0, rows, cols, mode_axis, count, weighted):
    half = count // 2
    r = lax.broadcasted_iota(jnp.int32, (rows, cols), 0) + row0
    c = lax.broadcasted_iota(jnp.int32, (rows, cols), 1)
    mode, point = (r, c) if mode_axis == 0 else (c, r)
    is_cos = mode <= half
    freq = jnp.where(is_cos, mode, mode - half).astype(F32)
    phase = freq * point.astype(F32) - jnp.where(is_cos, F32(0.0), F32(count // 4))
    phase = phase - F32(count) * jnp.floor(phase * F32(1.0 / count))
    value = -sine_turns(F32(0.25) - jnp.abs(phase * F32(1.0 / count) - F32(0.5)))
    if weighted:
        edge = (mode == 0) | (mode == half)
        value = value * jnp.where(edge, F32(1.0 / count), F32(2.0 / count))
    return value.astype(BF16)


def fill_table(ref, mode_axis, weighted):
    count = ref.shape[0]

    @pl.loop(0, count // ROWS)
    def _(i):
        at = pl.multiple_of(i * ROWS, ROWS)
        ref[pl.ds(at, ROWS), :] = trig_block(at, ROWS, count, mode_axis, count, weighted)


def taker(refs):
    refs = list(refs)

    def take(count=None):
        if count is None:
            return refs.pop(0)
        out, refs[:count] = refs[:count], []
        return out

    return take


def segments(modes_m, groups):
    ends, total = {modes_m}, 0
    for group in groups:
        total += group.shape[0]
        ends.add(total % modes_m or modes_m)
    ends = sorted(ends)
    return list(zip([0] + ends[:-1], ends))


def starts_of(groups):
    return [sum(g.shape[0] for g in groups[:n]) for n in range(len(groups))]


def band(groups, row, shift):
    for group in groups:
        if row < group.shape[0]:
            return group, pl.ds(pl.multiple_of(shift + row, BAND), BAND)
        row -= group.shape[0]


def read(groups, row, shift):
    group, at = band(groups, row, shift)
    return group[at, :]


def write(groups, row, shift, value):
    group, at = band(groups, row, shift)
    group[at, :] = value.astype(group.dtype)


def for_bands(lo, hi, body):
    @pl.loop(0, (hi - lo) // BAND)
    def _(i):
        body(pl.multiple_of(i * BAND, BAND))


def take_kernel(v, field, late, *refs):
    pieces, sems = refs[:-1], refs[-1]
    rows, early = field.shape[0], field.shape[0] - late.shape[0]
    copies = []
    for n, r in enumerate(range(0, rows, ROWS)):
        copies.append(pltpu.make_async_copy(v.at[pl.ds(r, ROWS)], field.at[pl.ds(r, ROWS)], sems.at[n]))
        copies[n].start()
    for n, r in enumerate(range(0, rows, ROWS)):
        copies[n].wait()
        value = field[r : r + ROWS, :].astype(BF16)
        if r >= early:
            late[r - early : r - early + ROWS, :] = value
        piece = pieces[r // pieces[0].shape[0]]
        at = r % piece.shape[0]
        piece[at : at + ROWS, :] = value


def take_start(v, chans):
    rows, modes_k = v.shape
    field, late, *pieces = kernel_call(
        take_kernel,
        "take_start",
        [v],
        [IN_HBM],
        [pltpu.VMEM(v.shape, F32), pltpu.VMEM((rows - EARLY_ROWS, modes_k), BF16)]
        + [pltpu.VMEM((rows // chans, modes_k), BF16)] * chans,
        scratch=[pltpu.SemaphoreType.DMA((rows // ROWS,))],
    )
    return field, late, pieces


def transform_kernel(build, awaited, *refs):
    take = taker(refs)
    chans = len(refs) - awaited - (14 if build else 13)
    x = take(chans)
    take(awaited)
    couple_far = take()
    tables_far = None if build else take(3)
    out = take()
    if build:
        tables_far, anal_m = take(3), take()
    one, phys, mixed, couple, synth_k, synth_mt, anal_kt, sems = take(8)
    near = (synth_k, synth_mt, anal_kt)
    _, modes_m, modes_k = out.shape
    load = pltpu.make_async_copy(couple_far, couple, sems.at[3])
    ends = [(n, f) if build else (f, n) for n, f in zip(near, tables_far)]
    moves = [pltpu.make_async_copy(src, dst, sems.at[i]) for i, (src, dst) in enumerate(ends)]
    if not build:
        for move in moves[:2]:
            move.start()
    load.start()
    if not build:
        moves[2].start()

    def ready(i, mode_axis, weighted):
        if build:
            fill_table(near[i], mode_axis, weighted)
            moves[i].start()
        else:
            moves[i].wait()

    ready(0, 0, False)
    for c in range(chans):

        @pl.loop(0, modes_m // ROWS)
        def _(i):
            at = pl.ds(pl.multiple_of(i * ROWS, ROWS), ROWS)
            one[c, at, :] = jnp.dot(x[c][at, :], synth_k[...], preferred_element_type=F32).astype(BF16)

    ready(1, 1, False)
    load.wait()

    @pl.loop(0, modes_k // COLS)
    def _(z):
        zs = pl.ds(pl.multiple_of(z * COLS, COLS), COLS)
        for j in range(chans):
            phys[j] = jnp.dot(synth_mt[...], one[j, :, zs], preferred_element_type=F32)

        @pl.loop(0, modes_m // BAND)
        def _(i):
            ts = pl.ds(pl.multiple_of(i * BAND, BAND), BAND)
            parts = [phys[j, ts, :] for j in range(chans)]
            for c in range(chans):
                total = couple[c, 0, ts, zs].astype(F32) * parts[0]
                for j in range(1, chans):
                    total += couple[c, j, ts, zs].astype(F32) * parts[j]
                mixed[c, ts, zs] = total.astype(BF16)

    ready(2, 1, True)
    for c in range(chans):

        @pl.loop(0, modes_m // ROWS)
        def _(i):
            at = pl.ds(pl.multiple_of(i * ROWS, ROWS), ROWS)
            out[c, at, :] = jnp.dot(mixed[c, at, :], anal_kt[...], preferred_element_type=F32).astype(BF16)

    if build:
        fill_table(anal_m, 0, True)
        for move in moves:
            move.wait()


def transform(x, couple, tables=None, awaited=()):
    chans, _, modes_m, modes_k = couple.shape
    shape = (chans, modes_m, modes_k)
    sizes = [(modes_k, modes_k), (modes_m, modes_m), (modes_k, modes_k)]
    build = tables is None
    far = [] if build else list(tables[:3])
    outs, out_specs = [pltpu.VMEM(shape, BF16)], [IN_VMEM]
    if build:
        outs += [pltpu.HBM(n, BF16) for n in sizes] + [pltpu.VMEM((modes_m, modes_m), BF16)]
        out_specs += [IN_HBM] * 3 + [IN_VMEM]
    result = kernel_call(
        functools.partial(transform_kernel, build, len(awaited)),
        "transform",
        [*x, *awaited, couple, *far],
        [IN_VMEM] * (chans + len(awaited)) + [IN_HBM] * (1 + len(far)),
        outs,
        out_specs=out_specs,
        scratch=[
            pltpu.VMEM(shape, BF16),
            pltpu.VMEM((chans, modes_m, COLS), F32),
            pltpu.VMEM(shape, BF16),
            pltpu.VMEM(couple.shape, BF16),
            *[pltpu.VMEM(n, BF16) for n in sizes],
            pltpu.SemaphoreType.DMA((4,)),
        ],
        limit=TRANSFORM_LIMIT,
        flops=MEDIUM if awaited else 1000,
    )
    return result[0], (result[1:] if build else tables)


def own_plane():
    return WINDOW_START + lax.axis_index("rad")


def paired_plane():
    return WINDOW_START + 1 - lax.axis_index("rad")


def inverse_divisor(row0, modes_m, modes_k, plane):
    m = lax.broadcasted_iota(jnp.int32, (BAND, 1), 0) + row0
    k = lax.broadcasted_iota(jnp.int32, (1, modes_k), 1)
    fm = jnp.where(m <= modes_m // 2, m, m - modes_m // 2).astype(F32) / F32(modes_m // 2)
    fk = jnp.where(k <= modes_k // 2, k, k - modes_k // 2).astype(F32) / F32(modes_k // 2)
    radius = (jnp.full((1, 1), plane, jnp.int32).astype(F32) + F32(0.5)) / F32(RADIAL_ALL)
    turning = F32(VISC_TURN) * fm * fm / (radius * radius)
    return F32(1.0) / (F32(1.0) + F32(VISC_AXIAL) * fk * fk + turning)


def add_tile(acc, n, value):
    value = sum(value[r : r + 8] for r in range(0, value.shape[0], 8))
    acc[n] += sum(value[:, k : k + 128] for k in range(0, value.shape[1], 128))


def local_kernel(counts, last, paired, advect, *refs):
    take = taker(refs)
    v, vb, recv = (take(n) for n in counts[:3])
    two, anal_m = take(), take()
    if last:
        u0, out_b = take(counts[3]), []
        out, scale, gram, spec, acc = take(5)
        acc[...] = jnp.zeros_like(acc)
    else:
        out, out_b, spec = take(), take(counts[3]), take()
    chans, modes_m, modes_k = two.shape
    half = modes_k // 2
    for c in range(chans):
        spec[c] = jnp.dot(anal_m[...], two[c], preferred_element_type=F32)
    wave = lax.broadcasted_iota(jnp.int32, (1, half), 1).astype(F32) * advect[0]

    def step(lo, shift):
        at = pl.ds(pl.multiple_of(shift + lo, BAND), BAND)
        inv = inverse_divisor(shift + lo, modes_m, modes_k, own_plane())
        if last:
            scale[at, :] = inv * F32(RADIAL_GAIN)
            if paired:
                mate = inverse_divisor(shift + lo, modes_m, modes_k, paired_plane()) * F32(RADIAL_GAIN**2)
        for c in range(chans):
            row = c * modes_m + lo
            own = read(v, row, shift)
            drift = jnp.concatenate([-wave * own[:, half:], wave * own[:, :half]], axis=1)
            mid = F32(-2.0 * RADIAL_GAIN) * read(vb, row, shift).astype(F32)
            total = own + spec[c, at, :] + drift + mid
            if last:
                x0 = read(u0, row, shift)
                if paired:
                    total += mate * x0
                for n, (a, b) in enumerate(((x0, x0), (x0, own), (own, own))):
                    add_tile(acc, n, a * b)
            value = total * inv - read(recv, row, shift).astype(F32)
            write([out], row, shift, value)
            if not last:
                write(out_b, row, shift, value)

    for lo, hi in segments(modes_m, [*v, *(u0 if last else out_b)]):
        for_bands(lo, hi, functools.partial(step, lo))

    if last:
        gram[...] = jnp.zeros_like(gram)
        for n in range(3):
            gram[n : n + 1, :] = jnp.sum(acc[n], axis=0, keepdims=True)


def local_first(advect, v, vb, recv, two, tables, sizes):
    chans, modes_m, modes_k = two.shape
    args = [advect, *v, *vb, *recv, two, tables[3]]
    part, *part_b = kernel_call(
        functools.partial(local_kernel, (len(v), len(vb), len(recv), len(sizes)), False, False),
        "local_first",
        args,
        [IN_SMEM] + [IN_VMEM] * (len(args) - 1),
        [pltpu.VMEM((chans * modes_m, modes_k), F32)] + [pltpu.VMEM((n, modes_k), BF16) for n in sizes],
        scratch=[pltpu.VMEM(two.shape, F32)],
    )
    return part, part_b


def local_last(advect, v, vb, recv, two, tables, u0, paired):
    chans, modes_m, modes_k = two.shape
    args = [advect, *v, *vb, *recv, two, tables[3], *u0]
    return kernel_call(
        functools.partial(local_kernel, (len(v), len(vb), len(recv), len(u0)), True, paired),
        "local_last",
        args,
        [IN_SMEM] + [IN_VMEM] * (len(args) - 1),
        [
            pltpu.VMEM((chans * modes_m, modes_k), F32),
            pltpu.VMEM((modes_m, modes_k), F32),
            pltpu.VMEM((8, 128), F32),
        ],
        scratch=[pltpu.VMEM(two.shape, F32), pltpu.VMEM((3, 8, 128), F32)],
    )


def added(sides, row, shift):
    return functools.reduce(lambda a, b: a + b, [read(s, row, shift).astype(F32) for s in sides])


def first_kernel(groups, count, part, *refs):
    take = taker(refs)
    sides = [take(groups) for _ in range(count)]
    out, out_b = take(), take(len(refs) - groups * count - 1)
    chans, (modes_m, modes_k) = len(out_b), out_b[0].shape

    def step(lo, shift):
        inv = inverse_divisor(shift + lo, modes_m, modes_k, own_plane()) * F32(RADIAL_GAIN)
        for c in range(chans):
            row = c * modes_m + lo
            value = read([part], row, shift) + added(sides, row, shift) * inv
            write([out], row, shift, value)
            write(out_b, row, shift, value)

    for lo, hi in segments(modes_m, sides[0]):
        for_bands(lo, hi, functools.partial(step, lo))


def first_image(part, sides, chans):
    rows, modes_k = part.shape
    args = [part, *(x for side in sides for x in side)]
    return kernel_call(
        functools.partial(first_kernel, len(sides[0]), len(sides)),
        "first_image",
        args,
        [IN_VMEM] * len(args),
        [pltpu.VMEM(part.shape, F32)] + [pltpu.VMEM((rows // chans, modes_k), BF16)] * chans,
        flops=LONG,
    )


def on_diagonal():
    rows, lanes = (lax.broadcasted_iota(jnp.int32, (8, 128), n) for n in (0, 1))
    return rows == lanes


def second_kernel(first, counts, done, scale, u1, part, before, *refs):
    take = taker(refs)
    u0, planes = take(counts[0]), take(counts[1])
    out, gram, acc = take(3)
    modes_m = scale.shape[0]
    acc[...] = jnp.zeros_like(acc)

    def step(row, shift):
        at = pl.ds(pl.multiple_of(shift + row % modes_m, BAND), BAND)
        near = added([[p] for p in planes], row - first, shift)
        x2 = read([part], row, shift) + near * scale[at, :]
        write([out], row - first, shift, x2)
        for n, x in enumerate((read(u0, row, shift), read([u1], row, shift), x2)):
            add_tile(acc, n, x * x2)

    end = first + out.shape[0]
    starts = {first, *starts_of(u0), *range(0, end, modes_m)}
    starts = [r for r in sorted(starts) if first <= r < end]
    for lo, hi in zip(starts, starts[1:] + [end]):
        for_bands(lo, hi, functools.partial(step, lo))

    rows = [jnp.sum(acc[n], axis=0, keepdims=True) for n in range(3)]
    total = before[...] + jnp.concatenate([jnp.zeros((3, 128), F32), *rows, jnp.zeros((2, 128), F32)], axis=0)
    if done:
        total = jnp.sum(total, axis=1, keepdims=True)
        total = jnp.sum(jnp.where(on_diagonal(), total, F32(0.0)), axis=0, keepdims=True)
    gram[...] = jnp.broadcast_to(total, gram.shape)


def second_image(first, scale, u0, u1, part, before, planes, slots=None):
    done = slots is not None
    tile = (slots, 128) if done else (8, 128)
    args = [scale, u1, part, before, *u0, *planes]
    return kernel_call(
        functools.partial(second_kernel, first, (len(u0), len(planes)), done),
        "second_image",
        args,
        [IN_VMEM] * len(args),
        [pltpu.VMEM(planes[0].shape, F32), pltpu.VMEM(tile, F32)],
        scratch=[pltpu.VMEM((3, 8, 128), F32)],
    )


def combine_kernel(cells, counts, grams, u1, *refs):
    take = taker(refs)
    u0, u2 = take(counts[0]), take(counts[1])
    out, hess, held, sems = take(4)
    total, modes_k = out.shape
    g = jnp.sum(grams[...], axis=0, keepdims=True) * F32(1.0 / cells)
    g = jnp.sum(jnp.where(on_diagonal(), g, F32(0.0)), axis=1, keepdims=True)
    g = jnp.broadcast_to(g, (8, 128))
    g00, g01, g11, g02, g12, g22 = (g[n : n + 1, :] for n in range(6))
    per_g00 = F32(1.0) / g00
    h11 = g01 * per_g00
    q = g11 - h11 * g01
    per_q = F32(1.0) / q
    w0 = g02 - h11 * g01
    w1 = g12 - h11 * g11
    ww = g22 - F32(2.0) * h11 * g12 + h11 * h11 * g11
    h22 = (w1 - h11 * w0) * per_q
    ratio = w0 * per_g00
    square = (ww - w0 * ratio) * per_q - h22 * h22
    c2 = F32(1.0) / jnp.sqrt(q * square)
    c1 = -(h11 + h22) * c2
    c0 = (h11 * h22 - ratio) * c2
    wide = [jnp.concatenate([x] * (modes_k // 128), axis=1) for x in (c0, c1, c2)]

    def copy_out(n):
        at = pl.ds(pl.multiple_of(n * CHUNK, CHUNK), CHUNK)
        return pltpu.make_async_copy(held.at[at], out.at[at], sems.at[n])

    def step(first, n):
        for r in range(0, CHUNK, BAND):
            row, shift = first + r, pl.multiple_of(n * CHUNK, CHUNK)
            value = wide[0] * read(u0, row, shift) + wide[1] * read([u1], row, shift)
            write([held], row, shift, value + wide[2] * read(u2, row, shift))
        copy_out(n + first // CHUNK).start()

    starts = sorted({*starts_of(u0), *starts_of(u2)})
    for first, end in zip(starts, starts[1:] + [total]):
        pl.loop(0, (end - first) // CHUNK)(functools.partial(step, first))
    n0, s = jnp.sqrt(g00), jnp.sqrt(q)
    for n, value in enumerate((n0, h11, s / n0, w0 / (s * n0), h22, jnp.sqrt(square))):
        hess[n] = value[0, 0]
    pl.loop(0, total // CHUNK)(lambda n: copy_out(n).wait())


def combine(cells, grams, u0, u1, u2):
    args = [grams, u1, *u0, *u2]
    return kernel_call(
        functools.partial(combine_kernel, cells, (len(u0), len(u2))),
        "combine",
        args,
        [IN_VMEM] * len(args),
        [jax.ShapeDtypeStruct(u1.shape, F32), jax.ShapeDtypeStruct((6,), F32)],
        out_specs=[IN_HBM, IN_SMEM],
        scratch=[pltpu.VMEM(u1.shape, F32), pltpu.SemaphoreType.DMA((u1.shape[0] // CHUNK,))],
    )


def shifted(value, axis, steps):
    count = lax.axis_size(axis)
    return lax.ppermute(value, axis, [(i, (i + steps) % count) for i in range(count)])


def neighbour_planes(value, axis):
    count = lax.axis_size(axis)
    if count == 2:
        return [lax.ppermute(value, axis, [(0, 1), (1, 0)])]
    up = [(i, i + 1) for i in range(count - 1)]
    return [lax.ppermute(value, axis, up), lax.ppermute(value, axis, [(b, a) for a, b in up])]


def on_device(start_vector, coupling, advect):
    _, chans, rows_here, modes_m, modes_k = start_vector.shape
    assert rows_here == 1
    rows = chans * modes_m
    start = start_vector.reshape(rows, modes_k)
    couple = coupling.reshape(chans, chans, modes_m, modes_k)
    devices = lax.axis_size("seg") * lax.axis_size("rad")
    cells = float(devices * start.size)
    paired = lax.axis_size("rad") == 2

    sizes = (rows - LATE_ROWS, LATE_ROWS) if paired else (modes_m,) * chans

    near_one = [neighbour_planes(start[:EARLY_ROWS].astype(BF16), "rad")]
    field, late, pieces = take_start(start, chans)
    near_one.append(neighbour_planes(late, "rad"))
    u0 = [field]
    next_one = [shifted(x, "seg", -1) for x in pieces]
    two, tables = transform(pieces, couple, awaited=near_one[0])
    part, part_b = local_first(advect, u0, pieces, next_one, two, tables, sizes)
    if paired:
        near_two = [neighbour_planes(x, "rad") for x in part_b]
    u1, *u1b = first_image(part, list(zip(*near_one)), chans)
    if not paired:
        near_two = [neighbour_planes(x, "rad") for x in u1b]
    next_two = [shifted(x, "seg", -1) for x in u1b]
    two, _ = transform(u1b, couple, tables)
    part, scale, gram = local_last(advect, [u1], u1b, next_two, two, tables, u0, paired)
    u2, first = [], 0
    for size, planes in zip(sizes, near_two):
        slots = devices if first + size == rows else None
        field, gram = second_image(first, scale, u0, u1, part, gram, planes, slots)
        first += size
        u2.append(field)
    grams = lax.all_to_all(gram, ("rad", "seg"), 0, 0)
    basis, hess = combine(cells, grams, u0, u1, u2)
    return basis.reshape(start_vector.shape), hess


def solution(mesh):
    return jax.shard_map(
        on_device,
        mesh=mesh,
        in_specs=(
            P("seg", None, "rad", None, None),
            P("seg", None, None, "rad", None, None),
            P("rad"),
        ),
        out_specs=(P("seg", None, "rad", None, None), P()),
        check_vma=False,
    )
```

```python
import functools
import math

import jax
import jax.numpy as jnp
from jax import lax
from jax.experimental import pallas as pl
from jax.experimental.pallas import tpu as pltpu
from jax.sharding import PartitionSpec as P

RADIAL_ALL = 256
WINDOW_START = 124
RADIAL_GAIN = 0.25
VISC_AXIAL = 4.0
VISC_TURN = 0.05

F32 = jnp.float32
BF16 = jnp.bfloat16
VMEM_LIMIT = 8 * 1024 * 1024
TRANSFORM_LIMIT = 22 * 1024 * 1024
ROWS = 128
COLS = 256
BAND = 16
LONG = 10**11
MEDIUM = 15 * 10**9
CHUNK = 64
EARLY_ROWS = 128
LATE_ROWS = 128

IN_SMEM = pl.BlockSpec(memory_space=pltpu.SMEM)
IN_VMEM = pl.BlockSpec(memory_space=pltpu.VMEM)
IN_HBM = pl.BlockSpec(memory_space=pltpu.HBM)


def kernel_call(body, name, args, in_specs, outs, out_specs=None, scratch=(), limit=VMEM_LIMIT, flops=1000):
    held = [
        a if s is IN_SMEM else pltpu.with_memory_space_constraint(a, s.memory_space)
        for a, s in zip(args, in_specs)
    ]
    more = {} if out_specs is None else {"out_specs": out_specs}
    return pl.pallas_call(
        body,
        out_shape=outs,
        in_specs=in_specs,
        scratch_shapes=list(scratch),
        compiler_params=pltpu.CompilerParams(vmem_limit_bytes=limit),
        cost_estimate=pl.CostEstimate(flops=flops, bytes_accessed=1000, transcendentals=0),
        name=name,
        **more,
    )(*held)


def sine_turns(y):
    x = y * F32(2.0 * math.pi)
    x2 = x * x
    acc = F32(1.0 / 6227020800.0)
    for c in (-1.0 / 39916800.0, 1.0 / 362880.0, -1.0 / 5040.0, 1.0 / 120.0, -1.0 / 6.0, 1.0):
        acc = acc * x2 + F32(c)
    return acc * x


def trig_block(row0, rows, cols, mode_axis, count, weighted):
    half = count // 2
    r = lax.broadcasted_iota(jnp.int32, (rows, cols), 0) + row0
    c = lax.broadcasted_iota(jnp.int32, (rows, cols), 1)
    mode, point = (r, c) if mode_axis == 0 else (c, r)
    is_cos = mode <= half
    freq = jnp.where(is_cos, mode, mode - half).astype(F32)
    phase = freq * point.astype(F32) - jnp.where(is_cos, F32(0.0), F32(count // 4))
    phase = phase - F32(count) * jnp.floor(phase * F32(1.0 / count))
    value = -sine_turns(F32(0.25) - jnp.abs(phase * F32(1.0 / count) - F32(0.5)))
    if weighted:
        edge = (mode == 0) | (mode == half)
        value = value * jnp.where(edge, F32(1.0 / count), F32(2.0 / count))
    return value.astype(BF16)


def fill_table(ref, mode_axis, weighted):
    count = ref.shape[0]

    @pl.loop(0, count // ROWS)
    def _(i):
        at = pl.multiple_of(i * ROWS, ROWS)
        ref[pl.ds(at, ROWS), :] = trig_block(at, ROWS, count, mode_axis, count, weighted)


def taker(refs):
    refs = list(refs)

    def take(count=None):
        if count is None:
            return refs.pop(0)
        out, refs[:count] = refs[:count], []
        return out

    return take


def segments(modes_m, groups):
    ends, total = {modes_m}, 0
    for group in groups:
        total += group.shape[0]
        ends.add(total % modes_m or modes_m)
    ends = sorted(ends)
    return list(zip([0] + ends[:-1], ends))


def starts_of(groups):
    return [sum(g.shape[0] for g in groups[:n]) for n in range(len(groups))]


def band(groups, row, shift):
    for group in groups:
        if row < group.shape[0]:
            return group, pl.ds(pl.multiple_of(shift + row, BAND), BAND)
        row -= group.shape[0]


def read(groups, row, shift):
    group, at = band(groups, row, shift)
    return group[at, :]


def write(groups, row, shift, value):
    group, at = band(groups, row, shift)
    group[at, :] = value.astype(group.dtype)


def for_bands(lo, hi, body):
    @pl.loop(0, (hi - lo) // BAND)
    def _(i):
        body(pl.multiple_of(i * BAND, BAND))


def take_kernel(first, v, *refs):
    take = taker(refs)
    early = [] if first == 0 else [take()]
    field, rounded = take(), take()
    pieces, sems = take(len(refs) - len(early) - 3), take()
    count = field.shape[0]
    step = count // sems.shape[0]
    copies = []
    for n, r in enumerate(range(0, count, step)):
        copies.append(
            pltpu.make_async_copy(v.at[pl.ds(first + r, step)], field.at[pl.ds(r, step)], sems.at[n])
        )
        copies[n].start()

    def lay(row, value):
        for n, piece in enumerate(pieces):
            at = row - n * piece.shape[0]
            if 0 <= at < piece.shape[0]:
                piece[at : at + value.shape[0], :] = value

    for r in range(0, first, ROWS):
        lay(r, early[0][r : r + ROWS, :])
    for n, r in enumerate(range(0, count, step)):
        copies[n].wait()
        value = field[r : r + step, :].astype(BF16)
        rounded[r : r + step, :] = value
        lay(first + r, value)


def take_rows(v, first, count, early=(), pieces=0):
    rows, modes_k = v.shape
    shapes = [pltpu.VMEM((count, modes_k), F32), pltpu.VMEM((count, modes_k), BF16)]
    field, rounded, *by_channel = kernel_call(
        functools.partial(take_kernel, first),
        "take_rows",
        [v, *early],
        [IN_HBM] + [IN_VMEM] * len(early),
        shapes + [pltpu.VMEM((rows // max(pieces, 1), modes_k), BF16)] * pieces,
        scratch=[pltpu.SemaphoreType.DMA((max(count // ROWS, 4),))],
    )
    return field, rounded, by_channel


def transform_kernel(build, awaited, *refs):
    take = taker(refs)
    chans = len(refs) - awaited - (14 if build else 13)
    x = take(chans)
    take(awaited)
    couple_far = take()
    tables_far = None if build else take(3)
    out = take()
    if build:
        tables_far, anal_m = take(3), take()
    one, phys, mixed, couple, synth_k, synth_mt, anal_kt, sems = take(8)
    near = (synth_k, synth_mt, anal_kt)
    _, modes_m, modes_k = out.shape
    load = pltpu.make_async_copy(couple_far, couple, sems.at[3])
    ends = [(n, f) if build else (f, n) for n, f in zip(near, tables_far)]
    moves = [pltpu.make_async_copy(src, dst, sems.at[i]) for i, (src, dst) in enumerate(ends)]
    if not build:
        for move in moves[:2]:
            move.start()
    load.start()
    if not build:
        moves[2].start()

    def ready(i, mode_axis, weighted):
        if build:
            fill_table(near[i], mode_axis, weighted)
            moves[i].start()
        else:
            moves[i].wait()

    ready(0, 0, False)
    for c in range(chans):

        @pl.loop(0, modes_m // ROWS)
        def _(i):
            at = pl.ds(pl.multiple_of(i * ROWS, ROWS), ROWS)
            one[c, at, :] = jnp.dot(x[c][at, :], synth_k[...], preferred_element_type=F32).astype(BF16)

    ready(1, 1, False)
    load.wait()

    @pl.loop(0, modes_k // COLS)
    def _(z):
        zs = pl.ds(pl.multiple_of(z * COLS, COLS), COLS)
        for j in range(chans):
            phys[j] = jnp.dot(synth_mt[...], one[j, :, zs], preferred_element_type=F32)

        @pl.loop(0, modes_m // BAND)
        def _(i):
            ts = pl.ds(pl.multiple_of(i * BAND, BAND), BAND)
            parts = [phys[j, ts, :] for j in range(chans)]
            for c in range(chans):
                total = couple[c, 0, ts, zs].astype(F32) * parts[0]
                for j in range(1, chans):
                    total += couple[c, j, ts, zs].astype(F32) * parts[j]
                mixed[c, ts, zs] = total.astype(BF16)

    ready(2, 1, True)
    for c in range(chans):

        @pl.loop(0, modes_m // ROWS)
        def _(i):
            at = pl.ds(pl.multiple_of(i * ROWS, ROWS), ROWS)
            out[c, at, :] = jnp.dot(mixed[c, at, :], anal_kt[...], preferred_element_type=F32).astype(BF16)

    if build:
        fill_table(anal_m, 0, True)
        for move in moves:
            move.wait()


def transform(x, couple, tables=None, awaited=()):
    chans, _, modes_m, modes_k = couple.shape
    shape = (chans, modes_m, modes_k)
    sizes = [(modes_k, modes_k), (modes_m, modes_m), (modes_k, modes_k)]
    build = tables is None
    far = [] if build else list(tables[:3])
    outs, out_specs = [pltpu.VMEM(shape, BF16)], [IN_VMEM]
    if build:
        outs += [pltpu.HBM(n, BF16) for n in sizes] + [pltpu.VMEM((modes_m, modes_m), BF16)]
        out_specs += [IN_HBM] * 3 + [IN_VMEM]
    result = kernel_call(
        functools.partial(transform_kernel, build, len(awaited)),
        "transform",
        [*x, *awaited, couple, *far],
        [IN_VMEM] * (chans + len(awaited)) + [IN_HBM] * (1 + len(far)),
        outs,
        out_specs=out_specs,
        scratch=[
            pltpu.VMEM(shape, BF16),
            pltpu.VMEM((chans, modes_m, COLS), F32),
            pltpu.VMEM(shape, BF16),
            pltpu.VMEM(couple.shape, BF16),
            *[pltpu.VMEM(n, BF16) for n in sizes],
            pltpu.SemaphoreType.DMA((4,)),
        ],
        limit=TRANSFORM_LIMIT,
        flops=MEDIUM if awaited else 1000,
    )
    return result[0], (result[1:] if build else tables)


def own_plane():
    return WINDOW_START + lax.axis_index("rad")


def paired_plane():
    return WINDOW_START + 1 - lax.axis_index("rad")


def inverse_divisor(row0, modes_m, modes_k, plane):
    m = lax.broadcasted_iota(jnp.int32, (BAND, 1), 0) + row0
    k = lax.broadcasted_iota(jnp.int32, (1, modes_k), 1)
    fm = jnp.where(m <= modes_m // 2, m, m - modes_m // 2).astype(F32) / F32(modes_m // 2)
    fk = jnp.where(k <= modes_k // 2, k, k - modes_k // 2).astype(F32) / F32(modes_k // 2)
    radius = (jnp.full((1, 1), plane, jnp.int32).astype(F32) + F32(0.5)) / F32(RADIAL_ALL)
    turning = F32(VISC_TURN) * fm * fm / (radius * radius)
    return F32(1.0) / (F32(1.0) + F32(VISC_AXIAL) * fk * fk + turning)


def add_tile(acc, n, value):
    value = sum(value[r : r + 8] for r in range(0, value.shape[0], 8))
    acc[n] += sum(value[:, k : k + 128] for k in range(0, value.shape[1], 128))


def local_kernel(counts, last, paired, advect, *refs):
    take = taker(refs)
    v, vb, recv = (take(n) for n in counts[:3])
    two, anal_m = take(), take()
    if last:
        u0, out_b = take(counts[3]), []
        out, scale, gram, spec, acc = take(5)
        acc[...] = jnp.zeros_like(acc)
    else:
        out, out_b, spec = take(), take(counts[3]), take()
    chans, modes_m, modes_k = two.shape
    half = modes_k // 2
    for c in range(chans):
        spec[c] = jnp.dot(anal_m[...], two[c], preferred_element_type=F32)
    wave = lax.broadcasted_iota(jnp.int32, (1, half), 1).astype(F32) * advect[0]

    def step(lo, shift):
        at = pl.ds(pl.multiple_of(shift + lo, BAND), BAND)
        inv = inverse_divisor(shift + lo, modes_m, modes_k, own_plane())
        if last:
            scale[at, :] = inv * F32(RADIAL_GAIN)
            if paired:
                mate = inverse_divisor(shift + lo, modes_m, modes_k, paired_plane()) * F32(RADIAL_GAIN**2)
        for c in range(chans):
            row = c * modes_m + lo
            own = read(v, row, shift)
            drift = jnp.concatenate([-wave * own[:, half:], wave * own[:, :half]], axis=1)
            mid = F32(-2.0 * RADIAL_GAIN) * read(vb, row, shift).astype(F32)
            total = own + spec[c, at, :] + drift + mid
            if last:
                x0 = read(u0, row, shift)
                if paired:
                    total += mate * x0
                for n, (a, b) in enumerate(((x0, x0), (x0, own), (own, own))):
                    add_tile(acc, n, a * b)
            value = total * inv - read(recv, row, shift).astype(F32)
            write([out], row, shift, value)
            if not last:
                write(out_b, row, shift, value)

    for lo, hi in segments(modes_m, [*v, *(u0 if last else out_b)]):
        for_bands(lo, hi, functools.partial(step, lo))

    if last:
        gram[...] = jnp.zeros_like(gram)
        for n in range(3):
            gram[n : n + 1, :] = jnp.sum(acc[n], axis=0, keepdims=True)


def local_first(advect, v, vb, recv, two, tables, sizes):
    chans, modes_m, modes_k = two.shape
    args = [advect, *v, *vb, *recv, two, tables[3]]
    part, *part_b = kernel_call(
        functools.partial(local_kernel, (len(v), len(vb), len(recv), len(sizes)), False, False),
        "local_first",
        args,
        [IN_SMEM] + [IN_VMEM] * (len(args) - 1),
        [pltpu.VMEM((chans * modes_m, modes_k), F32)] + [pltpu.VMEM((n, modes_k), BF16) for n in sizes],
        scratch=[pltpu.VMEM(two.shape, F32)],
    )
    return part, part_b


def local_last(advect, v, vb, recv, two, tables, u0, paired):
    chans, modes_m, modes_k = two.shape
    args = [advect, *v, *vb, *recv, two, tables[3], *u0]
    return kernel_call(
        functools.partial(local_kernel, (len(v), len(vb), len(recv), len(u0)), True, paired),
        "local_last",
        args,
        [IN_SMEM] + [IN_VMEM] * (len(args) - 1),
        [
            pltpu.VMEM((chans * modes_m, modes_k), F32),
            pltpu.VMEM((modes_m, modes_k), F32),
            pltpu.VMEM((8, 128), F32),
        ],
        scratch=[pltpu.VMEM(two.shape, F32), pltpu.VMEM((3, 8, 128), F32)],
    )


def added(sides, row, shift):
    return functools.reduce(lambda a, b: a + b, [read(s, row, shift).astype(F32) for s in sides])


def first_kernel(groups, count, part, *refs):
    take = taker(refs)
    sides = [take(groups) for _ in range(count)]
    out, out_b = take(), take(len(refs) - groups * count - 1)
    chans, (modes_m, modes_k) = len(out_b), out_b[0].shape

    def step(lo, shift):
        inv = inverse_divisor(shift + lo, modes_m, modes_k, own_plane()) * F32(RADIAL_GAIN)
        for c in range(chans):
            row = c * modes_m + lo
            value = read([part], row, shift) + added(sides, row, shift) * inv
            write([out], row, shift, value)
            write(out_b, row, shift, value)

    for lo, hi in segments(modes_m, sides[0]):
        for_bands(lo, hi, functools.partial(step, lo))


def first_image(part, sides, chans):
    rows, modes_k = part.shape
    args = [part, *(x for side in sides for x in side)]
    return kernel_call(
        functools.partial(first_kernel, len(sides[0]), len(sides)),
        "first_image",
        args,
        [IN_VMEM] * len(args),
        [pltpu.VMEM(part.shape, F32)] + [pltpu.VMEM((rows // chans, modes_k), BF16)] * chans,
        flops=LONG,
    )


def on_diagonal():
    rows, lanes = (lax.broadcasted_iota(jnp.int32, (8, 128), n) for n in (0, 1))
    return rows == lanes


def second_kernel(first, counts, done, scale, u1, part, before, *refs):
    take = taker(refs)
    u0, planes = take(counts[0]), take(counts[1])
    out, gram, acc = take(3)
    modes_m = scale.shape[0]
    acc[...] = jnp.zeros_like(acc)

    def step(row, shift):
        at = pl.ds(pl.multiple_of(shift + row % modes_m, BAND), BAND)
        near = added([[p] for p in planes], row - first, shift)
        x2 = read([part], row, shift) + near * scale[at, :]
        write([out], row - first, shift, x2)
        for n, x in enumerate((read(u0, row, shift), read([u1], row, shift), x2)):
            add_tile(acc, n, x * x2)

    end = first + out.shape[0]
    starts = {first, *starts_of(u0), *range(0, end, modes_m)}
    starts = [r for r in sorted(starts) if first <= r < end]
    for lo, hi in zip(starts, starts[1:] + [end]):
        for_bands(lo, hi, functools.partial(step, lo))

    rows = [jnp.sum(acc[n], axis=0, keepdims=True) for n in range(3)]
    total = before[...] + jnp.concatenate([jnp.zeros((3, 128), F32), *rows, jnp.zeros((2, 128), F32)], axis=0)
    if done:
        total = jnp.sum(total, axis=1, keepdims=True)
        total = jnp.sum(jnp.where(on_diagonal(), total, F32(0.0)), axis=0, keepdims=True)
    gram[...] = jnp.broadcast_to(total, gram.shape)


def second_image(first, scale, u0, u1, part, before, planes, slots=None):
    done = slots is not None
    tile = (slots, 128) if done else (8, 128)
    args = [scale, u1, part, before, *u0, *planes]
    return kernel_call(
        functools.partial(second_kernel, first, (len(u0), len(planes)), done),
        "second_image",
        args,
        [IN_VMEM] * len(args),
        [pltpu.VMEM(planes[0].shape, F32), pltpu.VMEM(tile, F32)],
        scratch=[pltpu.VMEM((3, 8, 128), F32)],
    )


def combine_kernel(cells, counts, grams, u1, *refs):
    take = taker(refs)
    u0, u2 = take(counts[0]), take(counts[1])
    out, hess, held, sems = take(4)
    total, modes_k = out.shape
    g = jnp.sum(grams[...], axis=0, keepdims=True) * F32(1.0 / cells)
    g = jnp.sum(jnp.where(on_diagonal(), g, F32(0.0)), axis=1, keepdims=True)
    g = jnp.broadcast_to(g, (8, 128))
    g00, g01, g11, g02, g12, g22 = (g[n : n + 1, :] for n in range(6))
    per_g00 = F32(1.0) / g00
    h11 = g01 * per_g00
    q = g11 - h11 * g01
    per_q = F32(1.0) / q
    w0 = g02 - h11 * g01
    w1 = g12 - h11 * g11
    ww = g22 - F32(2.0) * h11 * g12 + h11 * h11 * g11
    h22 = (w1 - h11 * w0) * per_q
    ratio = w0 * per_g00
    square = (ww - w0 * ratio) * per_q - h22 * h22
    c2 = F32(1.0) / jnp.sqrt(q * square)
    c1 = -(h11 + h22) * c2
    c0 = (h11 * h22 - ratio) * c2
    c0, c1, c2 = (x[0, 0] for x in (c0, c1, c2))

    def copy_out(n):
        at = pl.ds(pl.multiple_of(n * CHUNK, CHUNK), CHUNK)
        return pltpu.make_async_copy(held.at[at], out.at[at], sems.at[n])

    def step(first, n):
        for r in range(0, CHUNK, BAND):
            row, shift = first + r, pl.multiple_of(n * CHUNK, CHUNK)
            value = c0 * read(u0, row, shift) + c1 * read([u1], row, shift)
            write([held], row, shift, value + c2 * read(u2, row, shift))
        copy_out(n + first // CHUNK).start()

    starts = sorted({*starts_of(u0), *starts_of(u2)})
    for first, end in zip(starts, starts[1:] + [total]):
        pl.loop(0, (end - first) // CHUNK)(functools.partial(step, first))
    n0, s = jnp.sqrt(g00), jnp.sqrt(q)
    for n, value in enumerate((n0, h11, s / n0, w0 / (s * n0), h22, jnp.sqrt(square))):
        hess[n] = value[0, 0]
    pl.loop(0, total // CHUNK)(lambda n: copy_out(n).wait())


def combine(cells, grams, u0, u1, u2):
    args = [grams, u1, *u0, *u2]
    return kernel_call(
        functools.partial(combine_kernel, cells, (len(u0), len(u2))),
        "combine",
        args,
        [IN_VMEM] * len(args),
        [jax.ShapeDtypeStruct(u1.shape, F32), jax.ShapeDtypeStruct((6,), F32)],
        out_specs=[IN_HBM, IN_SMEM],
        scratch=[pltpu.VMEM(u1.shape, F32), pltpu.SemaphoreType.DMA((u1.shape[0] // CHUNK,))],
    )


def shifted(value, axis, steps):
    count = lax.axis_size(axis)
    return lax.ppermute(value, axis, [(i, (i + steps) % count) for i in range(count)])


def neighbour_planes(value, axis):
    count = lax.axis_size(axis)
    if count == 2:
        return [lax.ppermute(value, axis, [(0, 1), (1, 0)])]
    up = [(i, i + 1) for i in range(count - 1)]
    return [lax.ppermute(value, axis, up), lax.ppermute(value, axis, [(b, a) for a, b in up])]


def on_device(start_vector, coupling, advect):
    _, chans, rows_here, modes_m, modes_k = start_vector.shape
    assert rows_here == 1
    rows = chans * modes_m
    start = start_vector.reshape(rows, modes_k)
    couple = coupling.reshape(chans, chans, modes_m, modes_k)
    devices = lax.axis_size("seg") * lax.axis_size("rad")
    cells = float(devices * start.size)
    paired = lax.axis_size("rad") == 2

    early = EARLY_ROWS
    sizes = (rows - LATE_ROWS, LATE_ROWS) if paired else (modes_m,) * chans

    u0, u0b, near_one, pieces = [], [], [], None
    for first, size, parts in ((0, early, 0), (early, rows - early, chans)):
        field, rounded, pieces = take_rows(start, first, size, u0b, parts)
        u0.append(field)
        u0b.append(rounded)
        near_one.append(neighbour_planes(rounded, "rad"))
    next_one = [shifted(x, "seg", -1) for x in pieces]
    two, tables = transform(pieces, couple, awaited=near_one[0])
    part, part_b = local_first(advect, u0, pieces, next_one, two, tables, sizes)
    if paired:
        near_two = [neighbour_planes(x, "rad") for x in part_b]
    u1, *u1b = first_image(part, list(zip(*near_one)), chans)
    if not paired:
        near_two = [neighbour_planes(x, "rad") for x in u1b]
    next_two = [shifted(x, "seg", -1) for x in u1b]
    two, _ = transform(u1b, couple, tables)
    part, scale, gram = local_last(advect, [u1], u1b, next_two, two, tables, u0, paired)
    u2, first = [], 0
    for size, planes in zip(sizes, near_two):
        slots = devices if first + size == rows else None
        field, gram = second_image(first, scale, u0, u1, part, gram, planes, slots)
        first += size
        u2.append(field)
    grams = lax.all_to_all(gram, ("rad", "seg"), 0, 0)
    basis, hess = combine(cells, grams, u0, u1, u2)
    return basis.reshape(start_vector.shape), hess


def solution(mesh):
    return jax.shard_map(
        on_device,
        mesh=mesh,
        in_specs=(
            P("seg", None, "rad", None, None),
            P("seg", None, None, "rad", None, None),
            P("rad"),
        ),
        out_specs=(P("seg", None, "rad", None, None), P()),
        check_vma=False,
    )
```

```python
import functools
import math

import jax
import jax.numpy as jnp
from jax import lax
from jax.experimental import pallas as pl
from jax.experimental.pallas import tpu as pltpu
from jax.sharding import PartitionSpec as P

RADIAL_ALL = 256
WINDOW_START = 124
RADIAL_GAIN = 0.25
VISC_AXIAL = 4.0
VISC_TURN = 0.05

F32 = jnp.float32
BF16 = jnp.bfloat16
VMEM_LIMIT = 8 * 1024 * 1024
TRANSFORM_LIMIT = 22 * 1024 * 1024
ROWS = 128
COLS = 256
BAND = 16
LONG = 10**11
MEDIUM = 15 * 10**9
CHUNK = 64
EARLY_ROWS = 128
LATE_ROWS = 128

IN_SMEM = pl.BlockSpec(memory_space=pltpu.SMEM)
IN_VMEM = pl.BlockSpec(memory_space=pltpu.VMEM)
IN_HBM = pl.BlockSpec(memory_space=pltpu.HBM)


def kernel_call(body, name, args, in_specs, outs, out_specs=None, scratch=(), limit=VMEM_LIMIT, flops=1000):
    held = [
        a if s is IN_SMEM else pltpu.with_memory_space_constraint(a, s.memory_space)
        for a, s in zip(args, in_specs)
    ]
    more = {} if out_specs is None else {"out_specs": out_specs}
    return pl.pallas_call(
        body,
        out_shape=outs,
        in_specs=in_specs,
        scratch_shapes=list(scratch),
        compiler_params=pltpu.CompilerParams(vmem_limit_bytes=limit),
        cost_estimate=pl.CostEstimate(flops=flops, bytes_accessed=1000, transcendentals=0),
        name=name,
        **more,
    )(*held)


def sine_turns(y):
    x = y * F32(2.0 * math.pi)
    x2 = x * x
    acc = F32(1.0 / 6227020800.0)
    for c in (-1.0 / 39916800.0, 1.0 / 362880.0, -1.0 / 5040.0, 1.0 / 120.0, -1.0 / 6.0, 1.0):
        acc = acc * x2 + F32(c)
    return acc * x


def trig_block(row0, rows, cols, mode_axis, count, weighted):
    half = count // 2
    r = lax.broadcasted_iota(jnp.int32, (rows, cols), 0) + row0
    c = lax.broadcasted_iota(jnp.int32, (rows, cols), 1)
    mode, point = (r, c) if mode_axis == 0 else (c, r)
    is_cos = mode <= half
    freq = jnp.where(is_cos, mode, mode - half).astype(F32)
    phase = freq * point.astype(F32) - jnp.where(is_cos, F32(0.0), F32(count // 4))
    phase = phase - F32(count) * jnp.floor(phase * F32(1.0 / count))
    value = -sine_turns(F32(0.25) - jnp.abs(phase * F32(1.0 / count) - F32(0.5)))
    if weighted:
        edge = (mode == 0) | (mode == half)
        value = value * jnp.where(edge, F32(1.0 / count), F32(2.0 / count))
    return value.astype(BF16)


def fill_table(ref, mode_axis, weighted):
    count = ref.shape[0]

    @pl.loop(0, count // ROWS)
    def _(i):
        at = pl.multiple_of(i * ROWS, ROWS)
        ref[pl.ds(at, ROWS), :] = trig_block(at, ROWS, count, mode_axis, count, weighted)


def taker(refs):
    refs = list(refs)

    def take(count=None):
        if count is None:
            return refs.pop(0)
        out, refs[:count] = refs[:count], []
        return out

    return take


def segments(modes_m, groups):
    ends, total = {modes_m}, 0
    for group in groups:
        total += group.shape[0]
        ends.add(total % modes_m or modes_m)
    ends = sorted(ends)
    return list(zip([0] + ends[:-1], ends))


def starts_of(groups):
    return [sum(g.shape[0] for g in groups[:n]) for n in range(len(groups))]


def band(groups, row, shift):
    for group in groups:
        if row < group.shape[0]:
            return group, pl.ds(pl.multiple_of(shift + row, BAND), BAND)
        row -= group.shape[0]


def read(groups, row, shift):
    group, at = band(groups, row, shift)
    return group[at, :]


def write(groups, row, shift, value):
    group, at = band(groups, row, shift)
    group[at, :] = value.astype(group.dtype)


def for_bands(lo, hi, body):
    @pl.loop(0, (hi - lo) // BAND)
    def _(i):
        body(pl.multiple_of(i * BAND, BAND))


def take_kernel(first, v, *refs):
    take = taker(refs)
    early = [] if first == 0 else [take()]
    field, rounded = take(), take()
    pieces, sems = take(len(refs) - len(early) - 3), take()
    count = field.shape[0]
    copies = []
    for n, r in enumerate(range(0, count, ROWS)):
        copies.append(
            pltpu.make_async_copy(v.at[pl.ds(first + r, ROWS)], field.at[pl.ds(r, ROWS)], sems.at[n])
        )
        copies[n].start()

    def lay(row, value):
        for n, piece in enumerate(pieces):
            at = row - n * piece.shape[0]
            if 0 <= at < piece.shape[0]:
                piece[at : at + ROWS, :] = value

    for r in range(0, first, ROWS):
        lay(r, early[0][r : r + ROWS, :])
    for n, r in enumerate(range(0, count, ROWS)):
        copies[n].wait()
        value = field[r : r + ROWS, :].astype(BF16)
        rounded[r : r + ROWS, :] = value
        lay(first + r, value)


def take_rows(v, first, count, early=(), pieces=0):
    rows, modes_k = v.shape
    shapes = [pltpu.VMEM((count, modes_k), F32), pltpu.VMEM((count, modes_k), BF16)]
    field, rounded, *by_channel = kernel_call(
        functools.partial(take_kernel, first),
        "take_rows",
        [v, *early],
        [IN_HBM] + [IN_VMEM] * len(early),
        shapes + [pltpu.VMEM((rows // max(pieces, 1), modes_k), BF16)] * pieces,
        scratch=[pltpu.SemaphoreType.DMA((count // ROWS,))],
    )
    return field, rounded, by_channel


def transform_kernel(build, awaited, *refs):
    take = taker(refs)
    chans = len(refs) - awaited - (14 if build else 13)
    x = take(chans)
    take(awaited)
    couple_far = take()
    tables_far = None if build else take(3)
    out = take()
    if build:
        tables_far, anal_m = take(3), take()
    one, phys, mixed, couple, synth_k, synth_mt, anal_kt, sems = take(8)
    near = (synth_k, synth_mt, anal_kt)
    _, modes_m, modes_k = out.shape
    load = pltpu.make_async_copy(couple_far, couple, sems.at[3])
    ends = [(n, f) if build else (f, n) for n, f in zip(near, tables_far)]
    moves = [pltpu.make_async_copy(src, dst, sems.at[i]) for i, (src, dst) in enumerate(ends)]
    if not build:
        for move in moves[:2]:
            move.start()
    load.start()
    if not build:
        moves[2].start()

    def ready(i, mode_axis, weighted):
        if build:
            fill_table(near[i], mode_axis, weighted)
            moves[i].start()
        else:
            moves[i].wait()

    ready(0, 0, False)
    for c in range(chans):

        @pl.loop(0, modes_m // ROWS)
        def _(i):
            at = pl.ds(pl.multiple_of(i * ROWS, ROWS), ROWS)
            one[c, at, :] = jnp.dot(x[c][at, :], synth_k[...], preferred_element_type=F32).astype(BF16)

    ready(1, 1, False)
    load.wait()

    @pl.loop(0, modes_k // COLS)
    def _(z):
        zs = pl.ds(pl.multiple_of(z * COLS, COLS), COLS)
        for j in range(chans):
            phys[j] = jnp.dot(synth_mt[...], one[j, :, zs], preferred_element_type=F32)

        @pl.loop(0, modes_m // BAND)
        def _(i):
            ts = pl.ds(pl.multiple_of(i * BAND, BAND), BAND)
            parts = [phys[j, ts, :] for j in range(chans)]
            for c in range(chans):
                total = couple[c, 0, ts, zs].astype(F32) * parts[0]
                for j in range(1, chans):
                    total += couple[c, j, ts, zs].astype(F32) * parts[j]
                mixed[c, ts, zs] = total.astype(BF16)

    ready(2, 1, True)
    for c in range(chans):

        @pl.loop(0, modes_m // ROWS)
        def _(i):
            at = pl.ds(pl.multiple_of(i * ROWS, ROWS), ROWS)
            out[c, at, :] = jnp.dot(mixed[c, at, :], anal_kt[...], preferred_element_type=F32).astype(BF16)

    if build:
        fill_table(anal_m, 0, True)
        for move in moves:
            move.wait()


def transform(x, couple, tables=None, awaited=()):
    chans, _, modes_m, modes_k = couple.shape
    shape = (chans, modes_m, modes_k)
    sizes = [(modes_k, modes_k), (modes_m, modes_m), (modes_k, modes_k)]
    build = tables is None
    far = [] if build else list(tables[:3])
    outs, out_specs = [pltpu.VMEM(shape, BF16)], [IN_VMEM]
    if build:
        outs += [pltpu.HBM(n, BF16) for n in sizes] + [pltpu.VMEM((modes_m, modes_m), BF16)]
        out_specs += [IN_HBM] * 3 + [IN_VMEM]
    result = kernel_call(
        functools.partial(transform_kernel, build, len(awaited)),
        "transform",
        [*x, *awaited, couple, *far],
        [IN_VMEM] * (chans + len(awaited)) + [IN_HBM] * (1 + len(far)),
        outs,
        out_specs=out_specs,
        scratch=[
            pltpu.VMEM(shape, BF16),
            pltpu.VMEM((chans, modes_m, COLS), F32),
            pltpu.VMEM(shape, BF16),
            pltpu.VMEM(couple.shape, BF16),
            *[pltpu.VMEM(n, BF16) for n in sizes],
            pltpu.SemaphoreType.DMA((4,)),
        ],
        limit=TRANSFORM_LIMIT,
        flops=MEDIUM if awaited else 1000,
    )
    return result[0], (result[1:] if build else tables)


def own_plane():
    return WINDOW_START + lax.axis_index("rad")


def paired_plane():
    return WINDOW_START + 1 - lax.axis_index("rad")


def inverse_divisor(row0, modes_m, modes_k, plane):
    m = lax.broadcasted_iota(jnp.int32, (BAND, 1), 0) + row0
    k = lax.broadcasted_iota(jnp.int32, (1, modes_k), 1)
    fm = jnp.where(m <= modes_m // 2, m, m - modes_m // 2).astype(F32) / F32(modes_m // 2)
    fk = jnp.where(k <= modes_k // 2, k, k - modes_k // 2).astype(F32) / F32(modes_k // 2)
    radius = (jnp.full((1, 1), plane, jnp.int32).astype(F32) + F32(0.5)) / F32(RADIAL_ALL)
    turning = F32(VISC_TURN) * fm * fm / (radius * radius)
    return F32(1.0) / (F32(1.0) + F32(VISC_AXIAL) * fk * fk + turning)


def add_tile(acc, n, value):
    value = sum(value[r : r + 8] for r in range(0, value.shape[0], 8))
    acc[n] += sum(value[:, k : k + 128] for k in range(0, value.shape[1], 128))


def local_kernel(counts, last, paired, advect, *refs):
    take = taker(refs)
    v, vb, recv = (take(n) for n in counts[:3])
    two, anal_m = take(), take()
    if last:
        u0, out_b = take(counts[3]), []
        out, scale, gram, spec, acc = take(5)
        acc[...] = jnp.zeros_like(acc)
    else:
        out, out_b, spec = take(), take(counts[3]), take()
    chans, modes_m, modes_k = two.shape
    half = modes_k // 2
    for c in range(chans):
        spec[c] = jnp.dot(anal_m[...], two[c], preferred_element_type=F32)
    wave = lax.broadcasted_iota(jnp.int32, (1, half), 1).astype(F32) * advect[0]

    def step(lo, shift):
        at = pl.ds(pl.multiple_of(shift + lo, BAND), BAND)
        inv = inverse_divisor(shift + lo, modes_m, modes_k, own_plane())
        if last:
            scale[at, :] = inv * F32(RADIAL_GAIN)
            if paired:
                mate = inverse_divisor(shift + lo, modes_m, modes_k, paired_plane()) * F32(RADIAL_GAIN**2)
        for c in range(chans):
            row = c * modes_m + lo
            own = read(v, row, shift)
            drift = jnp.concatenate([-wave * own[:, half:], wave * own[:, :half]], axis=1)
            mid = F32(-2.0 * RADIAL_GAIN) * read(vb, row, shift).astype(F32)
            total = own + spec[c, at, :] + drift + mid
            if last:
                x0 = read(u0, row, shift)
                if paired:
                    total += mate * x0
                for n, (a, b) in enumerate(((x0, x0), (x0, own), (own, own))):
                    add_tile(acc, n, a * b)
            value = total * inv - read(recv, row, shift).astype(F32)
            write([out], row, shift, value)
            if not last:
                write(out_b, row, shift, value)

    for lo, hi in segments(modes_m, [*v, *(u0 if last else out_b)]):
        for_bands(lo, hi, functools.partial(step, lo))

    if last:
        gram[...] = jnp.zeros_like(gram)
        for n in range(3):
            gram[n : n + 1, :] = jnp.sum(acc[n], axis=0, keepdims=True)


def local_first(advect, v, vb, recv, two, tables, sizes):
    chans, modes_m, modes_k = two.shape
    args = [advect, *v, *vb, *recv, two, tables[3]]
    part, *part_b = kernel_call(
        functools.partial(local_kernel, (len(v), len(vb), len(recv), len(sizes)), False, False),
        "local_first",
        args,
        [IN_SMEM] + [IN_VMEM] * (len(args) - 1),
        [pltpu.VMEM((chans * modes_m, modes_k), F32)] + [pltpu.VMEM((n, modes_k), BF16) for n in sizes],
        scratch=[pltpu.VMEM(two.shape, F32)],
    )
    return part, part_b


def local_last(advect, v, vb, recv, two, tables, u0, paired):
    chans, modes_m, modes_k = two.shape
    args = [advect, *v, *vb, *recv, two, tables[3], *u0]
    return kernel_call(
        functools.partial(local_kernel, (len(v), len(vb), len(recv), len(u0)), True, paired),
        "local_last",
        args,
        [IN_SMEM] + [IN_VMEM] * (len(args) - 1),
        [
            pltpu.VMEM((chans * modes_m, modes_k), F32),
            pltpu.VMEM((modes_m, modes_k), F32),
            pltpu.VMEM((8, 128), F32),
        ],
        scratch=[pltpu.VMEM(two.shape, F32), pltpu.VMEM((3, 8, 128), F32)],
    )


def added(sides, row, shift):
    return functools.reduce(lambda a, b: a + b, [read(s, row, shift).astype(F32) for s in sides])


def first_kernel(groups, count, part, *refs):
    take = taker(refs)
    sides = [take(groups) for _ in range(count)]
    out, out_b = take(), take(len(refs) - groups * count - 1)
    chans, (modes_m, modes_k) = len(out_b), out_b[0].shape

    def step(lo, shift):
        inv = inverse_divisor(shift + lo, modes_m, modes_k, own_plane()) * F32(RADIAL_GAIN)
        for c in range(chans):
            row = c * modes_m + lo
            value = read([part], row, shift) + added(sides, row, shift) * inv
            write([out], row, shift, value)
            write(out_b, row, shift, value)

    for lo, hi in segments(modes_m, sides[0]):
        for_bands(lo, hi, functools.partial(step, lo))


def first_image(part, sides, chans):
    rows, modes_k = part.shape
    args = [part, *(x for side in sides for x in side)]
    return kernel_call(
        functools.partial(first_kernel, len(sides[0]), len(sides)),
        "first_image",
        args,
        [IN_VMEM] * len(args),
        [pltpu.VMEM(part.shape, F32)] + [pltpu.VMEM((rows // chans, modes_k), BF16)] * chans,
        flops=LONG,
    )


def on_diagonal():
    rows, lanes = (lax.broadcasted_iota(jnp.int32, (8, 128), n) for n in (0, 1))
    return rows == lanes


def second_kernel(first, counts, done, scale, u1, part, before, *refs):
    take = taker(refs)
    u0, planes = take(counts[0]), take(counts[1])
    out, gram, acc = take(3)
    modes_m = scale.shape[0]
    acc[...] = jnp.zeros_like(acc)

    def step(row, shift):
        at = pl.ds(pl.multiple_of(shift + row % modes_m, BAND), BAND)
        near = added([[p] for p in planes], row - first, shift)
        x2 = read([part], row, shift) + near * scale[at, :]
        write([out], row - first, shift, x2)
        for n, x in enumerate((read(u0, row, shift), read([u1], row, shift), x2)):
            add_tile(acc, n, x * x2)

    end = first + out.shape[0]
    starts = {first, *starts_of(u0), *range(0, end, modes_m)}
    starts = [r for r in sorted(starts) if first <= r < end]
    for lo, hi in zip(starts, starts[1:] + [end]):
        for_bands(lo, hi, functools.partial(step, lo))

    rows = [jnp.sum(acc[n], axis=0, keepdims=True) for n in range(3)]
    total = before[...] + jnp.concatenate([jnp.zeros((3, 128), F32), *rows, jnp.zeros((2, 128), F32)], axis=0)
    if done:
        total = jnp.sum(total, axis=1, keepdims=True)
        total = jnp.sum(jnp.where(on_diagonal(), total, F32(0.0)), axis=0, keepdims=True)
    gram[...] = jnp.broadcast_to(total, gram.shape)


def second_image(first, scale, u0, u1, part, before, planes, slots=None):
    done = slots is not None
    tile = (slots, 128) if done else (8, 128)
    args = [scale, u1, part, before, *u0, *planes]
    return kernel_call(
        functools.partial(second_kernel, first, (len(u0), len(planes)), done),
        "second_image",
        args,
        [IN_VMEM] * len(args),
        [pltpu.VMEM(planes[0].shape, F32), pltpu.VMEM(tile, F32)],
        scratch=[pltpu.VMEM((3, 8, 128), F32)],
    )


def combine_kernel(cells, counts, grams, u1, *refs):
    take = taker(refs)
    u0, u2 = take(counts[0]), take(counts[1])
    out, hess_out, held, hess, sems = take(5)
    total, modes_k = out.shape
    g = jnp.sum(grams[...], axis=0, keepdims=True) * F32(1.0 / cells)
    g = jnp.sum(jnp.where(on_diagonal(), g, F32(0.0)), axis=1, keepdims=True)
    g = jnp.broadcast_to(g, (8, 128))
    g00, g01, g11, g02, g12, g22 = (g[n : n + 1, :] for n in range(6))
    per_g00 = F32(1.0) / g00
    h11 = g01 * per_g00
    q = g11 - h11 * g01
    per_q = F32(1.0) / q
    w0 = g02 - h11 * g01
    w1 = g12 - h11 * g11
    ww = g22 - F32(2.0) * h11 * g12 + h11 * h11 * g11
    h22 = (w1 - h11 * w0) * per_q
    ratio = w0 * per_g00
    square = (ww - w0 * ratio) * per_q - h22 * h22
    c2 = F32(1.0) / jnp.sqrt(q * square)
    c1 = -(h11 + h22) * c2
    c0 = (h11 * h22 - ratio) * c2
    wide = [jnp.concatenate([x] * (modes_k // 128), axis=1) for x in (c0, c1, c2)]

    def copy_out(n):
        at = pl.ds(pl.multiple_of(n * CHUNK, CHUNK), CHUNK)
        return pltpu.make_async_copy(held.at[at], out.at[at], sems.at[n])

    def step(first, n):
        for r in range(0, CHUNK, BAND):
            row, shift = first + r, pl.multiple_of(n * CHUNK, CHUNK)
            value = wide[0] * read(u0, row, shift) + wide[1] * read([u1], row, shift)
            write([held], row, shift, value + wide[2] * read(u2, row, shift))
        copy_out(n + first // CHUNK).start()

    starts = sorted({*starts_of(u0), *starts_of(u2)})
    for first, end in zip(starts, starts[1:] + [total]):
        pl.loop(0, (end - first) // CHUNK)(functools.partial(step, first))
    n0, s = jnp.sqrt(g00), jnp.sqrt(q)
    for n, value in enumerate((n0, h11, s / n0, w0 / (s * n0), h22, jnp.sqrt(square))):
        hess[n] = value[0, 0]
    last = pltpu.make_async_copy(hess, hess_out, sems.at[total // CHUNK])
    last.start()
    pl.loop(0, total // CHUNK)(lambda n: copy_out(n).wait())
    last.wait()


def combine(cells, grams, u0, u1, u2):
    args = [grams, u1, *u0, *u2]
    return kernel_call(
        functools.partial(combine_kernel, cells, (len(u0), len(u2))),
        "combine",
        args,
        [IN_VMEM] * len(args),
        [jax.ShapeDtypeStruct(u1.shape, F32), jax.ShapeDtypeStruct((6,), F32)],
        out_specs=[IN_HBM, IN_HBM],
        scratch=[
            pltpu.VMEM(u1.shape, F32),
            pltpu.SMEM((6,), F32),
            pltpu.SemaphoreType.DMA((u1.shape[0] // CHUNK + 1,)),
        ],
    )


def shifted(value, axis, steps):
    count = lax.axis_size(axis)
    return lax.ppermute(value, axis, [(i, (i + steps) % count) for i in range(count)])


def neighbour_planes(value, axis):
    count = lax.axis_size(axis)
    if count == 2:
        return [lax.ppermute(value, axis, [(0, 1), (1, 0)])]
    up = [(i, i + 1) for i in range(count - 1)]
    return [lax.ppermute(value, axis, up), lax.ppermute(value, axis, [(b, a) for a, b in up])]


def on_device(start_vector, coupling, advect):
    _, chans, rows_here, modes_m, modes_k = start_vector.shape
    assert rows_here == 1
    rows = chans * modes_m
    start = start_vector.reshape(rows, modes_k)
    couple = coupling.reshape(chans, chans, modes_m, modes_k)
    devices = lax.axis_size("seg") * lax.axis_size("rad")
    cells = float(devices * start.size)
    paired = lax.axis_size("rad") == 2

    early = EARLY_ROWS
    sizes = (rows - LATE_ROWS, LATE_ROWS) if paired else (modes_m,) * chans

    u0, u0b, near_one, pieces = [], [], [], None
    for first, size, parts in ((0, early, 0), (early, rows - early, chans)):
        field, rounded, pieces = take_rows(start, first, size, u0b, parts)
        u0.append(field)
        u0b.append(rounded)
        near_one.append(neighbour_planes(rounded, "rad"))
    next_one = [shifted(x, "seg", -1) for x in pieces]
    two, tables = transform(pieces, couple, awaited=near_one[0])
    part, part_b = local_first(advect, u0, pieces, next_one, two, tables, sizes)
    if paired:
        near_two = [neighbour_planes(x, "rad") for x in part_b]
    u1, *u1b = first_image(part, list(zip(*near_one)), chans)
    if not paired:
        near_two = [neighbour_planes(x, "rad") for x in u1b]
    next_two = [shifted(x, "seg", -1) for x in u1b]
    two, _ = transform(u1b, couple, tables)
    part, scale, gram = local_last(advect, [u1], u1b, next_two, two, tables, u0, paired)
    u2, first = [], 0
    for size, planes in zip(sizes, near_two):
        slots = devices if first + size == rows else None
        field, gram = second_image(first, scale, u0, u1, part, gram, planes, slots)
        first += size
        u2.append(field)
    grams = lax.all_to_all(gram, ("rad", "seg"), 0, 0)
    basis, hess = combine(cells, grams, u0, u1, u2)
    return basis.reshape(start_vector.shape), hess


def solution(mesh):
    return jax.shard_map(
        on_device,
        mesh=mesh,
        in_specs=(
            P("seg", None, "rad", None, None),
            P("seg", None, None, "rad", None, None),
            P("rad"),
        ),
        out_specs=(P("seg", None, "rad", None, None), P()),
        check_vma=False,
    )
```

```python
import functools
import math

import jax
import jax.numpy as jnp
from jax import lax
from jax.experimental import pallas as pl
from jax.experimental.pallas import tpu as pltpu
from jax.sharding import PartitionSpec as P

RADIAL_ALL = 256
WINDOW_START = 124
RADIAL_GAIN = 0.25
VISC_AXIAL = 4.0
VISC_TURN = 0.05

F32 = jnp.float32
BF16 = jnp.bfloat16
VMEM_LIMIT = 8 * 1024 * 1024
TRANSFORM_LIMIT = 22 * 1024 * 1024
ROWS = 128
COLS = 256
BAND = 16
LONG = 10**11
MEDIUM = 15 * 10**9
CHUNK = 32
EARLY_ROWS = 128
LATE_ROWS = 128

IN_SMEM = pl.BlockSpec(memory_space=pltpu.SMEM)
IN_VMEM = pl.BlockSpec(memory_space=pltpu.VMEM)
IN_HBM = pl.BlockSpec(memory_space=pltpu.HBM)


def kernel_call(body, name, args, in_specs, outs, out_specs=None, scratch=(), limit=VMEM_LIMIT, flops=1000):
    held = [
        a if s is IN_SMEM else pltpu.with_memory_space_constraint(a, s.memory_space)
        for a, s in zip(args, in_specs)
    ]
    more = {} if out_specs is None else {"out_specs": out_specs}
    return pl.pallas_call(
        body,
        out_shape=outs,
        in_specs=in_specs,
        scratch_shapes=list(scratch),
        compiler_params=pltpu.CompilerParams(vmem_limit_bytes=limit),
        cost_estimate=pl.CostEstimate(flops=flops, bytes_accessed=1000, transcendentals=0),
        name=name,
        **more,
    )(*held)


def sine_turns(y):
    x = y * F32(2.0 * math.pi)
    x2 = x * x
    acc = F32(1.0 / 6227020800.0)
    for c in (-1.0 / 39916800.0, 1.0 / 362880.0, -1.0 / 5040.0, 1.0 / 120.0, -1.0 / 6.0, 1.0):
        acc = acc * x2 + F32(c)
    return acc * x


def trig_block(row0, rows, cols, mode_axis, count, weighted):
    half = count // 2
    r = lax.broadcasted_iota(jnp.int32, (rows, cols), 0) + row0
    c = lax.broadcasted_iota(jnp.int32, (rows, cols), 1)
    mode, point = (r, c) if mode_axis == 0 else (c, r)
    is_cos = mode <= half
    freq = jnp.where(is_cos, mode, mode - half).astype(F32)
    phase = freq * point.astype(F32) - jnp.where(is_cos, F32(0.0), F32(count // 4))
    phase = phase - F32(count) * jnp.floor(phase * F32(1.0 / count))
    value = -sine_turns(F32(0.25) - jnp.abs(phase * F32(1.0 / count) - F32(0.5)))
    if weighted:
        edge = (mode == 0) | (mode == half)
        value = value * jnp.where(edge, F32(1.0 / count), F32(2.0 / count))
    return value.astype(BF16)


def fill_table(ref, mode_axis, weighted):
    count = ref.shape[0]

    @pl.loop(0, count // ROWS)
    def _(i):
        at = pl.multiple_of(i * ROWS, ROWS)
        ref[pl.ds(at, ROWS), :] = trig_block(at, ROWS, count, mode_axis, count, weighted)


def taker(refs):
    refs = list(refs)

    def take(count=None):
        if count is None:
            return refs.pop(0)
        out, refs[:count] = refs[:count], []
        return out

    return take


def segments(modes_m, groups):
    ends, total = {modes_m}, 0
    for group in groups:
        total += group.shape[0]
        ends.add(total % modes_m or modes_m)
    ends = sorted(ends)
    return list(zip([0] + ends[:-1], ends))


def starts_of(groups):
    return [sum(g.shape[0] for g in groups[:n]) for n in range(len(groups))]


def band(groups, row, shift):
    for group in groups:
        if row < group.shape[0]:
            return group, pl.ds(pl.multiple_of(shift + row, BAND), BAND)
        row -= group.shape[0]


def read(groups, row, shift):
    group, at = band(groups, row, shift)
    return group[at, :]


def write(groups, row, shift, value):
    group, at = band(groups, row, shift)
    group[at, :] = value.astype(group.dtype)


def for_bands(lo, hi, body):
    @pl.loop(0, (hi - lo) // BAND)
    def _(i):
        body(pl.multiple_of(i * BAND, BAND))


def take_kernel(first, v, *refs):
    take = taker(refs)
    early = [] if first == 0 else [take()]
    field, rounded = take(), take()
    pieces, sems = take(len(refs) - len(early) - 3), take()
    count = field.shape[0]
    copies = []
    for n, r in enumerate(range(0, count, ROWS)):
        copies.append(
            pltpu.make_async_copy(v.at[pl.ds(first + r, ROWS)], field.at[pl.ds(r, ROWS)], sems.at[n])
        )
        copies[n].start()

    def lay(row, value):
        for n, piece in enumerate(pieces):
            at = row - n * piece.shape[0]
            if 0 <= at < piece.shape[0]:
                piece[at : at + ROWS, :] = value

    for r in range(0, first, ROWS):
        lay(r, early[0][r : r + ROWS, :])
    for n, r in enumerate(range(0, count, ROWS)):
        copies[n].wait()
        value = field[r : r + ROWS, :].astype(BF16)
        rounded[r : r + ROWS, :] = value
        lay(first + r, value)


def take_rows(v, first, count, early=(), pieces=0):
    rows, modes_k = v.shape
    shapes = [pltpu.VMEM((count, modes_k), F32), pltpu.VMEM((count, modes_k), BF16)]
    field, rounded, *by_channel = kernel_call(
        functools.partial(take_kernel, first),
        "take_rows",
        [v, *early],
        [IN_HBM] + [IN_VMEM] * len(early),
        shapes + [pltpu.VMEM((rows // max(pieces, 1), modes_k), BF16)] * pieces,
        scratch=[pltpu.SemaphoreType.DMA((count // ROWS,))],
    )
    return field, rounded, by_channel


def transform_kernel(build, awaited, *refs):
    take = taker(refs)
    chans = len(refs) - awaited - (14 if build else 13)
    x = take(chans)
    take(awaited)
    couple_far = take()
    tables_far = None if build else take(3)
    out = take()
    if build:
        tables_far, anal_m = take(3), take()
    one, phys, mixed, couple, synth_k, synth_mt, anal_kt, sems = take(8)
    near = (synth_k, synth_mt, anal_kt)
    _, modes_m, modes_k = out.shape
    load = pltpu.make_async_copy(couple_far, couple, sems.at[3])
    ends = [(n, f) if build else (f, n) for n, f in zip(near, tables_far)]
    moves = [pltpu.make_async_copy(src, dst, sems.at[i]) for i, (src, dst) in enumerate(ends)]
    if not build:
        for move in moves[:2]:
            move.start()
    load.start()
    if not build:
        moves[2].start()

    def ready(i, mode_axis, weighted):
        if build:
            fill_table(near[i], mode_axis, weighted)
            moves[i].start()
        else:
            moves[i].wait()

    ready(0, 0, False)
    for c in range(chans):

        @pl.loop(0, modes_m // ROWS)
        def _(i):
            at = pl.ds(pl.multiple_of(i * ROWS, ROWS), ROWS)
            one[c, at, :] = jnp.dot(x[c][at, :], synth_k[...], preferred_element_type=F32).astype(BF16)

    ready(1, 1, False)
    load.wait()

    @pl.loop(0, modes_k // COLS)
    def _(z):
        zs = pl.ds(pl.multiple_of(z * COLS, COLS), COLS)
        for j in range(chans):
            phys[j] = jnp.dot(synth_mt[...], one[j, :, zs], preferred_element_type=F32)

        @pl.loop(0, modes_m // BAND)
        def _(i):
            ts = pl.ds(pl.multiple_of(i * BAND, BAND), BAND)
            parts = [phys[j, ts, :] for j in range(chans)]
            for c in range(chans):
                total = couple[c, 0, ts, zs].astype(F32) * parts[0]
                for j in range(1, chans):
                    total += couple[c, j, ts, zs].astype(F32) * parts[j]
                mixed[c, ts, zs] = total.astype(BF16)

    ready(2, 1, True)
    for c in range(chans):

        @pl.loop(0, modes_m // ROWS)
        def _(i):
            at = pl.ds(pl.multiple_of(i * ROWS, ROWS), ROWS)
            out[c, at, :] = jnp.dot(mixed[c, at, :], anal_kt[...], preferred_element_type=F32).astype(BF16)

    if build:
        fill_table(anal_m, 0, True)
        for move in moves:
            move.wait()


def transform(x, couple, tables=None, awaited=()):
    chans, _, modes_m, modes_k = couple.shape
    shape = (chans, modes_m, modes_k)
    sizes = [(modes_k, modes_k), (modes_m, modes_m), (modes_k, modes_k)]
    build = tables is None
    far = [] if build else list(tables[:3])
    outs, out_specs = [pltpu.VMEM(shape, BF16)], [IN_VMEM]
    if build:
        outs += [pltpu.HBM(n, BF16) for n in sizes] + [pltpu.VMEM((modes_m, modes_m), BF16)]
        out_specs += [IN_HBM] * 3 + [IN_VMEM]
    result = kernel_call(
        functools.partial(transform_kernel, build, len(awaited)),
        "transform",
        [*x, *awaited, couple, *far],
        [IN_VMEM] * (chans + len(awaited)) + [IN_HBM] * (1 + len(far)),
        outs,
        out_specs=out_specs,
        scratch=[
            pltpu.VMEM(shape, BF16),
            pltpu.VMEM((chans, modes_m, COLS), F32),
            pltpu.VMEM(shape, BF16),
            pltpu.VMEM(couple.shape, BF16),
            *[pltpu.VMEM(n, BF16) for n in sizes],
            pltpu.SemaphoreType.DMA((4,)),
        ],
        limit=TRANSFORM_LIMIT,
        flops=MEDIUM if awaited else 1000,
    )
    return result[0], (result[1:] if build else tables)


def own_plane():
    return WINDOW_START + lax.axis_index("rad")


def paired_plane():
    return WINDOW_START + 1 - lax.axis_index("rad")


def inverse_divisor(row0, modes_m, modes_k, plane):
    m = lax.broadcasted_iota(jnp.int32, (BAND, 1), 0) + row0
    k = lax.broadcasted_iota(jnp.int32, (1, modes_k), 1)
    fm = jnp.where(m <= modes_m // 2, m, m - modes_m // 2).astype(F32) / F32(modes_m // 2)
    fk = jnp.where(k <= modes_k // 2, k, k - modes_k // 2).astype(F32) / F32(modes_k // 2)
    radius = (jnp.full((1, 1), plane, jnp.int32).astype(F32) + F32(0.5)) / F32(RADIAL_ALL)
    turning = F32(VISC_TURN) * fm * fm / (radius * radius)
    return F32(1.0) / (F32(1.0) + F32(VISC_AXIAL) * fk * fk + turning)


def add_tile(acc, n, value):
    value = sum(value[r : r + 8] for r in range(0, value.shape[0], 8))
    acc[n] += sum(value[:, k : k + 128] for k in range(0, value.shape[1], 128))


def local_kernel(counts, last, paired, advect, *refs):
    take = taker(refs)
    v, vb, recv = (take(n) for n in counts[:3])
    two, anal_m = take(), take()
    if last:
        u0, out_b = take(counts[3]), []
        out, scale, gram, spec, acc = take(5)
        acc[...] = jnp.zeros_like(acc)
    else:
        out, out_b, spec = take(), take(counts[3]), take()
    chans, modes_m, modes_k = two.shape
    half = modes_k // 2
    for c in range(chans):
        spec[c] = jnp.dot(anal_m[...], two[c], preferred_element_type=F32)
    wave = lax.broadcasted_iota(jnp.int32, (1, half), 1).astype(F32) * advect[0]

    def step(lo, shift):
        at = pl.ds(pl.multiple_of(shift + lo, BAND), BAND)
        inv = inverse_divisor(shift + lo, modes_m, modes_k, own_plane())
        if last:
            scale[at, :] = inv * F32(RADIAL_GAIN)
            if paired:
                mate = inverse_divisor(shift + lo, modes_m, modes_k, paired_plane()) * F32(RADIAL_GAIN**2)
        for c in range(chans):
            row = c * modes_m + lo
            own = read(v, row, shift)
            drift = jnp.concatenate([-wave * own[:, half:], wave * own[:, :half]], axis=1)
            mid = F32(-2.0 * RADIAL_GAIN) * read(vb, row, shift).astype(F32)
            total = own + spec[c, at, :] + drift + mid
            if last:
                x0 = read(u0, row, shift)
                if paired:
                    total += mate * x0
                for n, (a, b) in enumerate(((x0, x0), (x0, own), (own, own))):
                    add_tile(acc, n, a * b)
            value = total * inv - read(recv, row, shift).astype(F32)
            write([out], row, shift, value)
            if not last:
                write(out_b, row, shift, value)

    for lo, hi in segments(modes_m, [*v, *(u0 if last else out_b)]):
        for_bands(lo, hi, functools.partial(step, lo))

    if last:
        gram[...] = jnp.zeros_like(gram)
        for n in range(3):
            gram[n : n + 1, :] = jnp.sum(acc[n], axis=0, keepdims=True)


def local_first(advect, v, vb, recv, two, tables, sizes):
    chans, modes_m, modes_k = two.shape
    args = [advect, *v, *vb, *recv, two, tables[3]]
    part, *part_b = kernel_call(
        functools.partial(local_kernel, (len(v), len(vb), len(recv), len(sizes)), False, False),
        "local_first",
        args,
        [IN_SMEM] + [IN_VMEM] * (len(args) - 1),
        [pltpu.VMEM((chans * modes_m, modes_k), F32)] + [pltpu.VMEM((n, modes_k), BF16) for n in sizes],
        scratch=[pltpu.VMEM(two.shape, F32)],
    )
    return part, part_b


def local_last(advect, v, vb, recv, two, tables, u0, paired):
    chans, modes_m, modes_k = two.shape
    args = [advect, *v, *vb, *recv, two, tables[3], *u0]
    return kernel_call(
        functools.partial(local_kernel, (len(v), len(vb), len(recv), len(u0)), True, paired),
        "local_last",
        args,
        [IN_SMEM] + [IN_VMEM] * (len(args) - 1),
        [
            pltpu.VMEM((chans * modes_m, modes_k), F32),
            pltpu.VMEM((modes_m, modes_k), F32),
            pltpu.VMEM((8, 128), F32),
        ],
        scratch=[pltpu.VMEM(two.shape, F32), pltpu.VMEM((3, 8, 128), F32)],
    )


def added(sides, row, shift):
    return functools.reduce(lambda a, b: a + b, [read(s, row, shift).astype(F32) for s in sides])


def first_kernel(groups, count, part, *refs):
    take = taker(refs)
    sides = [take(groups) for _ in range(count)]
    out, out_b = take(), take(len(refs) - groups * count - 1)
    chans, (modes_m, modes_k) = len(out_b), out_b[0].shape

    def step(lo, shift):
        inv = inverse_divisor(shift + lo, modes_m, modes_k, own_plane()) * F32(RADIAL_GAIN)
        for c in range(chans):
            row = c * modes_m + lo
            value = read([part], row, shift) + added(sides, row, shift) * inv
            write([out], row, shift, value)
            write(out_b, row, shift, value)

    for lo, hi in segments(modes_m, sides[0]):
        for_bands(lo, hi, functools.partial(step, lo))


def first_image(part, sides, chans):
    rows, modes_k = part.shape
    args = [part, *(x for side in sides for x in side)]
    return kernel_call(
        functools.partial(first_kernel, len(sides[0]), len(sides)),
        "first_image",
        args,
        [IN_VMEM] * len(args),
        [pltpu.VMEM(part.shape, F32)] + [pltpu.VMEM((rows // chans, modes_k), BF16)] * chans,
        flops=LONG,
    )


def on_diagonal():
    rows, lanes = (lax.broadcasted_iota(jnp.int32, (8, 128), n) for n in (0, 1))
    return rows == lanes


def second_kernel(first, counts, done, scale, u1, part, before, *refs):
    take = taker(refs)
    u0, planes = take(counts[0]), take(counts[1])
    out, gram, acc = take(3)
    modes_m = scale.shape[0]
    acc[...] = jnp.zeros_like(acc)

    def step(row, shift):
        at = pl.ds(pl.multiple_of(shift + row % modes_m, BAND), BAND)
        near = added([[p] for p in planes], row - first, shift)
        x2 = read([part], row, shift) + near * scale[at, :]
        write([out], row - first, shift, x2)
        for n, x in enumerate((read(u0, row, shift), read([u1], row, shift), x2)):
            add_tile(acc, n, x * x2)

    end = first + out.shape[0]
    starts = {first, *starts_of(u0), *range(0, end, modes_m)}
    starts = [r for r in sorted(starts) if first <= r < end]
    for lo, hi in zip(starts, starts[1:] + [end]):
        for_bands(lo, hi, functools.partial(step, lo))

    rows = [jnp.sum(acc[n], axis=0, keepdims=True) for n in range(3)]
    total = before[...] + jnp.concatenate([jnp.zeros((3, 128), F32), *rows, jnp.zeros((2, 128), F32)], axis=0)
    if done:
        total = jnp.sum(total, axis=1, keepdims=True)
        total = jnp.sum(jnp.where(on_diagonal(), total, F32(0.0)), axis=0, keepdims=True)
    gram[...] = jnp.broadcast_to(total, gram.shape)


def second_image(first, scale, u0, u1, part, before, planes, slots=None):
    done = slots is not None
    tile = (slots, 128) if done else (8, 128)
    args = [scale, u1, part, before, *u0, *planes]
    return kernel_call(
        functools.partial(second_kernel, first, (len(u0), len(planes)), done),
        "second_image",
        args,
        [IN_VMEM] * len(args),
        [pltpu.VMEM(planes[0].shape, F32), pltpu.VMEM(tile, F32)],
        scratch=[pltpu.VMEM((3, 8, 128), F32)],
    )


def combine_kernel(cells, counts, grams, u1, *refs):
    take = taker(refs)
    u0, u2 = take(counts[0]), take(counts[1])
    out, hess_out, held, hess, sems = take(5)
    total, modes_k = out.shape
    g = jnp.sum(grams[...], axis=0, keepdims=True) * F32(1.0 / cells)
    g = jnp.sum(jnp.where(on_diagonal(), g, F32(0.0)), axis=1, keepdims=True)
    g = jnp.broadcast_to(g, (8, 128))
    g00, g01, g11, g02, g12, g22 = (g[n : n + 1, :] for n in range(6))
    per_g00 = F32(1.0) / g00
    h11 = g01 * per_g00
    q = g11 - h11 * g01
    per_q = F32(1.0) / q
    w0 = g02 - h11 * g01
    w1 = g12 - h11 * g11
    ww = g22 - F32(2.0) * h11 * g12 + h11 * h11 * g11
    h22 = (w1 - h11 * w0) * per_q
    ratio = w0 * per_g00
    square = (ww - w0 * ratio) * per_q - h22 * h22
    c2 = F32(1.0) / jnp.sqrt(q * square)
    c1 = -(h11 + h22) * c2
    c0 = (h11 * h22 - ratio) * c2
    c0, c1, c2 = (x[0, 0] for x in (c0, c1, c2))

    def copy_out(n):
        at = pl.ds(pl.multiple_of(n * CHUNK, CHUNK), CHUNK)
        return pltpu.make_async_copy(held.at[at], out.at[at], sems.at[n])

    def step(first, n):
        for r in range(0, CHUNK, BAND):
            row, shift = first + r, pl.multiple_of(n * CHUNK, CHUNK)
            value = c0 * read(u0, row, shift) + c1 * read([u1], row, shift)
            write([held], row, shift, value + c2 * read(u2, row, shift))
        copy_out(n + first // CHUNK).start()

    starts = sorted({*starts_of(u0), *starts_of(u2)})
    for first, end in zip(starts, starts[1:] + [total]):
        pl.loop(0, (end - first) // CHUNK)(functools.partial(step, first))
    n0, s = jnp.sqrt(g00), jnp.sqrt(q)
    for n, value in enumerate((n0, h11, s / n0, w0 / (s * n0), h22, jnp.sqrt(square))):
        hess[n] = value[0, 0]
    last = pltpu.make_async_copy(hess, hess_out, sems.at[total // CHUNK])
    last.start()
    pl.loop(0, total // CHUNK)(lambda n: copy_out(n).wait())
    last.wait()


def combine(cells, grams, u0, u1, u2):
    args = [grams, u1, *u0, *u2]
    return kernel_call(
        functools.partial(combine_kernel, cells, (len(u0), len(u2))),
        "combine",
        args,
        [IN_VMEM] * len(args),
        [jax.ShapeDtypeStruct(u1.shape, F32), jax.ShapeDtypeStruct((6,), F32)],
        out_specs=[IN_HBM, IN_HBM],
        scratch=[
            pltpu.VMEM(u1.shape, F32),
            pltpu.SMEM((6,), F32),
            pltpu.SemaphoreType.DMA((u1.shape[0] // CHUNK + 1,)),
        ],
    )


def shifted(value, axis, steps):
    count = lax.axis_size(axis)
    return lax.ppermute(value, axis, [(i, (i + steps) % count) for i in range(count)])


def neighbour_planes(value, axis):
    count = lax.axis_size(axis)
    if count == 2:
        return [lax.ppermute(value, axis, [(0, 1), (1, 0)])]
    up = [(i, i + 1) for i in range(count - 1)]
    return [lax.ppermute(value, axis, up), lax.ppermute(value, axis, [(b, a) for a, b in up])]


def on_device(start_vector, coupling, advect):
    _, chans, rows_here, modes_m, modes_k = start_vector.shape
    assert rows_here == 1
    rows = chans * modes_m
    start = start_vector.reshape(rows, modes_k)
    couple = coupling.reshape(chans, chans, modes_m, modes_k)
    devices = lax.axis_size("seg") * lax.axis_size("rad")
    cells = float(devices * start.size)
    paired = lax.axis_size("rad") == 2

    early = EARLY_ROWS
    sizes = (rows - LATE_ROWS, LATE_ROWS) if paired else (modes_m,) * chans

    u0, u0b, near_one, pieces = [], [], [], None
    for first, size, parts in ((0, early, 0), (early, rows - early, chans)):
        field, rounded, pieces = take_rows(start, first, size, u0b, parts)
        u0.append(field)
        u0b.append(rounded)
        near_one.append(neighbour_planes(rounded, "rad"))
    next_one = [shifted(x, "seg", -1) for x in pieces]
    two, tables = transform(pieces, couple, awaited=near_one[0])
    part, part_b = local_first(advect, u0, pieces, next_one, two, tables, sizes)
    if paired:
        near_two = [neighbour_planes(x, "rad") for x in part_b]
    u1, *u1b = first_image(part, list(zip(*near_one)), chans)
    if not paired:
        near_two = [neighbour_planes(x, "rad") for x in u1b]
    next_two = [shifted(x, "seg", -1) for x in u1b]
    two, _ = transform(u1b, couple, tables)
    part, scale, gram = local_last(advect, [u1], u1b, next_two, two, tables, u0, paired)
    u2, first = [], 0
    for size, planes in zip(sizes, near_two):
        slots = devices if first + size == rows else None
        field, gram = second_image(first, scale, u0, u1, part, gram, planes, slots)
        first += size
        u2.append(field)
    grams = lax.all_to_all(gram, ("rad", "seg"), 0, 0)
    basis, hess = combine(cells, grams, u0, u1, u2)
    return basis.reshape(start_vector.shape), hess


def solution(mesh):
    return jax.shard_map(
        on_device,
        mesh=mesh,
        in_specs=(
            P("seg", None, "rad", None, None),
            P("seg", None, None, "rad", None, None),
            P("rad"),
        ),
        out_specs=(P("seg", None, "rad", None, None), P()),
        check_vma=False,
    )
```

```python
import functools
import math

import jax
import jax.numpy as jnp
from jax import lax
from jax.experimental import pallas as pl
from jax.experimental.pallas import tpu as pltpu
from jax.sharding import PartitionSpec as P

RADIAL_ALL = 256
WINDOW_START = 124
RADIAL_GAIN = 0.25
VISC_AXIAL = 4.0
VISC_TURN = 0.05

F32 = jnp.float32
BF16 = jnp.bfloat16
VMEM_LIMIT = 8 * 1024 * 1024
TRANSFORM_LIMIT = 22 * 1024 * 1024
ROWS = 128
COLS = 256
BAND = 16
LONG = 10**11
MEDIUM = 15 * 10**9
CHUNK = 128
EARLY_ROWS = 128
LATE_ROWS = 128

IN_SMEM = pl.BlockSpec(memory_space=pltpu.SMEM)
IN_VMEM = pl.BlockSpec(memory_space=pltpu.VMEM)
IN_HBM = pl.BlockSpec(memory_space=pltpu.HBM)


def kernel_call(body, name, args, in_specs, outs, out_specs=None, scratch=(), limit=VMEM_LIMIT, flops=1000):
    held = [
        a if s is IN_SMEM else pltpu.with_memory_space_constraint(a, s.memory_space)
        for a, s in zip(args, in_specs)
    ]
    more = {} if out_specs is None else {"out_specs": out_specs}
    return pl.pallas_call(
        body,
        out_shape=outs,
        in_specs=in_specs,
        scratch_shapes=list(scratch),
        compiler_params=pltpu.CompilerParams(vmem_limit_bytes=limit),
        cost_estimate=pl.CostEstimate(flops=flops, bytes_accessed=1000, transcendentals=0),
        name=name,
        **more,
    )(*held)


def sine_turns(y):
    x = y * F32(2.0 * math.pi)
    x2 = x * x
    acc = F32(1.0 / 6227020800.0)
    for c in (-1.0 / 39916800.0, 1.0 / 362880.0, -1.0 / 5040.0, 1.0 / 120.0, -1.0 / 6.0, 1.0):
        acc = acc * x2 + F32(c)
    return acc * x


def trig_block(row0, rows, cols, mode_axis, count, weighted):
    half = count // 2
    r = lax.broadcasted_iota(jnp.int32, (rows, cols), 0) + row0
    c = lax.broadcasted_iota(jnp.int32, (rows, cols), 1)
    mode, point = (r, c) if mode_axis == 0 else (c, r)
    is_cos = mode <= half
    freq = jnp.where(is_cos, mode, mode - half).astype(F32)
    phase = freq * point.astype(F32) - jnp.where(is_cos, F32(0.0), F32(count // 4))
    phase = phase - F32(count) * jnp.floor(phase * F32(1.0 / count))
    value = -sine_turns(F32(0.25) - jnp.abs(phase * F32(1.0 / count) - F32(0.5)))
    if weighted:
        edge = (mode == 0) | (mode == half)
        value = value * jnp.where(edge, F32(1.0 / count), F32(2.0 / count))
    return value.astype(BF16)


def fill_table(ref, mode_axis, weighted):
    count = ref.shape[0]

    @pl.loop(0, count // ROWS)
    def _(i):
        at = pl.multiple_of(i * ROWS, ROWS)
        ref[pl.ds(at, ROWS), :] = trig_block(at, ROWS, count, mode_axis, count, weighted)


def taker(refs):
    refs = list(refs)

    def take(count=None):
        if count is None:
            return refs.pop(0)
        out, refs[:count] = refs[:count], []
        return out

    return take


def segments(modes_m, groups):
    ends, total = {modes_m}, 0
    for group in groups:
        total += group.shape[0]
        ends.add(total % modes_m or modes_m)
    ends = sorted(ends)
    return list(zip([0] + ends[:-1], ends))


def starts_of(groups):
    return [sum(g.shape[0] for g in groups[:n]) for n in range(len(groups))]


def band(groups, row, shift):
    for group in groups:
        if row < group.shape[0]:
            return group, pl.ds(pl.multiple_of(shift + row, BAND), BAND)
        row -= group.shape[0]


def read(groups, row, shift):
    group, at = band(groups, row, shift)
    return group[at, :]


def write(groups, row, shift, value):
    group, at = band(groups, row, shift)
    group[at, :] = value.astype(group.dtype)


def for_bands(lo, hi, body):
    @pl.loop(0, (hi - lo) // BAND)
    def _(i):
        body(pl.multiple_of(i * BAND, BAND))


def take_kernel(first, v, *refs):
    take = taker(refs)
    early = [] if first == 0 else [take()]
    field, rounded = take(), take()
    pieces, sems = take(len(refs) - len(early) - 3), take()
    count = field.shape[0]
    copies = []
    for n, r in enumerate(range(0, count, ROWS)):
        copies.append(
            pltpu.make_async_copy(v.at[pl.ds(first + r, ROWS)], field.at[pl.ds(r, ROWS)], sems.at[n])
        )
        copies[n].start()

    def lay(row, value):
        for n, piece in enumerate(pieces):
            at = row - n * piece.shape[0]
            if 0 <= at < piece.shape[0]:
                piece[at : at + ROWS, :] = value

    for r in range(0, first, ROWS):
        lay(r, early[0][r : r + ROWS, :])
    for n, r in enumerate(range(0, count, ROWS)):
        copies[n].wait()
        value = field[r : r + ROWS, :].astype(BF16)
        rounded[r : r + ROWS, :] = value
        lay(first + r, value)


def take_rows(v, first, count, early=(), pieces=0):
    rows, modes_k = v.shape
    shapes = [pltpu.VMEM((count, modes_k), F32), pltpu.VMEM((count, modes_k), BF16)]
    field, rounded, *by_channel = kernel_call(
        functools.partial(take_kernel, first),
        "take_rows",
        [v, *early],
        [IN_HBM] + [IN_VMEM] * len(early),
        shapes + [pltpu.VMEM((rows // max(pieces, 1), modes_k), BF16)] * pieces,
        scratch=[pltpu.SemaphoreType.DMA((count // ROWS,))],
    )
    return field, rounded, by_channel


def transform_kernel(build, awaited, *refs):
    take = taker(refs)
    chans = len(refs) - awaited - (14 if build else 13)
    x = take(chans)
    take(awaited)
    couple_far = take()
    tables_far = None if build else take(3)
    out = take()
    if build:
        tables_far, anal_m = take(3), take()
    one, phys, mixed, couple, synth_k, synth_mt, anal_kt, sems = take(8)
    near = (synth_k, synth_mt, anal_kt)
    _, modes_m, modes_k = out.shape
    load = pltpu.make_async_copy(couple_far, couple, sems.at[3])
    ends = [(n, f) if build else (f, n) for n, f in zip(near, tables_far)]
    moves = [pltpu.make_async_copy(src, dst, sems.at[i]) for i, (src, dst) in enumerate(ends)]
    if not build:
        for move in moves[:2]:
            move.start()
    load.start()
    if not build:
        moves[2].start()

    def ready(i, mode_axis, weighted):
        if build:
            fill_table(near[i], mode_axis, weighted)
            moves[i].start()
        else:
            moves[i].wait()

    ready(0, 0, False)
    for c in range(chans):

        @pl.loop(0, modes_m // ROWS)
        def _(i):
            at = pl.ds(pl.multiple_of(i * ROWS, ROWS), ROWS)
            one[c, at, :] = jnp.dot(x[c][at, :], synth_k[...], preferred_element_type=F32).astype(BF16)

    ready(1, 1, False)
    load.wait()

    @pl.loop(0, modes_k // COLS)
    def _(z):
        zs = pl.ds(pl.multiple_of(z * COLS, COLS), COLS)
        for j in range(chans):
            phys[j] = jnp.dot(synth_mt[...], one[j, :, zs], preferred_element_type=F32)

        @pl.loop(0, modes_m // BAND)
        def _(i):
            ts = pl.ds(pl.multiple_of(i * BAND, BAND), BAND)
            parts = [phys[j, ts, :] for j in range(chans)]
            for c in range(chans):
                total = couple[c, 0, ts, zs].astype(F32) * parts[0]
                for j in range(1, chans):
                    total += couple[c, j, ts, zs].astype(F32) * parts[j]
                mixed[c, ts, zs] = total.astype(BF16)

    ready(2, 1, True)
    for c in range(chans):

        @pl.loop(0, modes_m // ROWS)
        def _(i):
            at = pl.ds(pl.multiple_of(i * ROWS, ROWS), ROWS)
            out[c, at, :] = jnp.dot(mixed[c, at, :], anal_kt[...], preferred_element_type=F32).astype(BF16)

    if build:
        fill_table(anal_m, 0, True)
        for move in moves:
            move.wait()


def transform(x, couple, tables=None, awaited=()):
    chans, _, modes_m, modes_k = couple.shape
    shape = (chans, modes_m, modes_k)
    sizes = [(modes_k, modes_k), (modes_m, modes_m), (modes_k, modes_k)]
    build = tables is None
    far = [] if build else list(tables[:3])
    outs, out_specs = [pltpu.VMEM(shape, BF16)], [IN_VMEM]
    if build:
        outs += [pltpu.HBM(n, BF16) for n in sizes] + [pltpu.VMEM((modes_m, modes_m), BF16)]
        out_specs += [IN_HBM] * 3 + [IN_VMEM]
    result = kernel_call(
        functools.partial(transform_kernel, build, len(awaited)),
        "transform",
        [*x, *awaited, couple, *far],
        [IN_VMEM] * (chans + len(awaited)) + [IN_HBM] * (1 + len(far)),
        outs,
        out_specs=out_specs,
        scratch=[
            pltpu.VMEM(shape, BF16),
            pltpu.VMEM((chans, modes_m, COLS), F32),
            pltpu.VMEM(shape, BF16),
            pltpu.VMEM(couple.shape, BF16),
            *[pltpu.VMEM(n, BF16) for n in sizes],
            pltpu.SemaphoreType.DMA((4,)),
        ],
        limit=TRANSFORM_LIMIT,
        flops=MEDIUM if awaited else 1000,
    )
    return result[0], (result[1:] if build else tables)


def own_plane():
    return WINDOW_START + lax.axis_index("rad")


def paired_plane():
    return WINDOW_START + 1 - lax.axis_index("rad")


def inverse_divisor(row0, modes_m, modes_k, plane):
    m = lax.broadcasted_iota(jnp.int32, (BAND, 1), 0) + row0
    k = lax.broadcasted_iota(jnp.int32, (1, modes_k), 1)
    fm = jnp.where(m <= modes_m // 2, m, m - modes_m // 2).astype(F32) / F32(modes_m // 2)
    fk = jnp.where(k <= modes_k // 2, k, k - modes_k // 2).astype(F32) / F32(modes_k // 2)
    radius = (jnp.full((1, 1), plane, jnp.int32).astype(F32) + F32(0.5)) / F32(RADIAL_ALL)
    turning = F32(VISC_TURN) * fm * fm / (radius * radius)
    return F32(1.0) / (F32(1.0) + F32(VISC_AXIAL) * fk * fk + turning)


def add_tile(acc, n, value):
    value = sum(value[r : r + 8] for r in range(0, value.shape[0], 8))
    acc[n] += sum(value[:, k : k + 128] for k in range(0, value.shape[1], 128))


def local_kernel(counts, last, paired, advect, *refs):
    take = taker(refs)
    v, vb, recv = (take(n) for n in counts[:3])
    two, anal_m = take(), take()
    if last:
        u0, out_b = take(counts[3]), []
        out, scale, gram, spec, acc = take(5)
        acc[...] = jnp.zeros_like(acc)
    else:
        out, out_b, spec = take(), take(counts[3]), take()
    chans, modes_m, modes_k = two.shape
    half = modes_k // 2
    for c in range(chans):
        spec[c] = jnp.dot(anal_m[...], two[c], preferred_element_type=F32)
    wave = lax.broadcasted_iota(jnp.int32, (1, half), 1).astype(F32) * advect[0]

    def step(lo, shift):
        at = pl.ds(pl.multiple_of(shift + lo, BAND), BAND)
        inv = inverse_divisor(shift + lo, modes_m, modes_k, own_plane())
        if last:
            scale[at, :] = inv * F32(RADIAL_GAIN)
            if paired:
                mate = inverse_divisor(shift + lo, modes_m, modes_k, paired_plane()) * F32(RADIAL_GAIN**2)
        for c in range(chans):
            row = c * modes_m + lo
            own = read(v, row, shift)
            drift = jnp.concatenate([-wave * own[:, half:], wave * own[:, :half]], axis=1)
            mid = F32(-2.0 * RADIAL_GAIN) * read(vb, row, shift).astype(F32)
            total = own + spec[c, at, :] + drift + mid
            if last:
                x0 = read(u0, row, shift)
                if paired:
                    total += mate * x0
                for n, (a, b) in enumerate(((x0, x0), (x0, own), (own, own))):
                    add_tile(acc, n, a * b)
            value = total * inv - read(recv, row, shift).astype(F32)
            write([out], row, shift, value)
            if not last:
                write(out_b, row, shift, value)

    for lo, hi in segments(modes_m, [*v, *(u0 if last else out_b)]):
        for_bands(lo, hi, functools.partial(step, lo))

    if last:
        gram[...] = jnp.zeros_like(gram)
        for n in range(3):
            gram[n : n + 1, :] = jnp.sum(acc[n], axis=0, keepdims=True)


def local_first(advect, v, vb, recv, two, tables, sizes):
    chans, modes_m, modes_k = two.shape
    args = [advect, *v, *vb, *recv, two, tables[3]]
    part, *part_b = kernel_call(
        functools.partial(local_kernel, (len(v), len(vb), len(recv), len(sizes)), False, False),
        "local_first",
        args,
        [IN_SMEM] + [IN_VMEM] * (len(args) - 1),
        [pltpu.VMEM((chans * modes_m, modes_k), F32)] + [pltpu.VMEM((n, modes_k), BF16) for n in sizes],
        scratch=[pltpu.VMEM(two.shape, F32)],
    )
    return part, part_b


def local_last(advect, v, vb, recv, two, tables, u0, paired):
    chans, modes_m, modes_k = two.shape
    args = [advect, *v, *vb, *recv, two, tables[3], *u0]
    return kernel_call(
        functools.partial(local_kernel, (len(v), len(vb), len(recv), len(u0)), True, paired),
        "local_last",
        args,
        [IN_SMEM] + [IN_VMEM] * (len(args) - 1),
        [
            pltpu.VMEM((chans * modes_m, modes_k), F32),
            pltpu.VMEM((modes_m, modes_k), F32),
            pltpu.VMEM((8, 128), F32),
        ],
        scratch=[pltpu.VMEM(two.shape, F32), pltpu.VMEM((3, 8, 128), F32)],
    )


def added(sides, row, shift):
    return functools.reduce(lambda a, b: a + b, [read(s, row, shift).astype(F32) for s in sides])


def first_kernel(groups, count, part, *refs):
    take = taker(refs)
    sides = [take(groups) for _ in range(count)]
    out, out_b = take(), take(len(refs) - groups * count - 1)
    chans, (modes_m, modes_k) = len(out_b), out_b[0].shape

    def step(lo, shift):
        inv = inverse_divisor(shift + lo, modes_m, modes_k, own_plane()) * F32(RADIAL_GAIN)
        for c in range(chans):
            row = c * modes_m + lo
            value = read([part], row, shift) + added(sides, row, shift) * inv
            write([out], row, shift, value)
            write(out_b, row, shift, value)

    for lo, hi in segments(modes_m, sides[0]):
        for_bands(lo, hi, functools.partial(step, lo))


def first_image(part, sides, chans):
    rows, modes_k = part.shape
    args = [part, *(x for side in sides for x in side)]
    return kernel_call(
        functools.partial(first_kernel, len(sides[0]), len(sides)),
        "first_image",
        args,
        [IN_VMEM] * len(args),
        [pltpu.VMEM(part.shape, F32)] + [pltpu.VMEM((rows // chans, modes_k), BF16)] * chans,
        flops=LONG,
    )


def on_diagonal():
    rows, lanes = (lax.broadcasted_iota(jnp.int32, (8, 128), n) for n in (0, 1))
    return rows == lanes


def second_kernel(first, counts, done, scale, u1, part, before, *refs):
    take = taker(refs)
    u0, planes = take(counts[0]), take(counts[1])
    out, gram, acc = take(3)
    modes_m = scale.shape[0]
    acc[...] = jnp.zeros_like(acc)

    def step(row, shift):
        at = pl.ds(pl.multiple_of(shift + row % modes_m, BAND), BAND)
        near = added([[p] for p in planes], row - first, shift)
        x2 = read([part], row, shift) + near * scale[at, :]
        write([out], row - first, shift, x2)
        for n, x in enumerate((read(u0, row, shift), read([u1], row, shift), x2)):
            add_tile(acc, n, x * x2)

    end = first + out.shape[0]
    starts = {first, *starts_of(u0), *range(0, end, modes_m)}
    starts = [r for r in sorted(starts) if first <= r < end]
    for lo, hi in zip(starts, starts[1:] + [end]):
        for_bands(lo, hi, functools.partial(step, lo))

    rows = [jnp.sum(acc[n], axis=0, keepdims=True) for n in range(3)]
    total = before[...] + jnp.concatenate([jnp.zeros((3, 128), F32), *rows, jnp.zeros((2, 128), F32)], axis=0)
    if done:
        total = jnp.sum(total, axis=1, keepdims=True)
        total = jnp.sum(jnp.where(on_diagonal(), total, F32(0.0)), axis=0, keepdims=True)
    gram[...] = jnp.broadcast_to(total, gram.shape)


def second_image(first, scale, u0, u1, part, before, planes, slots=None):
    done = slots is not None
    tile = (slots, 128) if done else (8, 128)
    args = [scale, u1, part, before, *u0, *planes]
    return kernel_call(
        functools.partial(second_kernel, first, (len(u0), len(planes)), done),
        "second_image",
        args,
        [IN_VMEM] * len(args),
        [pltpu.VMEM(planes[0].shape, F32), pltpu.VMEM(tile, F32)],
        scratch=[pltpu.VMEM((3, 8, 128), F32)],
    )


def combine_kernel(cells, counts, grams, u1, *refs):
    take = taker(refs)
    u0, u2 = take(counts[0]), take(counts[1])
    out, hess_out, held, hess, sems = take(5)
    total, modes_k = out.shape
    g = jnp.sum(grams[...], axis=0, keepdims=True) * F32(1.0 / cells)
    g = jnp.sum(jnp.where(on_diagonal(), g, F32(0.0)), axis=1, keepdims=True)
    g = jnp.broadcast_to(g, (8, 128))
    g00, g01, g11, g02, g12, g22 = (g[n : n + 1, :] for n in range(6))
    per_g00 = F32(1.0) / g00
    h11 = g01 * per_g00
    q = g11 - h11 * g01
    per_q = F32(1.0) / q
    w0 = g02 - h11 * g01
    w1 = g12 - h11 * g11
    ww = g22 - F32(2.0) * h11 * g12 + h11 * h11 * g11
    h22 = (w1 - h11 * w0) * per_q
    ratio = w0 * per_g00
    square = (ww - w0 * ratio) * per_q - h22 * h22
    c2 = F32(1.0) / jnp.sqrt(q * square)
    c1 = -(h11 + h22) * c2
    c0 = (h11 * h22 - ratio) * c2
    c0, c1, c2 = (x[0, 0] for x in (c0, c1, c2))

    def copy_out(n):
        at = pl.ds(pl.multiple_of(n * CHUNK, CHUNK), CHUNK)
        return pltpu.make_async_copy(held.at[at], out.at[at], sems.at[n])

    def step(first, n):
        for r in range(0, CHUNK, BAND):
            row, shift = first + r, pl.multiple_of(n * CHUNK, CHUNK)
            value = c0 * read(u0, row, shift) + c1 * read([u1], row, shift)
            write([held], row, shift, value + c2 * read(u2, row, shift))
        copy_out(n + first // CHUNK).start()

    starts = sorted({*starts_of(u0), *starts_of(u2)})
    for first, end in zip(starts, starts[1:] + [total]):
        pl.loop(0, (end - first) // CHUNK)(functools.partial(step, first))
    n0, s = jnp.sqrt(g00), jnp.sqrt(q)
    for n, value in enumerate((n0, h11, s / n0, w0 / (s * n0), h22, jnp.sqrt(square))):
        hess[n] = value[0, 0]
    last = pltpu.make_async_copy(hess, hess_out, sems.at[total // CHUNK])
    last.start()
    pl.loop(0, total // CHUNK)(lambda n: copy_out(n).wait())
    last.wait()


def combine(cells, grams, u0, u1, u2):
    args = [grams, u1, *u0, *u2]
    return kernel_call(
        functools.partial(combine_kernel, cells, (len(u0), len(u2))),
        "combine",
        args,
        [IN_VMEM] * len(args),
        [jax.ShapeDtypeStruct(u1.shape, F32), jax.ShapeDtypeStruct((6,), F32)],
        out_specs=[IN_HBM, IN_HBM],
        scratch=[
            pltpu.VMEM(u1.shape, F32),
            pltpu.SMEM((6,), F32),
            pltpu.SemaphoreType.DMA((u1.shape[0] // CHUNK + 1,)),
        ],
    )


def shifted(value, axis, steps):
    count = lax.axis_size(axis)
    return lax.ppermute(value, axis, [(i, (i + steps) % count) for i in range(count)])


def neighbour_planes(value, axis):
    count = lax.axis_size(axis)
    if count == 2:
        return [lax.ppermute(value, axis, [(0, 1), (1, 0)])]
    up = [(i, i + 1) for i in range(count - 1)]
    return [lax.ppermute(value, axis, up), lax.ppermute(value, axis, [(b, a) for a, b in up])]


def on_device(start_vector, coupling, advect):
    _, chans, rows_here, modes_m, modes_k = start_vector.shape
    assert rows_here == 1
    rows = chans * modes_m
    start = start_vector.reshape(rows, modes_k)
    couple = coupling.reshape(chans, chans, modes_m, modes_k)
    devices = lax.axis_size("seg") * lax.axis_size("rad")
    cells = float(devices * start.size)
    paired = lax.axis_size("rad") == 2

    early = EARLY_ROWS
    sizes = (rows - LATE_ROWS, LATE_ROWS) if paired else (modes_m,) * chans

    u0, u0b, near_one, pieces = [], [], [], None
    for first, size, parts in ((0, early, 0), (early, rows - early, chans)):
        field, rounded, pieces = take_rows(start, first, size, u0b, parts)
        u0.append(field)
        u0b.append(rounded)
        near_one.append(neighbour_planes(rounded, "rad"))
    next_one = [shifted(x, "seg", -1) for x in pieces]
    two, tables = transform(pieces, couple, awaited=near_one[0])
    part, part_b = local_first(advect, u0, pieces, next_one, two, tables, sizes)
    if paired:
        near_two = [neighbour_planes(x, "rad") for x in part_b]
    u1, *u1b = first_image(part, list(zip(*near_one)), chans)
    if not paired:
        near_two = [neighbour_planes(x, "rad") for x in u1b]
    next_two = [shifted(x, "seg", -1) for x in u1b]
    two, _ = transform(u1b, couple, tables)
    part, scale, gram = local_last(advect, [u1], u1b, next_two, two, tables, u0, paired)
    u2, first = [], 0
    for size, planes in zip(sizes, near_two):
        slots = devices if first + size == rows else None
        field, gram = second_image(first, scale, u0, u1, part, gram, planes, slots)
        first += size
        u2.append(field)
    grams = lax.all_to_all(gram, ("rad", "seg"), 0, 0)
    basis, hess = combine(cells, grams, u0, u1, u2)
    return basis.reshape(start_vector.shape), hess


def solution(mesh):
    return jax.shard_map(
        on_device,
        mesh=mesh,
        in_specs=(
            P("seg", None, "rad", None, None),
            P("seg", None, None, "rad", None, None),
            P("rad"),
        ),
        out_specs=(P("seg", None, "rad", None, None), P()),
        check_vma=False,
    )
```

```python
import functools
import math

import jax
import jax.numpy as jnp
from jax import lax
from jax.experimental import pallas as pl
from jax.experimental.pallas import tpu as pltpu
from jax.sharding import PartitionSpec as P

RADIAL_ALL = 256
WINDOW_START = 124
RADIAL_GAIN = 0.25
VISC_AXIAL = 4.0
VISC_TURN = 0.05

F32 = jnp.float32
BF16 = jnp.bfloat16
VMEM_LIMIT = 8 * 1024 * 1024
TRANSFORM_LIMIT = 22 * 1024 * 1024
ROWS = 128
COLS = 256
BAND = 16
LONG = 10**11
MEDIUM = 15 * 10**9
CHUNK = 64
STEP = 64
EARLY_ROWS = 128
LATE_ROWS = 128

IN_SMEM = pl.BlockSpec(memory_space=pltpu.SMEM)
IN_VMEM = pl.BlockSpec(memory_space=pltpu.VMEM)
IN_HBM = pl.BlockSpec(memory_space=pltpu.HBM)


def kernel_call(body, name, args, in_specs, outs, out_specs=None, scratch=(), limit=VMEM_LIMIT, flops=1000):
    held = [
        a if s is IN_SMEM else pltpu.with_memory_space_constraint(a, s.memory_space)
        for a, s in zip(args, in_specs)
    ]
    more = {} if out_specs is None else {"out_specs": out_specs}
    return pl.pallas_call(
        body,
        out_shape=outs,
        in_specs=in_specs,
        scratch_shapes=list(scratch),
        compiler_params=pltpu.CompilerParams(vmem_limit_bytes=limit),
        cost_estimate=pl.CostEstimate(flops=flops, bytes_accessed=1000, transcendentals=0),
        name=name,
        **more,
    )(*held)


def sine_turns(y):
    x = y * F32(2.0 * math.pi)
    x2 = x * x
    acc = F32(1.0 / 6227020800.0)
    for c in (-1.0 / 39916800.0, 1.0 / 362880.0, -1.0 / 5040.0, 1.0 / 120.0, -1.0 / 6.0, 1.0):
        acc = acc * x2 + F32(c)
    return acc * x


def trig_block(row0, rows, cols, mode_axis, count, weighted):
    half = count // 2
    r = lax.broadcasted_iota(jnp.int32, (rows, cols), 0) + row0
    c = lax.broadcasted_iota(jnp.int32, (rows, cols), 1)
    mode, point = (r, c) if mode_axis == 0 else (c, r)
    is_cos = mode <= half
    freq = jnp.where(is_cos, mode, mode - half).astype(F32)
    phase = freq * point.astype(F32) - jnp.where(is_cos, F32(0.0), F32(count // 4))
    phase = phase - F32(count) * jnp.floor(phase * F32(1.0 / count))
    value = -sine_turns(F32(0.25) - jnp.abs(phase * F32(1.0 / count) - F32(0.5)))
    if weighted:
        edge = (mode == 0) | (mode == half)
        value = value * jnp.where(edge, F32(1.0 / count), F32(2.0 / count))
    return value.astype(BF16)


def fill_table(ref, mode_axis, weighted):
    count = ref.shape[0]

    @pl.loop(0, count // ROWS)
    def _(i):
        at = pl.multiple_of(i * ROWS, ROWS)
        ref[pl.ds(at, ROWS), :] = trig_block(at, ROWS, count, mode_axis, count, weighted)


def taker(refs):
    refs = list(refs)

    def take(count=None):
        if count is None:
            return refs.pop(0)
        out, refs[:count] = refs[:count], []
        return out

    return take


def segments(modes_m, groups):
    ends, total = {modes_m}, 0
    for group in groups:
        total += group.shape[0]
        ends.add(total % modes_m or modes_m)
    ends = sorted(ends)
    return list(zip([0] + ends[:-1], ends))


def starts_of(groups):
    return [sum(g.shape[0] for g in groups[:n]) for n in range(len(groups))]


def band(groups, row, shift):
    for group in groups:
        if row < group.shape[0]:
            return group, pl.ds(pl.multiple_of(shift + row, BAND), BAND)
        row -= group.shape[0]


def read(groups, row, shift):
    group, at = band(groups, row, shift)
    return group[at, :]


def write(groups, row, shift, value):
    group, at = band(groups, row, shift)
    group[at, :] = value.astype(group.dtype)


def for_bands(lo, hi, body):
    @pl.loop(0, (hi - lo) // BAND)
    def _(i):
        body(pl.multiple_of(i * BAND, BAND))


def take_kernel(first, v, *refs):
    take = taker(refs)
    early = [] if first == 0 else [take()]
    field, rounded = take(), take()
    pieces, sems = take(len(refs) - len(early) - 3), take()
    count = field.shape[0]
    copies = []
    for n, r in enumerate(range(0, count, ROWS)):
        copies.append(
            pltpu.make_async_copy(v.at[pl.ds(first + r, ROWS)], field.at[pl.ds(r, ROWS)], sems.at[n])
        )
        copies[n].start()

    def lay(row, value):
        for n, piece in enumerate(pieces):
            at = row - n * piece.shape[0]
            if 0 <= at < piece.shape[0]:
                piece[at : at + ROWS, :] = value

    for r in range(0, first, ROWS):
        lay(r, early[0][r : r + ROWS, :])
    for n, r in enumerate(range(0, count, ROWS)):
        copies[n].wait()
        value = field[r : r + ROWS, :].astype(BF16)
        rounded[r : r + ROWS, :] = value
        lay(first + r, value)


def take_rows(v, first, count, early=(), pieces=0):
    rows, modes_k = v.shape
    shapes = [pltpu.VMEM((count, modes_k), F32), pltpu.VMEM((count, modes_k), BF16)]
    field, rounded, *by_channel = kernel_call(
        functools.partial(take_kernel, first),
        "take_rows",
        [v, *early],
        [IN_HBM] + [IN_VMEM] * len(early),
        shapes + [pltpu.VMEM((rows // max(pieces, 1), modes_k), BF16)] * pieces,
        scratch=[pltpu.SemaphoreType.DMA((count // ROWS,))],
    )
    return field, rounded, by_channel


def transform_kernel(build, awaited, *refs):
    take = taker(refs)
    chans = len(refs) - awaited - (14 if build else 13)
    x = take(chans)
    take(awaited)
    couple_far = take()
    tables_far = None if build else take(3)
    out = take()
    if build:
        tables_far, anal_m = take(3), take()
    one, phys, mixed, couple, synth_k, synth_mt, anal_kt, sems = take(8)
    near = (synth_k, synth_mt, anal_kt)
    _, modes_m, modes_k = out.shape
    load = pltpu.make_async_copy(couple_far, couple, sems.at[3])
    ends = [(n, f) if build else (f, n) for n, f in zip(near, tables_far)]
    moves = [pltpu.make_async_copy(src, dst, sems.at[i]) for i, (src, dst) in enumerate(ends)]
    if not build:
        for move in moves[:2]:
            move.start()
    load.start()
    if not build:
        moves[2].start()

    def ready(i, mode_axis, weighted):
        if build:
            fill_table(near[i], mode_axis, weighted)
            moves[i].start()
        else:
            moves[i].wait()

    ready(0, 0, False)
    for c in range(chans):

        @pl.loop(0, modes_m // ROWS)
        def _(i):
            at = pl.ds(pl.multiple_of(i * ROWS, ROWS), ROWS)
            one[c, at, :] = jnp.dot(x[c][at, :], synth_k[...], preferred_element_type=F32).astype(BF16)

    ready(1, 1, False)
    load.wait()

    @pl.loop(0, modes_k // COLS)
    def _(z):
        zs = pl.ds(pl.multiple_of(z * COLS, COLS), COLS)
        for j in range(chans):
            phys[j] = jnp.dot(synth_mt[...], one[j, :, zs], preferred_element_type=F32)

        @pl.loop(0, modes_m // BAND)
        def _(i):
            ts = pl.ds(pl.multiple_of(i * BAND, BAND), BAND)
            parts = [phys[j, ts, :] for j in range(chans)]
            for c in range(chans):
                total = couple[c, 0, ts, zs].astype(F32) * parts[0]
                for j in range(1, chans):
                    total += couple[c, j, ts, zs].astype(F32) * parts[j]
                mixed[c, ts, zs] = total.astype(BF16)

    ready(2, 1, True)
    for c in range(chans):

        @pl.loop(0, modes_m // ROWS)
        def _(i):
            at = pl.ds(pl.multiple_of(i * ROWS, ROWS), ROWS)
            out[c, at, :] = jnp.dot(mixed[c, at, :], anal_kt[...], preferred_element_type=F32).astype(BF16)

    if build:
        fill_table(anal_m, 0, True)
        for move in moves:
            move.wait()


def transform(x, couple, tables=None, awaited=()):
    chans, _, modes_m, modes_k = couple.shape
    shape = (chans, modes_m, modes_k)
    sizes = [(modes_k, modes_k), (modes_m, modes_m), (modes_k, modes_k)]
    build = tables is None
    far = [] if build else list(tables[:3])
    outs, out_specs = [pltpu.VMEM(shape, BF16)], [IN_VMEM]
    if build:
        outs += [pltpu.HBM(n, BF16) for n in sizes] + [pltpu.VMEM((modes_m, modes_m), BF16)]
        out_specs += [IN_HBM] * 3 + [IN_VMEM]
    result = kernel_call(
        functools.partial(transform_kernel, build, len(awaited)),
        "transform",
        [*x, *awaited, couple, *far],
        [IN_VMEM] * (chans + len(awaited)) + [IN_HBM] * (1 + len(far)),
        outs,
        out_specs=out_specs,
        scratch=[
            pltpu.VMEM(shape, BF16),
            pltpu.VMEM((chans, modes_m, COLS), F32),
            pltpu.VMEM(shape, BF16),
            pltpu.VMEM(couple.shape, BF16),
            *[pltpu.VMEM(n, BF16) for n in sizes],
            pltpu.SemaphoreType.DMA((4,)),
        ],
        limit=TRANSFORM_LIMIT,
        flops=MEDIUM if awaited else 1000,
    )
    return result[0], (result[1:] if build else tables)


def own_plane():
    return WINDOW_START + lax.axis_index("rad")


def paired_plane():
    return WINDOW_START + 1 - lax.axis_index("rad")


def inverse_divisor(row0, modes_m, modes_k, plane):
    m = lax.broadcasted_iota(jnp.int32, (BAND, 1), 0) + row0
    k = lax.broadcasted_iota(jnp.int32, (1, modes_k), 1)
    fm = jnp.where(m <= modes_m // 2, m, m - modes_m // 2).astype(F32) / F32(modes_m // 2)
    fk = jnp.where(k <= modes_k // 2, k, k - modes_k // 2).astype(F32) / F32(modes_k // 2)
    radius = (jnp.full((1, 1), plane, jnp.int32).astype(F32) + F32(0.5)) / F32(RADIAL_ALL)
    turning = F32(VISC_TURN) * fm * fm / (radius * radius)
    return F32(1.0) / (F32(1.0) + F32(VISC_AXIAL) * fk * fk + turning)


def one_tile(value):
    value = sum(value[r : r + 8] for r in range(0, value.shape[0], 8))
    return sum(value[:, k : k + 128] for k in range(0, value.shape[1], 128))


def add_tile(acc, n, value):
    acc[n] += one_tile(value)


def local_kernel(counts, last, paired, advect, *refs):
    take = taker(refs)
    v, vb, recv = (take(n) for n in counts[:3])
    two, anal_m = take(), take()
    if last:
        u0, out_b = take(counts[3]), []
        out, scale, gram, spec, acc = take(5)
        acc[...] = jnp.zeros_like(acc)
    else:
        out, out_b, spec = take(), take(counts[3]), take()
    chans, modes_m, modes_k = two.shape
    half = modes_k // 2
    for c in range(chans):
        spec[c] = jnp.dot(anal_m[...], two[c], preferred_element_type=F32)
    wave = lax.broadcasted_iota(jnp.int32, (1, half), 1).astype(F32) * advect[0]

    def step(lo, shift):
        at = pl.ds(pl.multiple_of(shift + lo, BAND), BAND)
        inv = inverse_divisor(shift + lo, modes_m, modes_k, own_plane())
        if last:
            scale[at, :] = inv * F32(RADIAL_GAIN)
            if paired:
                mate = inverse_divisor(shift + lo, modes_m, modes_k, paired_plane()) * F32(RADIAL_GAIN**2)
        for c in range(chans):
            row = c * modes_m + lo
            own = read(v, row, shift)
            drift = jnp.concatenate([-wave * own[:, half:], wave * own[:, :half]], axis=1)
            mid = F32(-2.0 * RADIAL_GAIN) * read(vb, row, shift).astype(F32)
            total = own + spec[c, at, :] + drift + mid
            if last:
                x0 = read(u0, row, shift)
                if paired:
                    total += mate * x0
                for n, (a, b) in enumerate(((x0, x0), (x0, own), (own, own))):
                    add_tile(acc, n, a * b)
            value = total * inv - read(recv, row, shift).astype(F32)
            write([out], row, shift, value)
            if not last:
                write(out_b, row, shift, value)

    for lo, hi in segments(modes_m, [*v, *(u0 if last else out_b)]):
        for_bands(lo, hi, functools.partial(step, lo))

    if last:
        gram[...] = jnp.zeros_like(gram)
        for n in range(3):
            gram[n : n + 1, :] = jnp.sum(acc[n], axis=0, keepdims=True)


def local_first(advect, v, vb, recv, two, tables, sizes):
    chans, modes_m, modes_k = two.shape
    args = [advect, *v, *vb, *recv, two, tables[3]]
    part, *part_b = kernel_call(
        functools.partial(local_kernel, (len(v), len(vb), len(recv), len(sizes)), False, False),
        "local_first",
        args,
        [IN_SMEM] + [IN_VMEM] * (len(args) - 1),
        [pltpu.VMEM((chans * modes_m, modes_k), F32)] + [pltpu.VMEM((n, modes_k), BF16) for n in sizes],
        scratch=[pltpu.VMEM(two.shape, F32)],
    )
    return part, part_b


def local_last(advect, v, vb, recv, two, tables, u0, paired):
    chans, modes_m, modes_k = two.shape
    args = [advect, *v, *vb, *recv, two, tables[3], *u0]
    return kernel_call(
        functools.partial(local_kernel, (len(v), len(vb), len(recv), len(u0)), True, paired),
        "local_last",
        args,
        [IN_SMEM] + [IN_VMEM] * (len(args) - 1),
        [
            pltpu.VMEM((chans * modes_m, modes_k), F32),
            pltpu.VMEM((modes_m, modes_k), F32),
            pltpu.VMEM((8, 128), F32),
        ],
        scratch=[pltpu.VMEM(two.shape, F32), pltpu.VMEM((3, 8, 128), F32)],
    )


def added(sides, row, shift):
    return functools.reduce(lambda a, b: a + b, [read(s, row, shift).astype(F32) for s in sides])


def first_kernel(groups, count, part, *refs):
    take = taker(refs)
    sides = [take(groups) for _ in range(count)]
    out, out_b = take(), take(len(refs) - groups * count - 1)
    chans, (modes_m, modes_k) = len(out_b), out_b[0].shape

    def step(lo, shift):
        inv = inverse_divisor(shift + lo, modes_m, modes_k, own_plane()) * F32(RADIAL_GAIN)
        for c in range(chans):
            row = c * modes_m + lo
            value = read([part], row, shift) + added(sides, row, shift) * inv
            write([out], row, shift, value)
            write(out_b, row, shift, value)

    for lo, hi in segments(modes_m, sides[0]):
        for_bands(lo, hi, functools.partial(step, lo))


def first_image(part, sides, chans):
    rows, modes_k = part.shape
    args = [part, *(x for side in sides for x in side)]
    return kernel_call(
        functools.partial(first_kernel, len(sides[0]), len(sides)),
        "first_image",
        args,
        [IN_VMEM] * len(args),
        [pltpu.VMEM(part.shape, F32)] + [pltpu.VMEM((rows // chans, modes_k), BF16)] * chans,
        flops=LONG,
    )


def on_diagonal():
    rows, lanes = (lax.broadcasted_iota(jnp.int32, (8, 128), n) for n in (0, 1))
    return rows == lanes


def second_kernel(first, counts, done, scale, u1, part, before, *refs):
    take = taker(refs)
    u0, planes = take(counts[0]), take(counts[1])
    out, gram, acc = take(3)
    modes_m = scale.shape[0]
    acc[...] = jnp.zeros_like(acc)

    def step(start, i):
        shift = pl.multiple_of(i * STEP, STEP)
        totals = [None] * 3
        for row in range(start, start + STEP, BAND):
            at = pl.ds(pl.multiple_of(shift + row % modes_m, BAND), BAND)
            near = added([[p] for p in planes], row - first, shift)
            x2 = read([part], row, shift) + near * scale[at, :]
            write([out], row - first, shift, x2)
            for n, x in enumerate((read(u0, row, shift), read([u1], row, shift), x2)):
                value = one_tile(x * x2)
                totals[n] = value if totals[n] is None else totals[n] + value
        for n in range(3):
            acc[n] += totals[n]

    end = first + out.shape[0]
    starts = {first, *starts_of(u0), *range(0, end, modes_m)}
    starts = [r for r in sorted(starts) if first <= r < end]
    for lo, hi in zip(starts, starts[1:] + [end]):
        pl.loop(0, (hi - lo) // STEP)(functools.partial(step, lo))

    rows = [jnp.sum(acc[n], axis=0, keepdims=True) for n in range(3)]
    total = before[...] + jnp.concatenate([jnp.zeros((3, 128), F32), *rows, jnp.zeros((2, 128), F32)], axis=0)
    if done:
        total = jnp.sum(total, axis=1, keepdims=True)
        total = jnp.sum(jnp.where(on_diagonal(), total, F32(0.0)), axis=0, keepdims=True)
    gram[...] = jnp.broadcast_to(total, gram.shape)


def second_image(first, scale, u0, u1, part, before, planes, slots=None):
    done = slots is not None
    tile = (slots, 128) if done else (8, 128)
    args = [scale, u1, part, before, *u0, *planes]
    return kernel_call(
        functools.partial(second_kernel, first, (len(u0), len(planes)), done),
        "second_image",
        args,
        [IN_VMEM] * len(args),
        [pltpu.VMEM(planes[0].shape, F32), pltpu.VMEM(tile, F32)],
        scratch=[pltpu.VMEM((3, 8, 128), F32)],
    )


def combine_kernel(cells, counts, grams, u1, *refs):
    take = taker(refs)
    u0, u2 = take(counts[0]), take(counts[1])
    out, hess_out, held, hess, sems = take(5)
    total, modes_k = out.shape
    g = jnp.sum(grams[...], axis=0, keepdims=True) * F32(1.0 / cells)
    g = jnp.sum(jnp.where(on_diagonal(), g, F32(0.0)), axis=1, keepdims=True)
    g = jnp.broadcast_to(g, (8, 128))
    g00, g01, g11, g02, g12, g22 = (g[n : n + 1, :] for n in range(6))
    per_g00 = F32(1.0) / g00
    h11 = g01 * per_g00
    q = g11 - h11 * g01
    per_q = F32(1.0) / q
    w0 = g02 - h11 * g01
    w1 = g12 - h11 * g11
    ww = g22 - F32(2.0) * h11 * g12 + h11 * h11 * g11
    h22 = (w1 - h11 * w0) * per_q
    ratio = w0 * per_g00
    square = (ww - w0 * ratio) * per_q - h22 * h22
    c2 = F32(1.0) / jnp.sqrt(q * square)
    c1 = -(h11 + h22) * c2
    c0 = (h11 * h22 - ratio) * c2
    wide = [jnp.concatenate([x] * (modes_k // 128), axis=1) for x in (c0, c1, c2)]

    def copy_out(n):
        at = pl.ds(pl.multiple_of(n * CHUNK, CHUNK), CHUNK)
        return pltpu.make_async_copy(held.at[at], out.at[at], sems.at[n])

    def step(first, n):
        for r in range(0, CHUNK, BAND):
            row, shift = first + r, pl.multiple_of(n * CHUNK, CHUNK)
            value = wide[0] * read(u0, row, shift) + wide[1] * read([u1], row, shift)
            write([held], row, shift, value + wide[2] * read(u2, row, shift))
        copy_out(n + first // CHUNK).start()

    starts = sorted({*starts_of(u0), *starts_of(u2)})
    for first, end in zip(starts, starts[1:] + [total]):
        pl.loop(0, (end - first) // CHUNK)(functools.partial(step, first))
    n0, s = jnp.sqrt(g00), jnp.sqrt(q)
    for n, value in enumerate((n0, h11, s / n0, w0 / (s * n0), h22, jnp.sqrt(square))):
        hess[n] = value[0, 0]
    last = pltpu.make_async_copy(hess, hess_out, sems.at[total // CHUNK])
    last.start()
    pl.loop(0, total // CHUNK)(lambda n: copy_out(n).wait())
    last.wait()


def combine(cells, grams, u0, u1, u2):
    args = [grams, u1, *u0, *u2]
    return kernel_call(
        functools.partial(combine_kernel, cells, (len(u0), len(u2))),
        "combine",
        args,
        [IN_VMEM] * len(args),
        [jax.ShapeDtypeStruct(u1.shape, F32), jax.ShapeDtypeStruct((6,), F32)],
        out_specs=[IN_HBM, IN_HBM],
        scratch=[
            pltpu.VMEM(u1.shape, F32),
            pltpu.SMEM((6,), F32),
            pltpu.SemaphoreType.DMA((u1.shape[0] // CHUNK + 1,)),
        ],
    )


def shifted(value, axis, steps):
    count = lax.axis_size(axis)
    return lax.ppermute(value, axis, [(i, (i + steps) % count) for i in range(count)])


def neighbour_planes(value, axis):
    count = lax.axis_size(axis)
    if count == 2:
        return [lax.ppermute(value, axis, [(0, 1), (1, 0)])]
    up = [(i, i + 1) for i in range(count - 1)]
    return [lax.ppermute(value, axis, up), lax.ppermute(value, axis, [(b, a) for a, b in up])]


def on_device(start_vector, coupling, advect):
    _, chans, rows_here, modes_m, modes_k = start_vector.shape
    assert rows_here == 1
    rows = chans * modes_m
    start = start_vector.reshape(rows, modes_k)
    couple = coupling.reshape(chans, chans, modes_m, modes_k)
    devices = lax.axis_size("seg") * lax.axis_size("rad")
    cells = float(devices * start.size)
    paired = lax.axis_size("rad") == 2

    early = EARLY_ROWS
    sizes = (rows - LATE_ROWS, LATE_ROWS) if paired else (modes_m,) * chans

    u0, u0b, near_one, pieces = [], [], [], None
    for first, size, parts in ((0, early, 0), (early, rows - early, chans)):
        field, rounded, pieces = take_rows(start, first, size, u0b, parts)
        u0.append(field)
        u0b.append(rounded)
        near_one.append(neighbour_planes(rounded, "rad"))
    next_one = [shifted(x, "seg", -1) for x in pieces]
    two, tables = transform(pieces, couple, awaited=near_one[0])
    part, part_b = local_first(advect, u0, pieces, next_one, two, tables, sizes)
    if paired:
        near_two = [neighbour_planes(x, "rad") for x in part_b]
    u1, *u1b = first_image(part, list(zip(*near_one)), chans)
    if not paired:
        near_two = [neighbour_planes(x, "rad") for x in u1b]
    next_two = [shifted(x, "seg", -1) for x in u1b]
    two, _ = transform(u1b, couple, tables)
    part, scale, gram = local_last(advect, [u1], u1b, next_two, two, tables, u0, paired)
    u2, first = [], 0
    for size, planes in zip(sizes, near_two):
        slots = devices if first + size == rows else None
        field, gram = second_image(first, scale, u0, u1, part, gram, planes, slots)
        first += size
        u2.append(field)
    grams = lax.all_to_all(gram, ("rad", "seg"), 0, 0)
    basis, hess = combine(cells, grams, u0, u1, u2)
    return basis.reshape(start_vector.shape), hess


def solution(mesh):
    return jax.shard_map(
        on_device,
        mesh=mesh,
        in_specs=(
            P("seg", None, "rad", None, None),
            P("seg", None, None, "rad", None, None),
            P("rad"),
        ),
        out_specs=(P("seg", None, "rad", None, None), P()),
        check_vma=False,
    )
```

```python
import functools
import math

import jax
import jax.numpy as jnp
from jax import lax
from jax.experimental import pallas as pl
from jax.experimental.pallas import tpu as pltpu
from jax.sharding import PartitionSpec as P

RADIAL_ALL = 256
WINDOW_START = 124
RADIAL_GAIN = 0.25
VISC_AXIAL = 4.0
VISC_TURN = 0.05

F32 = jnp.float32
BF16 = jnp.bfloat16
VMEM_LIMIT = 8 * 1024 * 1024
TRANSFORM_LIMIT = 22 * 1024 * 1024
ROWS = 128
COLS = 256
BAND = 16
LONG = 10**11
MEDIUM = 15 * 10**9
CHUNK = 64
STEP = 64
EARLY_ROWS = 128
LATE_ROWS = 64

IN_SMEM = pl.BlockSpec(memory_space=pltpu.SMEM)
IN_VMEM = pl.BlockSpec(memory_space=pltpu.VMEM)
IN_HBM = pl.BlockSpec(memory_space=pltpu.HBM)


def kernel_call(body, name, args, in_specs, outs, out_specs=None, scratch=(), limit=VMEM_LIMIT, flops=1000):
    held = [
        a if s is IN_SMEM else pltpu.with_memory_space_constraint(a, s.memory_space)
        for a, s in zip(args, in_specs)
    ]
    more = {} if out_specs is None else {"out_specs": out_specs}
    return pl.pallas_call(
        body,
        out_shape=outs,
        in_specs=in_specs,
        scratch_shapes=list(scratch),
        compiler_params=pltpu.CompilerParams(vmem_limit_bytes=limit),
        cost_estimate=pl.CostEstimate(flops=flops, bytes_accessed=1000, transcendentals=0),
        name=name,
        **more,
    )(*held)


def sine_turns(y):
    x = y * F32(2.0 * math.pi)
    x2 = x * x
    acc = F32(1.0 / 6227020800.0)
    for c in (-1.0 / 39916800.0, 1.0 / 362880.0, -1.0 / 5040.0, 1.0 / 120.0, -1.0 / 6.0, 1.0):
        acc = acc * x2 + F32(c)
    return acc * x


def trig_block(row0, rows, cols, mode_axis, count, weighted):
    half = count // 2
    r = lax.broadcasted_iota(jnp.int32, (rows, cols), 0) + row0
    c = lax.broadcasted_iota(jnp.int32, (rows, cols), 1)
    mode, point = (r, c) if mode_axis == 0 else (c, r)
    is_cos = mode <= half
    freq = jnp.where(is_cos, mode, mode - half).astype(F32)
    phase = freq * point.astype(F32) - jnp.where(is_cos, F32(0.0), F32(count // 4))
    phase = phase - F32(count) * jnp.floor(phase * F32(1.0 / count))
    value = -sine_turns(F32(0.25) - jnp.abs(phase * F32(1.0 / count) - F32(0.5)))
    if weighted:
        edge = (mode == 0) | (mode == half)
        value = value * jnp.where(edge, F32(1.0 / count), F32(2.0 / count))
    return value.astype(BF16)


def fill_table(ref, mode_axis, weighted):
    count = ref.shape[0]

    @pl.loop(0, count // ROWS)
    def _(i):
        at = pl.multiple_of(i * ROWS, ROWS)
        ref[pl.ds(at, ROWS), :] = trig_block(at, ROWS, count, mode_axis, count, weighted)


def taker(refs):
    refs = list(refs)

    def take(count=None):
        if count is None:
            return refs.pop(0)
        out, refs[:count] = refs[:count], []
        return out

    return take


def segments(modes_m, groups):
    ends, total = {modes_m}, 0
    for group in groups:
        total += group.shape[0]
        ends.add(total % modes_m or modes_m)
    ends = sorted(ends)
    return list(zip([0] + ends[:-1], ends))


def starts_of(groups):
    return [sum(g.shape[0] for g in groups[:n]) for n in range(len(groups))]


def band(groups, row, shift):
    for group in groups:
        if row < group.shape[0]:
            return group, pl.ds(pl.multiple_of(shift + row, BAND), BAND)
        row -= group.shape[0]


def read(groups, row, shift):
    group, at = band(groups, row, shift)
    return group[at, :]


def write(groups, row, shift, value):
    group, at = band(groups, row, shift)
    group[at, :] = value.astype(group.dtype)


def for_bands(lo, hi, body):
    @pl.loop(0, (hi - lo) // BAND)
    def _(i):
        body(pl.multiple_of(i * BAND, BAND))


def take_kernel(first, v, *refs):
    take = taker(refs)
    early = [] if first == 0 else [take()]
    field, rounded = take(), take()
    pieces, sems = take(len(refs) - len(early) - 3), take()
    count = field.shape[0]
    copies = []
    for n, r in enumerate(range(0, count, ROWS)):
        copies.append(
            pltpu.make_async_copy(v.at[pl.ds(first + r, ROWS)], field.at[pl.ds(r, ROWS)], sems.at[n])
        )
        copies[n].start()

    def lay(row, value):
        for n, piece in enumerate(pieces):
            at = row - n * piece.shape[0]
            if 0 <= at < piece.shape[0]:
                piece[at : at + ROWS, :] = value

    for r in range(0, first, ROWS):
        lay(r, early[0][r : r + ROWS, :])
    for n, r in enumerate(range(0, count, ROWS)):
        copies[n].wait()
        value = field[r : r + ROWS, :].astype(BF16)
        rounded[r : r + ROWS, :] = value
        lay(first + r, value)


def take_rows(v, first, count, early=(), pieces=0):
    rows, modes_k = v.shape
    shapes = [pltpu.VMEM((count, modes_k), F32), pltpu.VMEM((count, modes_k), BF16)]
    field, rounded, *by_channel = kernel_call(
        functools.partial(take_kernel, first),
        "take_rows",
        [v, *early],
        [IN_HBM] + [IN_VMEM] * len(early),
        shapes + [pltpu.VMEM((rows // max(pieces, 1), modes_k), BF16)] * pieces,
        scratch=[pltpu.SemaphoreType.DMA((count // ROWS,))],
    )
    return field, rounded, by_channel


def transform_kernel(build, awaited, *refs):
    take = taker(refs)
    chans = len(refs) - awaited - (14 if build else 13)
    x = take(chans)
    take(awaited)
    couple_far = take()
    tables_far = None if build else take(3)
    out = take()
    if build:
        tables_far, anal_m = take(3), take()
    one, phys, mixed, couple, synth_k, synth_mt, anal_kt, sems = take(8)
    near = (synth_k, synth_mt, anal_kt)
    _, modes_m, modes_k = out.shape
    load = pltpu.make_async_copy(couple_far, couple, sems.at[3])
    ends = [(n, f) if build else (f, n) for n, f in zip(near, tables_far)]
    moves = [pltpu.make_async_copy(src, dst, sems.at[i]) for i, (src, dst) in enumerate(ends)]
    if not build:
        for move in moves[:2]:
            move.start()
    load.start()
    if not build:
        moves[2].start()

    def ready(i, mode_axis, weighted):
        if build:
            fill_table(near[i], mode_axis, weighted)
            moves[i].start()
        else:
            moves[i].wait()

    ready(0, 0, False)
    for c in range(chans):

        @pl.loop(0, modes_m // ROWS)
        def _(i):
            at = pl.ds(pl.multiple_of(i * ROWS, ROWS), ROWS)
            one[c, at, :] = jnp.dot(x[c][at, :], synth_k[...], preferred_element_type=F32).astype(BF16)

    ready(1, 1, False)
    load.wait()

    @pl.loop(0, modes_k // COLS)
    def _(z):
        zs = pl.ds(pl.multiple_of(z * COLS, COLS), COLS)
        for j in range(chans):
            phys[j] = jnp.dot(synth_mt[...], one[j, :, zs], preferred_element_type=F32)

        @pl.loop(0, modes_m // BAND)
        def _(i):
            ts = pl.ds(pl.multiple_of(i * BAND, BAND), BAND)
            parts = [phys[j, ts, :] for j in range(chans)]
            for c in range(chans):
                total = couple[c, 0, ts, zs].astype(F32) * parts[0]
                for j in range(1, chans):
                    total += couple[c, j, ts, zs].astype(F32) * parts[j]
                mixed[c, ts, zs] = total.astype(BF16)

    ready(2, 1, True)
    for c in range(chans):

        @pl.loop(0, modes_m // ROWS)
        def _(i):
            at = pl.ds(pl.multiple_of(i * ROWS, ROWS), ROWS)
            out[c, at, :] = jnp.dot(mixed[c, at, :], anal_kt[...], preferred_element_type=F32).astype(BF16)

    if build:
        fill_table(anal_m, 0, True)
        for move in moves:
            move.wait()


def transform(x, couple, tables=None, awaited=()):
    chans, _, modes_m, modes_k = couple.shape
    shape = (chans, modes_m, modes_k)
    sizes = [(modes_k, modes_k), (modes_m, modes_m), (modes_k, modes_k)]
    build = tables is None
    far = [] if build else list(tables[:3])
    outs, out_specs = [pltpu.VMEM(shape, BF16)], [IN_VMEM]
    if build:
        outs += [pltpu.HBM(n, BF16) for n in sizes] + [pltpu.VMEM((modes_m, modes_m), BF16)]
        out_specs += [IN_HBM] * 3 + [IN_VMEM]
    result = kernel_call(
        functools.partial(transform_kernel, build, len(awaited)),
        "transform",
        [*x, *awaited, couple, *far],
        [IN_VMEM] * (chans + len(awaited)) + [IN_HBM] * (1 + len(far)),
        outs,
        out_specs=out_specs,
        scratch=[
            pltpu.VMEM(shape, BF16),
            pltpu.VMEM((chans, modes_m, COLS), F32),
            pltpu.VMEM(shape, BF16),
            pltpu.VMEM(couple.shape, BF16),
            *[pltpu.VMEM(n, BF16) for n in sizes],
            pltpu.SemaphoreType.DMA((4,)),
        ],
        limit=TRANSFORM_LIMIT,
        flops=MEDIUM if awaited else 1000,
    )
    return result[0], (result[1:] if build else tables)


def own_plane():
    return WINDOW_START + lax.axis_index("rad")


def paired_plane():
    return WINDOW_START + 1 - lax.axis_index("rad")


def inverse_divisor(row0, modes_m, modes_k, plane):
    m = lax.broadcasted_iota(jnp.int32, (BAND, 1), 0) + row0
    k = lax.broadcasted_iota(jnp.int32, (1, modes_k), 1)
    fm = jnp.where(m <= modes_m // 2, m, m - modes_m // 2).astype(F32) / F32(modes_m // 2)
    fk = jnp.where(k <= modes_k // 2, k, k - modes_k // 2).astype(F32) / F32(modes_k // 2)
    radius = (jnp.full((1, 1), plane, jnp.int32).astype(F32) + F32(0.5)) / F32(RADIAL_ALL)
    turning = F32(VISC_TURN) * fm * fm / (radius * radius)
    return F32(1.0) / (F32(1.0) + F32(VISC_AXIAL) * fk * fk + turning)


def one_tile(value):
    value = sum(value[r : r + 8] for r in range(0, value.shape[0], 8))
    return sum(value[:, k : k + 128] for k in range(0, value.shape[1], 128))


def add_tile(acc, n, value):
    acc[n] += one_tile(value)


def local_kernel(counts, last, paired, advect, *refs):
    take = taker(refs)
    v, vb, recv = (take(n) for n in counts[:3])
    two, anal_m = take(), take()
    if last:
        u0, out_b = take(counts[3]), []
        out, scale, gram, spec, acc = take(5)
        acc[...] = jnp.zeros_like(acc)
    else:
        out, out_b, spec = take(), take(counts[3]), take()
    chans, modes_m, modes_k = two.shape
    half = modes_k // 2
    for c in range(chans):
        spec[c] = jnp.dot(anal_m[...], two[c], preferred_element_type=F32)
    wave = lax.broadcasted_iota(jnp.int32, (1, half), 1).astype(F32) * advect[0]

    def step(lo, shift):
        at = pl.ds(pl.multiple_of(shift + lo, BAND), BAND)
        inv = inverse_divisor(shift + lo, modes_m, modes_k, own_plane())
        if last:
            scale[at, :] = inv * F32(RADIAL_GAIN)
            if paired:
                mate = inverse_divisor(shift + lo, modes_m, modes_k, paired_plane()) * F32(RADIAL_GAIN**2)
        for c in range(chans):
            row = c * modes_m + lo
            own = read(v, row, shift)
            drift = jnp.concatenate([-wave * own[:, half:], wave * own[:, :half]], axis=1)
            mid = F32(-2.0 * RADIAL_GAIN) * read(vb, row, shift).astype(F32)
            total = own + spec[c, at, :] + drift + mid
            if last:
                x0 = read(u0, row, shift)
                if paired:
                    total += mate * x0
                for n, (a, b) in enumerate(((x0, x0), (x0, own), (own, own))):
                    add_tile(acc, n, a * b)
            value = total * inv - read(recv, row, shift).astype(F32)
            write([out], row, shift, value)
            if not last:
                write(out_b, row, shift, value)

    for lo, hi in segments(modes_m, [*v, *(u0 if last else out_b)]):
        for_bands(lo, hi, functools.partial(step, lo))

    if last:
        gram[...] = jnp.zeros_like(gram)
        for n in range(3):
            gram[n : n + 1, :] = jnp.sum(acc[n], axis=0, keepdims=True)


def local_first(advect, v, vb, recv, two, tables, sizes):
    chans, modes_m, modes_k = two.shape
    args = [advect, *v, *vb, *recv, two, tables[3]]
    part, *part_b = kernel_call(
        functools.partial(local_kernel, (len(v), len(vb), len(recv), len(sizes)), False, False),
        "local_first",
        args,
        [IN_SMEM] + [IN_VMEM] * (len(args) - 1),
        [pltpu.VMEM((chans * modes_m, modes_k), F32)] + [pltpu.VMEM((n, modes_k), BF16) for n in sizes],
        scratch=[pltpu.VMEM(two.shape, F32)],
    )
    return part, part_b


def local_last(advect, v, vb, recv, two, tables, u0, paired):
    chans, modes_m, modes_k = two.shape
    args = [advect, *v, *vb, *recv, two, tables[3], *u0]
    return kernel_call(
        functools.partial(local_kernel, (len(v), len(vb), len(recv), len(u0)), True, paired),
        "local_last",
        args,
        [IN_SMEM] + [IN_VMEM] * (len(args) - 1),
        [
            pltpu.VMEM((chans * modes_m, modes_k), F32),
            pltpu.VMEM((modes_m, modes_k), F32),
            pltpu.VMEM((8, 128), F32),
        ],
        scratch=[pltpu.VMEM(two.shape, F32), pltpu.VMEM((3, 8, 128), F32)],
    )


def added(sides, row, shift):
    return functools.reduce(lambda a, b: a + b, [read(s, row, shift).astype(F32) for s in sides])


def first_kernel(groups, count, part, *refs):
    take = taker(refs)
    sides = [take(groups) for _ in range(count)]
    out, out_b = take(), take(len(refs) - groups * count - 1)
    chans, (modes_m, modes_k) = len(out_b), out_b[0].shape

    def step(lo, shift):
        inv = inverse_divisor(shift + lo, modes_m, modes_k, own_plane()) * F32(RADIAL_GAIN)
        for c in range(chans):
            row = c * modes_m + lo
            value = read([part], row, shift) + added(sides, row, shift) * inv
            write([out], row, shift, value)
            write(out_b, row, shift, value)

    for lo, hi in segments(modes_m, sides[0]):
        for_bands(lo, hi, functools.partial(step, lo))


def first_image(part, sides, chans):
    rows, modes_k = part.shape
    args = [part, *(x for side in sides for x in side)]
    return kernel_call(
        functools.partial(first_kernel, len(sides[0]), len(sides)),
        "first_image",
        args,
        [IN_VMEM] * len(args),
        [pltpu.VMEM(part.shape, F32)] + [pltpu.VMEM((rows // chans, modes_k), BF16)] * chans,
        flops=LONG,
    )


def on_diagonal():
    rows, lanes = (lax.broadcasted_iota(jnp.int32, (8, 128), n) for n in (0, 1))
    return rows == lanes


def second_kernel(first, counts, done, scale, u1, part, before, *refs):
    take = taker(refs)
    u0, planes = take(counts[0]), take(counts[1])
    out, gram, acc = take(3)
    modes_m = scale.shape[0]
    acc[...] = jnp.zeros_like(acc)

    def step(start, i):
        shift = pl.multiple_of(i * STEP, STEP)
        totals = [None] * 3
        for row in range(start, start + STEP, BAND):
            at = pl.ds(pl.multiple_of(shift + row % modes_m, BAND), BAND)
            near = added([[p] for p in planes], row - first, shift)
            x2 = read([part], row, shift) + near * scale[at, :]
            write([out], row - first, shift, x2)
            for n, x in enumerate((read(u0, row, shift), read([u1], row, shift), x2)):
                value = one_tile(x * x2)
                totals[n] = value if totals[n] is None else totals[n] + value
        for n in range(3):
            acc[n] += totals[n]

    end = first + out.shape[0]
    starts = {first, *starts_of(u0), *range(0, end, modes_m)}
    starts = [r for r in sorted(starts) if first <= r < end]
    for lo, hi in zip(starts, starts[1:] + [end]):
        pl.loop(0, (hi - lo) // STEP)(functools.partial(step, lo))

    rows = [jnp.sum(acc[n], axis=0, keepdims=True) for n in range(3)]
    total = before[...] + jnp.concatenate([jnp.zeros((3, 128), F32), *rows, jnp.zeros((2, 128), F32)], axis=0)
    if done:
        total = jnp.sum(total, axis=1, keepdims=True)
        total = jnp.sum(jnp.where(on_diagonal(), total, F32(0.0)), axis=0, keepdims=True)
    gram[...] = jnp.broadcast_to(total, gram.shape)


def second_image(first, scale, u0, u1, part, before, planes, slots=None):
    done = slots is not None
    tile = (slots, 128) if done else (8, 128)
    args = [scale, u1, part, before, *u0, *planes]
    return kernel_call(
        functools.partial(second_kernel, first, (len(u0), len(planes)), done),
        "second_image",
        args,
        [IN_VMEM] * len(args),
        [pltpu.VMEM(planes[0].shape, F32), pltpu.VMEM(tile, F32)],
        scratch=[pltpu.VMEM((3, 8, 128), F32)],
    )


def combine_kernel(cells, counts, grams, u1, *refs):
    take = taker(refs)
    u0, u2 = take(counts[0]), take(counts[1])
    out, hess_out, held, hess, sems = take(5)
    total, modes_k = out.shape
    g = jnp.sum(grams[...], axis=0, keepdims=True) * F32(1.0 / cells)
    g = jnp.sum(jnp.where(on_diagonal(), g, F32(0.0)), axis=1, keepdims=True)
    g = jnp.broadcast_to(g, (8, 128))
    g00, g01, g11, g02, g12, g22 = (g[n : n + 1, :] for n in range(6))
    per_g00 = F32(1.0) / g00
    h11 = g01 * per_g00
    q = g11 - h11 * g01
    per_q = F32(1.0) / q
    w0 = g02 - h11 * g01
    w1 = g12 - h11 * g11
    ww = g22 - F32(2.0) * h11 * g12 + h11 * h11 * g11
    h22 = (w1 - h11 * w0) * per_q
    ratio = w0 * per_g00
    square = (ww - w0 * ratio) * per_q - h22 * h22
    c2 = F32(1.0) / jnp.sqrt(q * square)
    c1 = -(h11 + h22) * c2
    c0 = (h11 * h22 - ratio) * c2
    wide = [jnp.concatenate([x] * (modes_k // 128), axis=1) for x in (c0, c1, c2)]

    def copy_out(n):
        at = pl.ds(pl.multiple_of(n * CHUNK, CHUNK), CHUNK)
        return pltpu.make_async_copy(held.at[at], out.at[at], sems.at[n])

    def step(first, n):
        for r in range(0, CHUNK, BAND):
            row, shift = first + r, pl.multiple_of(n * CHUNK, CHUNK)
            value = wide[0] * read(u0, row, shift) + wide[1] * read([u1], row, shift)
            write([held], row, shift, value + wide[2] * read(u2, row, shift))
        copy_out(n + first // CHUNK).start()

    starts = sorted({*starts_of(u0), *starts_of(u2)})
    for first, end in zip(starts, starts[1:] + [total]):
        pl.loop(0, (end - first) // CHUNK)(functools.partial(step, first))
    n0, s = jnp.sqrt(g00), jnp.sqrt(q)
    for n, value in enumerate((n0, h11, s / n0, w0 / (s * n0), h22, jnp.sqrt(square))):
        hess[n] = value[0, 0]
    last = pltpu.make_async_copy(hess, hess_out, sems.at[total // CHUNK])
    last.start()
    pl.loop(0, total // CHUNK)(lambda n: copy_out(n).wait())
    last.wait()


def combine(cells, grams, u0, u1, u2):
    args = [grams, u1, *u0, *u2]
    return kernel_call(
        functools.partial(combine_kernel, cells, (len(u0), len(u2))),
        "combine",
        args,
        [IN_VMEM] * len(args),
        [jax.ShapeDtypeStruct(u1.shape, F32), jax.ShapeDtypeStruct((6,), F32)],
        out_specs=[IN_HBM, IN_HBM],
        scratch=[
            pltpu.VMEM(u1.shape, F32),
            pltpu.SMEM((6,), F32),
            pltpu.SemaphoreType.DMA((u1.shape[0] // CHUNK + 1,)),
        ],
    )


def shifted(value, axis, steps):
    count = lax.axis_size(axis)
    return lax.ppermute(value, axis, [(i, (i + steps) % count) for i in range(count)])


def neighbour_planes(value, axis):
    count = lax.axis_size(axis)
    if count == 2:
        return [lax.ppermute(value, axis, [(0, 1), (1, 0)])]
    up = [(i, i + 1) for i in range(count - 1)]
    return [lax.ppermute(value, axis, up), lax.ppermute(value, axis, [(b, a) for a, b in up])]


def on_device(start_vector, coupling, advect):
    _, chans, rows_here, modes_m, modes_k = start_vector.shape
    assert rows_here == 1
    rows = chans * modes_m
    start = start_vector.reshape(rows, modes_k)
    couple = coupling.reshape(chans, chans, modes_m, modes_k)
    devices = lax.axis_size("seg") * lax.axis_size("rad")
    cells = float(devices * start.size)
    paired = lax.axis_size("rad") == 2

    early = EARLY_ROWS
    sizes = (rows - LATE_ROWS, LATE_ROWS) if paired else (modes_m,) * chans

    u0, u0b, near_one, pieces = [], [], [], None
    for first, size, parts in ((0, early, 0), (early, rows - early, chans)):
        field, rounded, pieces = take_rows(start, first, size, u0b, parts)
        u0.append(field)
        u0b.append(rounded)
        near_one.append(neighbour_planes(rounded, "rad"))
    next_one = [shifted(x, "seg", -1) for x in pieces]
    two, tables = transform(pieces, couple, awaited=near_one[0])
    part, part_b = local_first(advect, u0, pieces, next_one, two, tables, sizes)
    if paired:
        near_two = [neighbour_planes(x, "rad") for x in part_b]
    u1, *u1b = first_image(part, list(zip(*near_one)), chans)
    if not paired:
        near_two = [neighbour_planes(x, "rad") for x in u1b]
    next_two = [shifted(x, "seg", -1) for x in u1b]
    two, _ = transform(u1b, couple, tables)
    part, scale, gram = local_last(advect, [u1], u1b, next_two, two, tables, u0, paired)
    u2, first = [], 0
    for size, planes in zip(sizes, near_two):
        slots = devices if first + size == rows else None
        field, gram = second_image(first, scale, u0, u1, part, gram, planes, slots)
        first += size
        u2.append(field)
    grams = lax.all_to_all(gram, ("rad", "seg"), 0, 0)
    basis, hess = combine(cells, grams, u0, u1, u2)
    return basis.reshape(start_vector.shape), hess


def solution(mesh):
    return jax.shard_map(
        on_device,
        mesh=mesh,
        in_specs=(
            P("seg", None, "rad", None, None),
            P("seg", None, None, "rad", None, None),
            P("rad"),
        ),
        out_specs=(P("seg", None, "rad", None, None), P()),
        check_vma=False,
    )
```

```python
import functools
import math

import jax
import jax.numpy as jnp
from jax import lax
from jax.experimental import pallas as pl
from jax.experimental.pallas import tpu as pltpu
from jax.sharding import PartitionSpec as P

RADIAL_ALL = 256
WINDOW_START = 124
RADIAL_GAIN = 0.25
VISC_AXIAL = 4.0
VISC_TURN = 0.05

F32 = jnp.float32
BF16 = jnp.bfloat16
VMEM_LIMIT = 8 * 1024 * 1024
TRANSFORM_LIMIT = 22 * 1024 * 1024
ROWS = 128
COLS = 256
BAND = 16
LONG = 10**11
MEDIUM = 15 * 10**9
CHUNK = 128
STEP = 64
EARLY_ROWS = 128
LATE_ROWS = 128

IN_SMEM = pl.BlockSpec(memory_space=pltpu.SMEM)
IN_VMEM = pl.BlockSpec(memory_space=pltpu.VMEM)
IN_HBM = pl.BlockSpec(memory_space=pltpu.HBM)


def kernel_call(body, name, args, in_specs, outs, out_specs=None, scratch=(), limit=VMEM_LIMIT, flops=1000):
    held = [
        a if s is IN_SMEM else pltpu.with_memory_space_constraint(a, s.memory_space)
        for a, s in zip(args, in_specs)
    ]
    more = {} if out_specs is None else {"out_specs": out_specs}
    return pl.pallas_call(
        body,
        out_shape=outs,
        in_specs=in_specs,
        scratch_shapes=list(scratch),
        compiler_params=pltpu.CompilerParams(vmem_limit_bytes=limit),
        cost_estimate=pl.CostEstimate(flops=flops, bytes_accessed=1000, transcendentals=0),
        name=name,
        **more,
    )(*held)


def sine_turns(y):
    x = y * F32(2.0 * math.pi)
    x2 = x * x
    acc = F32(1.0 / 6227020800.0)
    for c in (-1.0 / 39916800.0, 1.0 / 362880.0, -1.0 / 5040.0, 1.0 / 120.0, -1.0 / 6.0, 1.0):
        acc = acc * x2 + F32(c)
    return acc * x


def trig_block(row0, rows, cols, mode_axis, count, weighted):
    half = count // 2
    r = lax.broadcasted_iota(jnp.int32, (rows, cols), 0) + row0
    c = lax.broadcasted_iota(jnp.int32, (rows, cols), 1)
    mode, point = (r, c) if mode_axis == 0 else (c, r)
    is_cos = mode <= half
    freq = jnp.where(is_cos, mode, mode - half).astype(F32)
    phase = freq * point.astype(F32) - jnp.where(is_cos, F32(0.0), F32(count // 4))
    phase = phase - F32(count) * jnp.floor(phase * F32(1.0 / count))
    value = -sine_turns(F32(0.25) - jnp.abs(phase * F32(1.0 / count) - F32(0.5)))
    if weighted:
        edge = (mode == 0) | (mode == half)
        value = value * jnp.where(edge, F32(1.0 / count), F32(2.0 / count))
    return value.astype(BF16)


def fill_table(ref, mode_axis, weighted):
    count = ref.shape[0]

    @pl.loop(0, count // ROWS)
    def _(i):
        at = pl.multiple_of(i * ROWS, ROWS)
        ref[pl.ds(at, ROWS), :] = trig_block(at, ROWS, count, mode_axis, count, weighted)


def taker(refs):
    refs = list(refs)

    def take(count=None):
        if count is None:
            return refs.pop(0)
        out, refs[:count] = refs[:count], []
        return out

    return take


def segments(modes_m, groups):
    ends, total = {modes_m}, 0
    for group in groups:
        total += group.shape[0]
        ends.add(total % modes_m or modes_m)
    ends = sorted(ends)
    return list(zip([0] + ends[:-1], ends))


def starts_of(groups):
    return [sum(g.shape[0] for g in groups[:n]) for n in range(len(groups))]


def band(groups, row, shift):
    for group in groups:
        if row < group.shape[0]:
            return group, pl.ds(pl.multiple_of(shift + row, BAND), BAND)
        row -= group.shape[0]


def read(groups, row, shift):
    group, at = band(groups, row, shift)
    return group[at, :]


def write(groups, row, shift, value):
    group, at = band(groups, row, shift)
    group[at, :] = value.astype(group.dtype)


def for_bands(lo, hi, body):
    @pl.loop(0, (hi - lo) // BAND)
    def _(i):
        body(pl.multiple_of(i * BAND, BAND))


def take_kernel(first, v, *refs):
    take = taker(refs)
    early = [] if first == 0 else [take()]
    field, rounded = take(), take()
    pieces, sems = take(len(refs) - len(early) - 3), take()
    count = field.shape[0]
    copies = []
    for n, r in enumerate(range(0, count, ROWS)):
        copies.append(
            pltpu.make_async_copy(v.at[pl.ds(first + r, ROWS)], field.at[pl.ds(r, ROWS)], sems.at[n])
        )
        copies[n].start()

    def lay(row, value):
        for n, piece in enumerate(pieces):
            at = row - n * piece.shape[0]
            if 0 <= at < piece.shape[0]:
                piece[at : at + ROWS, :] = value

    for r in range(0, first, ROWS):
        lay(r, early[0][r : r + ROWS, :])
    for n, r in enumerate(range(0, count, ROWS)):
        copies[n].wait()
        value = field[r : r + ROWS, :].astype(BF16)
        rounded[r : r + ROWS, :] = value
        lay(first + r, value)


def take_rows(v, first, count, early=(), pieces=0):
    rows, modes_k = v.shape
    shapes = [pltpu.VMEM((count, modes_k), F32), pltpu.VMEM((count, modes_k), BF16)]
    field, rounded, *by_channel = kernel_call(
        functools.partial(take_kernel, first),
        "take_rows",
        [v, *early],
        [IN_HBM] + [IN_VMEM] * len(early),
        shapes + [pltpu.VMEM((rows // max(pieces, 1), modes_k), BF16)] * pieces,
        scratch=[pltpu.SemaphoreType.DMA((count // ROWS,))],
    )
    return field, rounded, by_channel


def transform_kernel(build, awaited, *refs):
    take = taker(refs)
    chans = len(refs) - awaited - (14 if build else 13)
    x = take(chans)
    take(awaited)
    couple_far = take()
    tables_far = None if build else take(3)
    out = take()
    if build:
        tables_far, anal_m = take(3), take()
    one, phys, mixed, couple, synth_k, synth_mt, anal_kt, sems = take(8)
    near = (synth_k, synth_mt, anal_kt)
    _, modes_m, modes_k = out.shape
    load = pltpu.make_async_copy(couple_far, couple, sems.at[3])
    ends = [(n, f) if build else (f, n) for n, f in zip(near, tables_far)]
    moves = [pltpu.make_async_copy(src, dst, sems.at[i]) for i, (src, dst) in enumerate(ends)]
    if not build:
        for move in moves[:2]:
            move.start()
    load.start()
    if not build:
        moves[2].start()

    def ready(i, mode_axis, weighted):
        if build:
            fill_table(near[i], mode_axis, weighted)
            moves[i].start()
        else:
            moves[i].wait()

    ready(0, 0, False)
    for c in range(chans):

        @pl.loop(0, modes_m // ROWS)
        def _(i):
            at = pl.ds(pl.multiple_of(i * ROWS, ROWS), ROWS)
            one[c, at, :] = jnp.dot(x[c][at, :], synth_k[...], preferred_element_type=F32).astype(BF16)

    ready(1, 1, False)
    load.wait()

    @pl.loop(0, modes_k // COLS)
    def _(z):
        zs = pl.ds(pl.multiple_of(z * COLS, COLS), COLS)
        for j in range(chans):
            phys[j] = jnp.dot(synth_mt[...], one[j, :, zs], preferred_element_type=F32)

        @pl.loop(0, modes_m // BAND)
        def _(i):
            ts = pl.ds(pl.multiple_of(i * BAND, BAND), BAND)
            parts = [phys[j, ts, :] for j in range(chans)]
            for c in range(chans):
                total = couple[c, 0, ts, zs].astype(F32) * parts[0]
                for j in range(1, chans):
                    total += couple[c, j, ts, zs].astype(F32) * parts[j]
                mixed[c, ts, zs] = total.astype(BF16)

    ready(2, 1, True)
    for c in range(chans):

        @pl.loop(0, modes_m // ROWS)
        def _(i):
            at = pl.ds(pl.multiple_of(i * ROWS, ROWS), ROWS)
            out[c, at, :] = jnp.dot(mixed[c, at, :], anal_kt[...], preferred_element_type=F32).astype(BF16)

    if build:
        fill_table(anal_m, 0, True)
        for move in moves:
            move.wait()


def transform(x, couple, tables=None, awaited=()):
    chans, _, modes_m, modes_k = couple.shape
    shape = (chans, modes_m, modes_k)
    sizes = [(modes_k, modes_k), (modes_m, modes_m), (modes_k, modes_k)]
    build = tables is None
    far = [] if build else list(tables[:3])
    outs, out_specs = [pltpu.VMEM(shape, BF16)], [IN_VMEM]
    if build:
        outs += [pltpu.HBM(n, BF16) for n in sizes] + [pltpu.VMEM((modes_m, modes_m), BF16)]
        out_specs += [IN_HBM] * 3 + [IN_VMEM]
    result = kernel_call(
        functools.partial(transform_kernel, build, len(awaited)),
        "transform",
        [*x, *awaited, couple, *far],
        [IN_VMEM] * (chans + len(awaited)) + [IN_HBM] * (1 + len(far)),
        outs,
        out_specs=out_specs,
        scratch=[
            pltpu.VMEM(shape, BF16),
            pltpu.VMEM((chans, modes_m, COLS), F32),
            pltpu.VMEM(shape, BF16),
            pltpu.VMEM(couple.shape, BF16),
            *[pltpu.VMEM(n, BF16) for n in sizes],
            pltpu.SemaphoreType.DMA((4,)),
        ],
        limit=TRANSFORM_LIMIT,
        flops=MEDIUM if awaited else 1000,
    )
    return result[0], (result[1:] if build else tables)


def own_plane():
    return WINDOW_START + lax.axis_index("rad")


def paired_plane():
    return WINDOW_START + 1 - lax.axis_index("rad")


def inverse_divisor(row0, modes_m, modes_k, plane):
    m = lax.broadcasted_iota(jnp.int32, (BAND, 1), 0) + row0
    k = lax.broadcasted_iota(jnp.int32, (1, modes_k), 1)
    fm = jnp.where(m <= modes_m // 2, m, m - modes_m // 2).astype(F32) / F32(modes_m // 2)
    fk = jnp.where(k <= modes_k // 2, k, k - modes_k // 2).astype(F32) / F32(modes_k // 2)
    radius = (jnp.full((1, 1), plane, jnp.int32).astype(F32) + F32(0.5)) / F32(RADIAL_ALL)
    turning = F32(VISC_TURN) * fm * fm / (radius * radius)
    return F32(1.0) / (F32(1.0) + F32(VISC_AXIAL) * fk * fk + turning)


def one_tile(value):
    value = sum(value[r : r + 8] for r in range(0, value.shape[0], 8))
    return sum(value[:, k : k + 128] for k in range(0, value.shape[1], 128))


def add_tile(acc, n, value):
    acc[n] += one_tile(value)


def local_kernel(counts, last, paired, advect, *refs):
    take = taker(refs)
    v, vb, recv = (take(n) for n in counts[:3])
    two, anal_m = take(), take()
    if last:
        u0, out_b = take(counts[3]), []
        out, scale, gram, spec, acc = take(5)
        acc[...] = jnp.zeros_like(acc)
    else:
        out, out_b, spec = take(), take(counts[3]), take()
    chans, modes_m, modes_k = two.shape
    half = modes_k // 2
    for c in range(chans):
        spec[c] = jnp.dot(anal_m[...], two[c], preferred_element_type=F32)
    wave = lax.broadcasted_iota(jnp.int32, (1, half), 1).astype(F32) * advect[0]

    def step(lo, shift):
        at = pl.ds(pl.multiple_of(shift + lo, BAND), BAND)
        inv = inverse_divisor(shift + lo, modes_m, modes_k, own_plane())
        if last:
            scale[at, :] = inv * F32(RADIAL_GAIN)
            if paired:
                mate = inverse_divisor(shift + lo, modes_m, modes_k, paired_plane()) * F32(RADIAL_GAIN**2)
        for c in range(chans):
            row = c * modes_m + lo
            own = read(v, row, shift)
            drift = jnp.concatenate([-wave * own[:, half:], wave * own[:, :half]], axis=1)
            mid = F32(-2.0 * RADIAL_GAIN) * read(vb, row, shift).astype(F32)
            total = own + spec[c, at, :] + drift + mid
            if last:
                x0 = read(u0, row, shift)
                if paired:
                    total += mate * x0
                for n, (a, b) in enumerate(((x0, x0), (x0, own), (own, own))):
                    add_tile(acc, n, a * b)
            value = total * inv - read(recv, row, shift).astype(F32)
            write([out], row, shift, value)
            if not last:
                write(out_b, row, shift, value)

    for lo, hi in segments(modes_m, [*v, *(u0 if last else out_b)]):
        for_bands(lo, hi, functools.partial(step, lo))

    if last:
        gram[...] = jnp.zeros_like(gram)
        for n in range(3):
            gram[n : n + 1, :] = jnp.sum(acc[n], axis=0, keepdims=True)


def local_first(advect, v, vb, recv, two, tables, sizes):
    chans, modes_m, modes_k = two.shape
    args = [advect, *v, *vb, *recv, two, tables[3]]
    part, *part_b = kernel_call(
        functools.partial(local_kernel, (len(v), len(vb), len(recv), len(sizes)), False, False),
        "local_first",
        args,
        [IN_SMEM] + [IN_VMEM] * (len(args) - 1),
        [pltpu.VMEM((chans * modes_m, modes_k), F32)] + [pltpu.VMEM((n, modes_k), BF16) for n in sizes],
        scratch=[pltpu.VMEM(two.shape, F32)],
    )
    return part, part_b


def local_last(advect, v, vb, recv, two, tables, u0, paired):
    chans, modes_m, modes_k = two.shape
    args = [advect, *v, *vb, *recv, two, tables[3], *u0]
    return kernel_call(
        functools.partial(local_kernel, (len(v), len(vb), len(recv), len(u0)), True, paired),
        "local_last",
        args,
        [IN_SMEM] + [IN_VMEM] * (len(args) - 1),
        [
            pltpu.VMEM((chans * modes_m, modes_k), F32),
            pltpu.VMEM((modes_m, modes_k), F32),
            pltpu.VMEM((8, 128), F32),
        ],
        scratch=[pltpu.VMEM(two.shape, F32), pltpu.VMEM((3, 8, 128), F32)],
    )


def added(sides, row, shift):
    return functools.reduce(lambda a, b: a + b, [read(s, row, shift).astype(F32) for s in sides])


def first_kernel(groups, count, part, *refs):
    take = taker(refs)
    sides = [take(groups) for _ in range(count)]
    out, out_b = take(), take(len(refs) - groups * count - 1)
    chans, (modes_m, modes_k) = len(out_b), out_b[0].shape

    def step(lo, shift):
        inv = inverse_divisor(shift + lo, modes_m, modes_k, own_plane()) * F32(RADIAL_GAIN)
        for c in range(chans):
            row = c * modes_m + lo
            value = read([part], row, shift) + added(sides, row, shift) * inv
            write([out], row, shift, value)
            write(out_b, row, shift, value)

    for lo, hi in segments(modes_m, sides[0]):
        for_bands(lo, hi, functools.partial(step, lo))


def first_image(part, sides, chans):
    rows, modes_k = part.shape
    args = [part, *(x for side in sides for x in side)]
    return kernel_call(
        functools.partial(first_kernel, len(sides[0]), len(sides)),
        "first_image",
        args,
        [IN_VMEM] * len(args),
        [pltpu.VMEM(part.shape, F32)] + [pltpu.VMEM((rows // chans, modes_k), BF16)] * chans,
        flops=LONG,
    )


def on_diagonal():
    rows, lanes = (lax.broadcasted_iota(jnp.int32, (8, 128), n) for n in (0, 1))
    return rows == lanes


def second_kernel(first, counts, done, scale, u1, part, before, *refs):
    take = taker(refs)
    u0, planes = take(counts[0]), take(counts[1])
    out, gram, acc = take(3)
    modes_m = scale.shape[0]
    acc[...] = jnp.zeros_like(acc)

    def step(start, i):
        shift = pl.multiple_of(i * STEP, STEP)
        totals = [None] * 3
        for row in range(start, start + STEP, BAND):
            at = pl.ds(pl.multiple_of(shift + row % modes_m, BAND), BAND)
            near = added([[p] for p in planes], row - first, shift)
            x2 = read([part], row, shift) + near * scale[at, :]
            write([out], row - first, shift, x2)
            for n, x in enumerate((read(u0, row, shift), read([u1], row, shift), x2)):
                value = one_tile(x * x2)
                totals[n] = value if totals[n] is None else totals[n] + value
        for n in range(3):
            acc[n] += totals[n]

    end = first + out.shape[0]
    starts = {first, *starts_of(u0), *range(0, end, modes_m)}
    starts = [r for r in sorted(starts) if first <= r < end]
    for lo, hi in zip(starts, starts[1:] + [end]):
        pl.loop(0, (hi - lo) // STEP)(functools.partial(step, lo))

    rows = [jnp.sum(acc[n], axis=0, keepdims=True) for n in range(3)]
    total = before[...] + jnp.concatenate([jnp.zeros((3, 128), F32), *rows, jnp.zeros((2, 128), F32)], axis=0)
    if done:
        total = jnp.sum(total, axis=1, keepdims=True)
        total = jnp.sum(jnp.where(on_diagonal(), total, F32(0.0)), axis=0, keepdims=True)
    gram[...] = jnp.broadcast_to(total, gram.shape)


def second_image(first, scale, u0, u1, part, before, planes, slots=None):
    done = slots is not None
    tile = (slots, 128) if done else (8, 128)
    args = [scale, u1, part, before, *u0, *planes]
    return kernel_call(
        functools.partial(second_kernel, first, (len(u0), len(planes)), done),
        "second_image",
        args,
        [IN_VMEM] * len(args),
        [pltpu.VMEM(planes[0].shape, F32), pltpu.VMEM(tile, F32)],
        scratch=[pltpu.VMEM((3, 8, 128), F32)],
    )


def combine_kernel(cells, counts, grams, u1, *refs):
    take = taker(refs)
    u0, u2 = take(counts[0]), take(counts[1])
    out, hess_out, held, hess, sems = take(5)
    total, modes_k = out.shape
    g = jnp.sum(grams[...], axis=0, keepdims=True) * F32(1.0 / cells)
    g = jnp.sum(jnp.where(on_diagonal(), g, F32(0.0)), axis=1, keepdims=True)
    g = jnp.broadcast_to(g, (8, 128))
    g00, g01, g11, g02, g12, g22 = (g[n : n + 1, :] for n in range(6))
    per_g00 = F32(1.0) / g00
    h11 = g01 * per_g00
    q = g11 - h11 * g01
    per_q = F32(1.0) / q
    w0 = g02 - h11 * g01
    w1 = g12 - h11 * g11
    ww = g22 - F32(2.0) * h11 * g12 + h11 * h11 * g11
    h22 = (w1 - h11 * w0) * per_q
    ratio = w0 * per_g00
    square = (ww - w0 * ratio) * per_q - h22 * h22
    c2 = F32(1.0) / jnp.sqrt(q * square)
    c1 = -(h11 + h22) * c2
    c0 = (h11 * h22 - ratio) * c2
    wide = [jnp.concatenate([x] * (modes_k // 128), axis=1) for x in (c0, c1, c2)]

    def copy_out(n):
        at = pl.ds(pl.multiple_of(n * CHUNK, CHUNK), CHUNK)
        return pltpu.make_async_copy(held.at[at], out.at[at], sems.at[n])

    def step(first, n):
        for r in range(0, CHUNK, BAND):
            row, shift = first + r, pl.multiple_of(n * CHUNK, CHUNK)
            value = wide[0] * read(u0, row, shift) + wide[1] * read([u1], row, shift)
            write([held], row, shift, value + wide[2] * read(u2, row, shift))
        copy_out(n + first // CHUNK).start()

    starts = sorted({*starts_of(u0), *starts_of(u2)})
    for first, end in zip(starts, starts[1:] + [total]):
        pl.loop(0, (end - first) // CHUNK)(functools.partial(step, first))
    n0, s = jnp.sqrt(g00), jnp.sqrt(q)
    for n, value in enumerate((n0, h11, s / n0, w0 / (s * n0), h22, jnp.sqrt(square))):
        hess[n] = value[0, 0]
    last = pltpu.make_async_copy(hess, hess_out, sems.at[total // CHUNK])
    last.start()
    pl.loop(0, total // CHUNK)(lambda n: copy_out(n).wait())
    last.wait()


def combine(cells, grams, u0, u1, u2):
    args = [grams, u1, *u0, *u2]
    return kernel_call(
        functools.partial(combine_kernel, cells, (len(u0), len(u2))),
        "combine",
        args,
        [IN_VMEM] * len(args),
        [jax.ShapeDtypeStruct(u1.shape, F32), jax.ShapeDtypeStruct((6,), F32)],
        out_specs=[IN_HBM, IN_HBM],
        scratch=[
            pltpu.VMEM(u1.shape, F32),
            pltpu.SMEM((6,), F32),
            pltpu.SemaphoreType.DMA((u1.shape[0] // CHUNK + 1,)),
        ],
    )


def shifted(value, axis, steps):
    count = lax.axis_size(axis)
    return lax.ppermute(value, axis, [(i, (i + steps) % count) for i in range(count)])


def neighbour_planes(value, axis):
    count = lax.axis_size(axis)
    if count == 2:
        return [lax.ppermute(value, axis, [(0, 1), (1, 0)])]
    up = [(i, i + 1) for i in range(count - 1)]
    return [lax.ppermute(value, axis, up), lax.ppermute(value, axis, [(b, a) for a, b in up])]


def on_device(start_vector, coupling, advect):
    _, chans, rows_here, modes_m, modes_k = start_vector.shape
    assert rows_here == 1
    rows = chans * modes_m
    start = start_vector.reshape(rows, modes_k)
    couple = coupling.reshape(chans, chans, modes_m, modes_k)
    devices = lax.axis_size("seg") * lax.axis_size("rad")
    cells = float(devices * start.size)
    paired = lax.axis_size("rad") == 2

    early = EARLY_ROWS
    sizes = (rows - LATE_ROWS, LATE_ROWS) if paired else (modes_m,) * chans

    u0, u0b, near_one, pieces = [], [], [], None
    for first, size, parts in ((0, early, 0), (early, rows - early, chans)):
        field, rounded, pieces = take_rows(start, first, size, u0b, parts)
        u0.append(field)
        u0b.append(rounded)
        near_one.append(neighbour_planes(rounded, "rad"))
    next_one = [shifted(x, "seg", -1) for x in pieces]
    two, tables = transform(pieces, couple, awaited=near_one[0])
    part, part_b = local_first(advect, u0, pieces, next_one, two, tables, sizes)
    if paired:
        near_two = [neighbour_planes(x, "rad") for x in part_b]
    u1, *u1b = first_image(part, list(zip(*near_one)), chans)
    if not paired:
        near_two = [neighbour_planes(x, "rad") for x in u1b]
    next_two = [shifted(x, "seg", -1) for x in u1b]
    two, _ = transform(u1b, couple, tables)
    part, scale, gram = local_last(advect, [u1], u1b, next_two, two, tables, u0, paired)
    u2, first = [], 0
    for size, planes in zip(sizes, near_two):
        slots = devices if first + size == rows else None
        field, gram = second_image(first, scale, u0, u1, part, gram, planes, slots)
        first += size
        u2.append(field)
    grams = lax.all_to_all(gram, ("rad", "seg"), 0, 0)
    basis, hess = combine(cells, grams, u0, u1, u2)
    return basis.reshape(start_vector.shape), hess


def solution(mesh):
    return jax.shard_map(
        on_device,
        mesh=mesh,
        in_specs=(
            P("seg", None, "rad", None, None),
            P("seg", None, None, "rad", None, None),
            P("rad"),
        ),
        out_specs=(P("seg", None, "rad", None, None), P()),
        check_vma=False,
    )
```

```python
import functools
import math

import jax
import jax.numpy as jnp
from jax import lax
from jax.experimental import pallas as pl
from jax.experimental.pallas import tpu as pltpu
from jax.sharding import PartitionSpec as P

RADIAL_ALL = 256
WINDOW_START = 124
RADIAL_GAIN = 0.25
VISC_AXIAL = 4.0
VISC_TURN = 0.05

F32 = jnp.float32
BF16 = jnp.bfloat16
VMEM_LIMIT = 8 * 1024 * 1024
TRANSFORM_LIMIT = 22 * 1024 * 1024
ROWS = 128
COLS = 256
BAND = 16
LONG = 10**11
MEDIUM = 15 * 10**9
CHUNK = 128
STEP = 64
EARLY_ROWS = 128
LATE_ROWS = 128

IN_SMEM = pl.BlockSpec(memory_space=pltpu.SMEM)
IN_VMEM = pl.BlockSpec(memory_space=pltpu.VMEM)
IN_HBM = pl.BlockSpec(memory_space=pltpu.HBM)


def kernel_call(body, name, args, in_specs, outs, out_specs=None, scratch=(), limit=VMEM_LIMIT, flops=1000):
    held = [
        a if s is IN_SMEM else pltpu.with_memory_space_constraint(a, s.memory_space)
        for a, s in zip(args, in_specs)
    ]
    more = {} if out_specs is None else {"out_specs": out_specs}
    return pl.pallas_call(
        body,
        out_shape=outs,
        in_specs=in_specs,
        scratch_shapes=list(scratch),
        compiler_params=pltpu.CompilerParams(vmem_limit_bytes=limit),
        cost_estimate=pl.CostEstimate(flops=flops, bytes_accessed=1000, transcendentals=0),
        name=name,
        **more,
    )(*held)


def sine_turns(y):
    x = y * F32(2.0 * math.pi)
    x2 = x * x
    acc = F32(1.0 / 6227020800.0)
    for c in (-1.0 / 39916800.0, 1.0 / 362880.0, -1.0 / 5040.0, 1.0 / 120.0, -1.0 / 6.0, 1.0):
        acc = acc * x2 + F32(c)
    return acc * x


def trig_block(row0, rows, cols, mode_axis, count, weighted):
    half = count // 2
    r = lax.broadcasted_iota(jnp.int32, (rows, cols), 0) + row0
    c = lax.broadcasted_iota(jnp.int32, (rows, cols), 1)
    mode, point = (r, c) if mode_axis == 0 else (c, r)
    is_cos = mode <= half
    freq = jnp.where(is_cos, mode, mode - half).astype(F32)
    phase = freq * point.astype(F32) - jnp.where(is_cos, F32(0.0), F32(count // 4))
    phase = phase - F32(count) * jnp.floor(phase * F32(1.0 / count))
    value = -sine_turns(F32(0.25) - jnp.abs(phase * F32(1.0 / count) - F32(0.5)))
    if weighted:
        edge = (mode == 0) | (mode == half)
        value = value * jnp.where(edge, F32(1.0 / count), F32(2.0 / count))
    return value.astype(BF16)


def fill_table(ref, mode_axis, weighted):
    count = ref.shape[0]

    @pl.loop(0, count // ROWS)
    def _(i):
        at = pl.multiple_of(i * ROWS, ROWS)
        ref[pl.ds(at, ROWS), :] = trig_block(at, ROWS, count, mode_axis, count, weighted)


def taker(refs):
    refs = list(refs)

    def take(count=None):
        if count is None:
            return refs.pop(0)
        out, refs[:count] = refs[:count], []
        return out

    return take


def segments(modes_m, groups):
    ends, total = {modes_m}, 0
    for group in groups:
        total += group.shape[0]
        ends.add(total % modes_m or modes_m)
    ends = sorted(ends)
    return list(zip([0] + ends[:-1], ends))


def starts_of(groups):
    return [sum(g.shape[0] for g in groups[:n]) for n in range(len(groups))]


def band(groups, row, shift):
    for group in groups:
        if row < group.shape[0]:
            return group, pl.ds(pl.multiple_of(shift + row, BAND), BAND)
        row -= group.shape[0]


def read(groups, row, shift):
    group, at = band(groups, row, shift)
    return group[at, :]


def write(groups, row, shift, value):
    group, at = band(groups, row, shift)
    group[at, :] = value.astype(group.dtype)


def for_bands(lo, hi, body):
    @pl.loop(0, (hi - lo) // BAND)
    def _(i):
        body(pl.multiple_of(i * BAND, BAND))


def take_kernel(first, v, *refs):
    take = taker(refs)
    early = [] if first == 0 else [take()]
    field, rounded = take(), take()
    pieces, sems = take(len(refs) - len(early) - 3), take()
    count = field.shape[0]
    copies = []
    for n, r in enumerate(range(0, count, ROWS)):
        copies.append(
            pltpu.make_async_copy(v.at[pl.ds(first + r, ROWS)], field.at[pl.ds(r, ROWS)], sems.at[n])
        )
        copies[n].start()

    def lay(row, value):
        for n, piece in enumerate(pieces):
            at = row - n * piece.shape[0]
            if 0 <= at < piece.shape[0]:
                piece[at : at + ROWS, :] = value

    for r in range(0, first, ROWS):
        lay(r, early[0][r : r + ROWS, :])
    for n, r in enumerate(range(0, count, ROWS)):
        copies[n].wait()
        value = field[r : r + ROWS, :].astype(BF16)
        rounded[r : r + ROWS, :] = value
        lay(first + r, value)


def take_rows(v, first, count, early=(), pieces=0):
    rows, modes_k = v.shape
    shapes = [pltpu.VMEM((count, modes_k), F32), pltpu.VMEM((count, modes_k), BF16)]
    field, rounded, *by_channel = kernel_call(
        functools.partial(take_kernel, first),
        "take_rows",
        [v, *early],
        [IN_HBM] + [IN_VMEM] * len(early),
        shapes + [pltpu.VMEM((rows // max(pieces, 1), modes_k), BF16)] * pieces,
        scratch=[pltpu.SemaphoreType.DMA((count // ROWS,))],
    )
    return field, rounded, by_channel


def transform_kernel(build, awaited, *refs):
    take = taker(refs)
    chans = len(refs) - awaited - (14 if build else 13)
    x = take(chans)
    take(awaited)
    couple_far = take()
    tables_far = None if build else take(3)
    out = take()
    if build:
        tables_far, anal_m = take(3), take()
    one, phys, mixed, couple, synth_k, synth_mt, anal_kt, sems = take(8)
    near = (synth_k, synth_mt, anal_kt)
    _, modes_m, modes_k = out.shape
    load = pltpu.make_async_copy(couple_far, couple, sems.at[3])
    ends = [(n, f) if build else (f, n) for n, f in zip(near, tables_far)]
    moves = [pltpu.make_async_copy(src, dst, sems.at[i]) for i, (src, dst) in enumerate(ends)]
    if not build:
        for move in moves[:2]:
            move.start()
    load.start()
    if not build:
        moves[2].start()

    def ready(i, mode_axis, weighted):
        if build:
            fill_table(near[i], mode_axis, weighted)
            moves[i].start()
        else:
            moves[i].wait()

    ready(0, 0, False)
    for c in range(chans):

        @pl.loop(0, modes_m // ROWS)
        def _(i):
            at = pl.ds(pl.multiple_of(i * ROWS, ROWS), ROWS)
            one[c, at, :] = jnp.dot(x[c][at, :], synth_k[...], preferred_element_type=F32).astype(BF16)

    ready(1, 1, False)
    load.wait()

    @pl.loop(0, modes_k // COLS)
    def _(z):
        zs = pl.ds(pl.multiple_of(z * COLS, COLS), COLS)
        for j in range(chans):
            phys[j] = jnp.dot(synth_mt[...], one[j, :, zs], preferred_element_type=F32)

        @pl.loop(0, modes_m // BAND)
        def _(i):
            ts = pl.ds(pl.multiple_of(i * BAND, BAND), BAND)
            parts = [phys[j, ts, :] for j in range(chans)]
            for c in range(chans):
                total = couple[c, 0, ts, zs].astype(F32) * parts[0]
                for j in range(1, chans):
                    total += couple[c, j, ts, zs].astype(F32) * parts[j]
                mixed[c, ts, zs] = total.astype(BF16)

    ready(2, 1, True)
    for c in range(chans):

        @pl.loop(0, modes_m // ROWS)
        def _(i):
            at = pl.ds(pl.multiple_of(i * ROWS, ROWS), ROWS)
            out[c, at, :] = jnp.dot(mixed[c, at, :], anal_kt[...], preferred_element_type=F32).astype(BF16)

    if build:
        fill_table(anal_m, 0, True)
        for move in moves:
            move.wait()


def transform(x, couple, tables=None, awaited=()):
    chans, _, modes_m, modes_k = couple.shape
    shape = (chans, modes_m, modes_k)
    sizes = [(modes_k, modes_k), (modes_m, modes_m), (modes_k, modes_k)]
    build = tables is None
    far = [] if build else list(tables[:3])
    outs, out_specs = [pltpu.VMEM(shape, BF16)], [IN_VMEM]
    if build:
        outs += [pltpu.HBM(n, BF16) for n in sizes] + [pltpu.VMEM((modes_m, modes_m), BF16)]
        out_specs += [IN_HBM] * 3 + [IN_VMEM]
    result = kernel_call(
        functools.partial(transform_kernel, build, len(awaited)),
        "transform",
        [*x, *awaited, couple, *far],
        [IN_VMEM] * (chans + len(awaited)) + [IN_HBM] * (1 + len(far)),
        outs,
        out_specs=out_specs,
        scratch=[
            pltpu.VMEM(shape, BF16),
            pltpu.VMEM((chans, modes_m, COLS), F32),
            pltpu.VMEM(shape, BF16),
            pltpu.VMEM(couple.shape, BF16),
            *[pltpu.VMEM(n, BF16) for n in sizes],
            pltpu.SemaphoreType.DMA((4,)),
        ],
        limit=TRANSFORM_LIMIT,
        flops=MEDIUM if awaited else 1000,
    )
    return result[0], (result[1:] if build else tables)


def own_plane():
    return WINDOW_START + lax.axis_index("rad")


def paired_plane():
    return WINDOW_START + 1 - lax.axis_index("rad")


def inverse_divisor(row0, modes_m, modes_k, plane):
    m = lax.broadcasted_iota(jnp.int32, (BAND, 1), 0) + row0
    k = lax.broadcasted_iota(jnp.int32, (1, modes_k), 1)
    fm = jnp.where(m <= modes_m // 2, m, m - modes_m // 2).astype(F32) / F32(modes_m // 2)
    fk = jnp.where(k <= modes_k // 2, k, k - modes_k // 2).astype(F32) / F32(modes_k // 2)
    radius = (jnp.full((1, 1), plane, jnp.int32).astype(F32) + F32(0.5)) / F32(RADIAL_ALL)
    turning = F32(VISC_TURN) * fm * fm / (radius * radius)
    return F32(1.0) / (F32(1.0) + F32(VISC_AXIAL) * fk * fk + turning)


def one_tile(value):
    value = sum(value[r : r + 8] for r in range(0, value.shape[0], 8))
    return sum(value[:, k : k + 128] for k in range(0, value.shape[1], 128))


def add_tile(acc, n, value):
    acc[n] += one_tile(value)


def local_kernel(counts, last, paired, advect, *refs):
    take = taker(refs)
    v, vb, recv = (take(n) for n in counts[:3])
    two, anal_m = take(), take()
    if last:
        u0, out_b = take(counts[3]), []
        out, scale, gram, spec, acc = take(5)
        acc[...] = jnp.zeros_like(acc)
    else:
        out, out_b, spec = take(), take(counts[3]), take()
    chans, modes_m, modes_k = two.shape
    half = modes_k // 2
    for c in range(chans):
        spec[c] = jnp.dot(anal_m[...], two[c], preferred_element_type=F32)
    wave = lax.broadcasted_iota(jnp.int32, (1, half), 1).astype(F32) * advect[0]

    def step(lo, shift):
        at = pl.ds(pl.multiple_of(shift + lo, BAND), BAND)
        inv = inverse_divisor(shift + lo, modes_m, modes_k, own_plane())
        if last:
            scale[at, :] = inv * F32(RADIAL_GAIN)
            if paired:
                mate = inverse_divisor(shift + lo, modes_m, modes_k, paired_plane()) * F32(RADIAL_GAIN**2)
        for c in range(chans):
            row = c * modes_m + lo
            own = read(v, row, shift)
            drift = jnp.concatenate([-wave * own[:, half:], wave * own[:, :half]], axis=1)
            mid = F32(-2.0 * RADIAL_GAIN) * read(vb, row, shift).astype(F32)
            total = own + spec[c, at, :] + drift + mid
            if last:
                x0 = read(u0, row, shift)
                if paired:
                    total += mate * x0
                for n, (a, b) in enumerate(((x0, x0), (x0, own), (own, own))):
                    add_tile(acc, n, a * b)
            value = total * inv - read(recv, row, shift).astype(F32)
            write([out], row, shift, value)
            if not last:
                write(out_b, row, shift, value)

    for lo, hi in segments(modes_m, [*v, *(u0 if last else out_b)]):
        for_bands(lo, hi, functools.partial(step, lo))

    if last:
        gram[...] = jnp.zeros_like(gram)
        for n in range(3):
            gram[n : n + 1, :] = jnp.sum(acc[n], axis=0, keepdims=True)


def local_first(advect, v, vb, recv, two, tables, sizes):
    chans, modes_m, modes_k = two.shape
    args = [advect, *v, *vb, *recv, two, tables[3]]
    part, *part_b = kernel_call(
        functools.partial(local_kernel, (len(v), len(vb), len(recv), len(sizes)), False, False),
        "local_first",
        args,
        [IN_SMEM] + [IN_VMEM] * (len(args) - 1),
        [pltpu.VMEM((chans * modes_m, modes_k), F32)] + [pltpu.VMEM((n, modes_k), BF16) for n in sizes],
        scratch=[pltpu.VMEM(two.shape, F32)],
    )
    return part, part_b


def local_last(advect, v, vb, recv, two, tables, u0, paired):
    chans, modes_m, modes_k = two.shape
    args = [advect, *v, *vb, *recv, two, tables[3], *u0]
    return kernel_call(
        functools.partial(local_kernel, (len(v), len(vb), len(recv), len(u0)), True, paired),
        "local_last",
        args,
        [IN_SMEM] + [IN_VMEM] * (len(args) - 1),
        [
            pltpu.VMEM((chans * modes_m, modes_k), F32),
            pltpu.VMEM((modes_m, modes_k), F32),
            pltpu.VMEM((8, 128), F32),
        ],
        scratch=[pltpu.VMEM(two.shape, F32), pltpu.VMEM((3, 8, 128), F32)],
    )


def added(sides, row, shift):
    return functools.reduce(lambda a, b: a + b, [read(s, row, shift).astype(F32) for s in sides])


def first_kernel(groups, count, part, *refs):
    take = taker(refs)
    sides = [take(groups) for _ in range(count)]
    out, out_b = take(), take(len(refs) - groups * count - 1)
    chans, (modes_m, modes_k) = len(out_b), out_b[0].shape

    def step(lo, shift):
        inv = inverse_divisor(shift + lo, modes_m, modes_k, own_plane()) * F32(RADIAL_GAIN)
        for c in range(chans):
            row = c * modes_m + lo
            value = read([part], row, shift) + added(sides, row, shift) * inv
            write([out], row, shift, value)
            write(out_b, row, shift, value)

    for lo, hi in segments(modes_m, sides[0]):
        for_bands(lo, hi, functools.partial(step, lo))


def first_image(part, sides, chans):
    rows, modes_k = part.shape
    args = [part, *(x for side in sides for x in side)]
    return kernel_call(
        functools.partial(first_kernel, len(sides[0]), len(sides)),
        "first_image",
        args,
        [IN_VMEM] * len(args),
        [pltpu.VMEM(part.shape, F32)] + [pltpu.VMEM((rows // chans, modes_k), BF16)] * chans,
        flops=LONG,
    )


def on_diagonal():
    rows, lanes = (lax.broadcasted_iota(jnp.int32, (8, 128), n) for n in (0, 1))
    return rows == lanes


def second_kernel(first, counts, done, scale, u1, part, before, *refs):
    take = taker(refs)
    u0, planes = take(counts[0]), take(counts[1])
    out, gram, acc = take(3)
    modes_m = scale.shape[0]
    acc[...] = jnp.zeros_like(acc)

    def step(start, i):
        shift = pl.multiple_of(i * STEP, STEP)
        totals = [None] * 3
        for row in range(start, start + STEP, BAND):
            at = pl.ds(pl.multiple_of(shift + row % modes_m, BAND), BAND)
            near = added([[p] for p in planes], row - first, shift)
            x2 = read([part], row, shift) + near * scale[at, :]
            write([out], row - first, shift, x2)
            for n, x in enumerate((read(u0, row, shift), read([u1], row, shift), x2)):
                value = one_tile(x * x2)
                totals[n] = value if totals[n] is None else totals[n] + value
        for n in range(3):
            acc[n] += totals[n]

    end = first + out.shape[0]
    starts = {first, *starts_of(u0), *range(0, end, modes_m)}
    starts = [r for r in sorted(starts) if first <= r < end]
    for lo, hi in zip(starts, starts[1:] + [end]):
        pl.loop(0, (hi - lo) // STEP)(functools.partial(step, lo))

    rows = [jnp.sum(acc[n], axis=0, keepdims=True) for n in range(3)]
    total = before[...] + jnp.concatenate([jnp.zeros((3, 128), F32), *rows, jnp.zeros((2, 128), F32)], axis=0)
    if done:
        total = jnp.sum(total, axis=1, keepdims=True)
        total = jnp.sum(jnp.where(on_diagonal(), total, F32(0.0)), axis=0, keepdims=True)
    gram[...] = jnp.broadcast_to(total, gram.shape)


def second_image(first, scale, u0, u1, part, before, planes, slots=None):
    done = slots is not None
    tile = (slots, 128) if done else (8, 128)
    args = [scale, u1, part, before, *u0, *planes]
    return kernel_call(
        functools.partial(second_kernel, first, (len(u0), len(planes)), done),
        "second_image",
        args,
        [IN_VMEM] * len(args),
        [pltpu.VMEM(planes[0].shape, F32), pltpu.VMEM(tile, F32)],
        scratch=[pltpu.VMEM((3, 8, 128), F32)],
    )


def combine_kernel(cells, counts, grams, u1, *refs):
    take = taker(refs)
    u0, u2 = take(counts[0]), take(counts[1])
    out, hess_out, held, hess, sems = take(5)
    total, modes_k = out.shape
    g = jnp.sum(grams[...], axis=0, keepdims=True) * F32(1.0 / cells)
    g = jnp.sum(jnp.where(on_diagonal(), g, F32(0.0)), axis=1, keepdims=True)
    g = jnp.broadcast_to(g, (8, 128))
    g00, g01, g11, g02, g12, g22 = (g[n : n + 1, :] for n in range(6))
    per_g00 = F32(1.0) / g00
    h11 = g01 * per_g00
    q = g11 - h11 * g01
    per_q = F32(1.0) / q
    w0 = g02 - h11 * g01
    w1 = g12 - h11 * g11
    ww = g22 - F32(2.0) * h11 * g12 + h11 * h11 * g11
    h22 = (w1 - h11 * w0) * per_q
    ratio = w0 * per_g00
    square = (ww - w0 * ratio) * per_q - h22 * h22
    c2 = F32(1.0) / jnp.sqrt(q * square)
    c1 = -(h11 + h22) * c2
    c0 = (h11 * h22 - ratio) * c2
    wide = [jnp.concatenate([x] * (modes_k // 128), axis=1) for x in (c0, c1, c2)]

    def copy_out(row, count, n):
        at = pl.ds(pl.multiple_of(row, count), count)
        return pltpu.make_async_copy(held.at[at], out.at[at], sems.at[n])

    def step(first, count, sem, n):
        for r in range(0, count, BAND):
            row, shift = first + r, pl.multiple_of(n * count, count)
            value = wide[0] * read(u0, row, shift) + wide[1] * read([u1], row, shift)
            write([held], row, shift, value + wide[2] * read(u2, row, shift))
        copy_out(first + n * count, count, sem + n).start()

    starts = sorted({*starts_of(u0), *starts_of(u2)})
    spans, sem = [], 0
    for first, end in zip(starts, starts[1:] + [total]):
        count = CHUNK // 2 if first == 0 else CHUNK
        spans.append((first, count, sem, (end - first) // count))
        sem += (end - first) // count
    for first, count, sem, steps in spans:
        pl.loop(0, steps)(functools.partial(step, first, count, sem))
    n0, s = jnp.sqrt(g00), jnp.sqrt(q)
    for n, value in enumerate((n0, h11, s / n0, w0 / (s * n0), h22, jnp.sqrt(square))):
        hess[n] = value[0, 0]
    last = pltpu.make_async_copy(hess, hess_out, sems.at[sems.shape[0] - 1])
    last.start()
    for first, count, sem, steps in spans:
        for n in range(steps):
            copy_out(first + n * count, count, sem + n).wait()
    last.wait()


def combine(cells, grams, u0, u1, u2):
    args = [grams, u1, *u0, *u2]
    return kernel_call(
        functools.partial(combine_kernel, cells, (len(u0), len(u2))),
        "combine",
        args,
        [IN_VMEM] * len(args),
        [jax.ShapeDtypeStruct(u1.shape, F32), jax.ShapeDtypeStruct((6,), F32)],
        out_specs=[IN_HBM, IN_HBM],
        scratch=[
            pltpu.VMEM(u1.shape, F32),
            pltpu.SMEM((6,), F32),
            pltpu.SemaphoreType.DMA((2 * (u1.shape[0] // CHUNK) + 1,)),
        ],
    )


def shifted(value, axis, steps):
    count = lax.axis_size(axis)
    return lax.ppermute(value, axis, [(i, (i + steps) % count) for i in range(count)])


def neighbour_planes(value, axis):
    count = lax.axis_size(axis)
    if count == 2:
        return [lax.ppermute(value, axis, [(0, 1), (1, 0)])]
    up = [(i, i + 1) for i in range(count - 1)]
    return [lax.ppermute(value, axis, up), lax.ppermute(value, axis, [(b, a) for a, b in up])]


def on_device(start_vector, coupling, advect):
    _, chans, rows_here, modes_m, modes_k = start_vector.shape
    assert rows_here == 1
    rows = chans * modes_m
    start = start_vector.reshape(rows, modes_k)
    couple = coupling.reshape(chans, chans, modes_m, modes_k)
    devices = lax.axis_size("seg") * lax.axis_size("rad")
    cells = float(devices * start.size)
    paired = lax.axis_size("rad") == 2

    early = EARLY_ROWS
    sizes = (rows - LATE_ROWS, LATE_ROWS) if paired else (modes_m,) * chans

    u0, u0b, near_one, pieces = [], [], [], None
    for first, size, parts in ((0, early, 0), (early, rows - early, chans)):
        field, rounded, pieces = take_rows(start, first, size, u0b, parts)
        u0.append(field)
        u0b.append(rounded)
        near_one.append(neighbour_planes(rounded, "rad"))
    next_one = [shifted(x, "seg", -1) for x in pieces]
    two, tables = transform(pieces, couple, awaited=near_one[0])
    part, part_b = local_first(advect, u0, pieces, next_one, two, tables, sizes)
    if paired:
        near_two = [neighbour_planes(x, "rad") for x in part_b]
    u1, *u1b = first_image(part, list(zip(*near_one)), chans)
    if not paired:
        near_two = [neighbour_planes(x, "rad") for x in u1b]
    next_two = [shifted(x, "seg", -1) for x in u1b]
    two, _ = transform(u1b, couple, tables)
    part, scale, gram = local_last(advect, [u1], u1b, next_two, two, tables, u0, paired)
    u2, first = [], 0
    for size, planes in zip(sizes, near_two):
        slots = devices if first + size == rows else None
        field, gram = second_image(first, scale, u0, u1, part, gram, planes, slots)
        first += size
        u2.append(field)
    grams = lax.all_to_all(gram, ("rad", "seg"), 0, 0)
    basis, hess = combine(cells, grams, u0, u1, u2)
    return basis.reshape(start_vector.shape), hess


def solution(mesh):
    return jax.shard_map(
        on_device,
        mesh=mesh,
        in_specs=(
            P("seg", None, "rad", None, None),
            P("seg", None, None, "rad", None, None),
            P("rad"),
        ),
        out_specs=(P("seg", None, "rad", None, None), P()),
        check_vma=False,
    )
```

```python
import functools
import math

import jax
import jax.numpy as jnp
from jax import lax
from jax.experimental import pallas as pl
from jax.experimental.pallas import tpu as pltpu
from jax.sharding import PartitionSpec as P

RADIAL_ALL = 256
WINDOW_START = 124
RADIAL_GAIN = 0.25
VISC_AXIAL = 4.0
VISC_TURN = 0.05

F32 = jnp.float32
BF16 = jnp.bfloat16
VMEM_LIMIT = 8 * 1024 * 1024
TRANSFORM_LIMIT = 22 * 1024 * 1024
ROWS = 128
COLS = 256
BAND = 16
LONG = 10**11
MEDIUM = 15 * 10**9
CHUNK = 128
STEP = 128
EARLY_ROWS = 128
LATE_ROWS = 128

IN_SMEM = pl.BlockSpec(memory_space=pltpu.SMEM)
IN_VMEM = pl.BlockSpec(memory_space=pltpu.VMEM)
IN_HBM = pl.BlockSpec(memory_space=pltpu.HBM)


def kernel_call(body, name, args, in_specs, outs, out_specs=None, scratch=(), limit=VMEM_LIMIT, flops=1000):
    held = [
        a if s is IN_SMEM else pltpu.with_memory_space_constraint(a, s.memory_space)
        for a, s in zip(args, in_specs)
    ]
    more = {} if out_specs is None else {"out_specs": out_specs}
    return pl.pallas_call(
        body,
        out_shape=outs,
        in_specs=in_specs,
        scratch_shapes=list(scratch),
        compiler_params=pltpu.CompilerParams(vmem_limit_bytes=limit),
        cost_estimate=pl.CostEstimate(flops=flops, bytes_accessed=1000, transcendentals=0),
        name=name,
        **more,
    )(*held)


def sine_turns(y):
    x = y * F32(2.0 * math.pi)
    x2 = x * x
    acc = F32(1.0 / 6227020800.0)
    for c in (-1.0 / 39916800.0, 1.0 / 362880.0, -1.0 / 5040.0, 1.0 / 120.0, -1.0 / 6.0, 1.0):
        acc = acc * x2 + F32(c)
    return acc * x


def trig_block(row0, rows, cols, mode_axis, count, weighted):
    half = count // 2
    r = lax.broadcasted_iota(jnp.int32, (rows, cols), 0) + row0
    c = lax.broadcasted_iota(jnp.int32, (rows, cols), 1)
    mode, point = (r, c) if mode_axis == 0 else (c, r)
    is_cos = mode <= half
    freq = jnp.where(is_cos, mode, mode - half).astype(F32)
    phase = freq * point.astype(F32) - jnp.where(is_cos, F32(0.0), F32(count // 4))
    phase = phase - F32(count) * jnp.floor(phase * F32(1.0 / count))
    value = -sine_turns(F32(0.25) - jnp.abs(phase * F32(1.0 / count) - F32(0.5)))
    if weighted:
        edge = (mode == 0) | (mode == half)
        value = value * jnp.where(edge, F32(1.0 / count), F32(2.0 / count))
    return value.astype(BF16)


def fill_table(ref, mode_axis, weighted):
    count = ref.shape[0]

    @pl.loop(0, count // ROWS)
    def _(i):
        at = pl.multiple_of(i * ROWS, ROWS)
        ref[pl.ds(at, ROWS), :] = trig_block(at, ROWS, count, mode_axis, count, weighted)


def taker(refs):
    refs = list(refs)

    def take(count=None):
        if count is None:
            return refs.pop(0)
        out, refs[:count] = refs[:count], []
        return out

    return take


def segments(modes_m, groups):
    ends, total = {modes_m}, 0
    for group in groups:
        total += group.shape[0]
        ends.add(total % modes_m or modes_m)
    ends = sorted(ends)
    return list(zip([0] + ends[:-1], ends))


def starts_of(groups):
    return [sum(g.shape[0] for g in groups[:n]) for n in range(len(groups))]


def band(groups, row, shift):
    for group in groups:
        if row < group.shape[0]:
            return group, pl.ds(pl.multiple_of(shift + row, BAND), BAND)
        row -= group.shape[0]


def read(groups, row, shift):
    group, at = band(groups, row, shift)
    return group[at, :]


def write(groups, row, shift, value):
    group, at = band(groups, row, shift)
    group[at, :] = value.astype(group.dtype)


def for_bands(lo, hi, body):
    @pl.loop(0, (hi - lo) // BAND)
    def _(i):
        body(pl.multiple_of(i * BAND, BAND))


def take_kernel(first, v, *refs):
    take = taker(refs)
    early = [] if first == 0 else [take()]
    field, rounded = take(), take()
    pieces, sems = take(len(refs) - len(early) - 3), take()
    count = field.shape[0]
    copies = []
    for n, r in enumerate(range(0, count, ROWS)):
        copies.append(
            pltpu.make_async_copy(v.at[pl.ds(first + r, ROWS)], field.at[pl.ds(r, ROWS)], sems.at[n])
        )
        copies[n].start()

    def lay(row, value):
        for n, piece in enumerate(pieces):
            at = row - n * piece.shape[0]
            if 0 <= at < piece.shape[0]:
                piece[at : at + ROWS, :] = value

    for r in range(0, first, ROWS):
        lay(r, early[0][r : r + ROWS, :])
    for n, r in enumerate(range(0, count, ROWS)):
        copies[n].wait()
        value = field[r : r + ROWS, :].astype(BF16)
        rounded[r : r + ROWS, :] = value
        lay(first + r, value)


def take_rows(v, first, count, early=(), pieces=0):
    rows, modes_k = v.shape
    shapes = [pltpu.VMEM((count, modes_k), F32), pltpu.VMEM((count, modes_k), BF16)]
    field, rounded, *by_channel = kernel_call(
        functools.partial(take_kernel, first),
        "take_rows",
        [v, *early],
        [IN_HBM] + [IN_VMEM] * len(early),
        shapes + [pltpu.VMEM((rows // max(pieces, 1), modes_k), BF16)] * pieces,
        scratch=[pltpu.SemaphoreType.DMA((count // ROWS,))],
    )
    return field, rounded, by_channel


def transform_kernel(build, awaited, *refs):
    take = taker(refs)
    chans = len(refs) - awaited - (14 if build else 13)
    x = take(chans)
    take(awaited)
    couple_far = take()
    tables_far = None if build else take(3)
    out = take()
    if build:
        tables_far, anal_m = take(3), take()
    one, phys, mixed, couple, synth_k, synth_mt, anal_kt, sems = take(8)
    near = (synth_k, synth_mt, anal_kt)
    _, modes_m, modes_k = out.shape
    load = pltpu.make_async_copy(couple_far, couple, sems.at[3])
    ends = [(n, f) if build else (f, n) for n, f in zip(near, tables_far)]
    moves = [pltpu.make_async_copy(src, dst, sems.at[i]) for i, (src, dst) in enumerate(ends)]
    if not build:
        for move in moves[:2]:
            move.start()
    load.start()
    if not build:
        moves[2].start()

    def ready(i, mode_axis, weighted):
        if build:
            fill_table(near[i], mode_axis, weighted)
            moves[i].start()
        else:
            moves[i].wait()

    ready(0, 0, False)
    for c in range(chans):

        @pl.loop(0, modes_m // ROWS)
        def _(i):
            at = pl.ds(pl.multiple_of(i * ROWS, ROWS), ROWS)
            one[c, at, :] = jnp.dot(x[c][at, :], synth_k[...], preferred_element_type=F32).astype(BF16)

    ready(1, 1, False)
    load.wait()

    @pl.loop(0, modes_k // COLS)
    def _(z):
        zs = pl.ds(pl.multiple_of(z * COLS, COLS), COLS)
        for j in range(chans):
            phys[j] = jnp.dot(synth_mt[...], one[j, :, zs], preferred_element_type=F32)

        @pl.loop(0, modes_m // BAND)
        def _(i):
            ts = pl.ds(pl.multiple_of(i * BAND, BAND), BAND)
            parts = [phys[j, ts, :] for j in range(chans)]
            for c in range(chans):
                total = couple[c, 0, ts, zs].astype(F32) * parts[0]
                for j in range(1, chans):
                    total += couple[c, j, ts, zs].astype(F32) * parts[j]
                mixed[c, ts, zs] = total.astype(BF16)

    ready(2, 1, True)
    for c in range(chans):

        @pl.loop(0, modes_m // ROWS)
        def _(i):
            at = pl.ds(pl.multiple_of(i * ROWS, ROWS), ROWS)
            out[c, at, :] = jnp.dot(mixed[c, at, :], anal_kt[...], preferred_element_type=F32).astype(BF16)

    if build:
        fill_table(anal_m, 0, True)
        for move in moves:
            move.wait()


def transform(x, couple, tables=None, awaited=()):
    chans, _, modes_m, modes_k = couple.shape
    shape = (chans, modes_m, modes_k)
    sizes = [(modes_k, modes_k), (modes_m, modes_m), (modes_k, modes_k)]
    build = tables is None
    far = [] if build else list(tables[:3])
    outs, out_specs = [pltpu.VMEM(shape, BF16)], [IN_VMEM]
    if build:
        outs += [pltpu.HBM(n, BF16) for n in sizes] + [pltpu.VMEM((modes_m, modes_m), BF16)]
        out_specs += [IN_HBM] * 3 + [IN_VMEM]
    result = kernel_call(
        functools.partial(transform_kernel, build, len(awaited)),
        "transform",
        [*x, *awaited, couple, *far],
        [IN_VMEM] * (chans + len(awaited)) + [IN_HBM] * (1 + len(far)),
        outs,
        out_specs=out_specs,
        scratch=[
            pltpu.VMEM(shape, BF16),
            pltpu.VMEM((chans, modes_m, COLS), F32),
            pltpu.VMEM(shape, BF16),
            pltpu.VMEM(couple.shape, BF16),
            *[pltpu.VMEM(n, BF16) for n in sizes],
            pltpu.SemaphoreType.DMA((4,)),
        ],
        limit=TRANSFORM_LIMIT,
        flops=MEDIUM if awaited else 1000,
    )
    return result[0], (result[1:] if build else tables)


def own_plane():
    return WINDOW_START + lax.axis_index("rad")


def paired_plane():
    return WINDOW_START + 1 - lax.axis_index("rad")


def inverse_divisor(row0, modes_m, modes_k, plane):
    m = lax.broadcasted_iota(jnp.int32, (BAND, 1), 0) + row0
    k = lax.broadcasted_iota(jnp.int32, (1, modes_k), 1)
    fm = jnp.where(m <= modes_m // 2, m, m - modes_m // 2).astype(F32) / F32(modes_m // 2)
    fk = jnp.where(k <= modes_k // 2, k, k - modes_k // 2).astype(F32) / F32(modes_k // 2)
    radius = (jnp.full((1, 1), plane, jnp.int32).astype(F32) + F32(0.5)) / F32(RADIAL_ALL)
    turning = F32(VISC_TURN) * fm * fm / (radius * radius)
    return F32(1.0) / (F32(1.0) + F32(VISC_AXIAL) * fk * fk + turning)


def one_tile(value):
    value = sum(value[r : r + 8] for r in range(0, value.shape[0], 8))
    return sum(value[:, k : k + 128] for k in range(0, value.shape[1], 128))


def add_tile(acc, n, value):
    acc[n] += one_tile(value)


def local_kernel(counts, last, paired, advect, *refs):
    take = taker(refs)
    v, vb, recv = (take(n) for n in counts[:3])
    two, anal_m = take(), take()
    if last:
        u0, out_b = take(counts[3]), []
        out, scale, gram, spec, acc = take(5)
        acc[...] = jnp.zeros_like(acc)
    else:
        out, out_b, spec = take(), take(counts[3]), take()
    chans, modes_m, modes_k = two.shape
    half = modes_k // 2
    for c in range(chans):
        spec[c] = jnp.dot(anal_m[...], two[c], preferred_element_type=F32)
    wave = lax.broadcasted_iota(jnp.int32, (1, half), 1).astype(F32) * advect[0]

    def step(lo, shift):
        at = pl.ds(pl.multiple_of(shift + lo, BAND), BAND)
        inv = inverse_divisor(shift + lo, modes_m, modes_k, own_plane())
        if last:
            scale[at, :] = inv * F32(RADIAL_GAIN)
            if paired:
                mate = inverse_divisor(shift + lo, modes_m, modes_k, paired_plane()) * F32(RADIAL_GAIN**2)
        for c in range(chans):
            row = c * modes_m + lo
            own = read(v, row, shift)
            drift = jnp.concatenate([-wave * own[:, half:], wave * own[:, :half]], axis=1)
            mid = F32(-2.0 * RADIAL_GAIN) * read(vb, row, shift).astype(F32)
            total = own + spec[c, at, :] + drift + mid
            if last:
                x0 = read(u0, row, shift)
                if paired:
                    total += mate * x0
                for n, (a, b) in enumerate(((x0, x0), (x0, own), (own, own))):
                    add_tile(acc, n, a * b)
            value = total * inv - read(recv, row, shift).astype(F32)
            write([out], row, shift, value)
            if not last:
                write(out_b, row, shift, value)

    for lo, hi in segments(modes_m, [*v, *(u0 if last else out_b)]):
        for_bands(lo, hi, functools.partial(step, lo))

    if last:
        gram[...] = jnp.zeros_like(gram)
        for n in range(3):
            gram[n : n + 1, :] = jnp.sum(acc[n], axis=0, keepdims=True)


def local_first(advect, v, vb, recv, two, tables, sizes):
    chans, modes_m, modes_k = two.shape
    args = [advect, *v, *vb, *recv, two, tables[3]]
    part, *part_b = kernel_call(
        functools.partial(local_kernel, (len(v), len(vb), len(recv), len(sizes)), False, False),
        "local_first",
        args,
        [IN_SMEM] + [IN_VMEM] * (len(args) - 1),
        [pltpu.VMEM((chans * modes_m, modes_k), F32)] + [pltpu.VMEM((n, modes_k), BF16) for n in sizes],
        scratch=[pltpu.VMEM(two.shape, F32)],
    )
    return part, part_b


def local_last(advect, v, vb, recv, two, tables, u0, paired):
    chans, modes_m, modes_k = two.shape
    args = [advect, *v, *vb, *recv, two, tables[3], *u0]
    return kernel_call(
        functools.partial(local_kernel, (len(v), len(vb), len(recv), len(u0)), True, paired),
        "local_last",
        args,
        [IN_SMEM] + [IN_VMEM] * (len(args) - 1),
        [
            pltpu.VMEM((chans * modes_m, modes_k), F32),
            pltpu.VMEM((modes_m, modes_k), F32),
            pltpu.VMEM((8, 128), F32),
        ],
        scratch=[pltpu.VMEM(two.shape, F32), pltpu.VMEM((3, 8, 128), F32)],
    )


def added(sides, row, shift):
    return functools.reduce(lambda a, b: a + b, [read(s, row, shift).astype(F32) for s in sides])


def first_kernel(groups, count, part, *refs):
    take = taker(refs)
    sides = [take(groups) for _ in range(count)]
    out, out_b = take(), take(len(refs) - groups * count - 1)
    chans, (modes_m, modes_k) = len(out_b), out_b[0].shape

    def step(lo, shift):
        inv = inverse_divisor(shift + lo, modes_m, modes_k, own_plane()) * F32(RADIAL_GAIN)
        for c in range(chans):
            row = c * modes_m + lo
            value = read([part], row, shift) + added(sides, row, shift) * inv
            write([out], row, shift, value)
            write(out_b, row, shift, value)

    for lo, hi in segments(modes_m, sides[0]):
        for_bands(lo, hi, functools.partial(step, lo))


def first_image(part, sides, chans):
    rows, modes_k = part.shape
    args = [part, *(x for side in sides for x in side)]
    return kernel_call(
        functools.partial(first_kernel, len(sides[0]), len(sides)),
        "first_image",
        args,
        [IN_VMEM] * len(args),
        [pltpu.VMEM(part.shape, F32)] + [pltpu.VMEM((rows // chans, modes_k), BF16)] * chans,
        flops=LONG,
    )


def on_diagonal():
    rows, lanes = (lax.broadcasted_iota(jnp.int32, (8, 128), n) for n in (0, 1))
    return rows == lanes


def second_kernel(first, counts, done, scale, u1, part, before, *refs):
    take = taker(refs)
    u0, planes = take(counts[0]), take(counts[1])
    out, gram, acc = take(3)
    modes_m = scale.shape[0]
    acc[...] = jnp.zeros_like(acc)

    def step(start, i):
        shift = pl.multiple_of(i * STEP, STEP)
        totals = [None] * 3
        for row in range(start, start + STEP, BAND):
            at = pl.ds(pl.multiple_of(shift + row % modes_m, BAND), BAND)
            near = added([[p] for p in planes], row - first, shift)
            x2 = read([part], row, shift) + near * scale[at, :]
            write([out], row - first, shift, x2)
            for n, x in enumerate((read(u0, row, shift), read([u1], row, shift), x2)):
                value = one_tile(x * x2)
                totals[n] = value if totals[n] is None else totals[n] + value
        for n in range(3):
            acc[n] += totals[n]

    end = first + out.shape[0]
    starts = {first, *starts_of(u0), *range(0, end, modes_m)}
    starts = [r for r in sorted(starts) if first <= r < end]
    for lo, hi in zip(starts, starts[1:] + [end]):
        pl.loop(0, (hi - lo) // STEP)(functools.partial(step, lo))

    rows = [jnp.sum(acc[n], axis=0, keepdims=True) for n in range(3)]
    total = before[...] + jnp.concatenate([jnp.zeros((3, 128), F32), *rows, jnp.zeros((2, 128), F32)], axis=0)
    if done:
        total = jnp.sum(total, axis=1, keepdims=True)
        total = jnp.sum(jnp.where(on_diagonal(), total, F32(0.0)), axis=0, keepdims=True)
    gram[...] = jnp.broadcast_to(total, gram.shape)


def second_image(first, scale, u0, u1, part, before, planes, slots=None):
    done = slots is not None
    tile = (slots, 128) if done else (8, 128)
    args = [scale, u1, part, before, *u0, *planes]
    return kernel_call(
        functools.partial(second_kernel, first, (len(u0), len(planes)), done),
        "second_image",
        args,
        [IN_VMEM] * len(args),
        [pltpu.VMEM(planes[0].shape, F32), pltpu.VMEM(tile, F32)],
        scratch=[pltpu.VMEM((3, 8, 128), F32)],
    )


def combine_kernel(cells, counts, grams, u1, *refs):
    take = taker(refs)
    u0, u2 = take(counts[0]), take(counts[1])
    out, hess_out, held, hess, sems = take(5)
    total, modes_k = out.shape
    g = jnp.sum(grams[...], axis=0, keepdims=True) * F32(1.0 / cells)
    g = jnp.sum(jnp.where(on_diagonal(), g, F32(0.0)), axis=1, keepdims=True)
    g = jnp.broadcast_to(g, (8, 128))
    g00, g01, g11, g02, g12, g22 = (g[n : n + 1, :] for n in range(6))
    per_g00 = F32(1.0) / g00
    h11 = g01 * per_g00
    q = g11 - h11 * g01
    per_q = F32(1.0) / q
    w0 = g02 - h11 * g01
    w1 = g12 - h11 * g11
    ww = g22 - F32(2.0) * h11 * g12 + h11 * h11 * g11
    h22 = (w1 - h11 * w0) * per_q
    ratio = w0 * per_g00
    square = (ww - w0 * ratio) * per_q - h22 * h22
    c2 = F32(1.0) / jnp.sqrt(q * square)
    c1 = -(h11 + h22) * c2
    c0 = (h11 * h22 - ratio) * c2
    wide = [jnp.concatenate([x] * (modes_k // 128), axis=1) for x in (c0, c1, c2)]

    def copy_out(n):
        at = pl.ds(pl.multiple_of(n * CHUNK, CHUNK), CHUNK)
        return pltpu.make_async_copy(held.at[at], out.at[at], sems.at[n])

    def step(first, n):
        for r in range(0, CHUNK, BAND):
            row, shift = first + r, pl.multiple_of(n * CHUNK, CHUNK)
            value = wide[0] * read(u0, row, shift) + wide[1] * read([u1], row, shift)
            write([held], row, shift, value + wide[2] * read(u2, row, shift))
        copy_out(n + first // CHUNK).start()

    starts = sorted({*starts_of(u0), *starts_of(u2)})
    for first, end in zip(starts, starts[1:] + [total]):
        pl.loop(0, (end - first) // CHUNK)(functools.partial(step, first))
    n0, s = jnp.sqrt(g00), jnp.sqrt(q)
    for n, value in enumerate((n0, h11, s / n0, w0 / (s * n0), h22, jnp.sqrt(square))):
        hess[n] = value[0, 0]
    last = pltpu.make_async_copy(hess, hess_out, sems.at[total // CHUNK])
    last.start()
    pl.loop(0, total // CHUNK)(lambda n: copy_out(n).wait())
    last.wait()


def combine(cells, grams, u0, u1, u2):
    args = [grams, u1, *u0, *u2]
    return kernel_call(
        functools.partial(combine_kernel, cells, (len(u0), len(u2))),
        "combine",
        args,
        [IN_VMEM] * len(args),
        [jax.ShapeDtypeStruct(u1.shape, F32), jax.ShapeDtypeStruct((6,), F32)],
        out_specs=[IN_HBM, IN_HBM],
        scratch=[
            pltpu.VMEM(u1.shape, F32),
            pltpu.SMEM((6,), F32),
            pltpu.SemaphoreType.DMA((u1.shape[0] // CHUNK + 1,)),
        ],
    )


def shifted(value, axis, steps):
    count = lax.axis_size(axis)
    return lax.ppermute(value, axis, [(i, (i + steps) % count) for i in range(count)])


def neighbour_planes(value, axis):
    count = lax.axis_size(axis)
    if count == 2:
        return [lax.ppermute(value, axis, [(0, 1), (1, 0)])]
    up = [(i, i + 1) for i in range(count - 1)]
    return [lax.ppermute(value, axis, up), lax.ppermute(value, axis, [(b, a) for a, b in up])]


def on_device(start_vector, coupling, advect):
    _, chans, rows_here, modes_m, modes_k = start_vector.shape
    assert rows_here == 1
    rows = chans * modes_m
    start = start_vector.reshape(rows, modes_k)
    couple = coupling.reshape(chans, chans, modes_m, modes_k)
    devices = lax.axis_size("seg") * lax.axis_size("rad")
    cells = float(devices * start.size)
    paired = lax.axis_size("rad") == 2

    early = EARLY_ROWS
    sizes = (rows - LATE_ROWS, LATE_ROWS) if paired else (modes_m,) * chans

    u0, u0b, near_one, pieces = [], [], [], None
    for first, size, parts in ((0, early, 0), (early, rows - early, chans)):
        field, rounded, pieces = take_rows(start, first, size, u0b, parts)
        u0.append(field)
        u0b.append(rounded)
        near_one.append(neighbour_planes(rounded, "rad"))
    next_one = [shifted(x, "seg", -1) for x in pieces]
    two, tables = transform(pieces, couple, awaited=near_one[0])
    part, part_b = local_first(advect, u0, pieces, next_one, two, tables, sizes)
    if paired:
        near_two = [neighbour_planes(x, "rad") for x in part_b]
    u1, *u1b = first_image(part, list(zip(*near_one)), chans)
    if not paired:
        near_two = [neighbour_planes(x, "rad") for x in u1b]
    next_two = [shifted(x, "seg", -1) for x in u1b]
    two, _ = transform(u1b, couple, tables)
    part, scale, gram = local_last(advect, [u1], u1b, next_two, two, tables, u0, paired)
    u2, first = [], 0
    for size, planes in zip(sizes, near_two):
        slots = devices if first + size == rows else None
        field, gram = second_image(first, scale, u0, u1, part, gram, planes, slots)
        first += size
        u2.append(field)
    grams = lax.all_to_all(gram, ("rad", "seg"), 0, 0)
    basis, hess = combine(cells, grams, u0, u1, u2)
    return basis.reshape(start_vector.shape), hess


def solution(mesh):
    return jax.shard_map(
        on_device,
        mesh=mesh,
        in_specs=(
            P("seg", None, "rad", None, None),
            P("seg", None, None, "rad", None, None),
            P("rad"),
        ),
        out_specs=(P("seg", None, "rad", None, None), P()),
        check_vma=False,
    )
```
